32 devices in a mesh: blk: 8 (over y, x, core), tp: 4 (over z).
Axes of the slice: x: 2, y: 2, z: 4, core: 2. Of those that a mesh axis runs over, the one named last changes fastest.
Arguments:
- patches: float32 [2048, 768], P('blk'), may hold values from -6 to 6
- window_ids: int32 [2048], replicated, may hold values from 0 to 31, as said below
- lead_index: int32 [2048], P('blk'), may hold values from 0 to 15
- lead_table: bfloat16 [16, 768], replicated, may hold values from -4 to 4
- attention_gain: float32 [768], replicated, may hold values from 0.5 to 1.5
- attention_bias: float32 [768], replicated, may hold values from -2 to 2
- query_key_value: bfloat16 [3, 768, 768], P(None, None, 'tp'), may hold values from -0.21875 to 0.21875
- out_weight: bfloat16 [768, 768], P('tp'), may hold values from -1.25 to 1.25
- feedforward_gain: float32 [768], replicated, may hold values from 0.5 to 1.5
- feedforward_bias: float32 [768], replicated, may hold values from -2 to 2
- up_weight: bfloat16 [768, 3072], P(None, 'tp'), may hold values from -0.21875 to 0.21875
- down_weight: bfloat16 [3072, 768], P('tp'), may hold values from -0.109375 to 0.109375
- gate_head: bfloat16 [3, 16, 768], P(None, 'tp'), may hold values from -0.109375 to 0.109375
- pixel_mask: int32 [16, 2048], P('tp', 'blk'), may hold values from 0 to 1
- cotangent: float32 [2048, 768], P('blk'), may hold values from -6 to 6
Outputs:
- block_out: float32 [2048, 768], P('blk')
- penalty: float32 [], replicated
- grad_patches: float32 [2048, 768], P('blk')
- grad_lead_table: float32 [16, 768], replicated
- grad_attention_gain: float32 [768], replicated
- grad_attention_bias: float32 [768], replicated
- grad_query_key_value: float32 [3, 768, 768], P(None, None, 'tp')
- grad_out_weight: float32 [768, 768], P('tp')
- grad_feedforward_gain: float32 [768], replicated
- grad_feedforward_bias: float32 [768], replicated
- grad_up_weight: float32 [768, 3072], P(None, 'tp')
- grad_down_weight: float32 [3072, 768], P('tp')
- grad_gate_head: float32 [3, 16, 768], P(None, 'tp')
The draws below stay inside these ranges and needn't reach their ends.
Inputs may be any that keep to these rules, and one draw needn't show every extreme that they name: `window_ids`: equal values mark the patches of one regional window; patch t lies in band t // 256; one window in every draw has patches in every band.
All inputs are finite; a program needn't handle non-finite values.
Results may differ from the reference program's by a relative error of at most 0.018.
Values may be sent and summed in bfloat16 or wider, within the bound.
A program may use at most 192 MiB of HBM per device.

```python
import math
import jax
import jax.numpy as jnp
from jax import lax

D = 768
HEADS = 12
HEAD_DIM = 64
FF = 3072
EXPERTS = 3
PIX = 16
LEADS = 16
COLS = 4
TOK_DEV = 256
TOKENS = 2048
PIXELS = 32768
N_BLK = 8


def draw_window_ids(key, part):
    key = jax.random.fold_in(key, 7)
    cut_key, start_key, span_key = jax.random.split(key, 3)
    cut_points = jnp.sort(jax.random.permutation(cut_key, TOK_DEV - 1)[:COLS - 1] + 1)
    columns = jnp.arange(TOK_DEV, dtype=jnp.int32)
    column_group = jnp.sum((columns[:, None] >= cut_points[None, :]).astype(jnp.int32), axis=1)
    band_index = jnp.arange(N_BLK, dtype=jnp.int32)
    group_index = jnp.arange(COLS, dtype=jnp.int32)
    window_start = jax.random.randint(start_key, (COLS, N_BLK), 0, 3) == 0
    spanning = jax.random.randint(span_key, (), 0, COLS - 1)
    window_start = jnp.where(group_index[:, None] == spanning, False, window_start)
    window_start = window_start | (group_index[:, None] == COLS - 1) & (band_index[None, :] == N_BLK - 1)
    window_start = window_start | (band_index[None, :] == 0)
    first_band = lax.cummax(jnp.where(window_start, band_index[None, :], 0), axis=1)
    window_ids = column_group[None, :] * N_BLK + jnp.transpose(first_band)[:, column_group]
    return window_ids.reshape(TOKENS).astype(jnp.int32)


def draw_pixel_mask(key, part):
    key = jax.random.fold_in(key, 11)
    band_of = jnp.arange(TOKENS, dtype=jnp.int32) // TOK_DEV
    threshold = 250 + 700 * band_of // max(N_BLK - 1, 1)
    rolled = jax.random.randint(key, (PIX, TOKENS), 0, 1000)
    return (rolled < threshold[None, :]).astype(jnp.int32)


def plant(drawn, own_key, least, largest):
    extent = drawn.shape
    place = [jax.random.randint(jax.random.fold_in(own_key, axis), (), 0, extent[axis]) for axis in range(len(extent))]
    drawn = drawn.at[tuple(place)].set(least)
    longest = extent.index(max(extent))
    place[longest] = (place[longest] + 1) % extent[longest]
    return drawn.at[tuple(place)].set(largest)


def steps_of(rng, extent, cuts, low, largest):
    def one(dim, shards_of):
        draws = jax.random.uniform(jax.random.fold_in(jax.random.fold_in(rng, 6), dim), (shards_of,), jnp.float32, low / len(cuts), largest / len(cuts))
        return jnp.repeat(jnp.exp(draws), extent[dim] // shards_of).reshape((-1,) + (1,) * (len(extent) - dim - 1))

    loudness = one(*cuts[0])
    for cut in cuts[1:]:
        loudness = loudness * one(*cut)
    return loudness


def centred(key, extent, deviation, most, pieces=(), kind=jnp.bfloat16):
    drawn = deviation * jax.random.normal(key, extent, jnp.float32)
    if pieces:
        drawn = drawn * steps_of(key, extent, pieces, -0.22, 0.18)
    return jnp.clip(drawn, -most, most).astype(kind)


def setup_inputs(seed: int = 0) -> dict:
    key_list = jax.random.split(jax.random.key(seed), 16)
    return {
        "patches": centred(key_list[0], (TOKENS, D), 1.0, 6.0, ((0, 8),), jnp.float32),
        "window_ids": draw_window_ids(jax.random.fold_in(key_list[15], 71), 0),
        "lead_index": plant(jax.random.randint(key_list[2], (TOKENS,), 0, LEADS), jax.random.fold_in(key_list[2], 1), 0, LEADS - 1).astype(jnp.int32),
        "lead_table": centred(key_list[3], (LEADS, D), 0.5, 4.0),
        "attention_gain": jnp.clip(1.0 + 0.1 * jax.random.normal(key_list[4], (D,), jnp.float32), 0.5, 1.5),
        "attention_bias": centred(key_list[5], (D,), 0.3, 2.0, (), jnp.float32),
        "query_key_value": centred(key_list[6], (3, D, D), D ** -0.5, 0.21875, ((2, 4),)),
        "out_weight": centred(key_list[7], (D, D), (D // 32) ** -0.5, 1.25, ((0, 4),)),
        "feedforward_gain": jnp.clip(1.0 + 0.1 * jax.random.normal(key_list[8], (D,), jnp.float32), 0.5, 1.5),
        "feedforward_bias": centred(key_list[9], (D,), 0.3, 2.0, (), jnp.float32),
        "up_weight": centred(key_list[10], (D, FF), D ** -0.5, 0.21875, ((1, 4),)),
        "down_weight": centred(key_list[11], (FF, D), FF ** -0.5, 0.109375, ((0, 4),)),
        "gate_head": centred(key_list[12], (EXPERTS, PIX, D), (4 * D) ** -0.5, 0.109375, ((1, 4),)),
        "pixel_mask": draw_pixel_mask(jax.random.fold_in(key_list[15], 71), 0),
        "cotangent": centred(key_list[14], (TOKENS, D), 1.0, 6.0, ((0, 8),), jnp.float32),
    }


@jax.custom_vjp
def low(v):
    return lax.optimization_barrier(v.astype(jnp.bfloat16)).astype(jnp.float32)

@jax.custom_vjp
def low_back(v):
    return v

def low_keep(v):
    return (low(v), None)

def low_pass(kept, grad):
    return (grad,)

def back_keep(v):
    return (v, None)

def back_low(kept, grad):
    return (low(grad),)
low.defvjp(low_keep, low_pass)
low_back.defvjp(back_keep, back_low)
HIGH = lax.Precision.HIGHEST
EPS = 1e-05
MASKED = -1e+30

def layer_norm(values, gain_vector, bias_vector):
    row_mean = lax.optimization_barrier(jnp.mean(values, axis=-1, keepdims=True))
    centered = values - row_mean
    variance = lax.optimization_barrier(jnp.mean(centered * centered, axis=-1, keepdims=True))
    return centered * lax.rsqrt(variance + EPS) * gain_vector + bias_vector

def attend(queries, key_rows, value_rows, window_ids):
    block_size = math.gcd(TOKENS, 256)
    query_blocks = queries.reshape(TOKENS // block_size, block_size, HEADS, HEAD_DIM)
    id_blocks = window_ids.reshape(TOKENS // block_size, block_size)
    score_scale = HEAD_DIM ** (-0.5)

    def one_block(operands):
        query_block, id_block = operands
        products = low_back(jnp.einsum('qhd,khd->hqk', query_block, key_rows, precision=HIGH))
        allowed = (id_block[:, None] == window_ids[None, :])[None]
        scores = jnp.where(allowed, products * score_scale, MASKED)
        weights = low(jax.nn.softmax(scores, axis=-1))
        return jnp.einsum('hqk,khd->qhd', weights, value_rows, precision=HIGH)
    outputs = lax.map(jax.checkpoint(one_block), (query_blocks, id_blocks))
    return outputs.reshape(TOKENS, HEADS * HEAD_DIM)

def forward(patches, lead_table, attention_gain, attention_bias, query_key_value, out_weight, feedforward_gain, feedforward_bias, up_weight, down_weight, gate_head, lead_index, window_ids, mask_float):
    hidden = patches + lead_table[lead_index]
    normed = low(layer_norm(hidden, attention_gain, attention_bias))
    projected = low(low_back(jnp.einsum('td,cde->cte', normed, query_key_value, precision=HIGH)))
    queries = projected[0].reshape(TOKENS, HEADS, HEAD_DIM)
    key_rows = projected[1].reshape(TOKENS, HEADS, HEAD_DIM)
    value_rows = projected[2].reshape(TOKENS, HEADS, HEAD_DIM)
    attended = low(low_back(attend(queries, key_rows, value_rows, window_ids)))
    branch = low_back(jnp.dot(attended, out_weight, precision=HIGH))
    middle = hidden + branch
    normed_two = low(layer_norm(middle, feedforward_gain, feedforward_bias))
    upward = low_back(jnp.dot(normed_two, up_weight, precision=HIGH))
    activated = low(jax.nn.gelu(upward, approximate=False))
    feedforward = low_back(jnp.dot(activated, down_weight, precision=HIGH))
    block_out = middle + feedforward
    logits = low_back(jnp.einsum('epd,td->ept', gate_head, low(block_out), precision=HIGH))
    log_probs = jax.nn.log_softmax(logits, axis=0)
    entropy = -lax.optimization_barrier(jnp.sum(jnp.exp(log_probs) * log_probs, axis=0))
    penalty = jnp.sum(mask_float * entropy) / jnp.sum(mask_float)
    return (block_out, penalty)

def reference(patches, window_ids, lead_index, lead_table, attention_gain, attention_bias, query_key_value, out_weight, feedforward_gain, feedforward_bias, up_weight, down_weight, gate_head, pixel_mask, cotangent):
    mask_float = pixel_mask.astype(jnp.float32)

    def objective_parts(patches, lead_table, attention_gain, attention_bias, query_key_value, out_weight, feedforward_gain, feedforward_bias, up_weight, down_weight, gate_head):
        return forward(patches, lead_table, attention_gain, attention_bias, query_key_value, out_weight, feedforward_gain, feedforward_bias, up_weight, down_weight, gate_head, lead_index, window_ids, mask_float)
    floats = (patches, lead_table.astype(jnp.float32), attention_gain, attention_bias, query_key_value.astype(jnp.float32), out_weight.astype(jnp.float32), feedforward_gain, feedforward_bias, up_weight.astype(jnp.float32), down_weight.astype(jnp.float32), gate_head.astype(jnp.float32))
    (block_out, penalty), pull_back = jax.vjp(objective_parts, *floats)
    grads = pull_back((cotangent, jnp.ones_like(penalty) * PIXELS))
    return (block_out, penalty, grads[0], grads[1], grads[2], grads[3], grads[4], grads[5], grads[6], grads[7], grads[8], grads[9], grads[10])
```

```python
from functools import partial
from types import SimpleNamespace

import jax
import jax.numpy as jnp
from jax import lax
from jax.experimental import pallas as pl
from jax.experimental.pallas import tpu as pltpu
from jax.sharding import PartitionSpec as P

HEAD_DIM = 64
EPS = 1e-05
MASKED = -1e30
SCALE = HEAD_DIM ** (-0.5)
GROUP = 8
F32 = jnp.float32
BF16 = jnp.bfloat16
MESH = pl.DeviceIdType.MESH
VMEM_LIMIT = 61 * 2**20
INV_SQRT2 = 0.7071067811865476
INV_SQRT_2PI = 0.3989422804014327


def dot(a, b, ca, cb):
    return lax.dot_general(a, b, (((ca,), (cb,)), ((), ())), preferred_element_type=F32)


def mm_nn(a, b):
    return dot(a, b, 1, 0)


def mm_nt(a, b):
    return dot(a, b, 1, 1)


def mm_tn(a, b):
    return dot(a, b, 0, 0)


def norm_stats(values):
    mean = jnp.mean(values, axis=-1, keepdims=True)
    centered = values - mean
    inverse = lax.rsqrt(jnp.mean(centered * centered, axis=-1, keepdims=True) + EPS)
    return centered * inverse, inverse


def norm_backward(incoming, unit_rows, inverse, gain):
    scaled = incoming * gain
    return inverse * (
        scaled
        - jnp.mean(scaled, axis=-1, keepdims=True)
        - unit_rows * jnp.mean(scaled * unit_rows, axis=-1, keepdims=True)
    )


def total(x):
    return jnp.sum(jnp.sum(x, axis=0, keepdims=True), axis=1, keepdims=True)


def dims_of(nb, nt, tokens, width, local_width, hidden, leads, pixels):
    s = SimpleNamespace(nb=nb, nt=nt, L=tokens, D=width, W=local_width, F=hidden, leads=leads)
    s.H = local_width // HEAD_DIM
    s.S = tokens // nt
    s.half = nb // 2
    s.groups = nb // GROUP
    s.pixels = pixels
    s.sizes = (hidden + width, local_width * 4)
    s.bases = (0, s.sizes[0])
    s.rows = sum(s.sizes)
    s.tail = (leads + 4 + 15) // 16 * 16
    return s


def scratch_of(s):
    L, D, W, F, nb, nt, S = s.L, s.D, s.W, s.F, s.nb, s.nt, s.S
    v = pltpu.VMEM
    out = {
        "patches": v((L, D), F32),
        "qkv": v((3, D, W), BF16),
        "ow": v((nt, W, D), BF16),
        "up": v((D, F), BF16),
        "down": v((F, D), BF16),
        "cot": v((L, D), F32),
        "gate": v((nt * 32, D), BF16),
        "mask": v((nt, 8, L), F32),
        "cnt": v((nb, 8, 128), F32),
        "u1": v((L, D), F32),
        "r1": v((L, 1), F32),
        "normed": v((L, D), BF16),
        "kv": v((nb, 2 * W, L), BF16),
        "qd": v((nb, 2 * W, L), BF16),
        "st": v((nb, 8, L), F32),
        "m": v((8, L), F32),
        "l": v((8, L), F32),
        "acc": v((W, L), F32),
        "att": v((nt, W, L), BF16),
        "mid": v((L, D), F32),
        "u2": v((L, D), F32),
        "r2": v((L, 1), F32),
        "n2low": v((L, D), BF16),
        "upw": v((L, F), F32),
        "actlow": v((L, F), BF16),
        "ffp": v((L, D), BF16),
        "ffr": v((nt - 1, S, D), BF16),
        "blow": v((L, D), BF16),
        "oglow": v((L, D), BF16),
        "n2p": v((L, D), BF16),
        "n2r": v((nt - 1, S, D), BF16),
        "n2g": v((L, D), BF16),
        "mglow": v((L, D), BF16),
        "dq": v((W, L), F32),
        "dk": v((W, L), F32),
        "dv": v((W, L), F32),
        "dp": v((3, W, L), BF16),
        "ngp": v((L, D), BF16),
        "ngr": v((nt - 1, S, D), BF16),
        "ngg": v((L, D), BF16),
        "va": v((GROUP, 32, D), BF16),
        "vb": v((GROUP, s.tail, D), BF16),
        "ent": v((nb, 8, 128), F32),
        "va_sum": v((32, D), F32),
        "vb_sum": v((s.tail, D), F32),
        "gsrc": v((s.rows, D), BF16),
        "gout": v((s.rows, D), BF16),
    }
    dma = pltpu.SemaphoreType.DMA
    out["loads"] = dma((8,))
    for name in ("zmask", "zgate", "zow", "zowr", "zatt", "zff", "zblk", "zn2", "zn2g", "zng", "zngg"):
        out[name + "_s"] = dma((nt - 1,))
        out[name + "_r"] = dma((nt - 1,))
    for name in ("kv", "q", "da", "st"):
        for part in ("_s", "_r", "_rs", "_rr"):
            out[name + part] = dma((s.half,))
    for name, count in (("cnt", nb), ("ent", nb), ("va", GROUP), ("vb", GROUP)):
        out[name + "_s"] = dma((count - 1,))
        out[name + "_r"] = dma((count - 1,))
    if s.groups > 1:
        for name, rows in (("va2", 32), ("vb2", s.tail)):
            out[name] = v((s.groups, rows, D), BF16)
            out[name + "_s"] = dma((s.groups - 1,))
            out[name + "_r"] = dma((s.groups - 1,))
    for i, rows in enumerate(s.sizes):
        hr = rows // 2
        qr = hr // 4
        out["core%d" % i] = v((hr, D), BF16)
        out["quart%d" % i] = v((3, qr, D), BF16)
        if s.groups > 1:
            out["sup%d" % i] = v((s.groups, qr, D), BF16)
            out["sup%d_s" % i] = dma((s.groups - 1,))
            out["sup%d_r" % i] = dma((s.groups - 1,))
        for part in ("c1", "c2"):
            out["%s%d_s" % (part, i)] = dma((1,))
            out["%s%d_r" % (part, i)] = dma((1,))
        for part in ("rs", "ag"):
            out["%s%d_s" % (part, i)] = dma((3,))
            out["%s%d_r" % (part, i)] = dma((3,))
    return out


def main_kernel(s, names, *refs):
    (
        patches,
        windows,
        leads_in,
        table,
        gain1,
        bias1,
        qkv,
        out_weight,
        gain2,
        bias2,
        up,
        down,
        gate,
        pixel_mask,
        cotangent,
        o_block,
        o_hidden,
        o_grads,
        o_va,
        o_vb,
    ) = refs[:20]
    k = SimpleNamespace(**dict(zip(names, refs[20:])))
    sem = vars(k)
    L, D, W, F, H, S, nb, nt = s.L, s.D, s.W, s.F, s.H, s.S, s.nb, s.nt
    b = lax.axis_index("blk")
    t = lax.axis_index("tp")
    core = lax.rem(b, 2)
    pair = b // 2
    sib = b + 1 - 2 * core
    mine = pl.ds(pl.multiple_of(t * S, S), S)

    def z_peer(j):
        return lax.rem(t + j, nt)

    def remote(src, dst, send, recv, device):
        return pltpu.make_async_remote_copy(
            src, dst, send, recv, device_id=device, device_id_type=MESH
        )

    def z_copy(name, j, src, dst):
        return remote(src, dst, sem[name + "_s"].at[j - 1], sem[name + "_r"].at[j - 1], (b, z_peer(j)))

    def z_from(j):
        return lax.rem(t + nt - j, nt)

    def rows_of(tt):
        return pl.ds(pl.multiple_of(tt * S, S), S)

    def ag_copy(name, at, i, dst_band):
        return remote(at(b), at(b), sem[name + "_s"].at[i], sem[name + "_r"].at[i], (dst_band, t))

    def relay_copy(name, at, i, band):
        return remote(at(band), at(band), sem[name + "_rs"].at[i], sem[name + "_rr"].at[i], (sib, t))

    def band_same(i):
        return lax.rem(b + nb - 2 * i, nb)

    def band_sib(i):
        return lax.rem(sib + nb - 2 * i, nb)

    def ag_start(name, at):
        @pl.loop(1, s.half)
        def _(i):
            ag_copy(name, at, i, lax.rem(b + 2 * i, nb)).start()

        relay_copy(name, at, 0, b).start()

    def ag_relay(name, at, i):
        band = band_same(i)
        remote(at(band), at(band), sem[name + "_s"].at[i], sem[name + "_r"].at[i], (sib, t)).wait_recv()
        relay_copy(name, at, i, band).start()

    def ag_wait_relay(name, at, i):
        relay_copy(name, at, i, band_sib(i)).wait_recv()

    def ag_finish(name, at):
        @pl.loop(1, s.half)
        def _(i):
            ag_copy(name, at, i, sib).wait_send()

        @pl.loop(0, s.half)
        def _(i):
            relay_copy(name, at, i, b).wait_send()

    every = (nb, b, lambda i: i)
    near = (GROUP, lax.rem(b, GROUP), lambda i: b // GROUP * GROUP + i)
    far = (s.groups, b // GROUP, lambda i: i * GROUP + lax.rem(b, GROUP))

    def swap_copy(name, members, i, slot, to):
        ref = sem[name]
        return remote(
            ref.at[slot],
            ref.at[slot],
            sem[name + "_s"].at[i - 1],
            sem[name + "_r"].at[i - 1],
            (members[2](to), t),
        )

    def swap_start(name, members):
        count, me, _ = members

        @pl.loop(1, count)
        def _(i):
            swap_copy(name, members, i, me, lax.rem(me + i, count)).start()

    def swap_wait(name, members):
        count, me, _ = members

        @pl.loop(1, count)
        def _(i):
            peer = lax.rem(me + count - i, count)
            swap_copy(name, members, i, peer, peer).wait_recv()

    def swap_finish(name, members):
        count, me, _ = members

        @pl.loop(1, count)
        def _(i):
            swap_copy(name, members, i, me, lax.rem(me + i, count)).wait_send()

    def swap_sum(name):
        swap_wait(name, near)
        out = slots_sum(sem[name], GROUP)
        if s.groups > 1:
            sem[name + "2"][far[1]] = out.astype(BF16)
            swap_start(name + "2", far)
            swap_wait(name + "2", far)
            out = slots_sum(sem[name + "2"], s.groups)
            swap_finish(name + "2", far)
        swap_finish(name, near)
        return out

    def slots_sum(ref, count):
        return lax.fori_loop(
            1, count, lambda i, acc: acc + ref[i].astype(F32), ref[0].astype(F32)
        )

    def rs_start(name, part, recv):
        for j in range(1, nt):
            z_copy(name, j, part.at[rows_of(z_peer(j))], recv.at[j - 1]).start()

    def rs_sum(name, part, recv):
        acc = part[mine, :].astype(F32)
        for j in range(1, nt):
            z_copy(name, j, part.at[rows_of(z_from(j))], recv.at[j - 1]).wait_recv()
            acc = acc + recv[j - 1].astype(F32)
        return acc

    def rs_finish(name, part, recv):
        for j in range(1, nt):
            z_copy(name, j, part.at[rows_of(z_peer(j))], recv.at[j - 1]).wait_send()

    def gather_start(name, ref):
        for j in range(1, nt):
            z_copy(name, j, ref.at[mine], ref.at[mine]).start()

    def gather_wait(name, ref):
        for j in range(1, nt):
            rows = rows_of(z_from(j))
            z_copy(name, j, ref.at[rows], ref.at[rows]).wait_recv()

    def gather_finish(name, ref):
        for j in range(1, nt):
            z_copy(name, j, ref.at[mine], ref.at[mine]).wait_send()

    quarter = lax.rem(pair, 4)
    first_pair = pair - quarter
    group = pair // 4

    def g_rows(i, half, q):
        hr = s.sizes[i] // 2
        qr = hr // 4
        return pl.ds(pl.multiple_of(s.bases[i] + half * hr + q * qr, 16), qr)

    def g_half(i, half):
        hr = s.sizes[i] // 2
        return pl.ds(pl.multiple_of(s.bases[i] + half * hr, 16), hr)

    def q_peer(j):
        return lax.rem(quarter + j, 4)

    def q_dev(j):
        return ((first_pair + q_peer(j)) * 2 + core, t)

    def c1_copy(i):
        return remote(
            k.gsrc.at[g_half(i, 1 - core)], sem["core%d" % i], sem["c1%d_s" % i].at[0], sem["c1%d_r" % i].at[0], (sib, t)
        )

    def rs_copy(i, j):
        qr = s.sizes[i] // 8
        src = sem["core%d" % i].at[pl.ds(pl.multiple_of(q_peer(j) * qr, 16), qr)]
        return remote(
            src, sem["quart%d" % i].at[j - 1], sem["rs%d_s" % i].at[j - 1], sem["rs%d_r" % i].at[j - 1], q_dev(j)
        )

    def ag_copy_g(i, j, q):
        rows = g_rows(i, core, q)
        return remote(
            k.gout.at[rows], k.gout.at[rows], sem["ag%d_s" % i].at[j - 1], sem["ag%d_r" % i].at[j - 1], q_dev(j)
        )

    def c2_copy(i, half):
        rows = g_half(i, half)
        return remote(
            k.gout.at[rows], k.gout.at[rows], sem["c2%d_s" % i].at[0], sem["c2%d_r" % i].at[0], (sib, t)
        )

    def sup_copy(i, j):
        ref = sem["sup%d" % i]
        dev = ((lax.rem(group + j, s.groups) * 4 + quarter) * 2 + core, t)
        return remote(ref.at[group], ref.at[group], sem["sup%d_s" % i].at[j - 1], sem["sup%d_r" % i].at[j - 1], dev)

    def grads_step1(i):
        c1_copy(i).start()

    def grads_step2(i):
        c1_copy(i).wait()
        hs = sem["core%d" % i]
        hs[...] = (k.gsrc[g_half(i, core), :].astype(F32) + hs[...].astype(F32)).astype(BF16)
        for j in range(1, 4):
            rs_copy(i, j).start()

    def grads_step3(i):
        qr = s.sizes[i] // 8
        acc = sem["core%d" % i][pl.ds(pl.multiple_of(quarter * qr, 16), qr), :].astype(F32)
        for j in range(1, 4):
            rs_copy(i, j).wait()
            acc = acc + sem["quart%d" % i][j - 1].astype(F32)
        if s.groups > 1:
            ref = sem["sup%d" % i]
            ref[group] = acc.astype(BF16)
            for j in range(1, s.groups):
                sup_copy(i, j).start()
            for j in range(1, s.groups):
                sup_copy(i, j).wait()
            acc = ref[0].astype(F32)
            for g in range(1, s.groups):
                acc = acc + ref[g].astype(F32)
        k.gout[g_rows(i, core, quarter), :] = acc.astype(BF16)
        for j in range(1, 4):
            ag_copy_g(i, j, quarter).start()

    def grads_step4(i):
        for j in range(1, 4):
            ag_copy_g(i, j, quarter).wait_send()
            ag_copy_g(i, j, lax.rem(quarter + 4 - j, 4)).wait_recv()
        c2_copy(i, core).start()

    def grads_step5(i):
        c2_copy(i, core).wait_send()
        c2_copy(i, 1 - core).wait_recv()

    loads = [
        pltpu.make_async_copy(patches, k.patches, k.loads.at[0]),
        pltpu.make_async_copy(qkv, k.qkv, k.loads.at[1]),
        pltpu.make_async_copy(out_weight, k.ow.at[t], k.loads.at[2]),
        pltpu.make_async_copy(up, k.up, k.loads.at[3]),
        pltpu.make_async_copy(down, k.down, k.loads.at[4]),
        pltpu.make_async_copy(cotangent, k.cot, k.loads.at[5]),
    ]
    for copy in loads:
        copy.start()
    barrier = pltpu.get_barrier_semaphore()

    @pl.loop(1, nb)
    def _(i):
        pl.semaphore_signal(barrier, inc=1, device_id=(lax.rem(b + i, nb), t), device_id_type=MESH)

    for j in range(1, nt):
        pl.semaphore_signal(barrier, inc=1, device_id=(b, z_peer(j)), device_id_type=MESH)

    lead_hot = (lax.broadcasted_iota(jnp.int32, (s.leads, L), 0) == leads_in[...]).astype(F32)
    loads[0].wait()
    hidden = k.patches[...] + mm_tn(lead_hot.astype(BF16), table[...])
    unit1, inverse1 = norm_stats(hidden)
    k.u1[...] = unit1
    k.r1[...] = inverse1
    k.mid[...] = hidden
    k.normed[...] = (unit1 * gain1[...] + bias1[...]).astype(BF16)
    loads[1].wait()

    def project(c):
        return jnp.transpose(mm_nn(k.normed[...], k.qkv[c]))

    k.kv[b, 0:W, :] = project(1).astype(BF16)
    k.kv[b, W : 2 * W, :] = project(2).astype(BF16)
    gate_pad = jnp.zeros((4, D), F32)
    gate_rows = []
    for e in range(3):
        gate_rows += [gate[e].astype(F32), gate_pad]
    gate_rows += [gate_pad, gate_pad]
    my_gate = pl.ds(pl.multiple_of(t * 32, 32), 32)
    k.gate[my_gate, :] = jnp.concatenate(gate_rows, axis=0).astype(BF16)
    k.mask[t] = jnp.concatenate([pixel_mask[...].astype(F32), jnp.zeros((4, L), F32)], axis=0)
    pl.semaphore_wait(barrier, nb - 1 + nt - 1)

    def kv_at(band):
        return k.kv.at[band]

    ag_start("kv", kv_at)
    for j in range(1, nt):
        z_copy("zmask", j, k.mask.at[t], k.mask.at[t]).start()
        z_copy("zgate", j, k.gate.at[my_gate], k.gate.at[my_gate]).start()
    hw = W // 2
    loads[2].wait()

    def ow_half(tt, c):
        return k.ow.at[tt, pl.ds(pl.multiple_of(c * hw, hw), hw)]

    for j in range(1, nt):
        z_copy("zow", j, ow_half(t, core), ow_half(t, core)).start()
    k.qd[b, 0:W, :] = (project(0).astype(BF16).astype(F32) * SCALE).astype(BF16)

    for j in range(1, nt):
        z_copy("zmask", j, k.mask.at[t], k.mask.at[z_from(j)]).wait_recv()
    k.cnt[b] = jnp.broadcast_to(total(jnp.sum(k.mask[...], axis=0)), (8, 128))
    swap_start("cnt", every)

    def id_row(band):
        return windows[pl.ds(band, 1), :].astype(F32)

    def id_column(band):
        return jnp.transpose(jnp.broadcast_to(id_row(band), (128, L)))[:, 0:1]

    def head(h):
        return pl.ds(h * HEAD_DIM, HEAD_DIM)

    def value_head(h):
        return pl.ds(W + h * HEAD_DIM, HEAD_DIM)

    k.m[...] = jnp.full((8, L), MASKED, F32)
    k.l[...] = jnp.zeros((8, L), F32)
    k.acc[...] = jnp.zeros((W, L), F32)

    def forward_band(band):
        allowed = id_column(band) == id_row(b)
        for h in range(H):
            scores = mm_tn(k.kv[band, head(h), :], k.qd[b, head(h), :])
            scores = jnp.where(allowed, scores, MASKED)
            high = k.m[h : h + 1, :]
            new_high = jnp.maximum(high, jnp.max(scores, axis=0, keepdims=True))
            weights = jnp.exp(scores - new_high)
            factor = jnp.exp(high - new_high)
            k.m[h : h + 1, :] = new_high
            k.l[h : h + 1, :] = k.l[h : h + 1, :] * factor + jnp.sum(weights, axis=0, keepdims=True)
            k.acc[head(h), :] = k.acc[head(h), :] * factor + mm_nn(
                k.kv[band, value_head(h), :], weights.astype(BF16)
            )

    @pl.loop(0, s.half)
    def _(i):
        @pl.when(i > 0)
        def _():
            ag_relay("kv", kv_at, i)

        forward_band(band_same(i))
        ag_wait_relay("kv", kv_at, i)
        forward_band(band_sib(i))

    for h in range(H):
        att = k.acc[head(h), :] / k.l[h : h + 1, :]
        k.acc[head(h), :] = att
        k.att[t, head(h), :] = att.astype(BF16)
        k.st[b, h : h + 1, :] = k.m[h : h + 1, :] + jnp.log(k.l[h : h + 1, :])
    for j in range(1, nt):
        z_copy("zatt", j, k.att.at[t], k.att.at[t]).start()

    def q_at(band):
        return k.qd.at[band, pl.ds(0, W)]

    def da_at(band):
        return k.qd.at[band, pl.ds(W, W)]

    def st_at(band):
        return k.st.at[band]

    ag_start("q", q_at)
    for j in range(1, nt):
        src = z_from(j)
        z_copy("zow", j, ow_half(src, core), ow_half(src, core)).wait_recv()
        remote(
            ow_half(src, core), ow_half(src, core), k.zowr_s.at[j - 1], k.zowr_r.at[j - 1], (sib, t)
        ).start()
    for j in range(1, nt):
        src = z_from(j)
        remote(
            ow_half(src, 1 - core), ow_half(src, 1 - core), k.zowr_s.at[j - 1], k.zowr_r.at[j - 1], (sib, t)
        ).wait_recv()
    for j in range(1, nt):
        z_copy("zatt", j, k.att.at[t], k.att.at[z_from(j)]).wait_recv()
        z_copy("zgate", j, k.gate.at[my_gate], k.gate.at[my_gate]).wait_recv()

    middle = k.mid[...] + mm_tn(
        k.att[...].reshape(nt * W, L), k.ow[...].reshape(nt * W, D)
    )
    k.mid[...] = middle
    unit2, inverse2 = norm_stats(middle)
    k.u2[...] = unit2
    k.r2[...] = inverse2
    k.n2low[...] = (unit2 * gain2[...] + bias2[...]).astype(BF16)
    loads[3].wait()
    loads[4].wait()
    upward = mm_nn(k.n2low[...], k.up[...])
    k.upw[...] = upward
    k.actlow[...] = (0.5 * upward * (1.0 + lax.erf(upward * INV_SQRT2))).astype(BF16)
    k.ffp[...] = mm_nn(k.actlow[...], k.down[...]).astype(BF16)
    rs_start("zff", k.ffp, k.ffr)
    upward = k.upw[...]
    k.upw[...] = 0.5 * (1.0 + lax.erf(upward * INV_SQRT2)) + upward * (
        jnp.exp(-0.5 * upward * upward) * INV_SQRT_2PI
    )

    @pl.loop(1, s.half)
    def _(i):
        ag_relay("q", q_at, i)

    swap_wait("cnt", every)
    block_slice = k.mid[mine, :] + rs_sum("zff", k.ffp, k.ffr)
    k.blow[mine, :] = block_slice.astype(BF16)
    gather_start("zblk", k.blow)
    loads[5].wait()
    pixel_count = jnp.sum(k.cnt[...], axis=0)[0:1, 0:1]
    gather_wait("zblk", k.blow)

    block_copy = pltpu.make_async_copy(k.blow, o_block, k.loads.at[6])
    block_copy.start()
    logits = mm_nt(k.gate[...], k.blow[...]).reshape(nt, 4, 8, L)
    parts = [logits[:, e] for e in range(3)]
    high = jnp.maximum(jnp.maximum(parts[0], parts[1]), parts[2])
    logs = jnp.log(sum(jnp.exp(x - high) for x in parts))
    log_probs = [x - high - logs for x in parts]
    probs = [jnp.exp(x) for x in log_probs]
    entropy = -sum(p * x for p, x in zip(probs, log_probs))
    mask = k.mask[...]
    entropy_sum = total(jnp.sum(mask * entropy, axis=0))
    weight = mask * (float(s.pixels) / pixel_count)[None]
    grads = [-p * (x + entropy) * weight for p, x in zip(probs, log_probs)]
    grads.append(jnp.zeros((nt, 8, L), F32))
    logit_grad = jnp.stack(grads, axis=1).reshape(nt * 32, L).astype(BF16)
    out_grad = k.cot[...] + mm_tn(logit_grad, k.gate[...])
    k.cot[...] = out_grad
    k.oglow[...] = out_grad.astype(BF16)

    upward_grad = (mm_nt(k.oglow[...], k.down[...]) * k.upw[...]).astype(BF16)
    k.n2p[...] = mm_nt(upward_grad, k.up[...]).astype(BF16)
    rs_start("zn2", k.n2p, k.n2r)
    k.gsrc[0:F, :] = mm_tn(k.actlow[...], k.oglow[...]).astype(BF16)
    k.gsrc[F : F + D, :] = mm_tn(k.n2low[...], upward_grad).astype(BF16)
    grads_step1(0)
    lg_rows = jnp.stack(grads, axis=1).reshape(nt, 32, L)
    pick = lax.broadcasted_iota(jnp.int32, (nt, 1, 1), 0) == t
    own_lg = jnp.sum(jnp.where(pick, lg_rows, 0.0), axis=0).astype(BF16)
    k.va[near[1]] = mm_nn(own_lg, k.blow[...]).astype(BF16)
    k.ent[b] = jnp.broadcast_to(entropy_sum / pixel_count, (8, 128))
    swap_start("va", near)
    swap_start("ent", every)
    grads_step2(0)
    k.n2g[mine, :] = rs_sum("zn2", k.n2p, k.n2r).astype(BF16)
    gather_start("zn2g", k.n2g)
    gather_wait("zn2g", k.n2g)
    n2_grad = k.n2g[...].astype(F32)
    gain2_grad = jnp.sum(n2_grad * k.u2[...], axis=0, keepdims=True)
    bias2_grad = jnp.sum(n2_grad, axis=0, keepdims=True)
    middle_grad = k.cot[...] + norm_backward(n2_grad, k.u2[...], k.r2[...], gain2[...])
    k.cot[...] = middle_grad
    k.mglow[...] = middle_grad.astype(BF16)

    att_grad = mm_nt(k.ow[t], k.mglow[...]).astype(BF16)
    k.qd[b, W : 2 * W, :] = att_grad
    weighted = att_grad.astype(F32) * k.acc[...]
    for h in range(H):
        k.st[b, H + h : H + h + 1, :] = jnp.sum(
            weighted[h * HEAD_DIM : (h + 1) * HEAD_DIM], axis=0, keepdims=True
        )
    ag_start("st", st_at)
    ag_start("da", da_at)
    k.gsrc[s.bases[1] : s.bases[1] + W, :] = mm_nn(k.att[t], k.mglow[...]).astype(BF16)
    k.dq[...] = jnp.zeros((W, L), F32)
    k.dk[...] = jnp.zeros((W, L), F32)
    k.dv[...] = jnp.zeros((W, L), F32)

    @pl.loop(0, nb)
    def _(band):
        allowed = id_column(band) == id_row(b)
        for h in range(H):
            keys = k.kv[band, head(h), :]
            scores = jnp.where(allowed, mm_tn(keys, k.qd[b, head(h), :]), MASKED)
            prob = jnp.exp(scores - k.st[b, h : h + 1, :])
            dots = mm_tn(k.kv[band, value_head(h), :], k.qd[b, value_head(h), :])
            grad = (prob * (dots - k.st[b, H + h : H + h + 1, :])).astype(BF16)
            k.dq[head(h), :] += mm_nn(keys, grad)

    @pl.loop(1, s.half)
    def _(i):
        ag_wait_relay("q", q_at, i)

    ag_wait_relay("q", q_at, 0)
    my_column = id_column(b)

    def backward_band(band):
        allowed = my_column == id_row(band)
        for h in range(H):
            queries = k.qd[band, head(h), :]
            att_grads = k.qd[band, value_head(h), :]
            scores = jnp.where(allowed, mm_tn(k.kv[b, head(h), :], queries), MASKED)
            prob = jnp.exp(scores - k.st[band, h : h + 1, :])
            dots = mm_tn(k.kv[b, value_head(h), :], att_grads)
            grad = (prob * (dots - k.st[band, H + h : H + h + 1, :])).astype(BF16)
            k.dk[head(h), :] += mm_nt(queries, grad)
            k.dv[head(h), :] += mm_nt(att_grads, prob.astype(BF16))

    @pl.loop(0, s.half)
    def _(i):
        @pl.when(i > 0)
        def _():
            ag_relay("st", st_at, i)
            ag_relay("da", da_at, i)

        backward_band(band_same(i))
        ag_wait_relay("st", st_at, i)
        ag_wait_relay("da", da_at, i)
        backward_band(band_sib(i))

    grads_step3(0)
    k.dp[0] = (k.dq[...] * SCALE).astype(BF16)
    k.dp[1] = k.dk[...].astype(BF16)
    k.dp[2] = k.dv[...].astype(BF16)
    n1_part = mm_nt(jnp.transpose(k.dp[0].astype(F32)).astype(BF16), k.qkv[0])
    n1_part += mm_nt(jnp.transpose(k.dp[1].astype(F32)).astype(BF16), k.qkv[1])
    n1_part += mm_nt(jnp.transpose(k.dp[2].astype(F32)).astype(BF16), k.qkv[2])
    k.ngp[...] = n1_part.astype(BF16)
    rs_start("zng", k.ngp, k.ngr)
    base = s.bases[1] + W
    k.gsrc[base : base + 3 * W, :] = mm_nn(k.dp[...].reshape(3 * W, L), k.normed[...]).astype(BF16)
    grads_step1(1)
    grads_step2(1)
    k.ngg[mine, :] = rs_sum("zng", k.ngp, k.ngr).astype(BF16)
    gather_start("zngg", k.ngg)
    grads_step4(0)
    grads_step3(1)
    grads_step5(0)
    gather_wait("zngg", k.ngg)
    n1_grad = k.ngg[...].astype(F32)
    unit1 = k.u1[...]
    gain1_grad = jnp.sum(n1_grad * unit1, axis=0, keepdims=True)
    bias1_grad = jnp.sum(n1_grad, axis=0, keepdims=True)
    hidden_grad = k.cot[...] + norm_backward(n1_grad, unit1, k.r1[...], gain1[...])
    k.patches[...] = hidden_grad
    hidden_copy = pltpu.make_async_copy(k.patches, o_hidden, k.loads.at[7])
    hidden_copy.start()
    hot = lead_hot.astype(BF16)
    coarse = hidden_grad.astype(BF16)
    fine = (hidden_grad - coarse.astype(F32)).astype(BF16)
    tail = [mm_nn(hot, coarse) + mm_nn(hot, fine), gain1_grad, bias1_grad, gain2_grad, bias2_grad]
    tail.append(jnp.zeros((s.tail - s.leads - 4, D), F32))
    k.vb[near[1]] = jnp.concatenate(tail, axis=0).astype(BF16)
    swap_start("vb", near)
    grads_step4(1)
    swap_wait("ent", every)
    k.va_sum[...] = swap_sum("va")
    k.va_sum[24:32, 0:128] = jnp.sum(k.ent[...], axis=0)
    k.vb_sum[...] = swap_sum("vb")
    grads_step5(1)

    outs = [
        pltpu.make_async_copy(k.gout, o_grads, k.loads.at[0]),
        pltpu.make_async_copy(k.va_sum, o_va, k.loads.at[1]),
        pltpu.make_async_copy(k.vb_sum, o_vb, k.loads.at[2]),
    ]
    for copy in outs:
        copy.start()

    for j in range(1, nt):
        z_copy("zmask", j, k.mask.at[t], k.mask.at[t]).wait_send()
        z_copy("zgate", j, k.gate.at[my_gate], k.gate.at[my_gate]).wait_send()
        z_copy("zow", j, ow_half(t, core), ow_half(t, core)).wait_send()
        remote(
            ow_half(t, core), ow_half(t, core), k.zowr_s.at[j - 1], k.zowr_r.at[j - 1], (sib, t)
        ).wait_send()
        z_copy("zatt", j, k.att.at[t], k.att.at[t]).wait_send()
    rs_finish("zff", k.ffp, k.ffr)
    gather_finish("zblk", k.blow)
    rs_finish("zn2", k.n2p, k.n2r)
    gather_finish("zn2g", k.n2g)
    rs_finish("zng", k.ngp, k.ngr)
    gather_finish("zngg", k.ngg)
    ag_finish("kv", kv_at)
    ag_finish("q", q_at)
    ag_finish("da", da_at)
    ag_finish("st", st_at)
    swap_finish("cnt", every)
    swap_finish("ent", every)
    block_copy.wait()
    hidden_copy.wait()
    for copy in outs:
        copy.wait()


def last_kernel(
    s, block, hidden, grads, va, vb,
    o_block, o_pen, o_hidden, o_lead, o_g1, o_b1, o_qkv, o_out, o_g2, o_b2, o_up, o_down, o_gate,
):
    o_block[...] = block[...].astype(F32)
    o_hidden[...] = hidden[...]
    o_down[...] = grads[0 : s.F, :].astype(F32)
    o_up[...] = grads[s.F : s.F + s.D, :].astype(F32)
    base = s.bases[1]
    o_out[...] = grads[base : base + s.W, :].astype(F32)
    for c in range(3):
        rows = grads[base + (c + 1) * s.W : base + (c + 2) * s.W, :]
        o_qkv[c] = jnp.transpose(rows.astype(F32))
    small = va[...]
    for e in range(3):
        o_gate[e] = small[8 * e : 8 * e + 4]
    o_pen[...] = small[24:25, 0:1]
    tail = vb[...]
    o_lead[...] = tail[0 : s.leads]
    o_g1[...] = tail[s.leads : s.leads + 1]
    o_b1[...] = tail[s.leads + 1 : s.leads + 2]
    o_g2[...] = tail[s.leads + 2 : s.leads + 3]
    o_b2[...] = tail[s.leads + 3 : s.leads + 4]


def local(
    nb,
    nt,
    patches,
    window_ids,
    lead_index,
    lead_table,
    attention_gain,
    attention_bias,
    query_key_value,
    out_weight,
    feedforward_gain,
    feedforward_bias,
    up_weight,
    down_weight,
    gate_head,
    pixel_mask,
    cotangent,
):
    L, D = patches.shape
    leads = lead_table.shape[0]
    W = out_weight.shape[0]
    F = up_weight.shape[1]
    s = dims_of(nb, nt, L, D, W, F, leads, L * nb * pixel_mask.shape[0] * nt)
    scratch = scratch_of(s)
    vm = pl.BlockSpec(memory_space=pltpu.VMEM)
    hbm = pl.BlockSpec(memory_space=pl.ANY)
    row = (1, D)
    block, hidden, grads, va, vb = pl.pallas_call(
        partial(main_kernel, s, tuple(scratch)),
        out_shape=(
            jax.ShapeDtypeStruct((L, D), BF16),
            jax.ShapeDtypeStruct((L, D), F32),
            jax.ShapeDtypeStruct((s.rows, D), BF16),
            jax.ShapeDtypeStruct((32, D), F32),
            jax.ShapeDtypeStruct((s.tail, D), F32),
        ),
        in_specs=[hbm, vm, vm, vm, vm, vm, hbm, hbm, vm, vm, hbm, hbm, vm, vm, hbm],
        out_specs=(hbm,) * 5,
        scratch_shapes=list(scratch.values()),
        compiler_params=pltpu.CompilerParams(
            collective_id=0, has_side_effects=True, vmem_limit_bytes=VMEM_LIMIT
        ),
        name="block_step",
    )(
        patches,
        window_ids.reshape(nb, L),
        lead_index.reshape(1, L),
        lead_table,
        attention_gain.reshape(row),
        attention_bias.reshape(row),
        query_key_value,
        out_weight,
        feedforward_gain.reshape(row),
        feedforward_bias.reshape(row),
        up_weight,
        down_weight,
        gate_head,
        pixel_mask,
        cotangent,
    )
    vec = jax.ShapeDtypeStruct(row, F32)
    outs = pl.pallas_call(
        partial(last_kernel, s),
        out_shape=(
            jax.ShapeDtypeStruct((L, D), F32),
            jax.ShapeDtypeStruct((1, 1), F32),
            jax.ShapeDtypeStruct((L, D), F32),
            jax.ShapeDtypeStruct((leads, D), F32),
            vec,
            vec,
            jax.ShapeDtypeStruct((3, D, W), F32),
            jax.ShapeDtypeStruct((W, D), F32),
            vec,
            vec,
            jax.ShapeDtypeStruct((D, F), F32),
            jax.ShapeDtypeStruct((F, D), F32),
            jax.ShapeDtypeStruct(gate_head.shape, F32),
        ),
        in_specs=[vm] * 5,
        out_specs=(vm,) * 13,
        compiler_params=pltpu.CompilerParams(vmem_limit_bytes=VMEM_LIMIT),
        name="write_out",
    )(block, hidden, grads, va, vb)
    outs = list(outs)
    outs[1] = outs[1].reshape(())
    for i in (4, 5, 8, 9):
        outs[i] = outs[i].reshape((D,))
    return tuple(outs)


def solution(mesh):
    in_specs = (
        P("blk", None),
        P(),
        P("blk"),
        P(),
        P(),
        P(),
        P(None, None, "tp"),
        P("tp", None),
        P(),
        P(),
        P(None, "tp"),
        P("tp", None),
        P(None, "tp", None),
        P("tp", "blk"),
        P("blk", None),
    )
    out_specs = (
        P("blk", None),
        P(),
        P("blk", None),
        P(),
        P(),
        P(),
        P(None, None, "tp"),
        P("tp", None),
        P(),
        P(),
        P(None, "tp"),
        P("tp", None),
        P(None, "tp", None),
    )
    return jax.shard_map(
        partial(local, mesh.shape["blk"], mesh.shape["tp"]),
        mesh=mesh,
        in_specs=in_specs,
        out_specs=out_specs,
        check_vma=False,
    )
```

```python
from functools import partial
from types import SimpleNamespace

import jax
import jax.numpy as jnp
from jax import lax
from jax.experimental import pallas as pl
from jax.experimental.pallas import tpu as pltpu
from jax.sharding import PartitionSpec as P

HEAD_DIM = 64
EPS = 1e-05
MASKED = -1e30
SCALE = HEAD_DIM ** (-0.5)
GROUP = 8
F32 = jnp.float32
BF16 = jnp.bfloat16
MESH = pl.DeviceIdType.MESH
VMEM_LIMIT = 61 * 2**20
INV_SQRT2 = 0.7071067811865476
INV_SQRT_2PI = 0.3989422804014327


def dot(a, b, ca, cb):
    return lax.dot_general(a, b, (((ca,), (cb,)), ((), ())), preferred_element_type=F32)


def mm_nn(a, b):
    return dot(a, b, 1, 0)


def mm_nt(a, b):
    return dot(a, b, 1, 1)


def mm_tn(a, b):
    return dot(a, b, 0, 0)


def norm_stats(values):
    mean = jnp.mean(values, axis=-1, keepdims=True)
    centered = values - mean
    inverse = lax.rsqrt(jnp.mean(centered * centered, axis=-1, keepdims=True) + EPS)
    return centered * inverse, inverse


def norm_backward(incoming, unit_rows, inverse, gain):
    scaled = incoming * gain
    return inverse * (
        scaled
        - jnp.mean(scaled, axis=-1, keepdims=True)
        - unit_rows * jnp.mean(scaled * unit_rows, axis=-1, keepdims=True)
    )


def row_of(ref):
    return ref[...].reshape(1, ref.shape[0])


def total(x):
    return jnp.sum(jnp.sum(x, axis=0, keepdims=True), axis=1, keepdims=True)


def dims_of(nb, nt, tokens, width, local_width, hidden, leads, pixels):
    s = SimpleNamespace(nb=nb, nt=nt, L=tokens, D=width, W=local_width, F=hidden, leads=leads)
    s.H = local_width // HEAD_DIM
    s.S = tokens // nt
    s.half = nb // 2
    s.groups = nb // GROUP
    s.pixels = pixels
    s.sizes = (hidden + width, local_width * 4)
    s.bases = (0, s.sizes[0])
    s.rows = sum(s.sizes)
    s.tail = (leads + 4 + 15) // 16 * 16
    return s


def scratch_of(s):
    L, D, W, F, nb, nt, S = s.L, s.D, s.W, s.F, s.nb, s.nt, s.S
    v = pltpu.VMEM
    out = {
        "patches": v((L, D), F32),
        "ids": v((nb, L), F32),
        "qkv": v((3, W, D), BF16),
        "ow": v((nt, W, D), BF16),
        "up": v((D, F), BF16),
        "down": v((F, D), BF16),
        "cot": v((L, D), F32),
        "gate": v((nt * 32, D), BF16),
        "mask": v((nt, 8, L), F32),
        "cnt": v((nb, 8, 128), F32),
        "u1": v((L, D), F32),
        "r1": v((L, 1), F32),
        "normed": v((L, D), BF16),
        "kv": v((nb, 2 * W, L), BF16),
        "qd": v((nb, 2 * W, L), BF16),
        "st": v((nb, 8, L), F32),
        "m": v((8, L), F32),
        "l": v((8, L), F32),
        "acc": v((W, L), F32),
        "att": v((nt, W, L), BF16),
        "mid": v((L, D), F32),
        "u2": v((L, D), F32),
        "r2": v((L, 1), F32),
        "n2low": v((L, D), BF16),
        "upw": v((L, F), F32),
        "actlow": v((L, F), BF16),
        "ffp": v((L, D), BF16),
        "ffr": v((nt - 1, S, D), BF16),
        "blow": v((L, D), BF16),
        "oglow": v((L, D), BF16),
        "n2p": v((L, D), BF16),
        "n2r": v((nt - 1, S, D), BF16),
        "n2g": v((L, D), BF16),
        "mglow": v((L, D), BF16),
        "dq": v((W, L), F32),
        "dk": v((W, L), F32),
        "dv": v((W, L), F32),
        "dp": v((3, W, L), BF16),
        "ngp": v((L, D), BF16),
        "ngr": v((nt - 1, S, D), BF16),
        "ngg": v((L, D), BF16),
        "va": v((GROUP, 32, D), BF16),
        "vb": v((GROUP, s.tail, D), BF16),
        "ent": v((nb, 8, 128), F32),
        "va_sum": v((32, D), F32),
        "vb_sum": v((s.tail, D), F32),
        "gsrc": v((s.rows, D), BF16),
        "gout": v((s.rows, D), BF16),
    }
    dma = pltpu.SemaphoreType.DMA
    out["loads"] = dma((8,))
    for name in ("zmask", "zgate", "zow", "zowr", "zatt", "zff", "zblk", "zn2", "zn2g", "zng", "zngg"):
        out[name + "_s"] = dma((nt - 1,))
        out[name + "_r"] = dma((nt - 1,))
    for name in ("kv", "q", "da", "st"):
        for part in ("_s", "_r", "_rs", "_rr"):
            out[name + part] = dma((s.half,))
    for name, count in (("cnt", nb), ("ent", nb), ("va", GROUP), ("vb", GROUP)):
        out[name + "_s"] = dma((count - 1,))
        out[name + "_r"] = dma((count - 1,))
    if s.groups > 1:
        for name, rows in (("va2", 32), ("vb2", s.tail)):
            out[name] = v((s.groups, rows, D), BF16)
            out[name + "_s"] = dma((s.groups - 1,))
            out[name + "_r"] = dma((s.groups - 1,))
    for i, rows in enumerate(s.sizes):
        hr = rows // 2
        qr = hr // 4
        out["core%d" % i] = v((hr, D), BF16)
        out["quart%d" % i] = v((3, qr, D), BF16)
        if s.groups > 1:
            out["sup%d" % i] = v((s.groups, qr, D), BF16)
            out["sup%d_s" % i] = dma((s.groups - 1,))
            out["sup%d_r" % i] = dma((s.groups - 1,))
        for part in ("c1", "c2"):
            out["%s%d_s" % (part, i)] = dma((1,))
            out["%s%d_r" % (part, i)] = dma((1,))
        for part in ("rs", "ag"):
            out["%s%d_s" % (part, i)] = dma((3,))
            out["%s%d_r" % (part, i)] = dma((3,))
    return out


def main_kernel(s, names, *refs):
    (
        patches,
        windows_in,
        leads_in,
        table,
        gain1,
        bias1,
        qkv,
        out_weight,
        gain2,
        bias2,
        up,
        down,
        gate,
        pixel_mask,
        cotangent,
        o_block,
        o_hidden,
        o_grads,
        o_va,
        o_vb,
    ) = refs[:20]
    k = SimpleNamespace(**dict(zip(names, refs[20:])))
    sem = vars(k)
    L, D, W, F, H, S, nb, nt = s.L, s.D, s.W, s.F, s.H, s.S, s.nb, s.nt
    b = lax.axis_index("blk")
    t = lax.axis_index("tp")
    core = lax.rem(b, 2)
    pair = b // 2
    sib = b + 1 - 2 * core
    mine = pl.ds(pl.multiple_of(t * S, S), S)

    def z_peer(j):
        return lax.rem(t + j, nt)

    def remote(src, dst, send, recv, device):
        return pltpu.make_async_remote_copy(
            src, dst, send, recv, device_id=device, device_id_type=MESH
        )

    def z_copy(name, j, src, dst):
        return remote(src, dst, sem[name + "_s"].at[j - 1], sem[name + "_r"].at[j - 1], (b, z_peer(j)))

    def z_from(j):
        return lax.rem(t + nt - j, nt)

    def rows_of(tt):
        return pl.ds(pl.multiple_of(tt * S, S), S)

    def ag_copy(name, at, i, dst_band):
        return remote(at(b), at(b), sem[name + "_s"].at[i], sem[name + "_r"].at[i], (dst_band, t))

    def relay_copy(name, at, i, band):
        return remote(at(band), at(band), sem[name + "_rs"].at[i], sem[name + "_rr"].at[i], (sib, t))

    def band_same(i):
        return lax.rem(b + nb - 2 * i, nb)

    def band_sib(i):
        return lax.rem(sib + nb - 2 * i, nb)

    def ag_start(name, at):
        @pl.loop(1, s.half)
        def _(i):
            ag_copy(name, at, i, lax.rem(b + 2 * i, nb)).start()

        relay_copy(name, at, 0, b).start()

    def ag_relay(name, at, i):
        band = band_same(i)
        remote(at(band), at(band), sem[name + "_s"].at[i], sem[name + "_r"].at[i], (sib, t)).wait_recv()
        relay_copy(name, at, i, band).start()

    def ag_wait_relay(name, at, i):
        relay_copy(name, at, i, band_sib(i)).wait_recv()

    def ag_finish(name, at):
        @pl.loop(1, s.half)
        def _(i):
            ag_copy(name, at, i, sib).wait_send()

        @pl.loop(0, s.half)
        def _(i):
            relay_copy(name, at, i, b).wait_send()

    every = (nb, b, lambda i: i)
    near = (GROUP, lax.rem(b, GROUP), lambda i: b // GROUP * GROUP + i)
    far = (s.groups, b // GROUP, lambda i: i * GROUP + lax.rem(b, GROUP))

    def swap_copy(name, members, i, slot, to):
        ref = sem[name]
        return remote(
            ref.at[slot],
            ref.at[slot],
            sem[name + "_s"].at[i - 1],
            sem[name + "_r"].at[i - 1],
            (members[2](to), t),
        )

    def swap_start(name, members):
        count, me, _ = members

        @pl.loop(1, count)
        def _(i):
            swap_copy(name, members, i, me, lax.rem(me + i, count)).start()

    def swap_wait(name, members):
        count, me, _ = members

        @pl.loop(1, count)
        def _(i):
            peer = lax.rem(me + count - i, count)
            swap_copy(name, members, i, peer, peer).wait_recv()

    def swap_finish(name, members):
        count, me, _ = members

        @pl.loop(1, count)
        def _(i):
            swap_copy(name, members, i, me, lax.rem(me + i, count)).wait_send()

    def swap_sum(name):
        swap_wait(name, near)
        out = slots_sum(sem[name], GROUP)
        if s.groups > 1:
            sem[name + "2"][far[1]] = out.astype(BF16)
            swap_start(name + "2", far)
            swap_wait(name + "2", far)
            out = slots_sum(sem[name + "2"], s.groups)
            swap_finish(name + "2", far)
        swap_finish(name, near)
        return out

    def slots_sum(ref, count):
        return lax.fori_loop(
            1, count, lambda i, acc: acc + ref[i].astype(F32), ref[0].astype(F32)
        )

    def rs_start(name, part, recv):
        for j in range(1, nt):
            z_copy(name, j, part.at[rows_of(z_peer(j))], recv.at[j - 1]).start()

    def rs_sum(name, part, recv):
        acc = part[mine, :].astype(F32)
        for j in range(1, nt):
            z_copy(name, j, part.at[rows_of(z_from(j))], recv.at[j - 1]).wait_recv()
            acc = acc + recv[j - 1].astype(F32)
        return acc

    def rs_finish(name, part, recv):
        for j in range(1, nt):
            z_copy(name, j, part.at[rows_of(z_peer(j))], recv.at[j - 1]).wait_send()

    def gather_start(name, ref):
        for j in range(1, nt):
            z_copy(name, j, ref.at[mine], ref.at[mine]).start()

    def gather_wait(name, ref):
        for j in range(1, nt):
            rows = rows_of(z_from(j))
            z_copy(name, j, ref.at[rows], ref.at[rows]).wait_recv()

    def gather_finish(name, ref):
        for j in range(1, nt):
            z_copy(name, j, ref.at[mine], ref.at[mine]).wait_send()

    quarter = lax.rem(pair, 4)
    first_pair = pair - quarter
    group = pair // 4

    def g_rows(i, half, q):
        hr = s.sizes[i] // 2
        qr = hr // 4
        return pl.ds(pl.multiple_of(s.bases[i] + half * hr + q * qr, 16), qr)

    def g_half(i, half):
        hr = s.sizes[i] // 2
        return pl.ds(pl.multiple_of(s.bases[i] + half * hr, 16), hr)

    def q_peer(j):
        return lax.rem(quarter + j, 4)

    def q_dev(j):
        return ((first_pair + q_peer(j)) * 2 + core, t)

    def c1_copy(i):
        return remote(
            k.gsrc.at[g_half(i, 1 - core)], sem["core%d" % i], sem["c1%d_s" % i].at[0], sem["c1%d_r" % i].at[0], (sib, t)
        )

    def rs_copy(i, j):
        qr = s.sizes[i] // 8
        src = sem["core%d" % i].at[pl.ds(pl.multiple_of(q_peer(j) * qr, 16), qr)]
        return remote(
            src, sem["quart%d" % i].at[j - 1], sem["rs%d_s" % i].at[j - 1], sem["rs%d_r" % i].at[j - 1], q_dev(j)
        )

    def ag_copy_g(i, j, q):
        rows = g_rows(i, core, q)
        return remote(
            k.gout.at[rows], k.gout.at[rows], sem["ag%d_s" % i].at[j - 1], sem["ag%d_r" % i].at[j - 1], q_dev(j)
        )

    def c2_copy(i, half):
        rows = g_half(i, half)
        return remote(
            k.gout.at[rows], k.gout.at[rows], sem["c2%d_s" % i].at[0], sem["c2%d_r" % i].at[0], (sib, t)
        )

    def sup_copy(i, j):
        ref = sem["sup%d" % i]
        dev = ((lax.rem(group + j, s.groups) * 4 + quarter) * 2 + core, t)
        return remote(ref.at[group], ref.at[group], sem["sup%d_s" % i].at[j - 1], sem["sup%d_r" % i].at[j - 1], dev)

    def grads_step1(i):
        c1_copy(i).start()

    def grads_step2(i):
        c1_copy(i).wait()
        hs = sem["core%d" % i]
        hs[...] = (k.gsrc[g_half(i, core), :].astype(F32) + hs[...].astype(F32)).astype(BF16)
        for j in range(1, 4):
            rs_copy(i, j).start()

    def grads_step3(i):
        qr = s.sizes[i] // 8
        acc = sem["core%d" % i][pl.ds(pl.multiple_of(quarter * qr, 16), qr), :].astype(F32)
        for j in range(1, 4):
            rs_copy(i, j).wait()
            acc = acc + sem["quart%d" % i][j - 1].astype(F32)
        if s.groups > 1:
            ref = sem["sup%d" % i]
            ref[group] = acc.astype(BF16)
            for j in range(1, s.groups):
                sup_copy(i, j).start()
            for j in range(1, s.groups):
                sup_copy(i, j).wait()
            acc = ref[0].astype(F32)
            for g in range(1, s.groups):
                acc = acc + ref[g].astype(F32)
        k.gout[g_rows(i, core, quarter), :] = acc.astype(BF16)
        for j in range(1, 4):
            ag_copy_g(i, j, quarter).start()

    def grads_step4(i):
        for j in range(1, 4):
            ag_copy_g(i, j, quarter).wait_send()
            ag_copy_g(i, j, lax.rem(quarter + 4 - j, 4)).wait_recv()
        c2_copy(i, core).start()

    def grads_step5(i):
        c2_copy(i, core).wait_send()
        c2_copy(i, 1 - core).wait_recv()

    loads = [
        pltpu.make_async_copy(patches, k.patches, k.loads.at[0]),
        pltpu.make_async_copy(qkv, k.qkv, k.loads.at[1]),
        pltpu.make_async_copy(out_weight, k.ow.at[t], k.loads.at[2]),
        pltpu.make_async_copy(up, k.up, k.loads.at[3]),
        pltpu.make_async_copy(down, k.down, k.loads.at[4]),
        pltpu.make_async_copy(cotangent, k.cot, k.loads.at[5]),
    ]
    for copy in loads:
        copy.start()
    barrier = pltpu.get_barrier_semaphore()

    @pl.loop(1, nb)
    def _(i):
        pl.semaphore_signal(barrier, inc=1, device_id=(lax.rem(b + i, nb), t), device_id_type=MESH)

    for j in range(1, nt):
        pl.semaphore_signal(barrier, inc=1, device_id=(b, z_peer(j)), device_id_type=MESH)

    lead_hot = (lax.broadcasted_iota(jnp.int32, (s.leads, L), 0) == row_of(leads_in)).astype(F32)
    loads[0].wait()
    hidden = k.patches[...] + mm_tn(lead_hot.astype(BF16), table[...])
    unit1, inverse1 = norm_stats(hidden)
    k.u1[...] = unit1
    k.r1[...] = inverse1
    k.mid[...] = hidden
    k.normed[...] = (unit1 * row_of(gain1) + row_of(bias1)).astype(BF16)
    loads[1].wait()

    def project(c):
        return mm_nt(k.qkv[c], k.normed[...])

    k.kv[b, 0:W, :] = project(1).astype(BF16)
    k.kv[b, W : 2 * W, :] = project(2).astype(BF16)
    gate_pad = jnp.zeros((4, D), F32)
    gate_rows = []
    for e in range(3):
        gate_rows += [gate[e].astype(F32), gate_pad]
    gate_rows += [gate_pad, gate_pad]
    my_gate = pl.ds(pl.multiple_of(t * 32, 32), 32)
    k.gate[my_gate, :] = jnp.concatenate(gate_rows, axis=0).astype(BF16)
    k.mask[t] = jnp.concatenate([pixel_mask[...].astype(F32), jnp.zeros((4, L), F32)], axis=0)
    pl.semaphore_wait(barrier, nb - 1 + nt - 1)

    def kv_at(band):
        return k.kv.at[band]

    ag_start("kv", kv_at)
    for j in range(1, nt):
        z_copy("zmask", j, k.mask.at[t], k.mask.at[t]).start()
        z_copy("zgate", j, k.gate.at[my_gate], k.gate.at[my_gate]).start()
    hw = W // 2
    loads[2].wait()

    def ow_half(tt, c):
        return k.ow.at[tt, pl.ds(pl.multiple_of(c * hw, hw), hw)]

    for j in range(1, nt):
        z_copy("zow", j, ow_half(t, core), ow_half(t, core)).start()
    k.qd[b, 0:W, :] = (project(0).astype(BF16).astype(F32) * SCALE).astype(BF16)

    for j in range(1, nt):
        z_copy("zmask", j, k.mask.at[t], k.mask.at[z_from(j)]).wait_recv()
    k.cnt[b] = jnp.broadcast_to(total(jnp.sum(k.mask[...], axis=0)), (8, 128))
    swap_start("cnt", every)

    k.ids[...] = windows_in[...].reshape(nb, L).astype(F32)

    def id_row(band):
        return k.ids[pl.ds(band, 1), :]

    def id_column(band):
        return jnp.transpose(jnp.broadcast_to(id_row(band), (128, L)))[:, 0:1]

    def head(h):
        return pl.ds(h * HEAD_DIM, HEAD_DIM)

    def value_head(h):
        return pl.ds(W + h * HEAD_DIM, HEAD_DIM)

    k.m[...] = jnp.full((8, L), MASKED, F32)
    k.l[...] = jnp.zeros((8, L), F32)
    k.acc[...] = jnp.zeros((W, L), F32)

    def forward_band(band):
        allowed = id_column(band) == id_row(b)
        for h in range(H):
            scores = mm_tn(k.kv[band, head(h), :], k.qd[b, head(h), :])
            scores = jnp.where(allowed, scores, MASKED)
            high = k.m[h : h + 1, :]
            new_high = jnp.maximum(high, jnp.max(scores, axis=0, keepdims=True))
            weights = jnp.exp(scores - new_high)
            factor = jnp.exp(high - new_high)
            k.m[h : h + 1, :] = new_high
            k.l[h : h + 1, :] = k.l[h : h + 1, :] * factor + jnp.sum(weights, axis=0, keepdims=True)
            k.acc[head(h), :] = k.acc[head(h), :] * factor + mm_nn(
                k.kv[band, value_head(h), :], weights.astype(BF16)
            )

    @pl.loop(0, s.half)
    def _(i):
        @pl.when(i > 0)
        def _():
            ag_relay("kv", kv_at, i)

        forward_band(band_same(i))
        ag_wait_relay("kv", kv_at, i)
        forward_band(band_sib(i))

    for h in range(H):
        att = k.acc[head(h), :] / k.l[h : h + 1, :]
        k.acc[head(h), :] = att
        k.att[t, head(h), :] = att.astype(BF16)
        k.st[b, h : h + 1, :] = k.m[h : h + 1, :] + jnp.log(k.l[h : h + 1, :])
    for j in range(1, nt):
        z_copy("zatt", j, k.att.at[t], k.att.at[t]).start()

    def q_at(band):
        return k.qd.at[band, pl.ds(0, W)]

    def da_at(band):
        return k.qd.at[band, pl.ds(W, W)]

    def st_at(band):
        return k.st.at[band]

    ag_start("q", q_at)
    for j in range(1, nt):
        src = z_from(j)
        z_copy("zow", j, ow_half(src, core), ow_half(src, core)).wait_recv()
        remote(
            ow_half(src, core), ow_half(src, core), k.zowr_s.at[j - 1], k.zowr_r.at[j - 1], (sib, t)
        ).start()
    for j in range(1, nt):
        src = z_from(j)
        remote(
            ow_half(src, 1 - core), ow_half(src, 1 - core), k.zowr_s.at[j - 1], k.zowr_r.at[j - 1], (sib, t)
        ).wait_recv()
    for j in range(1, nt):
        z_copy("zatt", j, k.att.at[t], k.att.at[z_from(j)]).wait_recv()
        z_copy("zgate", j, k.gate.at[my_gate], k.gate.at[my_gate]).wait_recv()

    middle = k.mid[...] + mm_tn(
        k.att[...].reshape(nt * W, L), k.ow[...].reshape(nt * W, D)
    )
    k.mid[...] = middle
    unit2, inverse2 = norm_stats(middle)
    k.u2[...] = unit2
    k.r2[...] = inverse2
    k.n2low[...] = (unit2 * row_of(gain2) + row_of(bias2)).astype(BF16)
    loads[3].wait()
    loads[4].wait()
    upward = mm_nn(k.n2low[...], k.up[...])
    k.upw[...] = upward
    k.actlow[...] = (0.5 * upward * (1.0 + lax.erf(upward * INV_SQRT2))).astype(BF16)
    k.ffp[...] = mm_nn(k.actlow[...], k.down[...]).astype(BF16)
    rs_start("zff", k.ffp, k.ffr)
    upward = k.upw[...]
    k.upw[...] = 0.5 * (1.0 + lax.erf(upward * INV_SQRT2)) + upward * (
        jnp.exp(-0.5 * upward * upward) * INV_SQRT_2PI
    )

    @pl.loop(1, s.half)
    def _(i):
        ag_relay("q", q_at, i)

    swap_wait("cnt", every)
    block_slice = k.mid[mine, :] + rs_sum("zff", k.ffp, k.ffr)
    k.blow[mine, :] = block_slice.astype(BF16)
    gather_start("zblk", k.blow)
    loads[5].wait()
    pixel_count = jnp.sum(k.cnt[...], axis=0)[0:1, 0:1]
    gather_wait("zblk", k.blow)

    block_copy = pltpu.make_async_copy(k.blow, o_block, k.loads.at[6])
    block_copy.start()
    logits = mm_nt(k.gate[...], k.blow[...]).reshape(nt, 4, 8, L)
    parts = [logits[:, e] for e in range(3)]
    high = jnp.maximum(jnp.maximum(parts[0], parts[1]), parts[2])
    logs = jnp.log(sum(jnp.exp(x - high) for x in parts))
    log_probs = [x - high - logs for x in parts]
    probs = [jnp.exp(x) for x in log_probs]
    entropy = -sum(p * x for p, x in zip(probs, log_probs))
    mask = k.mask[...]
    entropy_sum = total(jnp.sum(mask * entropy, axis=0))
    weight = mask * (float(s.pixels) / pixel_count)[None]
    grads = [-p * (x + entropy) * weight for p, x in zip(probs, log_probs)]
    grads.append(jnp.zeros((nt, 8, L), F32))
    logit_grad = jnp.stack(grads, axis=1).reshape(nt * 32, L).astype(BF16)
    out_grad = k.cot[...] + mm_tn(logit_grad, k.gate[...])
    k.cot[...] = out_grad
    k.oglow[...] = out_grad.astype(BF16)

    upward_grad = (mm_nt(k.oglow[...], k.down[...]) * k.upw[...]).astype(BF16)
    k.n2p[...] = mm_nt(upward_grad, k.up[...]).astype(BF16)
    rs_start("zn2", k.n2p, k.n2r)
    k.gsrc[0:F, :] = mm_tn(k.actlow[...], k.oglow[...]).astype(BF16)
    k.gsrc[F : F + D, :] = mm_tn(k.n2low[...], upward_grad).astype(BF16)
    grads_step1(0)
    lg_rows = jnp.stack(grads, axis=1).reshape(nt, 32, L)
    pick = lax.broadcasted_iota(jnp.int32, (nt, 1, 1), 0) == t
    own_lg = jnp.sum(jnp.where(pick, lg_rows, 0.0), axis=0).astype(BF16)
    k.va[near[1]] = mm_nn(own_lg, k.blow[...]).astype(BF16)
    k.ent[b] = jnp.broadcast_to(entropy_sum / pixel_count, (8, 128))
    swap_start("va", near)
    swap_start("ent", every)
    grads_step2(0)
    k.n2g[mine, :] = rs_sum("zn2", k.n2p, k.n2r).astype(BF16)
    gather_start("zn2g", k.n2g)
    gather_wait("zn2g", k.n2g)
    n2_grad = k.n2g[...].astype(F32)
    gain2_grad = jnp.sum(n2_grad * k.u2[...], axis=0, keepdims=True)
    bias2_grad = jnp.sum(n2_grad, axis=0, keepdims=True)
    middle_grad = k.cot[...] + norm_backward(n2_grad, k.u2[...], k.r2[...], row_of(gain2))
    k.cot[...] = middle_grad
    k.mglow[...] = middle_grad.astype(BF16)

    att_grad = mm_nt(k.ow[t], k.mglow[...]).astype(BF16)
    k.qd[b, W : 2 * W, :] = att_grad
    weighted = att_grad.astype(F32) * k.acc[...]
    for h in range(H):
        k.st[b, H + h : H + h + 1, :] = jnp.sum(
            weighted[h * HEAD_DIM : (h + 1) * HEAD_DIM], axis=0, keepdims=True
        )
    ag_start("st", st_at)
    ag_start("da", da_at)
    k.gsrc[s.bases[1] : s.bases[1] + W, :] = mm_nn(k.att[t], k.mglow[...]).astype(BF16)
    k.dq[...] = jnp.zeros((W, L), F32)
    k.dk[...] = jnp.zeros((W, L), F32)
    k.dv[...] = jnp.zeros((W, L), F32)

    @pl.loop(0, nb)
    def _(band):
        allowed = id_column(band) == id_row(b)
        for h in range(H):
            keys = k.kv[band, head(h), :]
            scores = jnp.where(allowed, mm_tn(keys, k.qd[b, head(h), :]), MASKED)
            prob = jnp.exp(scores - k.st[b, h : h + 1, :])
            dots = mm_tn(k.kv[band, value_head(h), :], k.qd[b, value_head(h), :])
            grad = (prob * (dots - k.st[b, H + h : H + h + 1, :])).astype(BF16)
            k.dq[head(h), :] += mm_nn(keys, grad)

    @pl.loop(1, s.half)
    def _(i):
        ag_wait_relay("q", q_at, i)

    ag_wait_relay("q", q_at, 0)
    my_column = id_column(b)

    def backward_band(band):
        allowed = my_column == id_row(band)
        for h in range(H):
            queries = k.qd[band, head(h), :]
            att_grads = k.qd[band, value_head(h), :]
            scores = jnp.where(allowed, mm_tn(k.kv[b, head(h), :], queries), MASKED)
            prob = jnp.exp(scores - k.st[band, h : h + 1, :])
            dots = mm_tn(k.kv[b, value_head(h), :], att_grads)
            grad = (prob * (dots - k.st[band, H + h : H + h + 1, :])).astype(BF16)
            k.dk[head(h), :] += mm_nt(queries, grad)
            k.dv[head(h), :] += mm_nt(att_grads, prob.astype(BF16))

    @pl.loop(0, s.half)
    def _(i):
        @pl.when(i > 0)
        def _():
            ag_relay("st", st_at, i)
            ag_relay("da", da_at, i)

        backward_band(band_same(i))
        ag_wait_relay("st", st_at, i)
        ag_wait_relay("da", da_at, i)
        backward_band(band_sib(i))

    grads_step3(0)
    k.dp[0] = (k.dq[...] * SCALE).astype(BF16)
    k.dp[1] = k.dk[...].astype(BF16)
    k.dp[2] = k.dv[...].astype(BF16)
    n1_part = mm_tn(k.dp[...].reshape(3 * W, L), k.qkv[...].reshape(3 * W, D))
    k.ngp[...] = n1_part.astype(BF16)
    rs_start("zng", k.ngp, k.ngr)
    base = s.bases[1] + W
    k.gsrc[base : base + 3 * W, :] = mm_nn(k.dp[...].reshape(3 * W, L), k.normed[...]).astype(BF16)
    grads_step1(1)
    grads_step2(1)
    k.ngg[mine, :] = rs_sum("zng", k.ngp, k.ngr).astype(BF16)
    gather_start("zngg", k.ngg)
    grads_step4(0)
    grads_step3(1)
    grads_step5(0)
    gather_wait("zngg", k.ngg)
    n1_grad = k.ngg[...].astype(F32)
    unit1 = k.u1[...]
    gain1_grad = jnp.sum(n1_grad * unit1, axis=0, keepdims=True)
    bias1_grad = jnp.sum(n1_grad, axis=0, keepdims=True)
    hidden_grad = k.cot[...] + norm_backward(n1_grad, unit1, k.r1[...], row_of(gain1))
    k.patches[...] = hidden_grad
    hidden_copy = pltpu.make_async_copy(k.patches, o_hidden, k.loads.at[7])
    hidden_copy.start()
    hot = lead_hot.astype(BF16)
    coarse = hidden_grad.astype(BF16)
    fine = (hidden_grad - coarse.astype(F32)).astype(BF16)
    tail = [mm_nn(hot, coarse) + mm_nn(hot, fine), gain1_grad, bias1_grad, gain2_grad, bias2_grad]
    tail.append(jnp.zeros((s.tail - s.leads - 4, D), F32))
    k.vb[near[1]] = jnp.concatenate(tail, axis=0).astype(BF16)
    swap_start("vb", near)
    grads_step4(1)
    swap_wait("ent", every)
    k.va_sum[...] = swap_sum("va")
    k.va_sum[24:32, 0:128] = jnp.sum(k.ent[...], axis=0)
    k.vb_sum[...] = swap_sum("vb")
    grads_step5(1)

    outs = [
        pltpu.make_async_copy(k.gout, o_grads, k.loads.at[0]),
        pltpu.make_async_copy(k.va_sum, o_va, k.loads.at[1]),
        pltpu.make_async_copy(k.vb_sum, o_vb, k.loads.at[2]),
    ]
    for copy in outs:
        copy.start()

    for j in range(1, nt):
        z_copy("zmask", j, k.mask.at[t], k.mask.at[t]).wait_send()
        z_copy("zgate", j, k.gate.at[my_gate], k.gate.at[my_gate]).wait_send()
        z_copy("zow", j, ow_half(t, core), ow_half(t, core)).wait_send()
        remote(
            ow_half(t, core), ow_half(t, core), k.zowr_s.at[j - 1], k.zowr_r.at[j - 1], (sib, t)
        ).wait_send()
        z_copy("zatt", j, k.att.at[t], k.att.at[t]).wait_send()
    rs_finish("zff", k.ffp, k.ffr)
    gather_finish("zblk", k.blow)
    rs_finish("zn2", k.n2p, k.n2r)
    gather_finish("zn2g", k.n2g)
    rs_finish("zng", k.ngp, k.ngr)
    gather_finish("zngg", k.ngg)
    ag_finish("kv", kv_at)
    ag_finish("q", q_at)
    ag_finish("da", da_at)
    ag_finish("st", st_at)
    swap_finish("cnt", every)
    swap_finish("ent", every)
    block_copy.wait()
    hidden_copy.wait()
    for copy in outs:
        copy.wait()


def last_kernel(
    s, block, hidden, grads, va, vb,
    o_block, o_pen, o_hidden, o_lead, o_g1, o_b1, o_qkv, o_out, o_g2, o_b2, o_up, o_down, o_gate,
):
    o_block[...] = block[...].astype(F32)
    o_hidden[...] = hidden[...]
    o_down[...] = grads[0 : s.F, :].astype(F32)
    o_up[...] = grads[s.F : s.F + s.D, :].astype(F32)
    base = s.bases[1]
    o_out[...] = grads[base : base + s.W, :].astype(F32)
    for c in range(3):
        rows = grads[base + (c + 1) * s.W : base + (c + 2) * s.W, :]
        o_qkv[c] = rows.astype(F32)
    small = va[...]
    for e in range(3):
        o_gate[e] = small[8 * e : 8 * e + 4]
    o_pen[...] = small[24:25, 0:1]
    tail = vb[...]
    o_lead[...] = tail[0 : s.leads]
    o_g1[...] = tail[s.leads + 0].reshape(s.D)
    o_b1[...] = tail[s.leads + 1].reshape(s.D)
    o_g2[...] = tail[s.leads + 2].reshape(s.D)
    o_b2[...] = tail[s.leads + 3].reshape(s.D)


def local(
    nb,
    nt,
    patches,
    window_ids,
    lead_index,
    lead_table,
    attention_gain,
    attention_bias,
    query_key_value,
    out_weight,
    feedforward_gain,
    feedforward_bias,
    up_weight,
    down_weight,
    gate_head,
    pixel_mask,
    cotangent,
):
    L, D = patches.shape
    leads = lead_table.shape[0]
    W = out_weight.shape[0]
    F = up_weight.shape[1]
    s = dims_of(nb, nt, L, D, W, F, leads, L * nb * pixel_mask.shape[0] * nt)
    scratch = scratch_of(s)
    vm = pl.BlockSpec(memory_space=pltpu.VMEM)
    hbm = pl.BlockSpec(memory_space=pl.ANY)
    block, hidden, grads, va, vb = pl.pallas_call(
        partial(main_kernel, s, tuple(scratch)),
        out_shape=(
            jax.ShapeDtypeStruct((L, D), BF16),
            jax.ShapeDtypeStruct((L, D), F32),
            jax.ShapeDtypeStruct((s.rows, D), BF16),
            jax.ShapeDtypeStruct((32, D), F32),
            jax.ShapeDtypeStruct((s.tail, D), F32),
        ),
        in_specs=[hbm, vm, vm, vm, vm, vm, hbm, hbm, vm, vm, hbm, hbm, vm, vm, hbm],
        out_specs=(hbm,) * 5,
        scratch_shapes=list(scratch.values()),
        compiler_params=pltpu.CompilerParams(
            collective_id=0, has_side_effects=True, vmem_limit_bytes=VMEM_LIMIT
        ),
        name="block_step",
    )(
        patches,
        window_ids,
        lead_index,
        lead_table,
        attention_gain,
        attention_bias,
        jnp.transpose(query_key_value, (0, 2, 1)),
        out_weight,
        feedforward_gain,
        feedforward_bias,
        up_weight,
        down_weight,
        gate_head,
        pixel_mask,
        cotangent,
    )
    vec = jax.ShapeDtypeStruct((D,), F32)
    outs = pl.pallas_call(
        partial(last_kernel, s),
        out_shape=(
            jax.ShapeDtypeStruct((L, D), F32),
            jax.ShapeDtypeStruct((1, 1), F32),
            jax.ShapeDtypeStruct((L, D), F32),
            jax.ShapeDtypeStruct((leads, D), F32),
            vec,
            vec,
            jax.ShapeDtypeStruct((3, W, D), F32),
            jax.ShapeDtypeStruct((W, D), F32),
            vec,
            vec,
            jax.ShapeDtypeStruct((D, F), F32),
            jax.ShapeDtypeStruct((F, D), F32),
            jax.ShapeDtypeStruct(gate_head.shape, F32),
        ),
        in_specs=[vm] * 5,
        out_specs=(vm,) * 13,
        compiler_params=pltpu.CompilerParams(vmem_limit_bytes=VMEM_LIMIT),
        name="write_out",
    )(block, hidden, grads, va, vb)
    outs = list(outs)
    outs[1] = outs[1].reshape(())
    outs[6] = jnp.transpose(outs[6], (0, 2, 1))
    return tuple(outs)


def solution(mesh):
    in_specs = (
        P("blk", None),
        P(),
        P("blk"),
        P(),
        P(),
        P(),
        P(None, None, "tp"),
        P("tp", None),
        P(),
        P(),
        P(None, "tp"),
        P("tp", None),
        P(None, "tp", None),
        P("tp", "blk"),
        P("blk", None),
    )
    out_specs = (
        P("blk", None),
        P(),
        P("blk", None),
        P(),
        P(),
        P(),
        P(None, None, "tp"),
        P("tp", None),
        P(),
        P(),
        P(None, "tp"),
        P("tp", None),
        P(None, "tp", None),
    )
    return jax.shard_map(
        partial(local, mesh.shape["blk"], mesh.shape["tp"]),
        mesh=mesh,
        in_specs=in_specs,
        out_specs=out_specs,
        check_vma=False,
    )
```

```python
from functools import partial
from types import SimpleNamespace

import jax
import jax.numpy as jnp
from jax import lax
from jax.experimental import pallas as pl
from jax.experimental.pallas import tpu as pltpu
from jax.sharding import PartitionSpec as P

HEAD_DIM = 64
EPS = 1e-05
MASKED = -1e30
SCALE = HEAD_DIM ** (-0.5)
GROUP = 8
F32 = jnp.float32
BF16 = jnp.bfloat16
MESH = pl.DeviceIdType.MESH
VMEM_LIMIT = 61 * 2**20
INV_SQRT2 = 0.7071067811865476
INV_SQRT_2PI = 0.3989422804014327


def dot(a, b, ca, cb):
    return lax.dot_general(a, b, (((ca,), (cb,)), ((), ())), preferred_element_type=F32)


def mm_nn(a, b):
    return dot(a, b, 1, 0)


def mm_nt(a, b):
    return dot(a, b, 1, 1)


def mm_tn(a, b):
    return dot(a, b, 0, 0)


def norm_stats(values):
    mean = jnp.mean(values, axis=-1, keepdims=True)
    centered = values - mean
    inverse = lax.rsqrt(jnp.mean(centered * centered, axis=-1, keepdims=True) + EPS)
    return centered * inverse, inverse


def norm_backward(incoming, unit_rows, inverse, gain):
    scaled = incoming * gain
    return inverse * (
        scaled
        - jnp.mean(scaled, axis=-1, keepdims=True)
        - unit_rows * jnp.mean(scaled * unit_rows, axis=-1, keepdims=True)
    )


def row_of(ref):
    return ref[...].reshape(1, ref.shape[0])


def total(x):
    return jnp.sum(jnp.sum(x, axis=0, keepdims=True), axis=1, keepdims=True)


def dims_of(nb, nt, tokens, width, local_width, hidden, leads, pixels):
    s = SimpleNamespace(nb=nb, nt=nt, L=tokens, D=width, W=local_width, F=hidden, leads=leads)
    s.H = local_width // HEAD_DIM
    s.S = tokens // nt
    s.half = nb // 2
    s.groups = nb // GROUP
    s.pixels = pixels
    s.sizes = (hidden + width, local_width * 2, local_width * 2)
    s.bases = (0, hidden + width, hidden + width + 2 * local_width)
    s.rows = sum(s.sizes)
    s.tail = (leads + 4 + 15) // 16 * 16
    return s


def scratch_of(s):
    L, D, W, F, nb, nt, S = s.L, s.D, s.W, s.F, s.nb, s.nt, s.S
    v = pltpu.VMEM
    out = {
        "patches": v((L, D), F32),
        "ids": v((nb, L), F32),
        "qkv": v((3, W, D), BF16),
        "ow": v((nt, W, D), BF16),
        "up": v((D, F), BF16),
        "down": v((F, D), BF16),
        "cot": v((L, D), F32),
        "gate": v((nt * 32, D), BF16),
        "mask": v((nt, 8, L), F32),
        "cnt": v((nb, 8, 128), F32),
        "u1": v((L, D), F32),
        "r1": v((L, 1), F32),
        "normed": v((L, D), BF16),
        "kv": v((nb, 2 * W, L), BF16),
        "qd": v((nb, 2 * W, L), BF16),
        "st": v((nb, 8, L), F32),
        "m": v((8, L), F32),
        "l": v((8, L), F32),
        "acc": v((W, L), F32),
        "att": v((nt, W, L), BF16),
        "mid": v((L, D), F32),
        "u2": v((L, D), F32),
        "r2": v((L, 1), F32),
        "n2low": v((L, D), BF16),
        "upw": v((L, F), F32),
        "actlow": v((L, F), BF16),
        "ffp": v((L, D), BF16),
        "ffr": v((nt - 1, S, D), BF16),
        "blow": v((L, D), BF16),
        "oglow": v((L, D), BF16),
        "n2p": v((L, D), BF16),
        "n2r": v((nt - 1, S, D), BF16),
        "n2g": v((L, D), BF16),
        "dasrc": v((nt, S, W), BF16),
        "datok": v((nt, S, W), BF16),
        "dq": v((W, L), F32),
        "dk": v((W, L), F32),
        "dv": v((W, L), F32),
        "dp": v((3, W, L), BF16),
        "ngp": v((L, D), BF16),
        "ngr": v((nt - 1, S, D), BF16),
        "ngg": v((L, D), BF16),
        "va": v((GROUP, 32, D), BF16),
        "vb": v((GROUP, s.tail, D), BF16),
        "ent": v((nb, 8, 128), F32),
        "va_sum": v((32, D), F32),
        "vb_sum": v((s.tail, D), F32),
        "gsrc": v((s.rows, D), BF16),
        "gout": v((s.rows, D), BF16),
    }
    dma = pltpu.SemaphoreType.DMA
    out["loads"] = dma((8,))
    for name in ("zmask", "zgate", "zow", "zowr", "zatt", "zff", "zblk", "zn2", "zn2g", "zda", "zng", "zngg"):
        out[name + "_s"] = dma((nt - 1,))
        out[name + "_r"] = dma((nt - 1,))
    for name in ("kv", "q", "da", "st"):
        for part in ("_s", "_r", "_rs", "_rr"):
            out[name + part] = dma((s.half,))
    for name, count in (("cnt", nb), ("ent", nb), ("va", GROUP), ("vb", GROUP)):
        out[name + "_s"] = dma((count - 1,))
        out[name + "_r"] = dma((count - 1,))
    if s.groups > 1:
        for name, rows in (("va2", 32), ("vb2", s.tail)):
            out[name] = v((s.groups, rows, D), BF16)
            out[name + "_s"] = dma((s.groups - 1,))
            out[name + "_r"] = dma((s.groups - 1,))
    for i, rows in enumerate(s.sizes):
        hr = rows // 2
        qr = hr // 4
        out["core%d" % i] = v((hr, D), BF16)
        out["quart%d" % i] = v((3, qr, D), BF16)
        if s.groups > 1:
            out["sup%d" % i] = v((s.groups, qr, D), BF16)
            out["sup%d_s" % i] = dma((s.groups - 1,))
            out["sup%d_r" % i] = dma((s.groups - 1,))
        for part in ("c1", "c2"):
            out["%s%d_s" % (part, i)] = dma((1,))
            out["%s%d_r" % (part, i)] = dma((1,))
        for part in ("rs", "ag"):
            out["%s%d_s" % (part, i)] = dma((3,))
            out["%s%d_r" % (part, i)] = dma((3,))
    return out


def main_kernel(s, names, *refs):
    (
        patches,
        windows_in,
        leads_in,
        table,
        gain1,
        bias1,
        qkv,
        out_weight,
        gain2,
        bias2,
        up,
        down,
        gate,
        pixel_mask,
        cotangent,
        o_block,
        o_hidden,
        o_grads,
        o_va,
        o_vb,
    ) = refs[:20]
    k = SimpleNamespace(**dict(zip(names, refs[20:])))
    sem = vars(k)
    L, D, W, F, H, S, nb, nt = s.L, s.D, s.W, s.F, s.H, s.S, s.nb, s.nt
    b = lax.axis_index("blk")
    t = lax.axis_index("tp")
    core = lax.rem(b, 2)
    pair = b // 2
    sib = b + 1 - 2 * core
    mine = pl.ds(pl.multiple_of(t * S, S), S)

    def z_peer(j):
        return lax.rem(t + j, nt)

    def remote(src, dst, send, recv, device):
        return pltpu.make_async_remote_copy(
            src, dst, send, recv, device_id=device, device_id_type=MESH
        )

    def z_copy(name, j, src, dst):
        return remote(src, dst, sem[name + "_s"].at[j - 1], sem[name + "_r"].at[j - 1], (b, z_peer(j)))

    def z_from(j):
        return lax.rem(t + nt - j, nt)

    def rows_of(tt):
        return pl.ds(pl.multiple_of(tt * S, S), S)

    def ag_copy(name, at, i, dst_band):
        return remote(at(b), at(b), sem[name + "_s"].at[i], sem[name + "_r"].at[i], (dst_band, t))

    def relay_copy(name, at, i, band):
        return remote(at(band), at(band), sem[name + "_rs"].at[i], sem[name + "_rr"].at[i], (sib, t))

    def band_same(i):
        return lax.rem(b + nb - 2 * i, nb)

    def band_sib(i):
        return lax.rem(sib + nb - 2 * i, nb)

    def ag_start(name, at):
        @pl.loop(1, s.half)
        def _(i):
            ag_copy(name, at, i, lax.rem(b + 2 * i, nb)).start()

        relay_copy(name, at, 0, b).start()

    def ag_relay(name, at, i):
        band = band_same(i)
        remote(at(band), at(band), sem[name + "_s"].at[i], sem[name + "_r"].at[i], (sib, t)).wait_recv()
        relay_copy(name, at, i, band).start()

    def ag_wait_relay(name, at, i):
        relay_copy(name, at, i, band_sib(i)).wait_recv()

    def ag_finish(name, at):
        @pl.loop(1, s.half)
        def _(i):
            ag_copy(name, at, i, sib).wait_send()

        @pl.loop(0, s.half)
        def _(i):
            relay_copy(name, at, i, b).wait_send()

    every = (nb, b, lambda i: i)
    near = (GROUP, lax.rem(b, GROUP), lambda i: b // GROUP * GROUP + i)
    far = (s.groups, b // GROUP, lambda i: i * GROUP + lax.rem(b, GROUP))

    def swap_copy(name, members, i, slot, to):
        ref = sem[name]
        return remote(
            ref.at[slot],
            ref.at[slot],
            sem[name + "_s"].at[i - 1],
            sem[name + "_r"].at[i - 1],
            (members[2](to), t),
        )

    def swap_start(name, members):
        count, me, _ = members

        @pl.loop(1, count)
        def _(i):
            swap_copy(name, members, i, me, lax.rem(me + i, count)).start()

    def swap_wait(name, members):
        count, me, _ = members

        @pl.loop(1, count)
        def _(i):
            peer = lax.rem(me + count - i, count)
            swap_copy(name, members, i, peer, peer).wait_recv()

    def swap_finish(name, members):
        count, me, _ = members

        @pl.loop(1, count)
        def _(i):
            swap_copy(name, members, i, me, lax.rem(me + i, count)).wait_send()

    def swap_sum(name):
        swap_wait(name, near)
        out = slots_sum(sem[name], GROUP)
        if s.groups > 1:
            sem[name + "2"][far[1]] = out.astype(BF16)
            swap_start(name + "2", far)
            swap_wait(name + "2", far)
            out = slots_sum(sem[name + "2"], s.groups)
            swap_finish(name + "2", far)
        swap_finish(name, near)
        return out

    def slots_sum(ref, count):
        return lax.fori_loop(
            1, count, lambda i, acc: acc + ref[i].astype(F32), ref[0].astype(F32)
        )

    def rs_start(name, part, recv):
        for j in range(1, nt):
            z_copy(name, j, part.at[rows_of(z_peer(j))], recv.at[j - 1]).start()

    def rs_sum(name, part, recv):
        acc = part[mine, :].astype(F32)
        for j in range(1, nt):
            z_copy(name, j, part.at[rows_of(z_from(j))], recv.at[j - 1]).wait_recv()
            acc = acc + recv[j - 1].astype(F32)
        return acc

    def rs_finish(name, part, recv):
        for j in range(1, nt):
            z_copy(name, j, part.at[rows_of(z_peer(j))], recv.at[j - 1]).wait_send()

    def gather_start(name, ref):
        for j in range(1, nt):
            z_copy(name, j, ref.at[mine], ref.at[mine]).start()

    def gather_wait(name, ref):
        for j in range(1, nt):
            rows = rows_of(z_from(j))
            z_copy(name, j, ref.at[rows], ref.at[rows]).wait_recv()

    def gather_finish(name, ref):
        for j in range(1, nt):
            z_copy(name, j, ref.at[mine], ref.at[mine]).wait_send()

    quarter = lax.rem(pair, 4)
    first_pair = pair - quarter
    group = pair // 4

    def g_rows(i, half, q):
        hr = s.sizes[i] // 2
        qr = hr // 4
        return pl.ds(pl.multiple_of(s.bases[i] + half * hr + q * qr, 16), qr)

    def g_half(i, half):
        hr = s.sizes[i] // 2
        return pl.ds(pl.multiple_of(s.bases[i] + half * hr, 16), hr)

    def q_peer(j):
        return lax.rem(quarter + j, 4)

    def q_dev(j):
        return ((first_pair + q_peer(j)) * 2 + core, t)

    def c1_copy(i):
        return remote(
            k.gsrc.at[g_half(i, 1 - core)], sem["core%d" % i], sem["c1%d_s" % i].at[0], sem["c1%d_r" % i].at[0], (sib, t)
        )

    def rs_copy(i, j):
        qr = s.sizes[i] // 8
        src = sem["core%d" % i].at[pl.ds(pl.multiple_of(q_peer(j) * qr, 16), qr)]
        return remote(
            src, sem["quart%d" % i].at[j - 1], sem["rs%d_s" % i].at[j - 1], sem["rs%d_r" % i].at[j - 1], q_dev(j)
        )

    def ag_copy_g(i, j, q):
        rows = g_rows(i, core, q)
        return remote(
            k.gout.at[rows], k.gout.at[rows], sem["ag%d_s" % i].at[j - 1], sem["ag%d_r" % i].at[j - 1], q_dev(j)
        )

    def c2_copy(i, half):
        rows = g_half(i, half)
        return remote(
            k.gout.at[rows], k.gout.at[rows], sem["c2%d_s" % i].at[0], sem["c2%d_r" % i].at[0], (sib, t)
        )

    def sup_copy(i, j):
        ref = sem["sup%d" % i]
        dev = ((lax.rem(group + j, s.groups) * 4 + quarter) * 2 + core, t)
        return remote(ref.at[group], ref.at[group], sem["sup%d_s" % i].at[j - 1], sem["sup%d_r" % i].at[j - 1], dev)

    def grads_step1(i):
        c1_copy(i).start()

    def grads_step2(i):
        c1_copy(i).wait()
        hs = sem["core%d" % i]
        hs[...] = (k.gsrc[g_half(i, core), :].astype(F32) + hs[...].astype(F32)).astype(BF16)
        for j in range(1, 4):
            rs_copy(i, j).start()

    def grads_step3(i):
        qr = s.sizes[i] // 8
        acc = sem["core%d" % i][pl.ds(pl.multiple_of(quarter * qr, 16), qr), :].astype(F32)
        for j in range(1, 4):
            rs_copy(i, j).wait()
            acc = acc + sem["quart%d" % i][j - 1].astype(F32)
        if s.groups > 1:
            ref = sem["sup%d" % i]
            ref[group] = acc.astype(BF16)
            for j in range(1, s.groups):
                sup_copy(i, j).start()
            for j in range(1, s.groups):
                sup_copy(i, j).wait()
            acc = ref[0].astype(F32)
            for g in range(1, s.groups):
                acc = acc + ref[g].astype(F32)
        k.gout[g_rows(i, core, quarter), :] = acc.astype(BF16)
        for j in range(1, 4):
            ag_copy_g(i, j, quarter).start()

    def grads_step4(i):
        for j in range(1, 4):
            ag_copy_g(i, j, quarter).wait_send()
            ag_copy_g(i, j, lax.rem(quarter + 4 - j, 4)).wait_recv()
        c2_copy(i, core).start()

    def grads_step5(i):
        c2_copy(i, core).wait_send()
        c2_copy(i, 1 - core).wait_recv()

    loads = [
        pltpu.make_async_copy(patches, k.patches, k.loads.at[0]),
        pltpu.make_async_copy(qkv, k.qkv, k.loads.at[1]),
        pltpu.make_async_copy(out_weight, k.ow.at[t], k.loads.at[2]),
        pltpu.make_async_copy(up, k.up, k.loads.at[3]),
        pltpu.make_async_copy(down, k.down, k.loads.at[4]),
        pltpu.make_async_copy(cotangent, k.cot, k.loads.at[5]),
    ]
    for copy in loads:
        copy.start()
    barrier = pltpu.get_barrier_semaphore()

    @pl.loop(1, nb)
    def _(i):
        pl.semaphore_signal(barrier, inc=1, device_id=(lax.rem(b + i, nb), t), device_id_type=MESH)

    for j in range(1, nt):
        pl.semaphore_signal(barrier, inc=1, device_id=(b, z_peer(j)), device_id_type=MESH)

    lead_hot = (lax.broadcasted_iota(jnp.int32, (s.leads, L), 0) == row_of(leads_in)).astype(F32)
    loads[0].wait()
    hidden = k.patches[...] + mm_tn(lead_hot.astype(BF16), table[...])
    unit1, inverse1 = norm_stats(hidden)
    k.u1[...] = unit1
    k.r1[...] = inverse1
    k.mid[...] = hidden
    k.normed[...] = (unit1 * row_of(gain1) + row_of(bias1)).astype(BF16)
    gate_pad = jnp.zeros((4, D), F32)
    gate_rows = []
    for e in range(3):
        gate_rows += [gate[e].astype(F32), gate_pad]
    gate_rows += [gate_pad, gate_pad]
    my_gate = pl.ds(pl.multiple_of(t * 32, 32), 32)
    k.gate[my_gate, :] = jnp.concatenate(gate_rows, axis=0).astype(BF16)
    k.mask[t] = jnp.concatenate([pixel_mask[...].astype(F32), jnp.zeros((4, L), F32)], axis=0)
    hw = W // 2

    def ow_half(tt, c):
        return k.ow.at[tt, pl.ds(pl.multiple_of(c * hw, hw), hw)]

    loads[2].wait()
    pl.semaphore_wait(barrier, nb - 1 + nt - 1)
    for j in range(1, nt):
        z_copy("zmask", j, k.mask.at[t], k.mask.at[t]).start()
        z_copy("zow", j, ow_half(t, core), ow_half(t, core)).start()
        z_copy("zgate", j, k.gate.at[my_gate], k.gate.at[my_gate]).start()
    loads[1].wait()

    def project(c):
        return mm_nt(k.qkv[c], k.normed[...])

    k.kv[b, 0:W, :] = project(1).astype(BF16)
    k.kv[b, W : 2 * W, :] = project(2).astype(BF16)

    def kv_at(band):
        return k.kv.at[band]

    ag_start("kv", kv_at)
    k.qd[b, 0:W, :] = (project(0).astype(BF16).astype(F32) * SCALE).astype(BF16)

    for j in range(1, nt):
        z_copy("zmask", j, k.mask.at[t], k.mask.at[z_from(j)]).wait_recv()
    k.cnt[b] = jnp.broadcast_to(total(jnp.sum(k.mask[...], axis=0)), (8, 128))
    swap_start("cnt", every)

    k.ids[...] = windows_in[...].reshape(nb, L).astype(F32)

    def id_row(band):
        return k.ids[pl.ds(band, 1), :]

    def id_column(band):
        return jnp.transpose(jnp.broadcast_to(id_row(band), (128, L)))[:, 0:1]

    def head(h):
        return pl.ds(h * HEAD_DIM, HEAD_DIM)

    def value_head(h):
        return pl.ds(W + h * HEAD_DIM, HEAD_DIM)

    k.m[...] = jnp.full((8, L), MASKED, F32)
    k.l[...] = jnp.zeros((8, L), F32)
    k.acc[...] = jnp.zeros((W, L), F32)

    def forward_bands(bands):
        tiles = [(h, i) for h in range(H) for i in range(len(bands))]
        allowed = [id_column(band) == id_row(b) for band in bands]
        scores = {
            (h, i): jnp.where(
                allowed[i], mm_tn(k.kv[bands[i], head(h), :], k.qd[b, head(h), :]), MASKED
            )
            for h, i in tiles
        }
        old_high = [k.m[h : h + 1, :] for h in range(H)]
        sums = [k.l[h : h + 1, :] for h in range(H)]
        outs = [k.acc[head(h), :] for h in range(H)]
        high = list(old_high)
        for h, i in tiles:
            high[h] = jnp.maximum(high[h], jnp.max(scores[h, i], axis=0, keepdims=True))
        weights = {(h, i): jnp.exp(scores[h, i] - high[h]) for h, i in tiles}
        factor = [jnp.exp(x - y) for x, y in zip(old_high, high)]
        outs = [x * f for x, f in zip(outs, factor)]
        sums = [x * f for x, f in zip(sums, factor)]
        for h, i in tiles:
            outs[h] += mm_nn(k.kv[bands[i], value_head(h), :], weights[h, i].astype(BF16))
            sums[h] += jnp.sum(weights[h, i], axis=0, keepdims=True)
        for h in range(H):
            k.m[h : h + 1, :] = high[h]
            k.l[h : h + 1, :] = sums[h]
            k.acc[head(h), :] = outs[h]

    @pl.loop(0, s.half)
    def _(i):
        @pl.when(i > 0)
        def _():
            ag_relay("kv", kv_at, i)

        ag_wait_relay("kv", kv_at, i)
        forward_bands([band_same(i), band_sib(i)])

    for h in range(H):
        att = k.acc[head(h), :] / k.l[h : h + 1, :]
        k.acc[head(h), :] = att
        k.att[t, head(h), :] = att.astype(BF16)
        k.st[b, h : h + 1, :] = k.m[h : h + 1, :] + jnp.log(k.l[h : h + 1, :])
    for j in range(1, nt):
        z_copy("zatt", j, k.att.at[t], k.att.at[t]).start()

    def q_at(band):
        return k.qd.at[band, pl.ds(0, W)]

    def da_at(band):
        return k.qd.at[band, pl.ds(W, W)]

    def st_at(band):
        return k.st.at[band]

    ag_start("q", q_at)
    for j in range(1, nt):
        src = z_from(j)
        z_copy("zow", j, ow_half(src, core), ow_half(src, core)).wait_recv()
        remote(
            ow_half(src, core), ow_half(src, core), k.zowr_s.at[j - 1], k.zowr_r.at[j - 1], (sib, t)
        ).start()
    for j in range(1, nt):
        src = z_from(j)
        remote(
            ow_half(src, 1 - core), ow_half(src, 1 - core), k.zowr_s.at[j - 1], k.zowr_r.at[j - 1], (sib, t)
        ).wait_recv()
    for j in range(1, nt):
        z_copy("zatt", j, k.att.at[t], k.att.at[z_from(j)]).wait_recv()
        z_copy("zgate", j, k.gate.at[my_gate], k.gate.at[my_gate]).wait_recv()

    middle = k.mid[...] + mm_tn(
        k.att[...].reshape(nt * W, L), k.ow[...].reshape(nt * W, D)
    )
    k.mid[...] = middle
    unit2, inverse2 = norm_stats(middle)
    k.u2[...] = unit2
    k.r2[...] = inverse2
    k.n2low[...] = (unit2 * row_of(gain2) + row_of(bias2)).astype(BF16)
    loads[3].wait()
    loads[4].wait()
    upward = mm_nn(k.n2low[...], k.up[...])
    k.upw[...] = upward
    k.actlow[...] = (0.5 * upward * (1.0 + lax.erf(upward * INV_SQRT2))).astype(BF16)
    k.ffp[...] = mm_nn(k.actlow[...], k.down[...]).astype(BF16)
    rs_start("zff", k.ffp, k.ffr)
    upward = k.upw[...]
    k.upw[...] = 0.5 * (1.0 + lax.erf(upward * INV_SQRT2)) + upward * (
        jnp.exp(-0.5 * upward * upward) * INV_SQRT_2PI
    )

    @pl.loop(1, s.half)
    def _(i):
        ag_relay("q", q_at, i)

    swap_wait("cnt", every)
    block_slice = k.mid[mine, :] + rs_sum("zff", k.ffp, k.ffr)
    k.blow[mine, :] = block_slice.astype(BF16)
    gather_start("zblk", k.blow)
    loads[5].wait()
    pixel_count = jnp.sum(k.cnt[...], axis=0)[0:1, 0:1]
    gather_wait("zblk", k.blow)

    block_copy = pltpu.make_async_copy(k.blow, o_block, k.loads.at[6])
    block_copy.start()
    logits = mm_nt(k.gate[...], k.blow[...]).reshape(nt, 4, 8, L)
    parts = [logits[:, e] for e in range(3)]
    high = jnp.maximum(jnp.maximum(parts[0], parts[1]), parts[2])
    logs = jnp.log(sum(jnp.exp(x - high) for x in parts))
    log_probs = [x - high - logs for x in parts]
    probs = [jnp.exp(x) for x in log_probs]
    entropy = -sum(p * x for p, x in zip(probs, log_probs))
    mask = k.mask[...]
    entropy_sum = total(jnp.sum(mask * entropy, axis=0))
    weight = mask * (float(s.pixels) / pixel_count)[None]
    grads = [-p * (x + entropy) * weight for p, x in zip(probs, log_probs)]
    grads.append(jnp.zeros((nt, 8, L), F32))
    logit_grad = jnp.stack(grads, axis=1).reshape(nt * 32, L).astype(BF16)
    out_grad = k.cot[...] + mm_tn(logit_grad, k.gate[...])
    k.cot[...] = out_grad
    k.oglow[...] = out_grad.astype(BF16)

    upward_grad = (mm_nt(k.oglow[...], k.down[...]) * k.upw[...]).astype(BF16)
    k.n2p[...] = mm_nt(upward_grad, k.up[...]).astype(BF16)
    rs_start("zn2", k.n2p, k.n2r)
    k.gsrc[0:F, :] = mm_tn(k.actlow[...], k.oglow[...]).astype(BF16)
    k.gsrc[F : F + D, :] = mm_tn(k.n2low[...], upward_grad).astype(BF16)
    grads_step1(0)
    lg_rows = jnp.stack(grads, axis=1).reshape(nt, 32, L)
    pick = lax.broadcasted_iota(jnp.int32, (nt, 1, 1), 0) == t
    own_lg = jnp.sum(jnp.where(pick, lg_rows, 0.0), axis=0).astype(BF16)
    k.va[near[1]] = mm_nn(own_lg, k.blow[...]).astype(BF16)
    k.ent[b] = jnp.broadcast_to(entropy_sum / pixel_count, (8, 128))
    swap_start("va", near)
    swap_start("ent", every)
    grads_step2(0)
    n2_low = rs_sum("zn2", k.n2p, k.n2r).astype(BF16)
    k.n2g[mine, :] = n2_low

    def middle_backward(n2_grad, rows):
        return k.cot[rows, :] + norm_backward(n2_grad, k.u2[rows, :], k.r2[rows, :], row_of(gain2))

    low_slice = middle_backward(n2_low.astype(F32), mine).astype(BF16)
    for tt in range(nt):
        k.dasrc[tt] = mm_nt(low_slice, k.ow[tt]).astype(BF16)
    for j in range(1, nt):
        z_copy("zda", j, k.dasrc.at[z_peer(j)], k.datok.at[t]).start()
    gather_start("zn2g", k.n2g)
    k.datok[t] = k.dasrc[t]
    for j in range(1, nt):
        z_copy("zda", j, k.dasrc.at[z_peer(j)], k.datok.at[z_from(j)]).wait_recv()
    att_grad = jnp.transpose(k.datok[...].reshape(L, W).astype(F32)).astype(BF16)
    k.qd[b, W : 2 * W, :] = att_grad
    weighted = att_grad.astype(F32) * k.acc[...]
    for h in range(H):
        k.st[b, H + h : H + h + 1, :] = jnp.sum(
            weighted[h * HEAD_DIM : (h + 1) * HEAD_DIM], axis=0, keepdims=True
        )
    ag_start("st", st_at)
    ag_start("da", da_at)
    k.dq[...] = jnp.zeros((W, L), F32)
    k.dk[...] = jnp.zeros((W, L), F32)
    k.dv[...] = jnp.zeros((W, L), F32)
    my_column = id_column(b)

    def score_grads(allowed, scores, dots, stats):
        probs = {
            (h, i): jnp.exp(jnp.where(allowed[i], x, MASKED) - stats[i][h : h + 1])
            for (h, i), x in scores.items()
        }
        grads = {
            (h, i): (x * (dots[h, i] - stats[i][H + h : H + h + 1])).astype(BF16)
            for (h, i), x in probs.items()
        }
        return probs, grads

    @pl.loop(0, s.half)
    def _(step):
        bands = [2 * step, 2 * step + 1]
        tiles = [(h, i) for h in range(H) for i in range(2)]
        allowed = [id_column(band) == id_row(b) for band in bands]
        scores = {(h, i): mm_tn(k.kv[bands[i], head(h), :], k.qd[b, head(h), :]) for h, i in tiles}
        dots = {
            (h, i): mm_tn(k.kv[bands[i], value_head(h), :], k.qd[b, value_head(h), :]) for h, i in tiles
        }
        outs = [k.dq[head(h), :] for h in range(H)]
        _, grads = score_grads(allowed, scores, dots, [k.st[b]] * 2)
        for h, i in tiles:
            outs[h] += mm_nn(k.kv[bands[i], head(h), :], grads[h, i])
        for h in range(H):
            k.dq[head(h), :] = outs[h]

    k.dp[0] = (k.dq[...] * SCALE).astype(BF16)
    base = s.bases[1]
    gather_wait("zn2g", k.n2g)
    n2_grad = k.n2g[...].astype(F32)
    gain2_grad = jnp.sum(n2_grad * k.u2[...], axis=0, keepdims=True)
    bias2_grad = jnp.sum(n2_grad, axis=0, keepdims=True)
    middle_grad = middle_backward(n2_grad, pl.ds(0, L))
    k.cot[...] = middle_grad
    k.gsrc[base : base + W, :] = mm_nn(k.att[t], middle_grad.astype(BF16)).astype(BF16)
    k.gsrc[base + W : base + 2 * W, :] = mm_nn(k.dp[0], k.normed[...]).astype(BF16)
    grads_step1(1)
    grads_step3(0)

    @pl.loop(1, s.half)
    def _(i):
        ag_wait_relay("q", q_at, i)

    ag_wait_relay("q", q_at, 0)

    def backward_bands(bands):
        tiles = [(h, i) for h in range(H) for i in range(len(bands))]
        allowed = [my_column == id_row(band) for band in bands]
        scores = {(h, i): mm_tn(k.kv[b, head(h), :], k.qd[bands[i], head(h), :]) for h, i in tiles}
        dots = {
            (h, i): mm_tn(k.kv[b, value_head(h), :], k.qd[bands[i], value_head(h), :]) for h, i in tiles
        }
        key_outs = [k.dk[head(h), :] for h in range(H)]
        value_outs = [k.dv[head(h), :] for h in range(H)]
        probs, grads = score_grads(allowed, scores, dots, [k.st[band] for band in bands])
        for h, i in tiles:
            key_outs[h] += mm_nt(k.qd[bands[i], head(h), :], grads[h, i])
            value_outs[h] += mm_nt(k.qd[bands[i], value_head(h), :], probs[h, i].astype(BF16))
        for h in range(H):
            k.dk[head(h), :] = key_outs[h]
            k.dv[head(h), :] = value_outs[h]

    @pl.loop(0, s.half)
    def _(i):
        @pl.when(i > 0)
        def _():
            ag_relay("st", st_at, i)
            ag_relay("da", da_at, i)

        ag_wait_relay("st", st_at, i)
        ag_wait_relay("da", da_at, i)
        backward_bands([band_same(i), band_sib(i)])

    grads_step2(1)
    k.dp[1] = k.dk[...].astype(BF16)
    k.dp[2] = k.dv[...].astype(BF16)
    n1_part = mm_tn(k.dp[...].reshape(3 * W, L), k.qkv[...].reshape(3 * W, D))
    k.ngp[...] = n1_part.astype(BF16)
    rs_start("zng", k.ngp, k.ngr)
    base = s.bases[2]
    k.gsrc[base : base + 2 * W, :] = mm_nn(k.dp[1:3].reshape(2 * W, L), k.normed[...]).astype(BF16)
    grads_step1(2)
    grads_step3(1)
    grads_step2(2)
    k.ngg[mine, :] = rs_sum("zng", k.ngp, k.ngr).astype(BF16)
    gather_start("zngg", k.ngg)
    grads_step4(0)
    grads_step4(1)
    grads_step3(2)
    gather_wait("zngg", k.ngg)
    n1_grad = k.ngg[...].astype(F32)
    unit1 = k.u1[...]
    gain1_grad = jnp.sum(n1_grad * unit1, axis=0, keepdims=True)
    bias1_grad = jnp.sum(n1_grad, axis=0, keepdims=True)
    hidden_grad = k.cot[...] + norm_backward(n1_grad, unit1, k.r1[...], row_of(gain1))
    k.patches[...] = hidden_grad
    hidden_copy = pltpu.make_async_copy(k.patches, o_hidden, k.loads.at[7])
    hidden_copy.start()
    hot = lead_hot.astype(BF16)
    coarse = hidden_grad.astype(BF16)
    fine = (hidden_grad - coarse.astype(F32)).astype(BF16)
    tail = [mm_nn(hot, coarse) + mm_nn(hot, fine), gain1_grad, bias1_grad, gain2_grad, bias2_grad]
    tail.append(jnp.zeros((s.tail - s.leads - 4, D), F32))
    k.vb[near[1]] = jnp.concatenate(tail, axis=0).astype(BF16)
    swap_start("vb", near)
    grads_step4(2)
    swap_wait("ent", every)
    k.va_sum[...] = swap_sum("va")
    k.va_sum[24:32, 0:128] = jnp.sum(k.ent[...], axis=0)
    k.vb_sum[...] = swap_sum("vb")
    for i in range(3):
        grads_step5(i)

    outs = [
        pltpu.make_async_copy(k.gout, o_grads, k.loads.at[0]),
        pltpu.make_async_copy(k.va_sum, o_va, k.loads.at[1]),
        pltpu.make_async_copy(k.vb_sum, o_vb, k.loads.at[2]),
    ]
    for copy in outs:
        copy.start()

    for j in range(1, nt):
        z_copy("zmask", j, k.mask.at[t], k.mask.at[t]).wait_send()
        z_copy("zgate", j, k.gate.at[my_gate], k.gate.at[my_gate]).wait_send()
        z_copy("zow", j, ow_half(t, core), ow_half(t, core)).wait_send()
        remote(
            ow_half(t, core), ow_half(t, core), k.zowr_s.at[j - 1], k.zowr_r.at[j - 1], (sib, t)
        ).wait_send()
        z_copy("zatt", j, k.att.at[t], k.att.at[t]).wait_send()
        z_copy("zda", j, k.dasrc.at[z_peer(j)], k.datok.at[t]).wait_send()
    rs_finish("zff", k.ffp, k.ffr)
    gather_finish("zblk", k.blow)
    rs_finish("zn2", k.n2p, k.n2r)
    gather_finish("zn2g", k.n2g)
    rs_finish("zng", k.ngp, k.ngr)
    gather_finish("zngg", k.ngg)
    ag_finish("kv", kv_at)
    ag_finish("q", q_at)
    ag_finish("da", da_at)
    ag_finish("st", st_at)
    swap_finish("cnt", every)
    swap_finish("ent", every)
    block_copy.wait()
    hidden_copy.wait()
    for copy in outs:
        copy.wait()


def last_kernel(
    s, block, hidden, grads, va, vb,
    o_block, o_pen, o_hidden, o_lead, o_g1, o_b1, o_qkv, o_out, o_g2, o_b2, o_up, o_down, o_gate,
):
    o_block[...] = block[...].astype(F32)
    o_hidden[...] = hidden[...]
    o_down[...] = grads[0 : s.F, :].astype(F32)
    o_up[...] = grads[s.F : s.F + s.D, :].astype(F32)
    base = s.bases[1]
    o_out[...] = grads[base : base + s.W, :].astype(F32)
    for c in range(3):
        rows = grads[base + (c + 1) * s.W : base + (c + 2) * s.W, :]
        o_qkv[c] = rows.astype(F32)
    small = va[...]
    for e in range(3):
        o_gate[e] = small[8 * e : 8 * e + 4]
    o_pen[...] = small[24:25, 0:1]
    tail = vb[...]
    o_lead[...] = tail[0 : s.leads]
    o_g1[...] = tail[s.leads + 0].reshape(s.D)
    o_b1[...] = tail[s.leads + 1].reshape(s.D)
    o_g2[...] = tail[s.leads + 2].reshape(s.D)
    o_b2[...] = tail[s.leads + 3].reshape(s.D)


def local(
    nb,
    nt,
    patches,
    window_ids,
    lead_index,
    lead_table,
    attention_gain,
    attention_bias,
    query_key_value,
    out_weight,
    feedforward_gain,
    feedforward_bias,
    up_weight,
    down_weight,
    gate_head,
    pixel_mask,
    cotangent,
):
    L, D = patches.shape
    leads = lead_table.shape[0]
    W = out_weight.shape[0]
    F = up_weight.shape[1]
    s = dims_of(nb, nt, L, D, W, F, leads, L * nb * pixel_mask.shape[0] * nt)
    scratch = scratch_of(s)
    vm = pl.BlockSpec(memory_space=pltpu.VMEM)
    hbm = pl.BlockSpec(memory_space=pl.ANY)
    block, hidden, grads, va, vb = pl.pallas_call(
        partial(main_kernel, s, tuple(scratch)),
        out_shape=(
            jax.ShapeDtypeStruct((L, D), BF16),
            jax.ShapeDtypeStruct((L, D), F32),
            jax.ShapeDtypeStruct((s.rows, D), BF16),
            jax.ShapeDtypeStruct((32, D), F32),
            jax.ShapeDtypeStruct((s.tail, D), F32),
        ),
        in_specs=[hbm, vm, vm, vm, vm, vm, hbm, hbm, vm, vm, hbm, hbm, vm, vm, hbm],
        out_specs=(hbm,) * 5,
        scratch_shapes=list(scratch.values()),
        compiler_params=pltpu.CompilerParams(
            collective_id=0, has_side_effects=True, vmem_limit_bytes=VMEM_LIMIT
        ),
        name="block_step",
    )(
        patches,
        window_ids,
        lead_index,
        lead_table,
        attention_gain,
        attention_bias,
        jnp.transpose(query_key_value, (0, 2, 1)),
        out_weight,
        feedforward_gain,
        feedforward_bias,
        up_weight,
        down_weight,
        gate_head,
        pixel_mask,
        cotangent,
    )
    vec = jax.ShapeDtypeStruct((D,), F32)
    outs = pl.pallas_call(
        partial(last_kernel, s),
        out_shape=(
            jax.ShapeDtypeStruct((L, D), F32),
            jax.ShapeDtypeStruct((1, 1), F32),
            jax.ShapeDtypeStruct((L, D), F32),
            jax.ShapeDtypeStruct((leads, D), F32),
            vec,
            vec,
            jax.ShapeDtypeStruct((3, W, D), F32),
            jax.ShapeDtypeStruct((W, D), F32),
            vec,
            vec,
            jax.ShapeDtypeStruct((D, F), F32),
            jax.ShapeDtypeStruct((F, D), F32),
            jax.ShapeDtypeStruct(gate_head.shape, F32),
        ),
        in_specs=[vm] * 5,
        out_specs=(vm,) * 13,
        compiler_params=pltpu.CompilerParams(vmem_limit_bytes=VMEM_LIMIT),
        name="write_out",
    )(block, hidden, grads, va, vb)
    outs = list(outs)
    outs[1] = outs[1].reshape(())
    outs[6] = jnp.transpose(outs[6], (0, 2, 1))
    return tuple(outs)


def solution(mesh):
    in_specs = (
        P("blk", None),
        P(),
        P("blk"),
        P(),
        P(),
        P(),
        P(None, None, "tp"),
        P("tp", None),
        P(),
        P(),
        P(None, "tp"),
        P("tp", None),
        P(None, "tp", None),
        P("tp", "blk"),
        P("blk", None),
    )
    out_specs = (
        P("blk", None),
        P(),
        P("blk", None),
        P(),
        P(),
        P(),
        P(None, None, "tp"),
        P("tp", None),
        P(),
        P(),
        P(None, "tp"),
        P("tp", None),
        P(None, "tp", None),
    )
    return jax.shard_map(
        partial(local, mesh.shape["blk"], mesh.shape["tp"]),
        mesh=mesh,
        in_specs=in_specs,
        out_specs=out_specs,
        check_vma=False,
    )
```

```python
from functools import partial
from types import SimpleNamespace

import jax
import jax.numpy as jnp
from jax import lax
from jax.experimental import pallas as pl
from jax.experimental.pallas import tpu as pltpu
from jax.sharding import PartitionSpec as P

HEAD_DIM = 64
EPS = 1e-05
MASKED = -1e30
SCALE = HEAD_DIM ** (-0.5)
GROUP = 8
F32 = jnp.float32
BF16 = jnp.bfloat16
MESH = pl.DeviceIdType.MESH
VMEM_LIMIT = 61 * 2**20
INV_SQRT2 = 0.7071067811865476
INV_SQRT_2PI = 0.3989422804014327


def dot(a, b, ca, cb):
    return lax.dot_general(a, b, (((ca,), (cb,)), ((), ())), preferred_element_type=F32)


def mm_nn(a, b):
    return dot(a, b, 1, 0)


def mm_nt(a, b):
    return dot(a, b, 1, 1)


def mm_tn(a, b):
    return dot(a, b, 0, 0)


def norm_stats(values):
    mean = jnp.mean(values, axis=-1, keepdims=True)
    centered = values - mean
    inverse = lax.rsqrt(jnp.mean(centered * centered, axis=-1, keepdims=True) + EPS)
    return centered * inverse, inverse


def norm_backward(incoming, unit_rows, inverse, gain):
    scaled = incoming * gain
    return inverse * (
        scaled
        - jnp.mean(scaled, axis=-1, keepdims=True)
        - unit_rows * jnp.mean(scaled * unit_rows, axis=-1, keepdims=True)
    )


def row_of(ref):
    return ref[...].reshape(1, ref.shape[0])


def total(x):
    return jnp.sum(jnp.sum(x, axis=0, keepdims=True), axis=1, keepdims=True)


def dims_of(nb, nt, tokens, width, local_width, hidden, leads, pixels):
    s = SimpleNamespace(nb=nb, nt=nt, L=tokens, D=width, W=local_width, F=hidden, leads=leads)
    s.H = local_width // HEAD_DIM
    s.T = tokens // 2
    s.R = s.T // nt
    s.half = nb // 2
    s.groups = nb // GROUP
    s.pixels = pixels
    s.sizes = (hidden, width, local_width * 2, local_width * 2)
    s.bases = tuple(sum(s.sizes[:i]) for i in range(4))
    s.rows = sum(s.sizes)
    s.tail = (leads + 4 + 15) // 16 * 16
    return s


def scratch_of(s):
    L, D, W, F, nb, nt, R = s.L, s.D, s.W, s.F, s.nb, s.nt, s.R
    v = pltpu.VMEM
    out = {
        "patches": v((L, D), F32),
        "windows": v((nb * L,), jnp.int32),
        "lead_index": v((L,), jnp.int32),
        "table": v((s.leads, D), BF16),
        "gain1": v((D,), F32),
        "bias1": v((D,), F32),
        "gain2": v((D,), F32),
        "bias2": v((D,), F32),
        "pix": v((4, L), jnp.int32),
        "head": v((3, 4, D), BF16),
        "ids": v((nb, L), F32),
        "qkv": v((3, W, D), BF16),
        "ow": v((nt, W, D), BF16),
        "up": v((D, F), BF16),
        "down": v((F, D), BF16),
        "cot": v((L, D), F32),
        "gatec": v((nt, 16, D), BF16),
        "gate": v((nt * 32, D), BF16),
        "mask": v((nt, 8, L), F32),
        "cnt": v((nb, 8, 128), F32),
        "u1": v((L, D), F32),
        "r1": v((L, 1), F32),
        "normed": v((L, D), BF16),
        "kv": v((nb, 2 * W, L), BF16),
        "qd": v((nb, 2 * W, L), BF16),
        "st": v((nb, 8, L), F32),
        "m": v((8, L), F32),
        "l": v((8, L), F32),
        "acc": v((W, L), F32),
        "att": v((nt, W, L), BF16),
        "mid": v((L, D), F32),
        "u2": v((L, D), F32),
        "r2": v((L, 1), F32),
        "n2low": v((L, D), BF16),
        "upw": v((L, F), F32),
        "actlow": v((L, F), BF16),
        "ffp": v((L, D), BF16),
        "ffr": v((2, nt - 1, R, D), BF16),
        "blow": v((L, D), BF16),
        "lg": v((nt * 32, L), BF16),
        "oglow": v((L, D), BF16),
        "ug": v((L, F), BF16),
        "n2p": v((L, D), BF16),
        "n2r": v((2, nt - 1, R, D), BF16),
        "n2g": v((L, D), BF16),
        "dasrc": v((2, nt, R, W), BF16),
        "datok": v((2, nt, R, W), BF16),
        "dq": v((W, L), F32),
        "dk": v((W, L), F32),
        "dv": v((W, L), F32),
        "dp": v((3, W, L), BF16),
        "ngp": v((L, D), BF16),
        "ngr": v((2, nt - 1, R, D), BF16),
        "ngg": v((L, D), BF16),
        "va": v((GROUP, 32, D), BF16),
        "vb": v((GROUP, s.tail, D), BF16),
        "ent": v((nb, 8, 128), F32),
        "va_sum": v((32, D), F32),
        "vb_sum": v((s.tail, D), F32),
        "gsrc": v((s.rows, D), BF16),
        "gout": v((s.rows, D), BF16),
    }
    dma = pltpu.SemaphoreType.DMA
    out["loads"] = dma((15,))
    out["stores"] = dma((8,))
    for name in ("zmask", "zgate", "zow", "zowr", "zatt", "zff", "zblk", "zn2", "zn2g", "zda", "zng", "zngg"):
        out[name + "_s"] = dma((2 * (nt - 1),))
        out[name + "_r"] = dma((2 * (nt - 1),))
    for name in ("kv", "q", "da0", "da1", "st"):
        for part in ("_s", "_r", "_rs", "_rr"):
            out[name + part] = dma((s.half,))
    for name, count in (("cnt", nb), ("ent", nb), ("va", GROUP), ("vb", GROUP)):
        out[name + "_s"] = dma((count - 1,))
        out[name + "_r"] = dma((count - 1,))
    if s.groups > 1:
        for name, rows in (("va2", 32), ("vb2", s.tail)):
            out[name] = v((s.groups, rows, D), BF16)
            out[name + "_s"] = dma((s.groups - 1,))
            out[name + "_r"] = dma((s.groups - 1,))
    for i, rows in enumerate(s.sizes):
        hr = rows // 2
        qr = hr // 4
        out["core%d" % i] = v((hr, D), BF16)
        out["quart%d" % i] = v((3, qr, D), BF16)
        if s.groups > 1:
            out["sup%d" % i] = v((s.groups, qr, D), BF16)
            out["sup%d_s" % i] = dma((s.groups - 1,))
            out["sup%d_r" % i] = dma((s.groups - 1,))
        out["gs%d" % i] = dma((8,))
        out["gr%d" % i] = dma((8,))
    return out


def main_kernel(s, names, *refs):
    (
        patches,
        windows_in,
        leads_in,
        table,
        gain1,
        bias1,
        qkv,
        out_weight,
        gain2,
        bias2,
        up,
        down,
        gate,
        pixel_mask,
        cotangent,
        o_block,
        o_hidden,
        o_grads,
        o_va,
        o_vb,
    ) = refs[:20]
    k = SimpleNamespace(**dict(zip(names, refs[20:])))
    sem = vars(k)
    L, D, W, F, H, T, R, nb, nt = s.L, s.D, s.W, s.F, s.H, s.T, s.R, s.nb, s.nt
    b = lax.axis_index("blk")
    t = lax.axis_index("tp")
    core = lax.rem(b, 2)
    pair = b // 2
    sib = b + 1 - 2 * core

    def z_peer(j):
        return lax.rem(t + j, nt)

    def z_from(j):
        return lax.rem(t + nt - j, nt)

    def remote(src, dst, send, recv, device):
        return pltpu.make_async_remote_copy(
            src, dst, send, recv, device_id=device, device_id_type=MESH
        )

    def z_copy(name, j, src, dst, h=0):
        i = h * (nt - 1) + j - 1
        return remote(src, dst, sem[name + "_s"].at[i], sem[name + "_r"].at[i], (b, z_peer(j)))

    def half(h):
        return pl.ds(h * T, T)

    def piece(h, tt):
        return pl.ds(pl.multiple_of(h * T + tt * R, R), R)

    def ag_copy(name, at, i, dst_band):
        return remote(at(b), at(b), sem[name + "_s"].at[i], sem[name + "_r"].at[i], (dst_band, t))

    def relay_copy(name, at, i, band):
        return remote(at(band), at(band), sem[name + "_rs"].at[i], sem[name + "_rr"].at[i], (sib, t))

    def band_same(i):
        return lax.rem(b + nb - 2 * i, nb)

    def band_sib(i):
        return lax.rem(sib + nb - 2 * i, nb)

    def ag_start(name, at):
        @pl.loop(1, s.half)
        def _(i):
            ag_copy(name, at, i, lax.rem(b + 2 * i, nb)).start()

        relay_copy(name, at, 0, b).start()

    def ag_relay(name, at, i):
        band = band_same(i)
        remote(at(band), at(band), sem[name + "_s"].at[i], sem[name + "_r"].at[i], (sib, t)).wait_recv()
        relay_copy(name, at, i, band).start()

    def ag_wait_relay(name, at, i):
        relay_copy(name, at, i, band_sib(i)).wait_recv()

    def ag_finish(name, at):
        @pl.loop(1, s.half)
        def _(i):
            ag_copy(name, at, i, sib).wait_send()

        @pl.loop(0, s.half)
        def _(i):
            relay_copy(name, at, i, b).wait_send()

    every = (nb, b, lambda i: i)
    near = (GROUP, lax.rem(b, GROUP), lambda i: b // GROUP * GROUP + i)
    far = (s.groups, b // GROUP, lambda i: i * GROUP + lax.rem(b, GROUP))

    def swap_copy(name, members, i, slot, to):
        ref = sem[name]
        return remote(
            ref.at[slot],
            ref.at[slot],
            sem[name + "_s"].at[i - 1],
            sem[name + "_r"].at[i - 1],
            (members[2](to), t),
        )

    def swap_start(name, members):
        count, me, _ = members

        @pl.loop(1, count)
        def _(i):
            swap_copy(name, members, i, me, lax.rem(me + i, count)).start()

    def swap_wait(name, members):
        count, me, _ = members

        @pl.loop(1, count)
        def _(i):
            peer = lax.rem(me + count - i, count)
            swap_copy(name, members, i, peer, peer).wait_recv()

    def swap_finish(name, members):
        count, me, _ = members

        @pl.loop(1, count)
        def _(i):
            swap_copy(name, members, i, me, lax.rem(me + i, count)).wait_send()

    def slots_sum(ref, count):
        return lax.fori_loop(
            1, count, lambda i, acc: acc + ref[i].astype(F32), ref[0].astype(F32)
        )

    def swap_sum(name):
        swap_wait(name, near)
        out = slots_sum(sem[name], GROUP)
        if s.groups > 1:
            sem[name + "2"][far[1]] = out.astype(BF16)
            swap_start(name + "2", far)
            swap_wait(name + "2", far)
            out = slots_sum(sem[name + "2"], s.groups)
            swap_finish(name + "2", far)
        swap_finish(name, near)
        return out

    def rs_start(name, h, part, recv):
        for j in range(1, nt):
            z_copy(name, j, part.at[piece(h, z_peer(j))], recv.at[h, j - 1], h).start()

    def rs_sum(name, h, part, recv):
        acc = part[piece(h, t), :].astype(F32)
        for j in range(1, nt):
            z_copy(name, j, part.at[piece(h, z_from(j))], recv.at[h, j - 1], h).wait_recv()
            acc = acc + recv[h, j - 1].astype(F32)
        return acc

    def rs_finish(name, part, recv):
        for h in range(2):
            for j in range(1, nt):
                z_copy(name, j, part.at[piece(h, z_peer(j))], recv.at[h, j - 1], h).wait_send()

    def gather_start(name, h, ref):
        for j in range(1, nt):
            z_copy(name, j, ref.at[piece(h, t)], ref.at[piece(h, t)], h).start()

    def gather_wait(name, h, ref):
        for j in range(1, nt):
            rows = piece(h, z_from(j))
            z_copy(name, j, ref.at[rows], ref.at[rows], h).wait_recv()

    def gather_finish(name, ref):
        for h in range(2):
            for j in range(1, nt):
                z_copy(name, j, ref.at[piece(h, t)], ref.at[piece(h, t)], h).wait_send()

    quarter = lax.rem(pair, 4)
    first_pair = pair - quarter
    group = pair // 4
    low_peer = quarter + 1 - 2 * lax.rem(quarter, 2)
    high_peer = lax.rem(quarter + 2, 4)
    first = low_peer * (1 - core) + high_peer * core
    second = low_peer * core + high_peer * (1 - core)
    across = lax.rem(low_peer + 2, 4)

    def g_rows(i, q):
        hr = s.sizes[i] // 2
        qr = hr // 4
        return pl.ds(pl.multiple_of(s.bases[i] + core * hr + q * qr, 16), qr)

    def g_half(i, c):
        hr = s.sizes[i] // 2
        return pl.ds(pl.multiple_of(s.bases[i] + c * hr, 16), hr)

    def q_rows(i, q):
        qr = s.sizes[i] // 8
        return pl.ds(pl.multiple_of(q * qr, 16), qr)

    def g_copy(i, slot, src, dst, q):
        dev = ((first_pair + q) * 2 + core, t)
        return remote(src, dst, sem["gs%d" % i].at[slot], sem["gr%d" % i].at[slot], dev)

    def sib_copy(i, slot, src, dst):
        return remote(src, dst, sem["gs%d" % i].at[slot], sem["gr%d" % i].at[slot], (sib, t))

    def c1_copy(i):
        return sib_copy(i, 0, k.gsrc.at[g_half(i, 1 - core)], sem["core%d" % i])

    def rs_copies(i):
        hs = sem["core%d" % i]
        land = sem["quart%d" % i]
        return (
            g_copy(i, 1, hs.at[q_rows(i, first)], land.at[0], first),
            g_copy(i, 2, hs.at[q_rows(i, across)], land.at[1], first),
        )

    def rs_copy_b(i):
        return g_copy(i, 3, sem["core%d" % i].at[q_rows(i, second)], sem["quart%d" % i].at[2], second)

    def out_copy(i, slot, q, to):
        rows = g_rows(i, q)
        return g_copy(i, slot, k.gout.at[rows], k.gout.at[rows], to)

    def c2_copy(i, c):
        rows = g_half(i, c)
        return sib_copy(i, 7, k.gout.at[rows], k.gout.at[rows])

    def sup_copy(i, j):
        ref = sem["sup%d" % i]
        dev = ((lax.rem(group + j, s.groups) * 4 + quarter) * 2 + core, t)
        return remote(ref.at[group], ref.at[group], sem["sup%d_s" % i].at[j - 1], sem["sup%d_r" % i].at[j - 1], dev)

    def grads1(i):
        c1_copy(i).start()

    def grads2(i):
        c1_copy(i).wait()
        hs = sem["core%d" % i]
        hs[...] = (k.gsrc[g_half(i, core), :].astype(F32) + hs[...].astype(F32)).astype(BF16)
        for copy in rs_copies(i):
            copy.start()

    def grads3(i):
        for copy in rs_copies(i):
            copy.wait()
        hs = sem["core%d" % i]
        rows = q_rows(i, second)
        hs[rows, :] = (hs[rows, :].astype(F32) + sem["quart%d" % i][1].astype(F32)).astype(BF16)
        rs_copy_b(i).start()

    def grads4(i):
        rs_copy_b(i).wait()
        land = sem["quart%d" % i]
        acc = sem["core%d" % i][q_rows(i, quarter), :].astype(F32)
        acc = acc + land[0].astype(F32) + land[2].astype(F32)
        if s.groups > 1:
            ref = sem["sup%d" % i]
            ref[group] = acc.astype(BF16)
            for j in range(1, s.groups):
                sup_copy(i, j).start()
            for j in range(1, s.groups):
                sup_copy(i, j).wait()
            acc = ref[0].astype(F32)
            for g in range(1, s.groups):
                acc = acc + ref[g].astype(F32)
        k.gout[g_rows(i, quarter), :] = acc.astype(BF16)
        out_copy(i, 4, quarter, second).start()

    def grads5(i):
        out_copy(i, 4, quarter, second).wait_send()
        out_copy(i, 4, second, second).wait_recv()
        out_copy(i, 5, quarter, first).start()
        out_copy(i, 6, second, first).start()

    def grads6(i):
        out_copy(i, 5, quarter, first).wait_send()
        out_copy(i, 6, second, first).wait_send()
        out_copy(i, 5, first, first).wait_recv()
        out_copy(i, 6, across, first).wait_recv()
        c2_copy(i, core).start()

    def grads_store(i):
        rows = pl.ds(s.bases[i], s.sizes[i])
        return pltpu.make_async_copy(k.gout.at[rows], o_grads.at[rows], k.stores.at[i])

    def grads7(i):
        c2_copy(i, core).wait_send()
        c2_copy(i, 1 - core).wait_recv()
        grads_store(i).start()

    def load(i, src, dst):
        return pltpu.make_async_copy(src, dst, k.loads.at[i])

    first_loads = [
        load(0, patches, k.patches),
        load(1, leads_in, k.lead_index),
        load(2, table, k.table),
        load(3, gain1, k.gain1),
        load(4, bias1, k.bias1),
    ]
    ow_load = load(5, out_weight, k.ow.at[t])
    small_loads = [
        load(6, pixel_mask, k.pix),
        load(7, gate, k.head),
        load(8, windows_in, k.windows),
    ]
    qkv_load = load(9, qkv, k.qkv)
    late_loads = [
        load(10, gain2, k.gain2),
        load(11, bias2, k.bias2),
        load(12, up, k.up),
        load(13, down, k.down),
        load(14, cotangent, k.cot),
    ]
    for copy in first_loads + small_loads + [qkv_load, ow_load]:
        copy.start()
    barrier = pltpu.get_barrier_semaphore()

    @pl.loop(1, nb)
    def _(i):
        pl.semaphore_signal(barrier, inc=1, device_id=(lax.rem(b + i, nb), t), device_id_type=MESH)

    for j in range(1, nt):
        pl.semaphore_signal(barrier, inc=1, device_id=(b, z_peer(j)), device_id_type=MESH)

    for copy in first_loads:
        copy.wait()
    lead_hot = lax.broadcasted_iota(jnp.int32, (s.leads, L), 0) == row_of(k.lead_index)
    lead_hot = lead_hot.astype(F32).astype(BF16)
    hidden = k.patches[...] + mm_tn(lead_hot, k.table[...])
    unit1, inverse1 = norm_stats(hidden)
    k.u1[...] = unit1
    k.r1[...] = inverse1
    k.mid[...] = hidden
    k.normed[...] = (unit1 * row_of(k.gain1) + row_of(k.bias1)).astype(BF16)
    for copy in small_loads:
        copy.wait()
    compact = [k.head[e].astype(F32) for e in range(3)] + [jnp.zeros((4, D), F32)]
    k.gatec[t] = jnp.concatenate(compact, axis=0).astype(BF16)
    k.mask[t] = jnp.concatenate([k.pix[...].astype(F32), jnp.zeros((4, L), F32)], axis=0)
    hw = W // 2

    def ow_half(tt, c):
        return k.ow.at[tt, pl.ds(pl.multiple_of(c * hw, hw), hw)]

    def ow_relay(j, tt, c):
        return remote(ow_half(tt, c), ow_half(tt, c), k.zowr_s.at[j - 1], k.zowr_r.at[j - 1], (sib, t))

    qkv_load.wait()

    def project(c):
        return mm_nt(k.qkv[c], k.normed[...])

    k.kv[b, 0:W, :] = project(1).astype(BF16)
    k.kv[b, W : 2 * W, :] = project(2).astype(BF16)
    ow_load.wait()
    pl.semaphore_wait(barrier, nb - 1 + nt - 1)

    def kv_at(band):
        return k.kv.at[band]

    ag_start("kv", kv_at)
    for j in range(1, nt):
        z_copy("zmask", j, k.mask.at[t], k.mask.at[t]).start()
        z_copy("zow", j, ow_half(t, core), ow_half(t, core)).start()
        z_copy("zgate", j, k.gatec.at[t], k.gatec.at[t]).start()
    for copy in late_loads:
        copy.start()
    k.qd[b, 0:W, :] = (project(0).astype(BF16).astype(F32) * SCALE).astype(BF16)

    k.ids[...] = k.windows[...].reshape(nb, L).astype(F32)

    def id_row(band):
        return k.ids[pl.ds(band, 1), :]

    def id_column(band):
        return jnp.transpose(jnp.broadcast_to(id_row(band), (128, L)))[:, 0:1]

    def head(h):
        return pl.ds(h * HEAD_DIM, HEAD_DIM)

    def value_head(h):
        return pl.ds(W + h * HEAD_DIM, HEAD_DIM)

    k.m[...] = jnp.full((8, L), MASKED, F32)
    k.l[...] = jnp.zeros((8, L), F32)
    k.acc[...] = jnp.zeros((W, L), F32)

    def forward_bands(bands):
        tiles = [(h, i) for h in range(H) for i in range(len(bands))]
        allowed = [id_column(band) == id_row(b) for band in bands]
        scores = {
            (h, i): jnp.where(
                allowed[i], mm_tn(k.kv[bands[i], head(h), :], k.qd[b, head(h), :]), MASKED
            )
            for h, i in tiles
        }
        old_high = [k.m[h : h + 1, :] for h in range(H)]
        sums = [k.l[h : h + 1, :] for h in range(H)]
        outs = [k.acc[head(h), :] for h in range(H)]
        high = list(old_high)
        for h, i in tiles:
            high[h] = jnp.maximum(high[h], jnp.max(scores[h, i], axis=0, keepdims=True))
        weights = {(h, i): jnp.exp(scores[h, i] - high[h]) for h, i in tiles}
        factor = [jnp.exp(x - y) for x, y in zip(old_high, high)]
        outs = [x * f for x, f in zip(outs, factor)]
        sums = [x * f for x, f in zip(sums, factor)]
        for h, i in tiles:
            outs[h] += mm_nn(k.kv[bands[i], value_head(h), :], weights[h, i].astype(BF16))
            sums[h] += jnp.sum(weights[h, i], axis=0, keepdims=True)
        for h in range(H):
            k.m[h : h + 1, :] = high[h]
            k.l[h : h + 1, :] = sums[h]
            k.acc[head(h), :] = outs[h]

    ag_wait_relay("kv", kv_at, 0)
    forward_bands([b, sib])
    for j in range(1, nt):
        z_copy("zmask", j, k.mask.at[t], k.mask.at[z_from(j)]).wait_recv()
    k.cnt[b] = jnp.broadcast_to(total(jnp.sum(k.mask[...], axis=0)), (8, 128))
    swap_start("cnt", every)

    @pl.loop(1, s.half)
    def _(i):
        ag_relay("kv", kv_at, i)
        ag_wait_relay("kv", kv_at, i)
        forward_bands([band_same(i), band_sib(i)])

    for h in range(H):
        att = k.acc[head(h), :] / k.l[h : h + 1, :]
        k.acc[head(h), :] = att
        k.att[t, head(h), :] = att.astype(BF16)
        k.st[b, h : h + 1, :] = k.m[h : h + 1, :] + jnp.log(k.l[h : h + 1, :])

    def att_half(tt, h):
        return k.att.at[tt, :, half(h)]

    for h in range(2):
        for j in range(1, nt):
            z_copy("zatt", j, att_half(t, h), att_half(t, h), h).start()

    def q_at(band):
        return k.qd.at[band, pl.ds(0, W)]

    def da_at(h):
        return lambda band: k.qd.at[band, pl.ds(W, W), half(h)]

    def st_at(band):
        return k.st.at[band]

    ag_start("q", q_at)
    for j in range(1, nt):
        src = z_from(j)
        z_copy("zow", j, ow_half(src, core), ow_half(src, core)).wait_recv()
        ow_relay(j, src, core).start()
    for copy in late_loads:
        copy.wait()
    for j in range(1, nt):
        ow_relay(j, z_from(j), 1 - core).wait_recv()

    for h in range(2):
        for j in range(1, nt):
            z_copy("zatt", j, att_half(z_from(j), h), att_half(z_from(j), h), h).wait_recv()
        rows = half(h)
        middle = k.mid[rows, :] + mm_tn(
            k.att[:, :, half(h)].reshape(nt * W, T), k.ow[...].reshape(nt * W, D)
        )
        k.mid[rows, :] = middle
        unit2, inverse2 = norm_stats(middle)
        k.u2[rows, :] = unit2
        k.r2[rows, :] = inverse2
        k.n2low[rows, :] = (unit2 * row_of(k.gain2) + row_of(k.bias2)).astype(BF16)
        upward = mm_nn(k.n2low[rows, :], k.up[...])
        k.upw[rows, :] = upward
        k.actlow[rows, :] = (0.5 * upward * (1.0 + lax.erf(upward * INV_SQRT2))).astype(BF16)
        k.ffp[rows, :] = mm_nn(k.actlow[rows, :], k.down[...]).astype(BF16)
        rs_start("zff", h, k.ffp, k.ffr)
    upward = k.upw[...]
    k.upw[...] = 0.5 * (1.0 + lax.erf(upward * INV_SQRT2)) + upward * (
        jnp.exp(-0.5 * upward * upward) * INV_SQRT_2PI
    )
    for j in range(1, nt):
        z_copy("zgate", j, k.gatec.at[t], k.gatec.at[z_from(j)]).wait_recv()
    for tt in range(nt):
        x = k.gatec[tt].astype(F32)
        pad = jnp.zeros((4, D), F32)
        parts = []
        for e in range(3):
            parts += [x[4 * e : 4 * e + 4], pad]
        k.gate[tt * 32 : (tt + 1) * 32, :] = jnp.concatenate(parts + [pad, pad], axis=0).astype(BF16)
    swap_wait("cnt", every)
    pixel_count = jnp.sum(k.cnt[...], axis=0)[0:1, 0:1]
    for h in range(2):
        block_piece = k.mid[piece(h, t), :] + rs_sum("zff", h, k.ffp, k.ffr)
        k.blow[piece(h, t), :] = block_piece.astype(BF16)
        gather_start("zblk", h, k.blow)

    @pl.loop(1, s.half)
    def _(i):
        ag_relay("q", q_at, i)

    entropy_sum = jnp.zeros((1, 1), F32)
    for h in range(2):
        rows = half(h)
        gather_wait("zblk", h, k.blow)
        logits = mm_nt(k.gate[...], k.blow[rows, :]).reshape(nt, 4, 8, T)
        parts = [logits[:, e] for e in range(3)]
        high = jnp.maximum(jnp.maximum(parts[0], parts[1]), parts[2])
        logs = jnp.log(sum(jnp.exp(x - high) for x in parts))
        log_probs = [x - high - logs for x in parts]
        probs = [jnp.exp(x) for x in log_probs]
        entropy = -sum(p * x for p, x in zip(probs, log_probs))
        mask = k.mask[:, :, half(h)]
        entropy_sum += total(jnp.sum(mask * entropy, axis=0))
        weight = mask * (float(s.pixels) / pixel_count)[None]
        grads = [-p * (x + entropy) * weight for p, x in zip(probs, log_probs)]
        grads.append(jnp.zeros((nt, 8, T), F32))
        k.lg[:, half(h)] = jnp.stack(grads, axis=1).reshape(nt * 32, T).astype(BF16)
        out_grad = k.cot[rows, :] + mm_tn(k.lg[:, half(h)], k.gate[...])
        k.cot[rows, :] = out_grad
        k.oglow[rows, :] = out_grad.astype(BF16)
        k.ug[rows, :] = (mm_nt(k.oglow[rows, :], k.down[...]) * k.upw[rows, :]).astype(BF16)
        k.n2p[rows, :] = mm_nt(k.ug[rows, :], k.up[...]).astype(BF16)
        rs_start("zn2", h, k.n2p, k.n2r)
    block_copy = pltpu.make_async_copy(k.blow, o_block, k.stores.at[4])
    block_copy.start()
    own_lg = k.lg[pl.ds(pl.multiple_of(t * 32, 32), 32), :]
    k.va[near[1]] = mm_nn(own_lg, k.blow[...]).astype(BF16)
    k.ent[b] = jnp.broadcast_to(entropy_sum / pixel_count, (8, 128))
    swap_start("va", near)
    swap_start("ent", every)
    k.gsrc[0:F, :] = mm_tn(k.actlow[...], k.oglow[...]).astype(BF16)
    grads1(0)
    k.gsrc[F : F + D, :] = mm_tn(k.n2low[...], k.ug[...]).astype(BF16)
    grads1(1)

    def middle_backward(n2_grad, rows):
        return k.cot[rows, :] + norm_backward(n2_grad, k.u2[rows, :], k.r2[rows, :], row_of(k.gain2))

    grads2(0)
    for h in range(2):
        rows = piece(h, t)
        n2_low = rs_sum("zn2", h, k.n2p, k.n2r).astype(BF16)
        k.n2g[rows, :] = n2_low
        low_piece = middle_backward(n2_low.astype(F32), rows).astype(BF16)
        for tt in range(nt):
            k.dasrc[h, tt] = mm_nt(low_piece, k.ow[tt]).astype(BF16)
        for j in range(1, nt):
            z_copy("zda", j, k.dasrc.at[h, z_peer(j)], k.datok.at[h, t], h).start()
        k.datok[h, t] = k.dasrc[h, t]
        if h == 0:
            grads2(1)
            grads3(0)
    for h in range(2):
        gather_start("zn2g", h, k.n2g)
    for h in range(2):
        for j in range(1, nt):
            z_copy("zda", j, k.dasrc.at[h, z_peer(j)], k.datok.at[h, z_from(j)], h).wait_recv()
        att_grad = jnp.transpose(k.datok[h].reshape(T, W).astype(F32)).astype(BF16)
        k.qd[b, W : 2 * W, half(h)] = att_grad
        ag_start("da%d" % h, da_at(h))
        weighted = att_grad.astype(F32) * k.acc[:, half(h)]
        for i in range(H):
            k.st[b, H + i : H + i + 1, half(h)] = jnp.sum(
                weighted[i * HEAD_DIM : (i + 1) * HEAD_DIM], axis=0, keepdims=True
            )
    ag_start("st", st_at)
    grads3(1)
    k.dq[...] = jnp.zeros((W, L), F32)
    k.dk[...] = jnp.zeros((W, L), F32)
    k.dv[...] = jnp.zeros((W, L), F32)
    my_column = id_column(b)

    def score_grads(allowed, scores, dots, stats):
        probs = {
            (h, i): jnp.exp(jnp.where(allowed[i], x, MASKED) - stats[i][h : h + 1])
            for (h, i), x in scores.items()
        }
        grads = {
            (h, i): (x * (dots[h, i] - stats[i][H + h : H + h + 1])).astype(BF16)
            for (h, i), x in probs.items()
        }
        return probs, grads

    @pl.loop(0, s.half)
    def _(step):
        bands = [2 * step, 2 * step + 1]
        tiles = [(h, i) for h in range(H) for i in range(2)]
        allowed = [id_column(band) == id_row(b) for band in bands]
        scores = {(h, i): mm_tn(k.kv[bands[i], head(h), :], k.qd[b, head(h), :]) for h, i in tiles}
        dots = {
            (h, i): mm_tn(k.kv[bands[i], value_head(h), :], k.qd[b, value_head(h), :]) for h, i in tiles
        }
        outs = [k.dq[head(h), :] for h in range(H)]
        _, grads = score_grads(allowed, scores, dots, [k.st[b]] * 2)
        for h, i in tiles:
            outs[h] += mm_nn(k.kv[bands[i], head(h), :], grads[h, i])
        for h in range(H):
            k.dq[head(h), :] = outs[h]

    grads4(0)
    k.dp[0] = (k.dq[...] * SCALE).astype(BF16)
    base = s.bases[2]
    for h in range(2):
        gather_wait("zn2g", h, k.n2g)
    n2_grad = k.n2g[...].astype(F32)
    gain2_grad = jnp.sum(n2_grad * k.u2[...], axis=0, keepdims=True)
    bias2_grad = jnp.sum(n2_grad, axis=0, keepdims=True)
    middle_grad = middle_backward(n2_grad, pl.ds(0, L))
    k.cot[...] = middle_grad
    k.gsrc[base : base + W, :] = mm_nn(k.att[t], middle_grad.astype(BF16)).astype(BF16)
    k.gsrc[base + W : base + 2 * W, :] = mm_nn(k.dp[0], k.normed[...]).astype(BF16)
    grads1(2)
    grads4(1)

    @pl.loop(1, s.half)
    def _(i):
        ag_wait_relay("q", q_at, i)

    ag_wait_relay("q", q_at, 0)

    def backward_bands(bands):
        tiles = [(h, i) for h in range(H) for i in range(len(bands))]
        allowed = [my_column == id_row(band) for band in bands]
        scores = {(h, i): mm_tn(k.kv[b, head(h), :], k.qd[bands[i], head(h), :]) for h, i in tiles}
        dots = {
            (h, i): mm_tn(k.kv[b, value_head(h), :], k.qd[bands[i], value_head(h), :]) for h, i in tiles
        }
        key_outs = [k.dk[head(h), :] for h in range(H)]
        value_outs = [k.dv[head(h), :] for h in range(H)]
        probs, grads = score_grads(allowed, scores, dots, [k.st[band] for band in bands])
        for h, i in tiles:
            key_outs[h] += mm_nt(k.qd[bands[i], head(h), :], grads[h, i])
            value_outs[h] += mm_nt(k.qd[bands[i], value_head(h), :], probs[h, i].astype(BF16))
        for h in range(H):
            k.dk[head(h), :] = key_outs[h]
            k.dv[head(h), :] = value_outs[h]

    def backward_loop(start, stop):
        @pl.loop(start, stop)
        def _(i):
            @pl.when(i > 0)
            def _():
                ag_relay("da0", da_at(0), i)
                ag_relay("da1", da_at(1), i)
                ag_relay("st", st_at, i)

            ag_wait_relay("da0", da_at(0), i)
            ag_wait_relay("da1", da_at(1), i)
            ag_wait_relay("st", st_at, i)
            backward_bands([band_same(i), band_sib(i)])

    backward_loop(0, s.half // 2)
    grads2(2)
    grads5(0)
    backward_loop(s.half // 2, s.half)
    k.dp[1] = k.dk[...].astype(BF16)
    k.dp[2] = k.dv[...].astype(BF16)
    for h in range(2):
        k.ngp[half(h), :] = mm_tn(
            k.dp[:, :, half(h)].reshape(3 * W, T), k.qkv[...].reshape(3 * W, D)
        ).astype(BF16)
        rs_start("zng", h, k.ngp, k.ngr)
    base = s.bases[3]
    k.gsrc[base : base + 2 * W, :] = mm_nn(k.dp[1:3].reshape(2 * W, L), k.normed[...]).astype(BF16)
    grads1(3)
    grads5(1)
    grads3(2)
    grads2(3)
    for h in range(2):
        k.ngg[piece(h, t), :] = rs_sum("zng", h, k.ngp, k.ngr).astype(BF16)
        gather_start("zngg", h, k.ngg)
        if h == 0:
            grads6(0)
            grads4(2)
    grads3(3)
    grads6(1)
    grads5(2)
    grads4(3)
    grads7(0)
    grads6(2)
    grads5(3)
    for h in range(2):
        gather_wait("zngg", h, k.ngg)
    n1_grad = k.ngg[...].astype(F32)
    unit1 = k.u1[...]
    gain1_grad = jnp.sum(n1_grad * unit1, axis=0, keepdims=True)
    bias1_grad = jnp.sum(n1_grad, axis=0, keepdims=True)
    hidden_grad = k.cot[...] + norm_backward(n1_grad, unit1, k.r1[...], row_of(k.gain1))
    k.patches[...] = hidden_grad
    hidden_copy = pltpu.make_async_copy(k.patches, o_hidden, k.stores.at[5])
    hidden_copy.start()
    coarse = hidden_grad.astype(BF16)
    fine = (hidden_grad - coarse.astype(F32)).astype(BF16)
    tail = [
        mm_nn(lead_hot, coarse) + mm_nn(lead_hot, fine),
        gain1_grad,
        bias1_grad,
        gain2_grad,
        bias2_grad,
        jnp.zeros((s.tail - s.leads - 4, D), F32),
    ]
    k.vb[near[1]] = jnp.concatenate(tail, axis=0).astype(BF16)
    swap_start("vb", near)
    grads7(1)
    grads6(3)
    grads7(2)
    swap_wait("ent", every)
    k.va_sum[...] = swap_sum("va")
    k.va_sum[24:32, 0:128] = jnp.sum(k.ent[...], axis=0)
    va_copy = pltpu.make_async_copy(k.va_sum, o_va, k.stores.at[6])
    va_copy.start()
    grads7(3)
    k.vb_sum[...] = swap_sum("vb")
    vb_copy = pltpu.make_async_copy(k.vb_sum, o_vb, k.stores.at[7])
    vb_copy.start()

    for j in range(1, nt):
        z_copy("zmask", j, k.mask.at[t], k.mask.at[t]).wait_send()
        z_copy("zgate", j, k.gatec.at[t], k.gatec.at[t]).wait_send()
        z_copy("zow", j, ow_half(t, core), ow_half(t, core)).wait_send()
        ow_relay(j, t, core).wait_send()
        for h in range(2):
            z_copy("zatt", j, att_half(t, h), att_half(t, h), h).wait_send()
            z_copy("zda", j, k.dasrc.at[h, z_peer(j)], k.datok.at[h, t], h).wait_send()
    rs_finish("zff", k.ffp, k.ffr)
    gather_finish("zblk", k.blow)
    rs_finish("zn2", k.n2p, k.n2r)
    gather_finish("zn2g", k.n2g)
    rs_finish("zng", k.ngp, k.ngr)
    gather_finish("zngg", k.ngg)
    for name, at in (("kv", kv_at), ("q", q_at), ("da0", da_at(0)), ("da1", da_at(1)), ("st", st_at)):
        ag_finish(name, at)
    swap_finish("cnt", every)
    swap_finish("ent", every)
    for i in range(4):
        grads_store(i).wait()
    for copy in (block_copy, hidden_copy, va_copy, vb_copy):
        copy.wait()


def last_kernel(
    s, cuts, block, hidden, grads, va, vb,
    o_block, o_hidden, o_qkv, o_out, o_up, o_down, o_pen, o_lead, o_g1, o_b1, o_g2, o_b2, o_gate,
    low, wide, low_block, wide_block, keep, load_sem, store_sem,
):
    outs = {"down": o_down, "up": o_up, "out": o_out, "q": o_qkv.at[0], "k": o_qkv.at[1], "v": o_qkv.at[2]}
    loads = [
        pltpu.make_async_copy(block, low_block, load_sem.at[0]),
        pltpu.make_async_copy(hidden, keep, load_sem.at[1]),
    ]
    stores = [
        pltpu.make_async_copy(wide_block, o_block, store_sem.at[0]),
        pltpu.make_async_copy(keep, o_hidden, store_sem.at[1]),
    ]
    for i, (row, name, start, size) in enumerate(cuts):
        rows = pl.ds(row, size)
        loads.append(pltpu.make_async_copy(grads.at[rows], low.at[rows], load_sem.at[i + 2]))
        stores.append(
            pltpu.make_async_copy(wide.at[rows], outs[name].at[pl.ds(start, size)], store_sem.at[i + 2])
        )
    for copy in loads:
        copy.start()
    loads[0].wait()
    wide_block[...] = low_block[...].astype(F32)
    stores[0].start()
    loads[1].wait()
    stores[1].start()
    for i, (row, name, start, size) in enumerate(cuts):
        loads[i + 2].wait()
        rows = pl.ds(row, size)
        wide[rows, :] = low[rows, :].astype(F32)
        stores[i + 2].start()
    small = va[...]
    for e in range(3):
        o_gate[e] = small[8 * e : 8 * e + 4]
    o_pen[...] = small[24:25, 0:1]
    tail = vb[...]
    o_lead[...] = tail[0 : s.leads]
    o_g1[...] = tail[s.leads].reshape(s.D)
    o_b1[...] = tail[s.leads + 1].reshape(s.D)
    o_g2[...] = tail[s.leads + 2].reshape(s.D)
    o_b2[...] = tail[s.leads + 3].reshape(s.D)
    for copy in stores:
        copy.wait()


def local(
    nb,
    nt,
    patches,
    window_ids,
    lead_index,
    lead_table,
    attention_gain,
    attention_bias,
    query_key_value,
    out_weight,
    feedforward_gain,
    feedforward_bias,
    up_weight,
    down_weight,
    gate_head,
    pixel_mask,
    cotangent,
):
    L, D = patches.shape
    leads = lead_table.shape[0]
    W = out_weight.shape[0]
    F = up_weight.shape[1]
    s = dims_of(nb, nt, L, D, W, F, leads, L * nb * pixel_mask.shape[0] * nt)
    scratch = scratch_of(s)
    vm = pl.BlockSpec(memory_space=pltpu.VMEM)
    block, hidden, grads, va, vb = pl.pallas_call(
        partial(main_kernel, s, tuple(scratch)),
        out_shape=(
            jax.ShapeDtypeStruct((L, D), BF16),
            jax.ShapeDtypeStruct((L, D), F32),
            jax.ShapeDtypeStruct((s.rows, D), BF16),
            jax.ShapeDtypeStruct((32, D), F32),
            jax.ShapeDtypeStruct((s.tail, D), F32),
        ),
        in_specs=[pl.BlockSpec(memory_space=pltpu.HBM)] * 15,
        out_specs=(pl.BlockSpec(memory_space=pl.ANY),) * 5,
        scratch_shapes=list(scratch.values()),
        compiler_params=pltpu.CompilerParams(
            collective_id=0,
            has_side_effects=True,
            vmem_limit_bytes=VMEM_LIMIT,
        ),
        cost_estimate=pl.CostEstimate(
            flops=2 * s.rows * D * L * 3 + 14 * L * nb * L * W, bytes_accessed=16 * 2**20, transcendentals=0
        ),
        name="block_step",
    )(
        patches,
        window_ids,
        lead_index,
        lead_table,
        attention_gain,
        attention_bias,
        jnp.transpose(query_key_value, (0, 2, 1)),
        out_weight,
        feedforward_gain,
        feedforward_bias,
        up_weight,
        down_weight,
        gate_head,
        pixel_mask,
        cotangent,
    )
    vec = jax.ShapeDtypeStruct((D,), F32)
    cuts = []
    row = 0
    for name, size in (("down", F), ("up", D), ("out", W), ("q", W), ("k", W), ("v", W)):
        for start in range(0, size, 256):
            cuts.append((row + start, name, start, min(256, size - start)))
        row += size
    hbm = pl.BlockSpec(memory_space=pl.ANY)
    wide, high, qkv_grad, out_grad, up_grad, down_grad, pen, lead, g1, b1, g2, b2, gates = pl.pallas_call(
        partial(last_kernel, s, cuts),
        out_shape=(
            jax.ShapeDtypeStruct((L, D), F32),
            jax.ShapeDtypeStruct((L, D), F32),
            jax.ShapeDtypeStruct((3, W, D), F32),
            jax.ShapeDtypeStruct((W, D), F32),
            jax.ShapeDtypeStruct((D, F), F32),
            jax.ShapeDtypeStruct((F, D), F32),
            jax.ShapeDtypeStruct((1, 1), F32),
            jax.ShapeDtypeStruct((leads, D), F32),
            vec,
            vec,
            vec,
            vec,
            jax.ShapeDtypeStruct(gate_head.shape, F32),
        ),
        in_specs=[hbm] * 3 + [vm] * 2,
        out_specs=(hbm,) * 6 + (vm,) * 7,
        scratch_shapes=[
            pltpu.VMEM((s.rows, D), BF16),
            pltpu.VMEM((s.rows, D), F32),
            pltpu.VMEM((L, D), BF16),
            pltpu.VMEM((L, D), F32),
            pltpu.VMEM((L, D), F32),
            pltpu.SemaphoreType.DMA((len(cuts) + 2,)),
            pltpu.SemaphoreType.DMA((len(cuts) + 2,)),
        ],
        compiler_params=pltpu.CompilerParams(vmem_limit_bytes=VMEM_LIMIT),
        name="write_out",
    )(block, hidden, grads, va, vb)
    return (
        wide,
        pen.reshape(()),
        high,
        lead,
        g1,
        b1,
        jnp.transpose(qkv_grad, (0, 2, 1)),
        out_grad,
        g2,
        b2,
        up_grad,
        down_grad,
        gates,
    )


def solution(mesh):
    in_specs = (
        P("blk", None),
        P(),
        P("blk"),
        P(),
        P(),
        P(),
        P(None, None, "tp"),
        P("tp", None),
        P(),
        P(),
        P(None, "tp"),
        P("tp", None),
        P(None, "tp", None),
        P("tp", "blk"),
        P("blk", None),
    )
    out_specs = (
        P("blk", None),
        P(),
        P("blk", None),
        P(),
        P(),
        P(),
        P(None, None, "tp"),
        P("tp", None),
        P(),
        P(),
        P(None, "tp"),
        P("tp", None),
        P(None, "tp", None),
    )
    return jax.shard_map(
        partial(local, mesh.shape["blk"], mesh.shape["tp"]),
        mesh=mesh,
        in_specs=in_specs,
        out_specs=out_specs,
        check_vma=False,
    )
```

```python
from functools import partial
from types import SimpleNamespace

import jax
import jax.numpy as jnp
from jax import lax
from jax.experimental import pallas as pl
from jax.experimental.pallas import tpu as pltpu
from jax.sharding import PartitionSpec as P

HEAD_DIM = 64
EPS = 1e-05
MASKED = -1e30
SCALE = HEAD_DIM ** (-0.5)
GROUP = 8
F32 = jnp.float32
BF16 = jnp.bfloat16
MESH = pl.DeviceIdType.MESH
VMEM_LIMIT = 61 * 2**20
INV_SQRT2 = 0.7071067811865476
INV_SQRT_2PI = 0.3989422804014327


def dot(a, b, ca, cb):
    return lax.dot_general(a, b, (((ca,), (cb,)), ((), ())), preferred_element_type=F32)


def mm_nn(a, b):
    return dot(a, b, 1, 0)


def mm_nt(a, b):
    return dot(a, b, 1, 1)


def mm_tn(a, b):
    return dot(a, b, 0, 0)


def norm_stats(values):
    mean = jnp.mean(values, axis=-1, keepdims=True)
    centered = values - mean
    inverse = lax.rsqrt(jnp.mean(centered * centered, axis=-1, keepdims=True) + EPS)
    return centered * inverse, inverse


def norm_backward(incoming, unit_rows, inverse, gain):
    scaled = incoming * gain
    return inverse * (
        scaled
        - jnp.mean(scaled, axis=-1, keepdims=True)
        - unit_rows * jnp.mean(scaled * unit_rows, axis=-1, keepdims=True)
    )


def row_of(ref):
    return ref[...].reshape(1, ref.shape[0])


def total(x):
    return jnp.sum(jnp.sum(x, axis=0, keepdims=True), axis=1, keepdims=True)


def dims_of(nb, nt, tokens, width, local_width, hidden, leads, pixels):
    s = SimpleNamespace(nb=nb, nt=nt, L=tokens, D=width, W=local_width, F=hidden, leads=leads)
    s.H = local_width // HEAD_DIM
    s.T = tokens // 2
    s.R = s.T // nt
    s.half = nb // 2
    s.groups = nb // GROUP
    s.pixels = pixels
    s.sizes = (hidden, width, local_width * 2 + 128, local_width * 2)
    s.bases = tuple(sum(s.sizes[:i]) for i in range(4))
    s.rows = sum(s.sizes)
    s.tail = (leads + 4 + 15) // 16 * 16
    return s


def scratch_of(s):
    L, D, W, F, nb, nt, R = s.L, s.D, s.W, s.F, s.nb, s.nt, s.R
    v = pltpu.VMEM
    out = {
        "patches": v((L, D), F32),
        "windows": v((nb * L,), jnp.int32),
        "lead_index": v((L,), jnp.int32),
        "table": v((s.leads, D), BF16),
        "gain1": v((D,), F32),
        "bias1": v((D,), F32),
        "gain2": v((D,), F32),
        "bias2": v((D,), F32),
        "pix": v((4, L), jnp.int32),
        "head": v((3, 4, D), BF16),
        "ids": v((nb, L), F32),
        "qkv": v((3, W, D), BF16),
        "ow": v((nt, W, D), BF16),
        "up": v((D, F), BF16),
        "down": v((F, D), BF16),
        "cot": v((L, D), F32),
        "gatec": v((nt, 16, D), BF16),
        "gate": v((nt * 32, D), BF16),
        "mask": v((nt, 8, L), F32),
        "cnt": v((nb, 8, 128), F32),
        "u1": v((L, D), F32),
        "r1": v((L, 1), F32),
        "normed": v((L, D), BF16),
        "kv": v((nb, 2 * W, L), BF16),
        "qd": v((nb, 2 * W, L), BF16),
        "st": v((nb, 8, L), F32),
        "m": v((8, L), F32),
        "l": v((8, L), F32),
        "acc": v((W, L), F32),
        "att": v((nt, W, L), BF16),
        "mid": v((L, D), F32),
        "u2": v((L, D), F32),
        "r2": v((L, 1), F32),
        "n2low": v((L, D), BF16),
        "upw": v((L, F), F32),
        "actlow": v((L, F), BF16),
        "ffp": v((L, D), BF16),
        "ffr": v((2, nt - 1, R, D), BF16),
        "blow": v((L, D), BF16),
        "lg": v((nt * 32, L), BF16),
        "oglow": v((L, D), BF16),
        "ug": v((L, F), BF16),
        "n2p": v((L, D), BF16),
        "n2r": v((2, nt - 1, R, D), BF16),
        "n2g": v((L, D), BF16),
        "dasrc": v((2, nt, R, W), BF16),
        "datok": v((2, nt, R, W), BF16),
        "dq": v((W, L), F32),
        "dk": v((W, L), F32),
        "dv": v((W, L), F32),
        "dp": v((3, W, L), BF16),
        "ngp": v((L, D), BF16),
        "ngr": v((2, nt - 1, R, D), BF16),
        "ngg": v((L, D), BF16),
        "vb": v((GROUP, s.tail, D), BF16),
        "ent": v((nb, 8, 128), F32),
        "ent_sum": v((8, 128), F32),
        "vb_sum": v((s.tail, D), F32),
        "gsrc": v((s.rows, D), BF16),
        "gout": v((s.rows, D), BF16),
    }
    dma = pltpu.SemaphoreType.DMA
    out["loads"] = dma((15,))
    out["stores"] = dma((8,))
    for name in ("zmask", "zgate", "zow", "zowy", "zowr", "zatt", "zff", "zblk", "zn2", "zn2g", "zda", "zng", "zngg"):
        out[name + "_s"] = dma((2 * (nt - 1),))
        out[name + "_r"] = dma((2 * (nt - 1),))
    for name in ("kv", "q", "da0", "da1", "st"):
        for part in ("_s", "_r", "_rs", "_rr"):
            out[name + part] = dma((s.half,))
    for name, count in (("cnt", nb), ("ent", nb), ("vb", GROUP)):
        out[name + "_s"] = dma((count - 1,))
        out[name + "_r"] = dma((count - 1,))
    if s.groups > 1:
        out["vb2"] = v((s.groups, s.tail, D), BF16)
        out["vb2_s"] = dma((s.groups - 1,))
        out["vb2_r"] = dma((s.groups - 1,))
    for i, rows in enumerate(s.sizes):
        hr = rows // 2
        qr = hr // 4
        out["core%d" % i] = v((hr, D), BF16)
        out["quart%d" % i] = v((3, qr, D), BF16)
        if s.groups > 1:
            out["sup%d" % i] = v((s.groups, qr, D), BF16)
            out["sup%d_s" % i] = dma((s.groups - 1,))
            out["sup%d_r" % i] = dma((s.groups - 1,))
        out["gs%d" % i] = dma((8,))
        out["gr%d" % i] = dma((8,))
    return out


def main_kernel(s, names, *refs):
    (
        patches,
        windows_in,
        leads_in,
        table,
        gain1,
        bias1,
        qkv,
        out_weight,
        gain2,
        bias2,
        up,
        down,
        gate,
        pixel_mask,
        cotangent,
        o_block,
        o_hidden,
        o_grads,
        o_ent,
        o_vb,
    ) = refs[:20]
    k = SimpleNamespace(**dict(zip(names, refs[20:])))
    sem = vars(k)
    L, D, W, F, H, T, R, nb, nt = s.L, s.D, s.W, s.F, s.H, s.T, s.R, s.nb, s.nt
    b = lax.axis_index("blk")
    t = lax.axis_index("tp")
    core = lax.rem(b, 2)
    pair = b // 2
    sib = b + 1 - 2 * core

    def z_peer(j):
        return lax.rem(t + j, nt)

    def z_from(j):
        return lax.rem(t + nt - j, nt)

    def remote(src, dst, send, recv, device):
        return pltpu.make_async_remote_copy(
            src, dst, send, recv, device_id=device, device_id_type=MESH
        )

    def z_copy(name, j, src, dst, h=0):
        i = h * (nt - 1) + j - 1
        return remote(src, dst, sem[name + "_s"].at[i], sem[name + "_r"].at[i], (b, z_peer(j)))

    def half(h):
        return pl.ds(h * T, T)

    def piece(h, tt):
        return pl.ds(pl.multiple_of(h * T + tt * R, R), R)

    def ag_copy(name, at, i, dst_band):
        return remote(at(b), at(b), sem[name + "_s"].at[i], sem[name + "_r"].at[i], (dst_band, t))

    def relay_copy(name, at, i, band):
        return remote(at(band), at(band), sem[name + "_rs"].at[i], sem[name + "_rr"].at[i], (sib, t))

    def band_same(i):
        return lax.rem(b + nb - 2 * i, nb)

    def band_sib(i):
        return lax.rem(sib + nb - 2 * i, nb)

    def ag_start(name, at):
        @pl.loop(1, s.half)
        def _(i):
            ag_copy(name, at, i, lax.rem(b + 2 * i, nb)).start()

        relay_copy(name, at, 0, b).start()

    def ag_relay(name, at, i):
        band = band_same(i)
        remote(at(band), at(band), sem[name + "_s"].at[i], sem[name + "_r"].at[i], (sib, t)).wait_recv()
        relay_copy(name, at, i, band).start()

    def ag_wait_relay(name, at, i):
        relay_copy(name, at, i, band_sib(i)).wait_recv()

    def ag_finish(name, at):
        @pl.loop(1, s.half)
        def _(i):
            ag_copy(name, at, i, sib).wait_send()

        @pl.loop(0, s.half)
        def _(i):
            relay_copy(name, at, i, b).wait_send()

    every = (nb, b, lambda i: i)
    near = (GROUP, lax.rem(b, GROUP), lambda i: b // GROUP * GROUP + i)
    far = (s.groups, b // GROUP, lambda i: i * GROUP + lax.rem(b, GROUP))

    def swap_copy(name, members, i, slot, to):
        ref = sem[name]
        return remote(
            ref.at[slot],
            ref.at[slot],
            sem[name + "_s"].at[i - 1],
            sem[name + "_r"].at[i - 1],
            (members[2](to), t),
        )

    def swap_start(name, members):
        count, me, _ = members

        @pl.loop(1, count)
        def _(i):
            swap_copy(name, members, i, me, lax.rem(me + i, count)).start()

    def swap_wait(name, members):
        count, me, _ = members

        @pl.loop(1, count)
        def _(i):
            peer = lax.rem(me + count - i, count)
            swap_copy(name, members, i, peer, peer).wait_recv()

    def swap_finish(name, members):
        count, me, _ = members

        @pl.loop(1, count)
        def _(i):
            swap_copy(name, members, i, me, lax.rem(me + i, count)).wait_send()

    def slots_sum(ref, count):
        return lax.fori_loop(
            1, count, lambda i, acc: acc + ref[i].astype(F32), ref[0].astype(F32)
        )

    def swap_sum(name):
        swap_wait(name, near)
        out = slots_sum(sem[name], GROUP)
        if s.groups > 1:
            sem[name + "2"][far[1]] = out.astype(BF16)
            swap_start(name + "2", far)
            swap_wait(name + "2", far)
            out = slots_sum(sem[name + "2"], s.groups)
            swap_finish(name + "2", far)
        swap_finish(name, near)
        return out

    def rs_start(name, h, part, recv):
        for j in range(1, nt):
            z_copy(name, j, part.at[piece(h, z_peer(j))], recv.at[h, j - 1], h).start()

    def rs_sum(name, h, part, recv):
        acc = part[piece(h, t), :].astype(F32)
        for j in range(1, nt):
            z_copy(name, j, part.at[piece(h, z_from(j))], recv.at[h, j - 1], h).wait_recv()
            acc = acc + recv[h, j - 1].astype(F32)
        return acc

    def rs_finish(name, part, recv):
        for h in range(2):
            for j in range(1, nt):
                z_copy(name, j, part.at[piece(h, z_peer(j))], recv.at[h, j - 1], h).wait_send()

    def gather_start(name, h, ref):
        for j in range(1, nt):
            z_copy(name, j, ref.at[piece(h, t)], ref.at[piece(h, t)], h).start()

    def gather_wait(name, h, ref):
        for j in range(1, nt):
            rows = piece(h, z_from(j))
            z_copy(name, j, ref.at[rows], ref.at[rows], h).wait_recv()

    def gather_finish(name, ref):
        for h in range(2):
            for j in range(1, nt):
                z_copy(name, j, ref.at[piece(h, t)], ref.at[piece(h, t)], h).wait_send()

    quarter = lax.rem(pair, 4)
    first_pair = pair - quarter
    group = pair // 4
    low_peer = quarter + 1 - 2 * lax.rem(quarter, 2)
    high_peer = lax.rem(quarter + 2, 4)
    first = low_peer * (1 - core) + high_peer * core
    second = low_peer * core + high_peer * (1 - core)
    across = lax.rem(low_peer + 2, 4)

    def g_rows(i, q):
        hr = s.sizes[i] // 2
        qr = hr // 4
        return pl.ds(pl.multiple_of(s.bases[i] + core * hr + q * qr, 16), qr)

    def g_half(i, c):
        hr = s.sizes[i] // 2
        return pl.ds(pl.multiple_of(s.bases[i] + c * hr, 16), hr)

    def q_rows(i, q):
        qr = s.sizes[i] // 8
        return pl.ds(pl.multiple_of(q * qr, 16), qr)

    def g_copy(i, slot, src, dst, q):
        dev = ((first_pair + q) * 2 + core, t)
        return remote(src, dst, sem["gs%d" % i].at[slot], sem["gr%d" % i].at[slot], dev)

    def sib_copy(i, slot, src, dst):
        return remote(src, dst, sem["gs%d" % i].at[slot], sem["gr%d" % i].at[slot], (sib, t))

    def c1_copy(i):
        return sib_copy(i, 0, k.gsrc.at[g_half(i, 1 - core)], sem["core%d" % i])

    def rs_copies(i):
        hs = sem["core%d" % i]
        land = sem["quart%d" % i]
        return (
            g_copy(i, 1, hs.at[q_rows(i, first)], land.at[0], first),
            g_copy(i, 2, hs.at[q_rows(i, across)], land.at[1], first),
        )

    def rs_copy_b(i):
        return g_copy(i, 3, sem["core%d" % i].at[q_rows(i, second)], sem["quart%d" % i].at[2], second)

    def out_copy(i, slot, q, to):
        rows = g_rows(i, q)
        return g_copy(i, slot, k.gout.at[rows], k.gout.at[rows], to)

    def c2_copy(i, c):
        rows = g_half(i, c)
        return sib_copy(i, 7, k.gout.at[rows], k.gout.at[rows])

    def sup_copy(i, j):
        ref = sem["sup%d" % i]
        dev = ((lax.rem(group + j, s.groups) * 4 + quarter) * 2 + core, t)
        return remote(ref.at[group], ref.at[group], sem["sup%d_s" % i].at[j - 1], sem["sup%d_r" % i].at[j - 1], dev)

    def q_peer(j):
        return lax.rem(quarter + j, 4)

    def direct_copy(i, j):
        src = sem["core%d" % i].at[q_rows(i, q_peer(j))]
        return g_copy(i, j, src, sem["quart%d" % i].at[j - 1], q_peer(j))

    def direct2(i):
        c1_copy(i).wait()
        hs = sem["core%d" % i]
        hs[...] = (k.gsrc[g_half(i, core), :].astype(F32) + hs[...].astype(F32)).astype(BF16)
        for j in range(1, 4):
            direct_copy(i, j).start()

    def direct3(i):
        acc = sem["core%d" % i][q_rows(i, quarter), :].astype(F32)
        for j in range(1, 4):
            direct_copy(i, j).wait()
            acc = acc + sem["quart%d" % i][j - 1].astype(F32)
        k.gout[g_rows(i, quarter), :] = across_groups(i, acc)
        for j in range(1, 4):
            out_copy(i, 3 + j, quarter, q_peer(j)).start()

    def direct6(i):
        for j in range(1, 4):
            out_copy(i, 3 + j, quarter, q_peer(j)).wait_send()
            out_copy(i, 3 + j, lax.rem(quarter + 4 - j, 4), q_peer(j)).wait_recv()
        c2_copy(i, core).start()

    def across_groups(i, acc):
        if s.groups > 1:
            ref = sem["sup%d" % i]
            ref[group] = acc.astype(BF16)
            for j in range(1, s.groups):
                sup_copy(i, j).start()
            for j in range(1, s.groups):
                sup_copy(i, j).wait()
            acc = ref[0].astype(F32)
            for g in range(1, s.groups):
                acc = acc + ref[g].astype(F32)
        return acc.astype(BF16)

    def grads1(i):
        c1_copy(i).start()

    def grads2(i):
        c1_copy(i).wait()
        hs = sem["core%d" % i]
        hs[...] = (k.gsrc[g_half(i, core), :].astype(F32) + hs[...].astype(F32)).astype(BF16)
        for copy in rs_copies(i):
            copy.start()

    def grads3(i):
        for copy in rs_copies(i):
            copy.wait()
        hs = sem["core%d" % i]
        rows = q_rows(i, second)
        hs[rows, :] = (hs[rows, :].astype(F32) + sem["quart%d" % i][1].astype(F32)).astype(BF16)
        rs_copy_b(i).start()

    def grads4(i):
        rs_copy_b(i).wait()
        land = sem["quart%d" % i]
        acc = sem["core%d" % i][q_rows(i, quarter), :].astype(F32)
        acc = acc + land[0].astype(F32) + land[2].astype(F32)
        k.gout[g_rows(i, quarter), :] = across_groups(i, acc)
        out_copy(i, 4, quarter, second).start()

    def grads5(i):
        out_copy(i, 4, quarter, second).wait_send()
        out_copy(i, 4, second, second).wait_recv()
        out_copy(i, 5, quarter, first).start()
        out_copy(i, 6, second, first).start()

    def grads6(i):
        out_copy(i, 5, quarter, first).wait_send()
        out_copy(i, 6, second, first).wait_send()
        out_copy(i, 5, first, first).wait_recv()
        out_copy(i, 6, across, first).wait_recv()
        c2_copy(i, core).start()

    def grads_store(i):
        rows = pl.ds(s.bases[i], s.sizes[i])
        return pltpu.make_async_copy(k.gout.at[rows], o_grads.at[rows], k.stores.at[i])

    def grads7(i):
        c2_copy(i, core).wait_send()
        c2_copy(i, 1 - core).wait_recv()
        grads_store(i).start()

    def load(i, src, dst):
        return pltpu.make_async_copy(src, dst, k.loads.at[i])

    first_loads = [
        load(0, patches, k.patches),
        load(1, leads_in, k.lead_index),
        load(2, table, k.table),
        load(3, gain1, k.gain1),
        load(4, bias1, k.bias1),
    ]
    ow_load = load(5, out_weight, k.ow.at[t])
    small_loads = [
        load(6, pixel_mask, k.pix),
        load(7, gate, k.head),
        load(8, windows_in, k.windows),
    ]
    qkv_load = load(9, qkv, k.qkv)
    late_loads = [
        load(10, gain2, k.gain2),
        load(11, bias2, k.bias2),
        load(12, up, k.up),
        load(13, down, k.down),
        load(14, cotangent, k.cot),
    ]
    for copy in first_loads + small_loads + [qkv_load, ow_load]:
        copy.start()
    barrier = pltpu.get_barrier_semaphore()

    @pl.loop(1, nb)
    def _(i):
        pl.semaphore_signal(barrier, inc=1, device_id=(lax.rem(b + i, nb), t), device_id_type=MESH)

    for j in range(1, nt):
        pl.semaphore_signal(barrier, inc=1, device_id=(b, z_peer(j)), device_id_type=MESH)

    for copy in first_loads:
        copy.wait()
    lead_hot = lax.broadcasted_iota(jnp.int32, (s.leads, L), 0) == row_of(k.lead_index)
    lead_hot = lead_hot.astype(F32).astype(BF16)
    hidden = k.patches[...] + mm_tn(lead_hot, k.table[...])
    unit1, inverse1 = norm_stats(hidden)
    k.u1[...] = unit1
    k.r1[...] = inverse1
    k.mid[...] = hidden
    k.normed[...] = (unit1 * row_of(k.gain1) + row_of(k.bias1)).astype(BF16)
    for copy in small_loads:
        copy.wait()
    compact = [k.head[e].astype(F32) for e in range(3)] + [jnp.zeros((4, D), F32)]
    k.gatec[t] = jnp.concatenate(compact, axis=0).astype(BF16)
    k.mask[t] = jnp.concatenate([k.pix[...].astype(F32), jnp.zeros((4, L), F32)], axis=0)
    part = W // 4
    upper = quarter // 2

    def ow_part(tt, c, u):
        return k.ow.at[tt, pl.ds(pl.multiple_of((c + 2 * u) * part, part), part)]

    def ow_copy(name, j, at, dev, second_set=0):
        i = second_set * (nt - 1) + j - 1
        return remote(at, at, sem[name + "_s"].at[i], sem[name + "_r"].at[i], (dev, t))

    high_dev = (first_pair + high_peer) * 2 + core

    qkv_load.wait()

    def project(c):
        return mm_nt(k.qkv[c], k.normed[...])

    k.kv[b, 0:W, :] = project(1).astype(BF16)
    k.kv[b, W : 2 * W, :] = project(2).astype(BF16)
    ow_load.wait()
    pl.semaphore_wait(barrier, nb - 1 + nt - 1)

    def kv_at(band):
        return k.kv.at[band]

    ag_start("kv", kv_at)
    for j in range(1, nt):
        z_copy("zmask", j, k.mask.at[t], k.mask.at[t]).start()
        z_copy("zow", j, ow_part(t, core, upper), ow_part(t, core, upper)).start()
        z_copy("zgate", j, k.gatec.at[t], k.gatec.at[t]).start()
    for copy in late_loads:
        copy.start()
    k.qd[b, 0:W, :] = (project(0).astype(BF16).astype(F32) * SCALE).astype(BF16)

    k.ids[...] = k.windows[...].reshape(nb, L).astype(F32)

    def id_row(band):
        return k.ids[pl.ds(band, 1), :]

    def id_column(band):
        return jnp.transpose(jnp.broadcast_to(id_row(band), (128, L)))[:, 0:1]

    def head(h):
        return pl.ds(h * HEAD_DIM, HEAD_DIM)

    def value_head(h):
        return pl.ds(W + h * HEAD_DIM, HEAD_DIM)

    k.m[...] = jnp.full((8, L), MASKED, F32)
    k.l[...] = jnp.zeros((8, L), F32)
    k.acc[...] = jnp.zeros((W, L), F32)

    def forward_bands(bands):
        tiles = [(h, i) for h in range(H) for i in range(len(bands))]
        allowed = [id_column(band) == id_row(b) for band in bands]
        scores = {
            (h, i): jnp.where(
                allowed[i], mm_tn(k.kv[bands[i], head(h), :], k.qd[b, head(h), :]), MASKED
            )
            for h, i in tiles
        }
        old_high = [k.m[h : h + 1, :] for h in range(H)]
        sums = [k.l[h : h + 1, :] for h in range(H)]
        outs = [k.acc[head(h), :] for h in range(H)]
        high = list(old_high)
        for h, i in tiles:
            high[h] = jnp.maximum(high[h], jnp.max(scores[h, i], axis=0, keepdims=True))
        weights = {(h, i): jnp.exp(scores[h, i] - high[h]) for h, i in tiles}
        factor = [jnp.exp(x - y) for x, y in zip(old_high, high)]
        outs = [x * f for x, f in zip(outs, factor)]
        sums = [x * f for x, f in zip(sums, factor)]
        for h, i in tiles:
            outs[h] += mm_nn(k.kv[bands[i], value_head(h), :], weights[h, i].astype(BF16))
            sums[h] += jnp.sum(weights[h, i], axis=0, keepdims=True)
        for h in range(H):
            k.m[h : h + 1, :] = high[h]
            k.l[h : h + 1, :] = sums[h]
            k.acc[head(h), :] = outs[h]

    def ow_pass_on():
        for j in range(1, nt):
            at = ow_part(z_from(j), core, upper)
            z_copy("zow", j, at, at).wait_recv()
            ow_copy("zowy", j, at, high_dev).start()
            ow_copy("zowr", j, at, sib).start()

    def ow_pass_second():
        for j in range(1, nt):
            at = ow_part(z_from(j), core, 1 - upper)
            ow_copy("zowy", j, at, high_dev).wait_recv()
            ow_copy("zowr", j, at, sib, 1).start()

    def ow_arrived():
        for j in range(1, nt):
            ow_copy("zowr", j, ow_part(z_from(j), 1 - core, upper), sib).wait_recv()
            ow_copy("zowr", j, ow_part(z_from(j), 1 - core, 1 - upper), sib, 1).wait_recv()

    ag_wait_relay("kv", kv_at, 0)
    forward_bands([b, sib])
    for j in range(1, nt):
        z_copy("zmask", j, k.mask.at[t], k.mask.at[z_from(j)]).wait_recv()
    k.cnt[b] = jnp.broadcast_to(total(jnp.sum(k.mask[...], axis=0)), (8, 128))
    swap_start("cnt", every)

    def forward_loop(start, stop):
        @pl.loop(start, stop)
        def _(i):
            ag_wait_relay("kv", kv_at, i)
            forward_bands([band_same(i), band_sib(i)])

    @pl.loop(1, s.half)
    def _(i):
        ag_relay("kv", kv_at, i)

    forward_loop(1, s.half // 2)
    ow_pass_on()
    forward_loop(s.half // 2, s.half)

    for h in range(H):
        att = k.acc[head(h), :] / k.l[h : h + 1, :]
        k.acc[head(h), :] = att
        k.att[t, head(h), :] = att.astype(BF16)
        k.st[b, h : h + 1, :] = k.m[h : h + 1, :] + jnp.log(k.l[h : h + 1, :])

    def att_half(tt, h):
        return k.att.at[tt, :, half(h)]

    for h in range(2):
        for j in range(1, nt):
            z_copy("zatt", j, att_half(t, h), att_half(t, h), h).start()

    def q_at(band):
        return k.qd.at[band, pl.ds(0, W)]

    def da_at(h):
        return lambda band: k.qd.at[band, pl.ds(W, W), half(h)]

    def st_at(band):
        return k.st.at[band]

    ag_start("q", q_at)
    ow_pass_second()
    for copy in late_loads:
        copy.wait()
    ow_arrived()

    for h in range(2):
        for j in range(1, nt):
            z_copy("zatt", j, att_half(z_from(j), h), att_half(z_from(j), h), h).wait_recv()
        rows = half(h)
        middle = k.mid[rows, :] + mm_tn(
            k.att[:, :, half(h)].reshape(nt * W, T), k.ow[...].reshape(nt * W, D)
        )
        k.mid[rows, :] = middle
        unit2, inverse2 = norm_stats(middle)
        k.u2[rows, :] = unit2
        k.r2[rows, :] = inverse2
        k.n2low[rows, :] = (unit2 * row_of(k.gain2) + row_of(k.bias2)).astype(BF16)
        upward = mm_nn(k.n2low[rows, :], k.up[...])
        k.upw[rows, :] = upward
        k.actlow[rows, :] = (0.5 * upward * (1.0 + lax.erf(upward * INV_SQRT2))).astype(BF16)
        k.ffp[rows, :] = mm_nn(k.actlow[rows, :], k.down[...]).astype(BF16)
        rs_start("zff", h, k.ffp, k.ffr)
    upward = k.upw[...]
    k.upw[...] = 0.5 * (1.0 + lax.erf(upward * INV_SQRT2)) + upward * (
        jnp.exp(-0.5 * upward * upward) * INV_SQRT_2PI
    )
    for j in range(1, nt):
        z_copy("zgate", j, k.gatec.at[t], k.gatec.at[z_from(j)]).wait_recv()
    for tt in range(nt):
        x = k.gatec[tt].astype(F32)
        pad = jnp.zeros((4, D), F32)
        parts = []
        for e in range(3):
            parts += [x[4 * e : 4 * e + 4], pad]
        k.gate[tt * 32 : (tt + 1) * 32, :] = jnp.concatenate(parts + [pad, pad], axis=0).astype(BF16)
    swap_wait("cnt", every)
    pixel_count = jnp.sum(k.cnt[...], axis=0)[0:1, 0:1]
    for h in range(2):
        block_piece = k.mid[piece(h, t), :] + rs_sum("zff", h, k.ffp, k.ffr)
        k.blow[piece(h, t), :] = block_piece.astype(BF16)
        gather_start("zblk", h, k.blow)

    @pl.loop(1, s.half)
    def _(i):
        ag_relay("q", q_at, i)

    entropy_sum = jnp.zeros((1, 1), F32)
    for h in range(2):
        rows = half(h)
        gather_wait("zblk", h, k.blow)
        logits = mm_nt(k.gate[...], k.blow[rows, :]).reshape(nt, 4, 8, T)
        parts = [logits[:, e] for e in range(3)]
        high = jnp.maximum(jnp.maximum(parts[0], parts[1]), parts[2])
        logs = jnp.log(sum(jnp.exp(x - high) for x in parts))
        log_probs = [x - high - logs for x in parts]
        probs = [jnp.exp(x) for x in log_probs]
        entropy = -sum(p * x for p, x in zip(probs, log_probs))
        mask = k.mask[:, :, half(h)]
        entropy_sum += total(jnp.sum(mask * entropy, axis=0))
        weight = mask * (float(s.pixels) / pixel_count)[None]
        grads = [-p * (x + entropy) * weight for p, x in zip(probs, log_probs)]
        grads.append(jnp.zeros((nt, 8, T), F32))
        k.lg[:, half(h)] = jnp.stack(grads, axis=1).reshape(nt * 32, T).astype(BF16)
        out_grad = k.cot[rows, :] + mm_tn(k.lg[:, half(h)], k.gate[...])
        k.cot[rows, :] = out_grad
        k.oglow[rows, :] = out_grad.astype(BF16)
        k.ug[rows, :] = (mm_nt(k.oglow[rows, :], k.down[...]) * k.upw[rows, :]).astype(BF16)
        k.n2p[rows, :] = mm_nt(k.ug[rows, :], k.up[...]).astype(BF16)
        rs_start("zn2", h, k.n2p, k.n2r)
    block_copy = pltpu.make_async_copy(k.blow, o_block, k.stores.at[4])
    block_copy.start()
    k.gsrc[0:F, :] = mm_tn(k.actlow[...], k.oglow[...]).astype(BF16)
    grads1(0)
    k.gsrc[F : F + D, :] = mm_tn(k.n2low[...], k.ug[...]).astype(BF16)
    grads1(1)
    own_lg = k.lg[pl.ds(pl.multiple_of(t * 32, 32), 32), :]
    base = s.bases[2] + 2 * W
    k.gsrc[base : base + 32, :] = mm_nn(own_lg, k.blow[...]).astype(BF16)
    k.gsrc[base + 32 : base + 128, :] = jnp.zeros((96, D), BF16)
    k.ent[b] = jnp.broadcast_to(entropy_sum / pixel_count, (8, 128))
    swap_start("ent", every)

    def middle_backward(n2_grad, rows):
        return k.cot[rows, :] + norm_backward(n2_grad, k.u2[rows, :], k.r2[rows, :], row_of(k.gain2))

    def attended_exchange(h):
        rows = piece(h, t)
        n2_low = rs_sum("zn2", h, k.n2p, k.n2r).astype(BF16)
        k.n2g[rows, :] = n2_low
        low_piece = middle_backward(n2_low.astype(F32), rows).astype(BF16)
        for tt in range(nt):
            k.dasrc[h, tt] = mm_nt(low_piece, k.ow[tt]).astype(BF16)
        for j in range(1, nt):
            z_copy("zda", j, k.dasrc.at[h, z_peer(j)], k.datok.at[h, t], h).start()
        k.datok[h, t] = k.dasrc[h, t]

    def attended_arrived(h):
        for j in range(1, nt):
            z_copy("zda", j, k.dasrc.at[h, z_peer(j)], k.datok.at[h, z_from(j)], h).wait_recv()
        att_grad = jnp.transpose(k.datok[h].reshape(T, W).astype(F32)).astype(BF16)
        k.qd[b, W : 2 * W, half(h)] = att_grad
        ag_start("da%d" % h, da_at(h))
        weighted = att_grad.astype(F32) * k.acc[:, half(h)]
        for i in range(H):
            k.st[b, H + i : H + i + 1, half(h)] = jnp.sum(
                weighted[i * HEAD_DIM : (i + 1) * HEAD_DIM], axis=0, keepdims=True
            )

    grads2(0)
    attended_exchange(0)
    grads2(1)
    attended_exchange(1)
    attended_arrived(0)
    attended_arrived(1)
    ag_start("st", st_at)
    for h in range(2):
        gather_start("zn2g", h, k.n2g)
    grads3(0)
    k.dq[...] = jnp.zeros((W, L), F32)
    k.dk[...] = jnp.zeros((W, L), F32)
    k.dv[...] = jnp.zeros((W, L), F32)
    my_column = id_column(b)

    def score_grads(allowed, scores, dots, stats):
        probs = {
            (h, i): jnp.exp(jnp.where(allowed[i], x, MASKED) - stats[i][h : h + 1])
            for (h, i), x in scores.items()
        }
        grads = {
            (h, i): (x * (dots[h, i] - stats[i][H + h : H + h + 1])).astype(BF16)
            for (h, i), x in probs.items()
        }
        return probs, grads

    @pl.loop(0, s.half)
    def _(step):
        bands = [2 * step, 2 * step + 1]
        tiles = [(h, i) for h in range(H) for i in range(2)]
        allowed = [id_column(band) == id_row(b) for band in bands]
        scores = {(h, i): mm_tn(k.kv[bands[i], head(h), :], k.qd[b, head(h), :]) for h, i in tiles}
        dots = {
            (h, i): mm_tn(k.kv[bands[i], value_head(h), :], k.qd[b, value_head(h), :]) for h, i in tiles
        }
        outs = [k.dq[head(h), :] for h in range(H)]
        _, grads = score_grads(allowed, scores, dots, [k.st[b]] * 2)
        for h, i in tiles:
            outs[h] += mm_nn(k.kv[bands[i], head(h), :], grads[h, i])
        for h in range(H):
            k.dq[head(h), :] = outs[h]

    grads3(1)
    @pl.loop(1, s.half)
    def _(i):
        ag_wait_relay("q", q_at, i)

    ag_wait_relay("q", q_at, 0)

    def backward_bands(bands):
        tiles = [(h, i) for h in range(H) for i in range(len(bands))]
        allowed = [my_column == id_row(band) for band in bands]
        scores = {(h, i): mm_tn(k.kv[b, head(h), :], k.qd[bands[i], head(h), :]) for h, i in tiles}
        dots = {
            (h, i): mm_tn(k.kv[b, value_head(h), :], k.qd[bands[i], value_head(h), :]) for h, i in tiles
        }
        key_outs = [k.dk[head(h), :] for h in range(H)]
        value_outs = [k.dv[head(h), :] for h in range(H)]
        probs, grads = score_grads(allowed, scores, dots, [k.st[band] for band in bands])
        for h, i in tiles:
            key_outs[h] += mm_nt(k.qd[bands[i], head(h), :], grads[h, i])
            value_outs[h] += mm_nt(k.qd[bands[i], value_head(h), :], probs[h, i].astype(BF16))
        for h in range(H):
            k.dk[head(h), :] = key_outs[h]
            k.dv[head(h), :] = value_outs[h]

    def backward_loop(start, stop):
        @pl.loop(start, stop)
        def _(i):
            ag_wait_relay("da0", da_at(0), i)
            ag_wait_relay("da1", da_at(1), i)
            ag_wait_relay("st", st_at, i)
            backward_bands([band_same(i), band_sib(i)])

    backward_loop(0, 1)
    grads4(0)

    @pl.loop(1, s.half)
    def _(i):
        ag_relay("da0", da_at(0), i)
        ag_relay("da1", da_at(1), i)
        ag_relay("st", st_at, i)

    backward_loop(1, s.half // 2)
    grads4(1)
    backward_loop(s.half // 2, s.half)
    grads5(0)
    k.dp[0] = (k.dq[...] * SCALE).astype(BF16)
    k.dp[1] = k.dk[...].astype(BF16)
    k.dp[2] = k.dv[...].astype(BF16)
    for h in range(2):
        k.ngp[half(h), :] = mm_tn(
            k.dp[:, :, half(h)].reshape(3 * W, T), k.qkv[...].reshape(3 * W, D)
        ).astype(BF16)
        rs_start("zng", h, k.ngp, k.ngr)
    base = s.bases[2]
    for h in range(2):
        gather_wait("zn2g", h, k.n2g)
    n2_grad = k.n2g[...].astype(F32)
    gain2_grad = jnp.sum(n2_grad * k.u2[...], axis=0, keepdims=True)
    bias2_grad = jnp.sum(n2_grad, axis=0, keepdims=True)
    middle_grad = middle_backward(n2_grad, pl.ds(0, L))
    k.cot[...] = middle_grad
    k.gsrc[base : base + W, :] = mm_nn(k.att[t], middle_grad.astype(BF16)).astype(BF16)
    k.gsrc[base + W : base + 2 * W, :] = mm_nn(k.dp[0], k.normed[...]).astype(BF16)
    grads1(2)

    base = s.bases[3]
    k.gsrc[base : base + 2 * W, :] = mm_nn(k.dp[1:3].reshape(2 * W, L), k.normed[...]).astype(BF16)
    grads1(3)
    grads5(1)
    k.ngg[piece(0, t), :] = rs_sum("zng", 0, k.ngp, k.ngr).astype(BF16)
    gather_start("zngg", 0, k.ngg)
    direct2(2)
    direct2(3)
    grads6(0)
    k.ngg[piece(1, t), :] = rs_sum("zng", 1, k.ngp, k.ngr).astype(BF16)
    gather_start("zngg", 1, k.ngg)
    grads6(1)
    direct3(2)
    direct3(3)
    grads7(0)
    grads7(1)
    swap_wait("ent", every)
    k.ent_sum[...] = jnp.sum(k.ent[...], axis=0)
    ent_copy = pltpu.make_async_copy(k.ent_sum, o_ent, k.stores.at[6])
    ent_copy.start()
    gather_wait("zngg", 0, k.ngg)
    direct6(2)
    direct6(3)
    gather_wait("zngg", 1, k.ngg)
    n1_grad = k.ngg[...].astype(F32)
    unit1 = k.u1[...]
    gain1_grad = jnp.sum(n1_grad * unit1, axis=0, keepdims=True)
    bias1_grad = jnp.sum(n1_grad, axis=0, keepdims=True)
    hidden_grad = k.cot[...] + norm_backward(n1_grad, unit1, k.r1[...], row_of(k.gain1))
    k.patches[...] = hidden_grad
    hidden_copy = pltpu.make_async_copy(k.patches, o_hidden, k.stores.at[5])
    hidden_copy.start()
    coarse = hidden_grad.astype(BF16)
    fine = (hidden_grad - coarse.astype(F32)).astype(BF16)
    tail = [
        mm_nn(lead_hot, coarse) + mm_nn(lead_hot, fine),
        gain1_grad,
        bias1_grad,
        gain2_grad,
        bias2_grad,
        jnp.zeros((s.tail - s.leads - 4, D), F32),
    ]
    k.vb[near[1]] = jnp.concatenate(tail, axis=0).astype(BF16)
    swap_start("vb", near)
    grads7(2)
    grads7(3)
    k.vb_sum[...] = swap_sum("vb")
    vb_copy = pltpu.make_async_copy(k.vb_sum, o_vb, k.stores.at[7])
    vb_copy.start()

    for j in range(1, nt):
        z_copy("zmask", j, k.mask.at[t], k.mask.at[t]).wait_send()
        z_copy("zgate", j, k.gatec.at[t], k.gatec.at[t]).wait_send()
        z_copy("zow", j, ow_part(t, core, upper), ow_part(t, core, upper)).wait_send()
        at = ow_part(z_from(j), core, upper)
        ow_copy("zowy", j, at, high_dev).wait_send()
        ow_copy("zowr", j, at, sib).wait_send()
        ow_copy("zowr", j, at, sib, 1).wait_send()
        for h in range(2):
            z_copy("zatt", j, att_half(t, h), att_half(t, h), h).wait_send()
            z_copy("zda", j, k.dasrc.at[h, z_peer(j)], k.datok.at[h, t], h).wait_send()
    rs_finish("zff", k.ffp, k.ffr)
    gather_finish("zblk", k.blow)
    rs_finish("zn2", k.n2p, k.n2r)
    gather_finish("zn2g", k.n2g)
    rs_finish("zng", k.ngp, k.ngr)
    gather_finish("zngg", k.ngg)
    for name, at in (("kv", kv_at), ("q", q_at), ("da0", da_at(0)), ("da1", da_at(1)), ("st", st_at)):
        ag_finish(name, at)
    swap_finish("cnt", every)
    swap_finish("ent", every)
    for i in range(4):
        grads_store(i).wait()
    for copy in (block_copy, hidden_copy, ent_copy, vb_copy):
        copy.wait()


def last_kernel(
    s, cuts, block, hidden, grads, ent, vb,
    o_block, o_hidden, o_qkv, o_out, o_up, o_down, o_pen, o_lead, o_g1, o_b1, o_g2, o_b2, o_gate,
    low, wide, low_block, wide_block, keep, load_sem, store_sem,
):
    outs = {"down": o_down, "up": o_up, "out": o_out, "q": o_qkv.at[0], "k": o_qkv.at[1], "v": o_qkv.at[2]}
    loads = [
        pltpu.make_async_copy(block, low_block, load_sem.at[0]),
        pltpu.make_async_copy(hidden, keep, load_sem.at[1]),
    ]
    stores = [
        pltpu.make_async_copy(wide_block, o_block, store_sem.at[0]),
        pltpu.make_async_copy(keep, o_hidden, store_sem.at[1]),
    ]
    for i, (row, name, start, size) in enumerate(cuts):
        rows = pl.ds(row, size)
        loads.append(pltpu.make_async_copy(grads.at[rows], low.at[rows], load_sem.at[i + 2]))
        stores.append(
            pltpu.make_async_copy(wide.at[rows], outs[name].at[pl.ds(start, size)], store_sem.at[i + 2])
        )
    gate_rows = pl.ds(s.bases[2] + 2 * s.W, 32)
    gate_load = pltpu.make_async_copy(grads.at[gate_rows], low.at[gate_rows], load_sem.at[len(cuts) + 2])
    for copy in loads + [gate_load]:
        copy.start()
    loads[0].wait()
    wide_block[...] = low_block[...].astype(F32)
    stores[0].start()
    loads[1].wait()
    stores[1].start()
    for i, (row, name, start, size) in enumerate(cuts):
        loads[i + 2].wait()
        rows = pl.ds(row, size)
        wide[rows, :] = low[rows, :].astype(F32)
        stores[i + 2].start()
    gate_load.wait()
    small = low[gate_rows, :].astype(F32)
    for e in range(3):
        o_gate[e] = small[8 * e : 8 * e + 4]
    o_pen[...] = ent[0:1, 0:1]
    tail = vb[...]
    o_lead[...] = tail[0 : s.leads]
    o_g1[...] = tail[s.leads].reshape(s.D)
    o_b1[...] = tail[s.leads + 1].reshape(s.D)
    o_g2[...] = tail[s.leads + 2].reshape(s.D)
    o_b2[...] = tail[s.leads + 3].reshape(s.D)
    for copy in stores:
        copy.wait()


def local(
    nb,
    nt,
    patches,
    window_ids,
    lead_index,
    lead_table,
    attention_gain,
    attention_bias,
    query_key_value,
    out_weight,
    feedforward_gain,
    feedforward_bias,
    up_weight,
    down_weight,
    gate_head,
    pixel_mask,
    cotangent,
):
    L, D = patches.shape
    leads = lead_table.shape[0]
    W = out_weight.shape[0]
    F = up_weight.shape[1]
    s = dims_of(nb, nt, L, D, W, F, leads, L * nb * pixel_mask.shape[0] * nt)
    scratch = scratch_of(s)
    vm = pl.BlockSpec(memory_space=pltpu.VMEM)
    block, hidden, grads, ent, vb = pl.pallas_call(
        partial(main_kernel, s, tuple(scratch)),
        out_shape=(
            jax.ShapeDtypeStruct((L, D), BF16),
            jax.ShapeDtypeStruct((L, D), F32),
            jax.ShapeDtypeStruct((s.rows, D), BF16),
            jax.ShapeDtypeStruct((8, 128), F32),
            jax.ShapeDtypeStruct((s.tail, D), F32),
        ),
        in_specs=[pl.BlockSpec(memory_space=pltpu.HBM)] * 15,
        out_specs=(pl.BlockSpec(memory_space=pl.ANY),) * 5,
        scratch_shapes=list(scratch.values()),
        compiler_params=pltpu.CompilerParams(
            collective_id=0,
            has_side_effects=True,
            vmem_limit_bytes=VMEM_LIMIT,
        ),
        cost_estimate=pl.CostEstimate(
            flops=2 * s.rows * D * L * 3 + 14 * L * nb * L * W, bytes_accessed=16 * 2**20, transcendentals=0
        ),
        name="block_step",
    )(
        patches,
        window_ids,
        lead_index,
        lead_table,
        attention_gain,
        attention_bias,
        jnp.transpose(query_key_value, (0, 2, 1)),
        out_weight,
        feedforward_gain,
        feedforward_bias,
        up_weight,
        down_weight,
        gate_head,
        pixel_mask,
        cotangent,
    )
    vec = jax.ShapeDtypeStruct((D,), F32)
    cuts = []
    first = s.bases[2]
    places = (
        ("down", 0, F),
        ("up", F, D),
        ("out", first, W),
        ("q", first + W, W),
        ("k", s.bases[3], W),
        ("v", s.bases[3] + W, W),
    )
    for name, row, size in places:
        for start in range(0, size, 256):
            cuts.append((row + start, name, start, min(256, size - start)))
    hbm = pl.BlockSpec(memory_space=pl.ANY)
    wide, high, qkv_grad, out_grad, up_grad, down_grad, pen, lead, g1, b1, g2, b2, gates = pl.pallas_call(
        partial(last_kernel, s, cuts),
        out_shape=(
            jax.ShapeDtypeStruct((L, D), F32),
            jax.ShapeDtypeStruct((L, D), F32),
            jax.ShapeDtypeStruct((3, W, D), F32),
            jax.ShapeDtypeStruct((W, D), F32),
            jax.ShapeDtypeStruct((D, F), F32),
            jax.ShapeDtypeStruct((F, D), F32),
            jax.ShapeDtypeStruct((1, 1), F32),
            jax.ShapeDtypeStruct((leads, D), F32),
            vec,
            vec,
            vec,
            vec,
            jax.ShapeDtypeStruct(gate_head.shape, F32),
        ),
        in_specs=[hbm] * 3 + [vm] * 2,
        out_specs=(hbm,) * 6 + (vm,) * 7,
        scratch_shapes=[
            pltpu.VMEM((s.rows, D), BF16),
            pltpu.VMEM((s.rows, D), F32),
            pltpu.VMEM((L, D), BF16),
            pltpu.VMEM((L, D), F32),
            pltpu.VMEM((L, D), F32),
            pltpu.SemaphoreType.DMA((len(cuts) + 3,)),
            pltpu.SemaphoreType.DMA((len(cuts) + 2,)),
        ],
        compiler_params=pltpu.CompilerParams(vmem_limit_bytes=VMEM_LIMIT),
        name="write_out",
    )(block, hidden, grads, ent, vb)
    return (
        wide,
        pen.reshape(()),
        high,
        lead,
        g1,
        b1,
        jnp.transpose(qkv_grad, (0, 2, 1)),
        out_grad,
        g2,
        b2,
        up_grad,
        down_grad,
        gates,
    )


def solution(mesh):
    in_specs = (
        P("blk", None),
        P(),
        P("blk"),
        P(),
        P(),
        P(),
        P(None, None, "tp"),
        P("tp", None),
        P(),
        P(),
        P(None, "tp"),
        P("tp", None),
        P(None, "tp", None),
        P("tp", "blk"),
        P("blk", None),
    )
    out_specs = (
        P("blk", None),
        P(),
        P("blk", None),
        P(),
        P(),
        P(),
        P(None, None, "tp"),
        P("tp", None),
        P(),
        P(),
        P(None, "tp"),
        P("tp", None),
        P(None, "tp", None),
    )
    return jax.shard_map(
        partial(local, mesh.shape["blk"], mesh.shape["tp"]),
        mesh=mesh,
        in_specs=in_specs,
        out_specs=out_specs,
        check_vma=False,
    )
```

```python
from functools import partial
from types import SimpleNamespace

import jax
import jax.numpy as jnp
from jax import lax
from jax.experimental import pallas as pl
from jax.experimental.pallas import tpu as pltpu
from jax.sharding import PartitionSpec as P

HEAD_DIM = 64
EPS = 1e-05
MASKED = -1e30
SCALE = HEAD_DIM ** (-0.5)
GROUP = 8
F32 = jnp.float32
BF16 = jnp.bfloat16
MESH = pl.DeviceIdType.MESH
VMEM_LIMIT = 61 * 2**20
INV_SQRT2 = 0.7071067811865476
INV_SQRT_2PI = 0.3989422804014327


def dot(a, b, ca, cb):
    return lax.dot_general(a, b, (((ca,), (cb,)), ((), ())), preferred_element_type=F32)


def mm_nn(a, b):
    return dot(a, b, 1, 0)


def mm_nt(a, b):
    return dot(a, b, 1, 1)


def mm_tn(a, b):
    return dot(a, b, 0, 0)


def norm_stats(values):
    mean = jnp.mean(values, axis=-1, keepdims=True)
    centered = values - mean
    inverse = lax.rsqrt(jnp.mean(centered * centered, axis=-1, keepdims=True) + EPS)
    return centered * inverse, inverse


def norm_backward(incoming, unit_rows, inverse, gain):
    scaled = incoming * gain
    return inverse * (
        scaled
        - jnp.mean(scaled, axis=-1, keepdims=True)
        - unit_rows * jnp.mean(scaled * unit_rows, axis=-1, keepdims=True)
    )


def row_of(ref):
    return ref[...].reshape(1, ref.shape[0])


def total(x):
    return jnp.sum(jnp.sum(x, axis=0, keepdims=True), axis=1, keepdims=True)


def dims_of(nb, nt, tokens, width, local_width, hidden, leads, pixels):
    s = SimpleNamespace(nb=nb, nt=nt, L=tokens, D=width, W=local_width, F=hidden, leads=leads)
    s.H = local_width // HEAD_DIM
    s.T = tokens // 2
    s.R = s.T // nt
    s.half = nb // 2
    s.groups = nb // GROUP
    s.pixels = pixels
    s.sizes = (hidden, width + 128, local_width * 2, local_width * 2)
    s.bases = tuple(sum(s.sizes[:i]) for i in range(4))
    s.rows = sum(s.sizes)
    s.tail = (leads + 4 + 15) // 16 * 16
    return s


def scratch_of(s):
    L, D, W, F, nb, nt, R = s.L, s.D, s.W, s.F, s.nb, s.nt, s.R
    v = pltpu.VMEM
    out = {
        "patches": v((L, D), F32),
        "windows": v((nb * L,), jnp.int32),
        "lead_index": v((L,), jnp.int32),
        "table": v((s.leads, D), BF16),
        "gain1": v((D,), F32),
        "bias1": v((D,), F32),
        "gain2": v((D,), F32),
        "bias2": v((D,), F32),
        "pix": v((4, L), jnp.int32),
        "head": v((3, 4, D), BF16),
        "ids": v((nb, L), F32),
        "qkv": v((3, W, D), BF16),
        "ow": v((nt, W, D), BF16),
        "up": v((D, F), BF16),
        "down": v((F, D), BF16),
        "cot": v((L, D), F32),
        "gatec": v((nt, 16, D), BF16),
        "gate": v((nt * 32, D), BF16),
        "mask": v((nt, 8, L), F32),
        "cnt": v((nb, 8, 128), F32),
        "u1": v((L, D), F32),
        "r1": v((L, 1), F32),
        "normed": v((L, D), BF16),
        "kv": v((nb, 2 * W, L), BF16),
        "qd": v((nb, 2 * W, L), BF16),
        "st": v((nb, 8, L), F32),
        "m": v((8, L), F32),
        "l": v((8, L), F32),
        "acc": v((W, L), F32),
        "att": v((nt, W, L), BF16),
        "mid": v((L, D), F32),
        "u2": v((L, D), F32),
        "r2": v((L, 1), F32),
        "n2low": v((L, D), BF16),
        "upw": v((L, F), F32),
        "actlow": v((L, F), BF16),
        "ffp": v((L, D), BF16),
        "ffr": v((2, nt - 1, R, D), BF16),
        "blow": v((L, D), BF16),
        "lg": v((nt * 32, L), BF16),
        "oglow": v((L, D), BF16),
        "ug": v((L, F), BF16),
        "n2p": v((L, D), BF16),
        "n2r": v((2, nt - 1, R, D), BF16),
        "n2g": v((L, D), BF16),
        "dasrc": v((2, nt, R, W), BF16),
        "datok": v((2, nt, R, W), BF16),
        "dq": v((W, L), F32),
        "dk": v((W, L), F32),
        "dv": v((W, L), F32),
        "dp": v((3, W, L), BF16),
        "ngp": v((L, D), BF16),
        "ngr": v((2, nt - 1, R, D), BF16),
        "ngg": v((L, D), BF16),
        "vb": v((GROUP, s.tail, D), BF16),
        "ent": v((nb, 8, 128), F32),
        "ent_sum": v((8, 128), F32),
        "vb_sum": v((s.tail, D), F32),
        "gsrc": v((s.rows, D), BF16),
        "gout": v((s.rows, D), BF16),
    }
    dma = pltpu.SemaphoreType.DMA
    out["loads"] = dma((15,))
    out["stores"] = dma((8,))
    for name in ("zmask", "zgate", "zow", "zowy", "zowr", "zowq"):
        out[name + "_s"] = dma((1,))
        out[name + "_r"] = dma((1,))
    for name in ("zatt", "zff", "zblk", "zn2", "zn2g", "zda", "zng", "zngg"):
        out[name + "_s"] = dma((2,))
        out[name + "_r"] = dma((2,))
    for name in ("kv", "q", "da0", "da1", "st"):
        count = s.half if name == "kv" else 1
        out[name + "_s"] = dma((1,))
        out[name + "_r"] = dma((count,))
        out[name + "_rs"] = dma((1,))
        out[name + "_rr"] = dma((count,))
    for name in ("cnt", "ent", "vb"):
        out[name + "_s"] = dma((1,))
        out[name + "_r"] = dma((1,))
    if s.groups > 1:
        out["vb2"] = v((s.groups, s.tail, D), BF16)
        out["vb2_s"] = dma((1,))
        out["vb2_r"] = dma((1,))
    for i, rows in enumerate(s.sizes):
        hr = rows // 2
        qr = hr // 4
        out["core%d" % i] = v((hr, D), BF16)
        out["quart%d" % i] = v((3, qr, D), BF16)
        if s.groups > 1:
            out["sup%d" % i] = v((s.groups, qr, D), BF16)
            out["sup%d_s" % i] = dma((1,))
            out["sup%d_r" % i] = dma((1,))
        out["gs%d" % i] = dma((6 if i < 2 else 4,))
        out["gr%d" % i] = dma((6 if i < 2 else 4,))
    return out


def main_kernel(s, names, *refs):
    (
        patches,
        windows_in,
        leads_in,
        table,
        gain1,
        bias1,
        qkv,
        out_weight,
        gain2,
        bias2,
        up,
        down,
        gate,
        pixel_mask,
        cotangent,
        o_block,
        o_hidden,
        o_grads,
        o_ent,
        o_vb,
    ) = refs[:20]
    k = SimpleNamespace(**dict(zip(names, refs[20:])))
    sem = vars(k)
    L, D, W, F, H, T, R, nb, nt = s.L, s.D, s.W, s.F, s.H, s.T, s.R, s.nb, s.nt
    b = lax.axis_index("blk")
    t = lax.axis_index("tp")
    core = lax.rem(b, 2)
    pair = b // 2
    sib = b + 1 - 2 * core

    def z_peer(j):
        return lax.rem(t + j, nt)

    def z_from(j):
        return lax.rem(t + nt - j, nt)

    def remote(src, dst, send, recv, device):
        return pltpu.make_async_remote_copy(
            src, dst, send, recv, device_id=device, device_id_type=MESH
        )

    def z_copy(name, j, src, dst, h=0):
        return remote(src, dst, sem[name + "_s"].at[h], sem[name + "_r"].at[h], (b, z_peer(j)))

    def z_all(name, ref, h=0):
        return z_copy(name, 1, ref, ref, h)

    def half(h):
        return pl.ds(h * T, T)

    def piece(h, tt):
        return pl.ds(pl.multiple_of(h * T + tt * R, R), R)

    def ag_copy(name, at, i, dst_band):
        slot = i if name == "kv" else 0
        return remote(at(b), at(b), sem[name + "_s"].at[0], sem[name + "_r"].at[slot], (dst_band, t))

    def relay_copy(name, at, i, band):
        slot = i if name == "kv" else 0
        return remote(at(band), at(band), sem[name + "_rs"].at[0], sem[name + "_rr"].at[slot], (sib, t))

    def band_same(i):
        return lax.rem(b + nb - 2 * i, nb)

    def band_sib(i):
        return lax.rem(sib + nb - 2 * i, nb)

    def ag_start(name, at):
        @pl.loop(1, s.half)
        def _(i):
            ag_copy(name, at, i, lax.rem(b + 2 * i, nb)).start()

        relay_copy(name, at, 0, b).start()

    def ag_wait(name, at, i):
        band = band_same(i)
        remote(at(band), at(band), sem[name + "_s"].at[0], sem[name + "_r"].at[i], (sib, t)).wait_recv()

    def ag_relay(name, at, i):
        relay_copy(name, at, i, band_same(i)).start()

    def ag_wait_relay(name, at, i):
        relay_copy(name, at, i, band_sib(i)).wait_recv()

    def ag_pass_on(name, at, all_at):
        ref = all_at(s.half - 1)
        remote(ref, ref, sem[name + "_s"].at[0], sem[name + "_r"].at[0], (sib, t)).wait_recv()

        @pl.loop(1, s.half)
        def _(i):
            ag_relay(name, at, i)

    def ag_arrived(name, all_at):
        ref = all_at(s.half)
        remote(ref, ref, sem[name + "_rs"].at[0], sem[name + "_rr"].at[0], (sib, t)).wait_recv()

    def ag_finish(name, all_at):
        ref = all_at(s.half - 1)
        remote(ref, ref, sem[name + "_s"].at[0], sem[name + "_r"].at[0], (sib, t)).wait_send()
        ref = all_at(s.half)
        remote(ref, ref, sem[name + "_rs"].at[0], sem[name + "_rr"].at[0], (sib, t)).wait_send()

    every = (nb, b, lambda i: i)
    near = (GROUP, lax.rem(b, GROUP), lambda i: b // GROUP * GROUP + i)
    far = (s.groups, b // GROUP, lambda i: i * GROUP + lax.rem(b, GROUP))

    def swap_copy(name, members, ref, to):
        return remote(ref, ref, sem[name + "_s"].at[0], sem[name + "_r"].at[0], (members[2](to), t))

    def swap_start(name, members):
        count, me, _ = members

        @pl.loop(1, count)
        def _(i):
            swap_copy(name, members, sem[name].at[me], lax.rem(me + i, count)).start()

    def swap_all(name, members):
        return swap_copy(name, members, sem[name].at[pl.ds(0, members[0] - 1)], 0)

    def swap_wait(name, members):
        swap_all(name, members).wait_recv()

    def swap_finish(name, members):
        swap_all(name, members).wait_send()

    def slots_sum(ref, count):
        return lax.fori_loop(
            1, count, lambda i, acc: acc + ref[i].astype(F32), ref[0].astype(F32)
        )

    def swap_sum(name):
        swap_wait(name, near)
        out = slots_sum(sem[name], GROUP)
        if s.groups > 1:
            sem[name + "2"][far[1]] = out.astype(BF16)
            swap_start(name + "2", far)
            swap_wait(name + "2", far)
            out = slots_sum(sem[name + "2"], s.groups)
            swap_finish(name + "2", far)
        swap_finish(name, near)
        return out

    def rs_start(name, h, part, recv):
        for j in range(1, nt):
            z_copy(name, j, part.at[piece(h, z_peer(j))], recv.at[h, j - 1], h).start()

    def rs_sum(name, h, part, recv):
        z_all(name, recv.at[h], h).wait_recv()
        acc = part[piece(h, t), :].astype(F32)
        for j in range(1, nt):
            acc = acc + recv[h, j - 1].astype(F32)
        return acc

    def rs_finish(name, recv):
        for h in range(2):
            z_all(name, recv.at[h], h).wait_send()

    def gather_start(name, h, ref):
        for j in range(1, nt):
            z_copy(name, j, ref.at[piece(h, t)], ref.at[piece(h, t)], h).start()

    def gather_all(name, h, ref):
        return z_all(name, ref.at[pl.ds(h * T, (nt - 1) * R)], h)

    def gather_wait(name, h, ref):
        gather_all(name, h, ref).wait_recv()

    def gather_finish(name, ref):
        for h in range(2):
            gather_all(name, h, ref).wait_send()

    quarter = lax.rem(pair, 4)
    first_pair = pair - quarter
    group = pair // 4
    low_peer = quarter + 1 - 2 * lax.rem(quarter, 2)
    high_peer = lax.rem(quarter + 2, 4)
    first = low_peer * (1 - core) + high_peer * core
    second = low_peer * core + high_peer * (1 - core)
    across = lax.rem(low_peer + 2, 4)

    def g_rows(i, q):
        hr = s.sizes[i] // 2
        qr = hr // 4
        return pl.ds(pl.multiple_of(s.bases[i] + core * hr + q * qr, 16), qr)

    def g_half(i, c):
        hr = s.sizes[i] // 2
        return pl.ds(pl.multiple_of(s.bases[i] + c * hr, 16), hr)

    def q_rows(i, q):
        qr = s.sizes[i] // 8
        return pl.ds(pl.multiple_of(q * qr, 16), qr)

    def g_copy(i, slot, src, dst, q):
        dev = ((first_pair + q) * 2 + core, t)
        return remote(src, dst, sem["gs%d" % i].at[slot], sem["gr%d" % i].at[slot], dev)

    def sib_copy(i, slot, src, dst):
        return remote(src, dst, sem["gs%d" % i].at[slot], sem["gr%d" % i].at[slot], (sib, t))

    def c1_copy(i):
        return sib_copy(i, 0, k.gsrc.at[g_half(i, 1 - core)], sem["core%d" % i])

    def rs_copies(i):
        hs = sem["core%d" % i]
        land = sem["quart%d" % i]
        return (
            g_copy(i, 1, hs.at[q_rows(i, first)], land.at[0], first),
            g_copy(i, 1, hs.at[q_rows(i, across)], land.at[1], first),
        )

    def land_all(i, slot, count):
        ref = sem["quart%d" % i].at[pl.ds(0, count)]
        return g_copy(i, slot, ref, ref, first)

    def out_all(i, slot, count):
        ref = k.gout.at[pl.ds(s.bases[i], count * (s.sizes[i] // 8))]
        return g_copy(i, slot, ref, ref, first)

    def rs_copy_b(i):
        return g_copy(i, 2, sem["core%d" % i].at[q_rows(i, second)], sem["quart%d" % i].at[2], second)

    def out_copy(i, slot, q, to):
        rows = g_rows(i, q)
        return g_copy(i, slot, k.gout.at[rows], k.gout.at[rows], to)

    def c2_copy(i, c):
        rows = g_half(i, c)
        return sib_copy(i, 3, k.gout.at[rows], k.gout.at[rows])

    def across_groups(i, acc):
        if s.groups > 1:
            ref = sem["sup%d" % i]
            ref[group] = acc.astype(BF16)

            def copy(j, at):
                dev = ((lax.rem(group + j, s.groups) * 4 + quarter) * 2 + core, t)
                return remote(at, at, sem["sup%d_s" % i].at[0], sem["sup%d_r" % i].at[0], dev)

            for j in range(1, s.groups):
                copy(j, ref.at[group]).start()
            copy(1, ref.at[pl.ds(0, s.groups - 1)]).wait()
            acc = ref[0].astype(F32)
            for g in range(1, s.groups):
                acc = acc + ref[g].astype(F32)
        return acc.astype(BF16)

    def grads1(i):
        c1_copy(i).start()

    def pair_sum(i):
        c1_copy(i).wait()
        hs = sem["core%d" % i]
        hs[...] = (k.gsrc[g_half(i, core), :].astype(F32) + hs[...].astype(F32)).astype(BF16)

    def grads2(i):
        pair_sum(i)
        for copy in rs_copies(i):
            copy.start()

    def grads3(i):
        land_all(i, 1, 2).wait()
        hs = sem["core%d" % i]
        rows = q_rows(i, second)
        hs[rows, :] = (hs[rows, :].astype(F32) + sem["quart%d" % i][1].astype(F32)).astype(BF16)
        rs_copy_b(i).start()

    def grads4(i):
        rs_copy_b(i).wait()
        land = sem["quart%d" % i]
        acc = sem["core%d" % i][q_rows(i, quarter), :].astype(F32)
        acc = acc + land[0].astype(F32) + land[2].astype(F32)
        k.gout[g_rows(i, quarter), :] = across_groups(i, acc)
        out_copy(i, 4, quarter, second).start()

    def grads5(i):
        out_copy(i, 4, quarter, second).wait_send()
        out_copy(i, 4, second, second).wait_recv()
        out_copy(i, 5, quarter, first).start()
        out_copy(i, 5, second, first).start()

    def grads6(i):
        out_all(i, 5, 2).wait()
        c2_copy(i, core).start()

    def q_peer(j):
        return lax.rem(quarter + j, 4)

    def direct2(i):
        pair_sum(i)
        for j in range(1, 4):
            src = sem["core%d" % i].at[q_rows(i, q_peer(j))]
            g_copy(i, 1, src, sem["quart%d" % i].at[j - 1], q_peer(j)).start()

    def direct3(i):
        land_all(i, 1, 3).wait()
        acc = sem["core%d" % i][q_rows(i, quarter), :].astype(F32)
        for j in range(3):
            acc = acc + sem["quart%d" % i][j].astype(F32)
        k.gout[g_rows(i, quarter), :] = across_groups(i, acc)
        for j in range(1, 4):
            out_copy(i, 2, quarter, q_peer(j)).start()

    def direct6(i):
        out_all(i, 2, 3).wait()
        c2_copy(i, core).start()

    def grads_store(i):
        rows = pl.ds(s.bases[i], s.sizes[i])
        return pltpu.make_async_copy(k.gout.at[rows], o_grads.at[rows], k.stores.at[i])

    def grads7(i):
        c2_copy(i, core).wait_send()
        c2_copy(i, 1 - core).wait_recv()
        grads_store(i).start()

    def load(i, src, dst):
        return pltpu.make_async_copy(src, dst, k.loads.at[i])

    first_loads = [
        load(0, patches, k.patches),
        load(1, leads_in, k.lead_index),
        load(2, table, k.table),
        load(3, gain1, k.gain1),
        load(4, bias1, k.bias1),
    ]
    ow_load = load(5, out_weight, k.ow.at[t])
    small_loads = [
        load(6, pixel_mask, k.pix),
        load(7, gate, k.head),
        load(8, windows_in, k.windows),
    ]
    qkv_load = load(9, qkv, k.qkv)
    late_loads = [
        load(10, gain2, k.gain2),
        load(11, bias2, k.bias2),
        load(12, up, k.up),
        load(13, down, k.down),
        load(14, cotangent, k.cot),
    ]
    for copy in first_loads + small_loads + [qkv_load, ow_load]:
        copy.start()
    barrier = pltpu.get_barrier_semaphore()

    @pl.loop(1, nb)
    def _(i):
        pl.semaphore_signal(barrier, inc=1, device_id=(lax.rem(b + i, nb), t), device_id_type=MESH)

    for j in range(1, nt):
        pl.semaphore_signal(barrier, inc=1, device_id=(b, z_peer(j)), device_id_type=MESH)

    for copy in first_loads:
        copy.wait()
    lead_hot = lax.broadcasted_iota(jnp.int32, (s.leads, L), 0) == row_of(k.lead_index)
    lead_hot = lead_hot.astype(F32).astype(BF16)
    hidden = k.patches[...] + mm_tn(lead_hot, k.table[...])
    unit1, inverse1 = norm_stats(hidden)
    k.u1[...] = unit1
    k.r1[...] = inverse1
    k.mid[...] = hidden
    k.normed[...] = (unit1 * row_of(k.gain1) + row_of(k.bias1)).astype(BF16)
    for copy in small_loads:
        copy.wait()
    compact = [k.head[e].astype(F32) for e in range(3)] + [jnp.zeros((4, D), F32)]
    k.gatec[t] = jnp.concatenate(compact, axis=0).astype(BF16)
    k.mask[t] = jnp.concatenate([k.pix[...].astype(F32), jnp.zeros((4, L), F32)], axis=0)
    part = W // 4
    upper = quarter // 2

    def ow_part(tt, c, u):
        return k.ow.at[tt, pl.ds(pl.multiple_of((c + 2 * u) * part, part), part)]

    def ow_copy(name, at, dev):
        return remote(at, at, sem[name + "_s"].at[0], sem[name + "_r"].at[0], (dev, t))

    ow_all = k.ow.at[pl.ds(0, nt - 1), pl.ds(0, part)]
    high_dev = (first_pair + high_peer) * 2 + core

    qkv_load.wait()

    def project(c):
        return mm_nt(k.qkv[c], k.normed[...])

    k.kv[b, 0:W, :] = project(1).astype(BF16)
    k.kv[b, W : 2 * W, :] = project(2).astype(BF16)
    ow_load.wait()
    pl.semaphore_wait(barrier, nb - 1 + nt - 1)

    def kv_at(band):
        return k.kv.at[band]

    ag_start("kv", kv_at)
    for j in range(1, nt):
        z_copy("zmask", j, k.mask.at[t], k.mask.at[t]).start()
        z_copy("zow", j, ow_part(t, core, upper), ow_part(t, core, upper)).start()
        z_copy("zgate", j, k.gatec.at[t], k.gatec.at[t]).start()
    for copy in late_loads:
        copy.start()
    k.qd[b, 0:W, :] = (project(0).astype(BF16).astype(F32) * SCALE).astype(BF16)

    k.ids[...] = k.windows[...].reshape(nb, L).astype(F32)

    def id_row(band):
        return k.ids[pl.ds(band, 1), :]

    def id_column(band):
        return jnp.transpose(jnp.broadcast_to(id_row(band), (128, L)))[:, 0:1]

    def head(h):
        return pl.ds(h * HEAD_DIM, HEAD_DIM)

    def value_head(h):
        return pl.ds(W + h * HEAD_DIM, HEAD_DIM)

    k.m[...] = jnp.full((8, L), MASKED, F32)
    k.l[...] = jnp.zeros((8, L), F32)
    k.acc[...] = jnp.zeros((W, L), F32)

    def forward_bands(bands):
        tiles = [(h, i) for h in range(H) for i in range(len(bands))]
        allowed = [id_column(band) == id_row(b) for band in bands]
        scores = {
            (h, i): jnp.where(
                allowed[i], mm_tn(k.kv[bands[i], head(h), :], k.qd[b, head(h), :]), MASKED
            )
            for h, i in tiles
        }
        old_high = [k.m[h : h + 1, :] for h in range(H)]
        sums = [k.l[h : h + 1, :] for h in range(H)]
        outs = [k.acc[head(h), :] for h in range(H)]
        high = list(old_high)
        for h, i in tiles:
            high[h] = jnp.maximum(high[h], jnp.max(scores[h, i], axis=0, keepdims=True))
        weights = {(h, i): jnp.exp(scores[h, i] - high[h]) for h, i in tiles}
        factor = [jnp.exp(x - y) for x, y in zip(old_high, high)]
        outs = [x * f for x, f in zip(outs, factor)]
        sums = [x * f for x, f in zip(sums, factor)]
        for h, i in tiles:
            outs[h] += mm_nn(k.kv[bands[i], value_head(h), :], weights[h, i].astype(BF16))
            sums[h] += jnp.sum(weights[h, i], axis=0, keepdims=True)
        for h in range(H):
            k.m[h : h + 1, :] = high[h]
            k.l[h : h + 1, :] = sums[h]
            k.acc[head(h), :] = outs[h]

    def ow_pass_on():
        z_all("zow", ow_all).wait_recv()
        for j in range(1, nt):
            at = ow_part(z_from(j), core, upper)
            ow_copy("zowy", at, high_dev).start()
            ow_copy("zowr", at, sib).start()

    def ow_pass_second():
        ow_copy("zowy", ow_all, high_dev).wait_recv()
        for j in range(1, nt):
            ow_copy("zowq", ow_part(z_from(j), core, 1 - upper), sib).start()

    ag_wait_relay("kv", kv_at, 0)
    forward_bands([b, sib])
    z_all("zmask", k.mask.at[pl.ds(0, nt - 1)]).wait_recv()
    k.cnt[b] = jnp.broadcast_to(total(jnp.sum(k.mask[...], axis=0)), (8, 128))
    swap_start("cnt", every)

    @pl.loop(1, s.half)
    def _(i):
        ag_wait("kv", kv_at, i)
        ag_relay("kv", kv_at, i)

    @pl.loop(0, s.half // 2 - 1)
    def _(i):
        forward_bands([band_same(2 * i + 1), band_same(2 * i + 2)])

    ag_wait_relay("kv", kv_at, 1)
    forward_bands([band_same(s.half - 1), band_sib(1)])
    ow_pass_on()

    @pl.loop(1, s.half // 2)
    def _(i):
        ag_wait_relay("kv", kv_at, 2 * i)
        ag_wait_relay("kv", kv_at, 2 * i + 1)
        forward_bands([band_sib(2 * i), band_sib(2 * i + 1)])

    for h in range(H):
        att = k.acc[head(h), :] / k.l[h : h + 1, :]
        k.acc[head(h), :] = att
        k.att[t, head(h), :] = att.astype(BF16)
        k.st[b, h : h + 1, :] = k.m[h : h + 1, :] + jnp.log(k.l[h : h + 1, :])

    def att_half(tt, h):
        return k.att.at[tt, :, half(h)]

    for h in range(2):
        for j in range(1, nt):
            z_copy("zatt", j, att_half(t, h), att_half(t, h), h).start()

    def q_at(band):
        return k.qd.at[band, pl.ds(0, W)]

    def da_at(h):
        return lambda band: k.qd.at[band, pl.ds(W, W), half(h)]

    def st_at(band):
        return k.st.at[band]

    def q_all(count):
        return k.qd.at[pl.ds(0, count), pl.ds(0, W)]

    def da_all(h):
        return lambda count: k.qd.at[pl.ds(0, count), pl.ds(W, W), half(h)]

    def st_all(count):
        return k.st.at[pl.ds(0, count)]

    ag_start("q", q_at)
    ow_pass_second()
    for copy in late_loads:
        copy.wait()
    ow_copy("zowr", ow_all, sib).wait_recv()
    ow_copy("zowq", ow_all, sib).wait_recv()

    for h in range(2):
        z_all("zatt", k.att.at[pl.ds(0, nt - 1), :, half(h)], h).wait_recv()
        rows = half(h)
        middle = k.mid[rows, :] + mm_tn(
            k.att[:, :, half(h)].reshape(nt * W, T), k.ow[...].reshape(nt * W, D)
        )
        k.mid[rows, :] = middle
        unit2, inverse2 = norm_stats(middle)
        k.u2[rows, :] = unit2
        k.r2[rows, :] = inverse2
        k.n2low[rows, :] = (unit2 * row_of(k.gain2) + row_of(k.bias2)).astype(BF16)
        upward = mm_nn(k.n2low[rows, :], k.up[...])
        k.upw[rows, :] = upward
        k.actlow[rows, :] = (0.5 * upward * (1.0 + lax.erf(upward * INV_SQRT2))).astype(BF16)
        k.ffp[rows, :] = mm_nn(k.actlow[rows, :], k.down[...]).astype(BF16)
        rs_start("zff", h, k.ffp, k.ffr)
    upward = k.upw[...]
    k.upw[...] = 0.5 * (1.0 + lax.erf(upward * INV_SQRT2)) + upward * (
        jnp.exp(-0.5 * upward * upward) * INV_SQRT_2PI
    )
    z_all("zgate", k.gatec.at[pl.ds(0, nt - 1)]).wait_recv()
    for tt in range(nt):
        x = k.gatec[tt].astype(F32)
        pad = jnp.zeros((4, D), F32)
        parts = []
        for e in range(3):
            parts += [x[4 * e : 4 * e + 4], pad]
        k.gate[tt * 32 : (tt + 1) * 32, :] = jnp.concatenate(parts + [pad, pad], axis=0).astype(BF16)
    swap_wait("cnt", every)
    pixel_count = jnp.sum(k.cnt[...], axis=0)[0:1, 0:1]
    for h in range(2):
        block_piece = k.mid[piece(h, t), :] + rs_sum("zff", h, k.ffp, k.ffr)
        k.blow[piece(h, t), :] = block_piece.astype(BF16)
        gather_start("zblk", h, k.blow)

    ag_pass_on("q", q_at, q_all)

    entropy_sum = jnp.zeros((1, 1), F32)
    for h in range(2):
        rows = half(h)
        gather_wait("zblk", h, k.blow)
        logits = mm_nt(k.gate[...], k.blow[rows, :]).reshape(nt, 4, 8, T)
        parts = [logits[:, e] for e in range(3)]
        high = jnp.maximum(jnp.maximum(parts[0], parts[1]), parts[2])
        logs = jnp.log(sum(jnp.exp(x - high) for x in parts))
        log_probs = [x - high - logs for x in parts]
        probs = [jnp.exp(x) for x in log_probs]
        entropy = -sum(p * x for p, x in zip(probs, log_probs))
        mask = k.mask[:, :, half(h)]
        entropy_sum += total(jnp.sum(mask * entropy, axis=0))
        weight = mask * (float(s.pixels) / pixel_count)[None]
        grads = [-p * (x + entropy) * weight for p, x in zip(probs, log_probs)]
        grads.append(jnp.zeros((nt, 8, T), F32))
        k.lg[:, half(h)] = jnp.stack(grads, axis=1).reshape(nt * 32, T).astype(BF16)
        out_grad = k.cot[rows, :] + mm_tn(k.lg[:, half(h)], k.gate[...])
        k.cot[rows, :] = out_grad
        k.oglow[rows, :] = out_grad.astype(BF16)
        k.ug[rows, :] = (mm_nt(k.oglow[rows, :], k.down[...]) * k.upw[rows, :]).astype(BF16)
        k.n2p[rows, :] = mm_nt(k.ug[rows, :], k.up[...]).astype(BF16)
        rs_start("zn2", h, k.n2p, k.n2r)
    block_copy = pltpu.make_async_copy(k.blow, o_block, k.stores.at[4])
    block_copy.start()
    k.gsrc[0:F, :] = mm_tn(k.actlow[...], k.oglow[...]).astype(BF16)
    grads1(0)
    k.gsrc[F : F + D, :] = mm_tn(k.n2low[...], k.ug[...]).astype(BF16)
    own_lg = k.lg[pl.ds(pl.multiple_of(t * 32, 32), 32), :]
    base = s.bases[1] + D
    k.gsrc[base : base + 32, :] = mm_nn(own_lg, k.blow[...]).astype(BF16)
    k.gsrc[base + 32 : base + 128, :] = jnp.zeros((96, D), BF16)
    grads1(1)
    k.ent[b] = jnp.broadcast_to(entropy_sum / pixel_count, (8, 128))
    swap_start("ent", every)

    def middle_backward(n2_grad, rows):
        return k.cot[rows, :] + norm_backward(n2_grad, k.u2[rows, :], k.r2[rows, :], row_of(k.gain2))

    def attended_exchange(h):
        rows = piece(h, t)
        n2_low = rs_sum("zn2", h, k.n2p, k.n2r).astype(BF16)
        k.n2g[rows, :] = n2_low
        low_piece = middle_backward(n2_low.astype(F32), rows).astype(BF16)
        for tt in range(nt):
            k.dasrc[h, tt] = mm_nt(low_piece, k.ow[tt]).astype(BF16)
        for j in range(1, nt):
            z_copy("zda", j, k.dasrc.at[h, z_peer(j)], k.datok.at[h, t], h).start()
        k.datok[h, t] = k.dasrc[h, t]

    def attended_arrived(h):
        z_all("zda", k.datok.at[h, pl.ds(0, nt - 1)], h).wait_recv()
        att_grad = jnp.transpose(k.datok[h].reshape(T, W).astype(F32)).astype(BF16)
        k.qd[b, W : 2 * W, half(h)] = att_grad
        ag_start("da%d" % h, da_at(h))
        weighted = att_grad.astype(F32) * k.acc[:, half(h)]
        for i in range(H):
            k.st[b, H + i : H + i + 1, half(h)] = jnp.sum(
                weighted[i * HEAD_DIM : (i + 1) * HEAD_DIM], axis=0, keepdims=True
            )

    grads2(0)
    attended_exchange(0)
    grads2(1)
    attended_exchange(1)
    attended_arrived(0)
    attended_arrived(1)
    ag_start("st", st_at)
    for h in range(2):
        gather_start("zn2g", h, k.n2g)
    grads3(0)
    grads3(1)
    k.dq[...] = jnp.zeros((W, L), F32)
    k.dk[...] = jnp.zeros((W, L), F32)
    k.dv[...] = jnp.zeros((W, L), F32)
    my_column = id_column(b)

    def score_grads(allowed, scores, dots, stats):
        probs = {
            (h, i): jnp.exp(jnp.where(allowed[i], x, MASKED) - stats[i][h : h + 1])
            for (h, i), x in scores.items()
        }
        grads = {
            (h, i): (x * (dots[h, i] - stats[i][H + h : H + h + 1])).astype(BF16)
            for (h, i), x in probs.items()
        }
        return probs, grads

    @pl.loop(0, s.half)
    def _(step):
        bands = [2 * step, 2 * step + 1]
        tiles = [(h, i) for h in range(H) for i in range(2)]
        allowed = [id_column(band) == id_row(b) for band in bands]
        scores = {(h, i): mm_tn(k.kv[bands[i], head(h), :], k.qd[b, head(h), :]) for h, i in tiles}
        dots = {
            (h, i): mm_tn(k.kv[bands[i], value_head(h), :], k.qd[b, value_head(h), :]) for h, i in tiles
        }
        outs = [k.dq[head(h), :] for h in range(H)]
        _, grads = score_grads(allowed, scores, dots, [k.st[b]] * 2)
        for h, i in tiles:
            outs[h] += mm_nn(k.kv[bands[i], head(h), :], grads[h, i])
        for h in range(H):
            k.dq[head(h), :] = outs[h]

    grads4(0)
    grads4(1)
    ag_arrived("q", q_all)

    def backward_bands(bands):
        tiles = [(h, i) for h in range(H) for i in range(len(bands))]
        allowed = [my_column == id_row(band) for band in bands]
        scores = {(h, i): mm_tn(k.kv[b, head(h), :], k.qd[bands[i], head(h), :]) for h, i in tiles}
        dots = {
            (h, i): mm_tn(k.kv[b, value_head(h), :], k.qd[bands[i], value_head(h), :]) for h, i in tiles
        }
        key_outs = [k.dk[head(h), :] for h in range(H)]
        value_outs = [k.dv[head(h), :] for h in range(H)]
        probs, grads = score_grads(allowed, scores, dots, [k.st[band] for band in bands])
        for h, i in tiles:
            key_outs[h] += mm_nt(k.qd[bands[i], head(h), :], grads[h, i])
            value_outs[h] += mm_nt(k.qd[bands[i], value_head(h), :], probs[h, i].astype(BF16))
        for h in range(H):
            k.dk[head(h), :] = key_outs[h]
            k.dv[head(h), :] = value_outs[h]

    for name, at, all_at in (
        ("da0", da_at(0), da_all(0)),
        ("da1", da_at(1), da_all(1)),
        ("st", st_at, st_all),
    ):
        ag_pass_on(name, at, all_at)
        ag_arrived(name, all_at)

    def backward_loop(start, stop):
        @pl.loop(start, stop)
        def _(i):
            backward_bands([band_same(i), band_sib(i)])

    backward_loop(0, s.half // 2)
    grads5(0)
    backward_loop(s.half // 2, s.half)
    grads5(1)
    k.dp[0] = (k.dq[...] * SCALE).astype(BF16)
    k.dp[1] = k.dk[...].astype(BF16)
    k.dp[2] = k.dv[...].astype(BF16)
    for h in range(2):
        k.ngp[half(h), :] = mm_tn(
            k.dp[:, :, half(h)].reshape(3 * W, T), k.qkv[...].reshape(3 * W, D)
        ).astype(BF16)
        rs_start("zng", h, k.ngp, k.ngr)
    base = s.bases[2]
    for h in range(2):
        gather_wait("zn2g", h, k.n2g)
    n2_grad = k.n2g[...].astype(F32)
    gain2_grad = jnp.sum(n2_grad * k.u2[...], axis=0, keepdims=True)
    bias2_grad = jnp.sum(n2_grad, axis=0, keepdims=True)
    middle_grad = middle_backward(n2_grad, pl.ds(0, L))
    k.cot[...] = middle_grad
    k.gsrc[base : base + W, :] = mm_nn(k.att[t], middle_grad.astype(BF16)).astype(BF16)
    k.gsrc[base + W : base + 2 * W, :] = mm_nn(k.dp[0], k.normed[...]).astype(BF16)
    grads1(2)

    base = s.bases[3]
    k.gsrc[base : base + 2 * W, :] = mm_nn(k.dp[1:3].reshape(2 * W, L), k.normed[...]).astype(BF16)
    grads1(3)
    k.ngg[piece(0, t), :] = rs_sum("zng", 0, k.ngp, k.ngr).astype(BF16)
    gather_start("zngg", 0, k.ngg)
    direct2(2)
    direct2(3)
    grads6(0)
    k.ngg[piece(1, t), :] = rs_sum("zng", 1, k.ngp, k.ngr).astype(BF16)
    gather_start("zngg", 1, k.ngg)
    grads6(1)
    direct3(2)
    direct3(3)
    grads7(0)
    grads7(1)
    swap_wait("ent", every)
    k.ent_sum[...] = jnp.sum(k.ent[...], axis=0)
    ent_copy = pltpu.make_async_copy(k.ent_sum, o_ent, k.stores.at[6])
    ent_copy.start()
    gather_wait("zngg", 0, k.ngg)
    direct6(2)
    direct6(3)
    gather_wait("zngg", 1, k.ngg)
    n1_grad = k.ngg[...].astype(F32)
    unit1 = k.u1[...]
    gain1_grad = jnp.sum(n1_grad * unit1, axis=0, keepdims=True)
    bias1_grad = jnp.sum(n1_grad, axis=0, keepdims=True)
    hidden_grad = k.cot[...] + norm_backward(n1_grad, unit1, k.r1[...], row_of(k.gain1))
    k.patches[...] = hidden_grad
    hidden_copy = pltpu.make_async_copy(k.patches, o_hidden, k.stores.at[5])
    hidden_copy.start()
    coarse = hidden_grad.astype(BF16)
    fine = (hidden_grad - coarse.astype(F32)).astype(BF16)
    tail = [
        mm_nn(lead_hot, coarse) + mm_nn(lead_hot, fine),
        gain1_grad,
        bias1_grad,
        gain2_grad,
        bias2_grad,
        jnp.zeros((s.tail - s.leads - 4, D), F32),
    ]
    k.vb[near[1]] = jnp.concatenate(tail, axis=0).astype(BF16)
    swap_start("vb", near)
    grads7(2)
    grads7(3)
    k.vb_sum[...] = swap_sum("vb")
    vb_copy = pltpu.make_async_copy(k.vb_sum, o_vb, k.stores.at[7])
    vb_copy.start()

    z_all("zmask", k.mask.at[pl.ds(0, nt - 1)]).wait_send()
    z_all("zgate", k.gatec.at[pl.ds(0, nt - 1)]).wait_send()
    z_all("zow", ow_all).wait_send()
    for name in ("zowy", "zowr", "zowq"):
        ow_copy(name, ow_all, sib).wait_send()
    for h in range(2):
        z_all("zatt", k.att.at[pl.ds(0, nt - 1), :, half(h)], h).wait_send()
        z_all("zda", k.datok.at[h, pl.ds(0, nt - 1)], h).wait_send()
    rs_finish("zff", k.ffr)
    gather_finish("zblk", k.blow)
    rs_finish("zn2", k.n2r)
    gather_finish("zn2g", k.n2g)
    rs_finish("zng", k.ngr)
    gather_finish("zngg", k.ngg)
    ag_finish("kv", lambda count: k.kv.at[pl.ds(0, count)])
    ag_finish("q", q_all)
    ag_finish("da0", da_all(0))
    ag_finish("da1", da_all(1))
    ag_finish("st", st_all)
    swap_finish("cnt", every)
    swap_finish("ent", every)
    for i in range(4):
        grads_store(i).wait()
    for copy in (block_copy, hidden_copy, ent_copy, vb_copy):
        copy.wait()


def last_kernel(
    s, cuts, block, hidden, grads, ent, vb,
    o_block, o_hidden, o_qkv, o_out, o_up, o_down, o_pen, o_lead, o_g1, o_b1, o_g2, o_b2, o_gate,
    low, wide, low_block, wide_block, keep, load_sem, store_sem,
):
    outs = {"down": o_down, "up": o_up, "out": o_out, "q": o_qkv.at[0], "k": o_qkv.at[1], "v": o_qkv.at[2]}
    loads = [
        pltpu.make_async_copy(block, low_block, load_sem.at[0]),
        pltpu.make_async_copy(hidden, keep, load_sem.at[1]),
    ]
    stores = [
        pltpu.make_async_copy(wide_block, o_block, store_sem.at[0]),
        pltpu.make_async_copy(keep, o_hidden, store_sem.at[1]),
    ]
    for i, (row, name, start, size) in enumerate(cuts):
        rows = pl.ds(row, size)
        loads.append(pltpu.make_async_copy(grads.at[rows], low.at[rows], load_sem.at[i + 2]))
        stores.append(
            pltpu.make_async_copy(wide.at[rows], outs[name].at[pl.ds(start, size)], store_sem.at[i + 2])
        )
    gate_rows = pl.ds(s.bases[1] + s.D, 32)
    gate_load = pltpu.make_async_copy(grads.at[gate_rows], low.at[gate_rows], load_sem.at[len(cuts) + 2])
    for copy in loads + [gate_load]:
        copy.start()
    loads[0].wait()
    wide_block[...] = low_block[...].astype(F32)
    stores[0].start()
    loads[1].wait()
    stores[1].start()
    for i, (row, name, start, size) in enumerate(cuts):
        loads[i + 2].wait()
        rows = pl.ds(row, size)
        wide[rows, :] = low[rows, :].astype(F32)
        stores[i + 2].start()
    gate_load.wait()
    small = low[gate_rows, :].astype(F32)
    for e in range(3):
        o_gate[e] = small[8 * e : 8 * e + 4]
    o_pen[...] = ent[0:1, 0:1]
    tail = vb[...]
    o_lead[...] = tail[0 : s.leads]
    o_g1[...] = tail[s.leads].reshape(s.D)
    o_b1[...] = tail[s.leads + 1].reshape(s.D)
    o_g2[...] = tail[s.leads + 2].reshape(s.D)
    o_b2[...] = tail[s.leads + 3].reshape(s.D)
    for copy in stores:
        copy.wait()


def local(
    nb,
    nt,
    patches,
    window_ids,
    lead_index,
    lead_table,
    attention_gain,
    attention_bias,
    query_key_value,
    out_weight,
    feedforward_gain,
    feedforward_bias,
    up_weight,
    down_weight,
    gate_head,
    pixel_mask,
    cotangent,
):
    L, D = patches.shape
    leads = lead_table.shape[0]
    W = out_weight.shape[0]
    F = up_weight.shape[1]
    s = dims_of(nb, nt, L, D, W, F, leads, L * nb * pixel_mask.shape[0] * nt)
    scratch = scratch_of(s)
    vm = pl.BlockSpec(memory_space=pltpu.VMEM)
    block, hidden, grads, ent, vb = pl.pallas_call(
        partial(main_kernel, s, tuple(scratch)),
        out_shape=(
            jax.ShapeDtypeStruct((L, D), BF16),
            jax.ShapeDtypeStruct((L, D), F32),
            jax.ShapeDtypeStruct((s.rows, D), BF16),
            jax.ShapeDtypeStruct((8, 128), F32),
            jax.ShapeDtypeStruct((s.tail, D), F32),
        ),
        in_specs=[pl.BlockSpec(memory_space=pltpu.HBM)] * 15,
        out_specs=(pl.BlockSpec(memory_space=pl.ANY),) * 5,
        scratch_shapes=list(scratch.values()),
        compiler_params=pltpu.CompilerParams(
            collective_id=0,
            has_side_effects=True,
            vmem_limit_bytes=VMEM_LIMIT,
        ),
        cost_estimate=pl.CostEstimate(
            flops=2 * s.rows * D * L * 3 + 14 * L * nb * L * W, bytes_accessed=16 * 2**20, transcendentals=0
        ),
        name="block_step",
    )(
        patches,
        window_ids,
        lead_index,
        lead_table,
        attention_gain,
        attention_bias,
        jnp.transpose(query_key_value, (0, 2, 1)),
        out_weight,
        feedforward_gain,
        feedforward_bias,
        up_weight,
        down_weight,
        gate_head,
        pixel_mask,
        cotangent,
    )
    vec = jax.ShapeDtypeStruct((D,), F32)
    cuts = []
    first = s.bases[2]
    places = (
        ("down", 0, F),
        ("up", F, D),
        ("out", first, W),
        ("q", first + W, W),
        ("k", s.bases[3], W),
        ("v", s.bases[3] + W, W),
    )
    for name, row, size in places:
        for start in range(0, size, 256):
            cuts.append((row + start, name, start, min(256, size - start)))
    hbm = pl.BlockSpec(memory_space=pl.ANY)
    wide, high, qkv_grad, out_grad, up_grad, down_grad, pen, lead, g1, b1, g2, b2, gates = pl.pallas_call(
        partial(last_kernel, s, cuts),
        out_shape=(
            jax.ShapeDtypeStruct((L, D), F32),
            jax.ShapeDtypeStruct((L, D), F32),
            jax.ShapeDtypeStruct((3, W, D), F32),
            jax.ShapeDtypeStruct((W, D), F32),
            jax.ShapeDtypeStruct((D, F), F32),
            jax.ShapeDtypeStruct((F, D), F32),
            jax.ShapeDtypeStruct((1, 1), F32),
            jax.ShapeDtypeStruct((leads, D), F32),
            vec,
            vec,
            vec,
            vec,
            jax.ShapeDtypeStruct(gate_head.shape, F32),
        ),
        in_specs=[hbm] * 3 + [vm] * 2,
        out_specs=(hbm,) * 6 + (vm,) * 7,
        scratch_shapes=[
            pltpu.VMEM((s.rows, D), BF16),
            pltpu.VMEM((s.rows, D), F32),
            pltpu.VMEM((L, D), BF16),
            pltpu.VMEM((L, D), F32),
            pltpu.VMEM((L, D), F32),
            pltpu.SemaphoreType.DMA((len(cuts) + 3,)),
            pltpu.SemaphoreType.DMA((len(cuts) + 2,)),
        ],
        compiler_params=pltpu.CompilerParams(vmem_limit_bytes=VMEM_LIMIT),
        name="write_out",
    )(block, hidden, grads, ent, vb)
    return (
        wide,
        pen.reshape(()),
        high,
        lead,
        g1,
        b1,
        jnp.transpose(qkv_grad, (0, 2, 1)),
        out_grad,
        g2,
        b2,
        up_grad,
        down_grad,
        gates,
    )


def solution(mesh):
    in_specs = (
        P("blk", None),
        P(),
        P("blk"),
        P(),
        P(),
        P(),
        P(None, None, "tp"),
        P("tp", None),
        P(),
        P(),
        P(None, "tp"),
        P("tp", None),
        P(None, "tp", None),
        P("tp", "blk"),
        P("blk", None),
    )
    out_specs = (
        P("blk", None),
        P(),
        P("blk", None),
        P(),
        P(),
        P(),
        P(None, None, "tp"),
        P("tp", None),
        P(),
        P(),
        P(None, "tp"),
        P("tp", None),
        P(None, "tp", None),
    )
    return jax.shard_map(
        partial(local, mesh.shape["blk"], mesh.shape["tp"]),
        mesh=mesh,
        in_specs=in_specs,
        out_specs=out_specs,
        check_vma=False,
    )
```

```python
from functools import partial
from types import SimpleNamespace

import jax
import jax.numpy as jnp
from jax import lax
from jax.experimental import pallas as pl
from jax.experimental.pallas import tpu as pltpu
from jax.sharding import PartitionSpec as P

HEAD_DIM = 64
EPS = 1e-05
MASKED = -1e30
SCALE = HEAD_DIM ** (-0.5)
GROUP = 8
F32 = jnp.float32
BF16 = jnp.bfloat16
MESH = pl.DeviceIdType.MESH
VMEM_LIMIT = 61 * 2**20
INV_SQRT2 = 0.7071067811865476
INV_SQRT_2PI = 0.3989422804014327


def dot(a, b, ca, cb):
    return lax.dot_general(a, b, (((ca,), (cb,)), ((), ())), preferred_element_type=F32)


def mm_nn(a, b):
    return dot(a, b, 1, 0)


def mm_nt(a, b):
    return dot(a, b, 1, 1)


def mm_tn(a, b):
    return dot(a, b, 0, 0)


def norm_stats(values):
    mean = jnp.mean(values, axis=-1, keepdims=True)
    centered = values - mean
    inverse = lax.rsqrt(jnp.mean(centered * centered, axis=-1, keepdims=True) + EPS)
    return centered * inverse, inverse


def norm_backward(incoming, unit_rows, inverse, gain):
    scaled = incoming * gain
    return inverse * (
        scaled
        - jnp.mean(scaled, axis=-1, keepdims=True)
        - unit_rows * jnp.mean(scaled * unit_rows, axis=-1, keepdims=True)
    )


def row_of(ref):
    return ref[...].reshape(1, ref.shape[0])


def total(x):
    return jnp.sum(jnp.sum(x, axis=0, keepdims=True), axis=1, keepdims=True)


def dims_of(nb, nt, tokens, width, local_width, hidden, leads, pixels):
    s = SimpleNamespace(nb=nb, nt=nt, L=tokens, D=width, W=local_width, F=hidden, leads=leads)
    s.H = local_width // HEAD_DIM
    s.T = tokens // 2
    s.R = s.T // nt
    s.half = nb // 2
    s.groups = nb // GROUP
    s.pixels = pixels
    s.sizes = (hidden, width + 128, local_width * 2, local_width * 2)
    s.bases = tuple(sum(s.sizes[:i]) for i in range(4))
    s.rows = sum(s.sizes)
    s.packed = (4 * width // 128 + 15) // 16 * 16
    return s


def scratch_of(s):
    L, D, W, F, nb, nt, R = s.L, s.D, s.W, s.F, s.nb, s.nt, s.R
    v = pltpu.VMEM
    out = {
        "patches": v((L, D), F32),
        "windows": v((nb * L,), jnp.int32),
        "lead_index": v((L,), jnp.int32),
        "table": v((s.leads, D), BF16),
        "gain1": v((D,), F32),
        "bias1": v((D,), F32),
        "gain2": v((D,), F32),
        "bias2": v((D,), F32),
        "pix": v((4, L), jnp.int32),
        "head": v((3, 4, D), BF16),
        "ids": v((nb, L), F32),
        "qkv": v((3, W, D), BF16),
        "ow": v((nt, W, D), BF16),
        "up": v((D, F), BF16),
        "down": v((F, D), BF16),
        "cot": v((L, D), F32),
        "gatec": v((nt, 16, D), BF16),
        "gate": v((nt * 32, D), BF16),
        "mask": v((nt, 8, L), F32),
        "cnt": v((nb, 8, 128), F32),
        "u1": v((L, D), F32),
        "r1": v((L, 1), F32),
        "normed": v((L, D), BF16),
        "kv": v((nb, 2 * W, L), BF16),
        "qd": v((nb, 2 * W, L), BF16),
        "st": v((nb, 8, L), F32),
        "m": v((8, L), F32),
        "l": v((8, L), F32),
        "acc": v((W, L), F32),
        "att": v((nt, W, L), BF16),
        "mid": v((L, D), F32),
        "u2": v((L, D), F32),
        "r2": v((L, 1), F32),
        "n2low": v((L, D), BF16),
        "upw": v((L, F), F32),
        "actlow": v((L, F), BF16),
        "ffp": v((L, D), BF16),
        "ffr": v((2, nt - 1, R, D), BF16),
        "blow": v((L, D), BF16),
        "lg": v((nt * 32, L), BF16),
        "oglow": v((L, D), BF16),
        "ug": v((L, F), BF16),
        "n2p": v((L, D), BF16),
        "n2r": v((2, nt - 1, R, D), BF16),
        "n2g": v((L, D), BF16),
        "dasrc": v((2, nt, R, W), BF16),
        "datok": v((2, nt, R, W), BF16),
        "dq": v((W, L), F32),
        "dk": v((W, L), F32),
        "dv": v((W, L), F32),
        "dp": v((3, W, L), BF16),
        "ngp": v((L, D), BF16),
        "ngr": v((2, nt - 1, R, D), BF16),
        "ngg": v((L, D), BF16),
        "vb": v((GROUP, s.leads, D), BF16),
        "vc": v((GROUP, s.packed, 128), BF16),
        "ent": v((nb, 8, 128), F32),
        "ent_sum": v((8, 128), F32),
        "vb_sum": v((s.leads, D), F32),
        "vc_sum": v((s.packed, 128), F32),
        "gsrc": v((s.rows, D), BF16),
        "gout": v((s.rows, D), BF16),
    }
    dma = pltpu.SemaphoreType.DMA
    out["loads"] = dma((15,))
    out["stores"] = dma((9,))
    for name in ("zmask", "zgate", "zow", "zowy", "zowr", "zowq"):
        out[name + "_s"] = dma((1,))
        out[name + "_r"] = dma((1,))
    for name in ("zatt", "zff", "zblk", "zn2", "zn2g", "zda", "zng", "zngg"):
        out[name + "_s"] = dma((2,))
        out[name + "_r"] = dma((2,))
    for name in ("kv", "q", "da0", "da1", "st"):
        count = s.half if name == "kv" else 2
        out[name + "_s"] = dma((1,))
        out[name + "_r"] = dma((count,))
        out[name + "_rs"] = dma((1,))
        out[name + "_rr"] = dma((count,))
    for name in ("cnt", "ent", "vb", "vc"):
        out[name + "_s"] = dma((1,))
        out[name + "_r"] = dma((1,))
    if s.groups > 1:
        out["vb2"] = v((s.groups, s.leads, D), BF16)
        out["vc2"] = v((s.groups, s.packed, 128), BF16)
        for name in ("vb2", "vc2"):
            out[name + "_s"] = dma((1,))
            out[name + "_r"] = dma((1,))
    for i, rows in enumerate(s.sizes):
        hr = rows // 2
        qr = hr // 4
        out["core%d" % i] = v((hr, D), BF16)
        out["quart%d" % i] = v((3, qr, D), BF16)
        if s.groups > 1:
            out["sup%d" % i] = v((s.groups, qr, D), BF16)
            out["sup%d_s" % i] = dma((1,))
            out["sup%d_r" % i] = dma((1,))
        out["gs%d" % i] = dma((6 if i < 2 else 4,))
        out["gr%d" % i] = dma((6 if i < 2 else 4,))
    return out


def main_kernel(s, names, *refs):
    (
        patches,
        windows_in,
        leads_in,
        table,
        gain1,
        bias1,
        qkv,
        out_weight,
        gain2,
        bias2,
        up,
        down,
        gate,
        pixel_mask,
        cotangent,
        o_block,
        o_hidden,
        o_grads,
        o_ent,
        o_vb,
        o_vc,
    ) = refs[:21]
    k = SimpleNamespace(**dict(zip(names, refs[21:])))
    sem = vars(k)
    L, D, W, F, H, T, R, nb, nt = s.L, s.D, s.W, s.F, s.H, s.T, s.R, s.nb, s.nt
    b = lax.axis_index("blk")
    t = lax.axis_index("tp")
    core = lax.rem(b, 2)
    pair = b // 2
    sib = b + 1 - 2 * core

    def z_peer(j):
        return lax.rem(t + j, nt)

    def z_from(j):
        return lax.rem(t + nt - j, nt)

    def remote(src, dst, send, recv, device):
        return pltpu.make_async_remote_copy(
            src, dst, send, recv, device_id=device, device_id_type=MESH
        )

    def z_copy(name, j, src, dst, h=0):
        return remote(src, dst, sem[name + "_s"].at[h], sem[name + "_r"].at[h], (b, z_peer(j)))

    def z_all(name, ref, h=0):
        return z_copy(name, 1, ref, ref, h)

    def half(h):
        return pl.ds(h * T, T)

    def piece(h, tt):
        return pl.ds(pl.multiple_of(h * T + tt * R, R), R)

    def ag_copy(name, at, i, dst_band):
        slot = i if name == "kv" else 0
        return remote(at(b), at(b), sem[name + "_s"].at[0], sem[name + "_r"].at[slot], (dst_band, t))

    def relay_copy(name, at, i, band):
        slot = i if name == "kv" or isinstance(i, int) else 1
        return remote(at(band), at(band), sem[name + "_rs"].at[0], sem[name + "_rr"].at[slot], (sib, t))

    def band_same(i):
        return lax.rem(b + nb - 2 * i, nb)

    def band_sib(i):
        return lax.rem(sib + nb - 2 * i, nb)

    def ag_start(name, at):
        @pl.loop(1, s.half)
        def _(i):
            ag_copy(name, at, i, lax.rem(b + 2 * i, nb)).start()

        relay_copy(name, at, 0, b).start()

    def ag_wait(name, at, i):
        band = band_same(i)
        remote(at(band), at(band), sem[name + "_s"].at[0], sem[name + "_r"].at[i], (sib, t)).wait_recv()

    def ag_relay(name, at, i):
        relay_copy(name, at, i, band_same(i)).start()

    def ag_wait_relay(name, at, i):
        relay_copy(name, at, i, band_sib(i)).wait_recv()

    def ag_pass_on(name, at, all_at):
        ref = all_at(s.half - 1)
        remote(ref, ref, sem[name + "_s"].at[0], sem[name + "_r"].at[0], (sib, t)).wait_recv()

        @pl.loop(1, s.half)
        def _(i):
            ag_relay(name, at, i)

    def ag_arrived(name, all_at):
        ref = all_at(s.half - 1)
        remote(ref, ref, sem[name + "_rs"].at[0], sem[name + "_rr"].at[1], (sib, t)).wait_recv()

    def ag_finish(name, all_at):
        ref = all_at(s.half - 1)
        remote(ref, ref, sem[name + "_s"].at[0], sem[name + "_r"].at[0], (sib, t)).wait_send()
        ref = all_at(s.half)
        remote(ref, ref, sem[name + "_rs"].at[0], sem[name + "_rr"].at[0], (sib, t)).wait_send()

    every = (nb, b, lambda i: i)
    near = (GROUP, lax.rem(b, GROUP), lambda i: b // GROUP * GROUP + i)
    far = (s.groups, b // GROUP, lambda i: i * GROUP + lax.rem(b, GROUP))

    def swap_copy(name, members, ref, to):
        return remote(ref, ref, sem[name + "_s"].at[0], sem[name + "_r"].at[0], (members[2](to), t))

    def swap_start(name, members):
        count, me, _ = members

        @pl.loop(1, count)
        def _(i):
            swap_copy(name, members, sem[name].at[me], lax.rem(me + i, count)).start()

    def swap_all(name, members):
        return swap_copy(name, members, sem[name].at[pl.ds(0, members[0] - 1)], 0)

    def swap_wait(name, members):
        swap_all(name, members).wait_recv()

    def swap_finish(name, members):
        swap_all(name, members).wait_send()

    def slots_sum(ref, count):
        return lax.fori_loop(
            1, count, lambda i, acc: acc + ref[i].astype(F32), ref[0].astype(F32)
        )

    def swap_sum(name):
        swap_wait(name, near)
        out = slots_sum(sem[name], GROUP)
        if s.groups > 1:
            sem[name + "2"][far[1]] = out.astype(BF16)
            swap_start(name + "2", far)
            swap_wait(name + "2", far)
            out = slots_sum(sem[name + "2"], s.groups)
            swap_finish(name + "2", far)
        swap_finish(name, near)
        return out

    def rs_start(name, h, part, recv):
        for j in range(1, nt):
            z_copy(name, j, part.at[piece(h, z_peer(j))], recv.at[h, j - 1], h).start()

    def rs_sum(name, h, part, recv):
        z_all(name, recv.at[h], h).wait_recv()
        acc = part[piece(h, t), :].astype(F32)
        for j in range(1, nt):
            acc = acc + recv[h, j - 1].astype(F32)
        return acc

    def rs_finish(name, recv):
        for h in range(2):
            z_all(name, recv.at[h], h).wait_send()

    def gather_start(name, h, ref):
        for j in range(1, nt):
            z_copy(name, j, ref.at[piece(h, t)], ref.at[piece(h, t)], h).start()

    def gather_all(name, h, ref):
        return z_all(name, ref.at[pl.ds(h * T, (nt - 1) * R)], h)

    def gather_wait(name, h, ref):
        gather_all(name, h, ref).wait_recv()

    def gather_finish(name, ref):
        for h in range(2):
            gather_all(name, h, ref).wait_send()

    quarter = lax.rem(pair, 4)
    first_pair = pair - quarter
    group = pair // 4
    low_peer = quarter + 1 - 2 * lax.rem(quarter, 2)
    high_peer = lax.rem(quarter + 2, 4)
    first = low_peer * (1 - core) + high_peer * core
    second = low_peer * core + high_peer * (1 - core)
    across = lax.rem(low_peer + 2, 4)

    def g_rows(i, q):
        hr = s.sizes[i] // 2
        qr = hr // 4
        return pl.ds(pl.multiple_of(s.bases[i] + core * hr + q * qr, 16), qr)

    def g_half(i, c):
        hr = s.sizes[i] // 2
        return pl.ds(pl.multiple_of(s.bases[i] + c * hr, 16), hr)

    def q_rows(i, q):
        qr = s.sizes[i] // 8
        return pl.ds(pl.multiple_of(q * qr, 16), qr)

    def g_copy(i, slot, src, dst, q):
        dev = ((first_pair + q) * 2 + core, t)
        return remote(src, dst, sem["gs%d" % i].at[slot], sem["gr%d" % i].at[slot], dev)

    def sib_copy(i, slot, src, dst):
        return remote(src, dst, sem["gs%d" % i].at[slot], sem["gr%d" % i].at[slot], (sib, t))

    def c1_copy(i):
        return sib_copy(i, 0, k.gsrc.at[g_half(i, 1 - core)], sem["core%d" % i])

    def rs_copies(i):
        hs = sem["core%d" % i]
        land = sem["quart%d" % i]
        return (
            g_copy(i, 1, hs.at[q_rows(i, first)], land.at[0], first),
            g_copy(i, 1, hs.at[q_rows(i, across)], land.at[1], first),
        )

    def land_all(i, slot, count):
        ref = sem["quart%d" % i].at[pl.ds(0, count)]
        return g_copy(i, slot, ref, ref, first)

    def out_all(i, slot, count):
        ref = k.gout.at[pl.ds(s.bases[i], count * (s.sizes[i] // 8))]
        return g_copy(i, slot, ref, ref, first)

    def rs_copy_b(i):
        return g_copy(i, 2, sem["core%d" % i].at[q_rows(i, second)], sem["quart%d" % i].at[2], second)

    def out_copy(i, slot, q, to):
        rows = g_rows(i, q)
        return g_copy(i, slot, k.gout.at[rows], k.gout.at[rows], to)

    def c2_copy(i, c):
        rows = g_half(i, c)
        return sib_copy(i, 3, k.gout.at[rows], k.gout.at[rows])

    def across_groups(i, acc):
        if s.groups > 1:
            ref = sem["sup%d" % i]
            ref[group] = acc.astype(BF16)

            def copy(j, at):
                dev = ((lax.rem(group + j, s.groups) * 4 + quarter) * 2 + core, t)
                return remote(at, at, sem["sup%d_s" % i].at[0], sem["sup%d_r" % i].at[0], dev)

            for j in range(1, s.groups):
                copy(j, ref.at[group]).start()
            copy(1, ref.at[pl.ds(0, s.groups - 1)]).wait()
            acc = ref[0].astype(F32)
            for g in range(1, s.groups):
                acc = acc + ref[g].astype(F32)
        return acc.astype(BF16)

    def grads1(i):
        c1_copy(i).start()

    def pair_sum(i):
        c1_copy(i).wait()
        hs = sem["core%d" % i]
        hs[...] = (k.gsrc[g_half(i, core), :].astype(F32) + hs[...].astype(F32)).astype(BF16)

    def grads2(i):
        pair_sum(i)
        for copy in rs_copies(i):
            copy.start()

    def grads3(i):
        land_all(i, 1, 2).wait()
        hs = sem["core%d" % i]
        rows = q_rows(i, second)
        hs[rows, :] = (hs[rows, :].astype(F32) + sem["quart%d" % i][1].astype(F32)).astype(BF16)
        rs_copy_b(i).start()

    def grads4(i):
        rs_copy_b(i).wait()
        land = sem["quart%d" % i]
        acc = sem["core%d" % i][q_rows(i, quarter), :].astype(F32)
        acc = acc + land[0].astype(F32) + land[2].astype(F32)
        k.gout[g_rows(i, quarter), :] = across_groups(i, acc)
        out_copy(i, 4, quarter, second).start()

    def grads5(i):
        out_copy(i, 4, quarter, second).wait_send()
        out_copy(i, 4, second, second).wait_recv()
        out_copy(i, 5, quarter, first).start()
        out_copy(i, 5, second, first).start()

    def grads6(i):
        out_all(i, 5, 2).wait()
        c2_copy(i, core).start()

    def q_peer(j):
        return lax.rem(quarter + j, 4)

    def direct2(i):
        pair_sum(i)
        for j in range(1, 4):
            src = sem["core%d" % i].at[q_rows(i, q_peer(j))]
            g_copy(i, 1, src, sem["quart%d" % i].at[j - 1], q_peer(j)).start()

    def direct3(i):
        land_all(i, 1, 3).wait()
        acc = sem["core%d" % i][q_rows(i, quarter), :].astype(F32)
        for j in range(3):
            acc = acc + sem["quart%d" % i][j].astype(F32)
        k.gout[g_rows(i, quarter), :] = across_groups(i, acc)
        for j in range(1, 4):
            out_copy(i, 2, quarter, q_peer(j)).start()

    def direct6(i):
        out_all(i, 2, 3).wait()
        c2_copy(i, core).start()

    def grads_store(i):
        rows = pl.ds(s.bases[i], s.sizes[i])
        return pltpu.make_async_copy(k.gout.at[rows], o_grads.at[rows], k.stores.at[i])

    def grads7(i):
        c2_copy(i, core).wait_send()
        c2_copy(i, 1 - core).wait_recv()
        grads_store(i).start()

    def load(i, src, dst):
        return pltpu.make_async_copy(src, dst, k.loads.at[i])

    first_loads = [
        load(0, patches, k.patches),
        load(1, leads_in, k.lead_index),
        load(2, table, k.table),
        load(3, gain1, k.gain1),
        load(4, bias1, k.bias1),
    ]
    ow_load = load(5, out_weight, k.ow.at[t])
    small_loads = [
        load(6, pixel_mask, k.pix),
        load(7, gate, k.head),
        load(8, windows_in, k.windows),
    ]
    qkv_load = load(9, qkv, k.qkv)
    late_loads = [
        load(10, gain2, k.gain2),
        load(11, bias2, k.bias2),
        load(12, up, k.up),
        load(13, down, k.down),
        load(14, cotangent, k.cot),
    ]
    for copy in first_loads + small_loads + [qkv_load, ow_load]:
        copy.start()
    barrier = pltpu.get_barrier_semaphore()

    @pl.loop(1, nb)
    def _(i):
        pl.semaphore_signal(barrier, inc=1, device_id=(lax.rem(b + i, nb), t), device_id_type=MESH)

    for j in range(1, nt):
        pl.semaphore_signal(barrier, inc=1, device_id=(b, z_peer(j)), device_id_type=MESH)

    for copy in first_loads:
        copy.wait()
    lead_hot = lax.broadcasted_iota(jnp.int32, (s.leads, L), 0) == row_of(k.lead_index)
    lead_hot = lead_hot.astype(F32).astype(BF16)
    hidden = k.patches[...] + mm_tn(lead_hot, k.table[...])
    unit1, inverse1 = norm_stats(hidden)
    k.u1[...] = unit1
    k.r1[...] = inverse1
    k.mid[...] = hidden
    k.normed[...] = (unit1 * row_of(k.gain1) + row_of(k.bias1)).astype(BF16)
    for copy in small_loads:
        copy.wait()
    compact = [k.head[e].astype(F32) for e in range(3)] + [jnp.zeros((4, D), F32)]
    k.gatec[t] = jnp.concatenate(compact, axis=0).astype(BF16)
    k.mask[t] = jnp.concatenate([k.pix[...].astype(F32), jnp.zeros((4, L), F32)], axis=0)
    part = W // 4
    upper = quarter // 2

    def ow_part(tt, c, u):
        return k.ow.at[tt, pl.ds(pl.multiple_of((c + 2 * u) * part, part), part)]

    def ow_copy(name, at, dev):
        return remote(at, at, sem[name + "_s"].at[0], sem[name + "_r"].at[0], (dev, t))

    ow_all = k.ow.at[pl.ds(0, nt - 1), pl.ds(0, part)]
    high_dev = (first_pair + high_peer) * 2 + core

    qkv_load.wait()

    def project(c):
        return mm_nt(k.qkv[c], k.normed[...])

    k.kv[b, 0:W, :] = project(1).astype(BF16)
    k.kv[b, W : 2 * W, :] = project(2).astype(BF16)
    ow_load.wait()
    pl.semaphore_wait(barrier, nb - 1 + nt - 1)

    def kv_at(band):
        return k.kv.at[band]

    ag_start("kv", kv_at)
    for j in range(1, nt):
        z_copy("zmask", j, k.mask.at[t], k.mask.at[t]).start()
        z_copy("zow", j, ow_part(t, core, upper), ow_part(t, core, upper)).start()
        z_copy("zgate", j, k.gatec.at[t], k.gatec.at[t]).start()
    for copy in late_loads:
        copy.start()
    k.qd[b, 0:W, :] = (project(0).astype(BF16).astype(F32) * SCALE).astype(BF16)

    k.ids[...] = k.windows[...].reshape(nb, L).astype(F32)

    def id_row(band):
        return k.ids[pl.ds(band, 1), :]

    def id_column(band):
        return jnp.transpose(jnp.broadcast_to(id_row(band), (128, L)))[:, 0:1]

    def head(h):
        return pl.ds(h * HEAD_DIM, HEAD_DIM)

    def value_head(h):
        return pl.ds(W + h * HEAD_DIM, HEAD_DIM)

    k.m[...] = jnp.full((8, L), MASKED, F32)
    k.l[...] = jnp.zeros((8, L), F32)
    k.acc[...] = jnp.zeros((W, L), F32)

    def forward_bands(bands):
        tiles = [(h, i) for h in range(H) for i in range(len(bands))]
        allowed = [id_column(band) == id_row(b) for band in bands]
        scores = {
            (h, i): jnp.where(
                allowed[i], mm_tn(k.kv[bands[i], head(h), :], k.qd[b, head(h), :]), MASKED
            )
            for h, i in tiles
        }
        old_high = [k.m[h : h + 1, :] for h in range(H)]
        sums = [k.l[h : h + 1, :] for h in range(H)]
        outs = [k.acc[head(h), :] for h in range(H)]
        high = list(old_high)
        for h, i in tiles:
            high[h] = jnp.maximum(high[h], jnp.max(scores[h, i], axis=0, keepdims=True))
        weights = {(h, i): jnp.exp(scores[h, i] - high[h]) for h, i in tiles}
        factor = [jnp.exp(x - y) for x, y in zip(old_high, high)]
        outs = [x * f for x, f in zip(outs, factor)]
        sums = [x * f for x, f in zip(sums, factor)]
        for h, i in tiles:
            outs[h] += mm_nn(k.kv[bands[i], value_head(h), :], weights[h, i].astype(BF16))
            sums[h] += jnp.sum(weights[h, i], axis=0, keepdims=True)
        for h in range(H):
            k.m[h : h + 1, :] = high[h]
            k.l[h : h + 1, :] = sums[h]
            k.acc[head(h), :] = outs[h]

    def ow_pass_on():
        z_all("zow", ow_all).wait_recv()
        for j in range(1, nt):
            at = ow_part(z_from(j), core, upper)
            ow_copy("zowy", at, high_dev).start()
            ow_copy("zowr", at, sib).start()

    def ow_pass_second():
        ow_copy("zowy", ow_all, high_dev).wait_recv()
        for j in range(1, nt):
            ow_copy("zowq", ow_part(z_from(j), core, 1 - upper), sib).start()

    ag_wait_relay("kv", kv_at, 0)
    forward_bands([b, sib])
    z_all("zmask", k.mask.at[pl.ds(0, nt - 1)]).wait_recv()
    k.cnt[b] = jnp.broadcast_to(total(jnp.sum(k.mask[...], axis=0)), (8, 128))
    swap_start("cnt", every)

    @pl.loop(1, s.half)
    def _(i):
        ag_wait("kv", kv_at, i)
        ag_relay("kv", kv_at, i)

    @pl.loop(0, s.half // 2 - 1)
    def _(i):
        forward_bands([band_same(2 * i + 1), band_same(2 * i + 2)])

    ag_wait_relay("kv", kv_at, 1)
    forward_bands([band_same(s.half - 1), band_sib(1)])
    ow_pass_on()

    @pl.loop(1, s.half // 2)
    def _(i):
        ag_wait_relay("kv", kv_at, 2 * i)
        ag_wait_relay("kv", kv_at, 2 * i + 1)
        forward_bands([band_sib(2 * i), band_sib(2 * i + 1)])

    for h in range(H):
        att = k.acc[head(h), :] / k.l[h : h + 1, :]
        k.acc[head(h), :] = att
        k.att[t, head(h), :] = att.astype(BF16)
        k.st[b, h : h + 1, :] = k.m[h : h + 1, :] + jnp.log(k.l[h : h + 1, :])

    def att_half(tt, h):
        return k.att.at[tt, :, half(h)]

    for h in range(2):
        for j in range(1, nt):
            z_copy("zatt", j, att_half(t, h), att_half(t, h), h).start()

    def q_at(band):
        return k.qd.at[band, pl.ds(0, W)]

    def da_at(h):
        return lambda band: k.qd.at[band, pl.ds(W, W), half(h)]

    def st_at(band):
        return k.st.at[band]

    def q_all(count):
        return k.qd.at[pl.ds(0, count), pl.ds(0, W)]

    def da_all(h):
        return lambda count: k.qd.at[pl.ds(0, count), pl.ds(W, W), half(h)]

    def st_all(count):
        return k.st.at[pl.ds(0, count)]

    ag_start("q", q_at)
    ow_pass_second()
    for copy in late_loads:
        copy.wait()
    ow_copy("zowr", ow_all, sib).wait_recv()
    ow_copy("zowq", ow_all, sib).wait_recv()

    for h in range(2):
        z_all("zatt", k.att.at[pl.ds(0, nt - 1), :, half(h)], h).wait_recv()
        rows = half(h)
        middle = k.mid[rows, :] + mm_tn(
            k.att[:, :, half(h)].reshape(nt * W, T), k.ow[...].reshape(nt * W, D)
        )
        k.mid[rows, :] = middle
        unit2, inverse2 = norm_stats(middle)
        k.u2[rows, :] = unit2
        k.r2[rows, :] = inverse2
        k.n2low[rows, :] = (unit2 * row_of(k.gain2) + row_of(k.bias2)).astype(BF16)
        upward = mm_nn(k.n2low[rows, :], k.up[...])
        k.upw[rows, :] = upward
        k.actlow[rows, :] = (0.5 * upward * (1.0 + lax.erf(upward * INV_SQRT2))).astype(BF16)
        k.ffp[rows, :] = mm_nn(k.actlow[rows, :], k.down[...]).astype(BF16)
        rs_start("zff", h, k.ffp, k.ffr)
    upward = k.upw[...]
    k.upw[...] = 0.5 * (1.0 + lax.erf(upward * INV_SQRT2)) + upward * (
        jnp.exp(-0.5 * upward * upward) * INV_SQRT_2PI
    )
    z_all("zgate", k.gatec.at[pl.ds(0, nt - 1)]).wait_recv()
    for tt in range(nt):
        x = k.gatec[tt].astype(F32)
        pad = jnp.zeros((4, D), F32)
        parts = []
        for e in range(3):
            parts += [x[4 * e : 4 * e + 4], pad]
        k.gate[tt * 32 : (tt + 1) * 32, :] = jnp.concatenate(parts + [pad, pad], axis=0).astype(BF16)
    swap_wait("cnt", every)
    pixel_count = jnp.sum(k.cnt[...], axis=0)[0:1, 0:1]
    for h in range(2):
        block_piece = k.mid[piece(h, t), :] + rs_sum("zff", h, k.ffp, k.ffr)
        k.blow[piece(h, t), :] = block_piece.astype(BF16)
        gather_start("zblk", h, k.blow)

    ag_pass_on("q", q_at, q_all)

    entropy_sum = jnp.zeros((1, 1), F32)
    for h in range(2):
        rows = half(h)
        gather_wait("zblk", h, k.blow)
        logits = mm_nt(k.gate[...], k.blow[rows, :]).reshape(nt, 4, 8, T)
        parts = [logits[:, e] for e in range(3)]
        high = jnp.maximum(jnp.maximum(parts[0], parts[1]), parts[2])
        logs = jnp.log(sum(jnp.exp(x - high) for x in parts))
        log_probs = [x - high - logs for x in parts]
        probs = [jnp.exp(x) for x in log_probs]
        entropy = -sum(p * x for p, x in zip(probs, log_probs))
        mask = k.mask[:, :, half(h)]
        entropy_sum += total(jnp.sum(mask * entropy, axis=0))
        weight = mask * (float(s.pixels) / pixel_count)[None]
        grads = [-p * (x + entropy) * weight for p, x in zip(probs, log_probs)]
        grads.append(jnp.zeros((nt, 8, T), F32))
        k.lg[:, half(h)] = jnp.stack(grads, axis=1).reshape(nt * 32, T).astype(BF16)
        out_grad = k.cot[rows, :] + mm_tn(k.lg[:, half(h)], k.gate[...])
        k.cot[rows, :] = out_grad
        k.oglow[rows, :] = out_grad.astype(BF16)
        k.ug[rows, :] = (mm_nt(k.oglow[rows, :], k.down[...]) * k.upw[rows, :]).astype(BF16)
        k.n2p[rows, :] = mm_nt(k.ug[rows, :], k.up[...]).astype(BF16)
        rs_start("zn2", h, k.n2p, k.n2r)
    block_copy = pltpu.make_async_copy(k.blow, o_block, k.stores.at[4])
    block_copy.start()
    k.gsrc[0:F, :] = mm_tn(k.actlow[...], k.oglow[...]).astype(BF16)
    grads1(0)
    k.gsrc[F : F + D, :] = mm_tn(k.n2low[...], k.ug[...]).astype(BF16)
    own_lg = k.lg[pl.ds(pl.multiple_of(t * 32, 32), 32), :]
    base = s.bases[1] + D
    k.gsrc[base : base + 32, :] = mm_nn(own_lg, k.blow[...]).astype(BF16)
    k.gsrc[base + 32 : base + 128, :] = jnp.zeros((96, D), BF16)
    grads1(1)
    k.ent[b] = jnp.broadcast_to(entropy_sum / pixel_count, (8, 128))
    swap_start("ent", every)

    def middle_backward(n2_grad, rows):
        return k.cot[rows, :] + norm_backward(n2_grad, k.u2[rows, :], k.r2[rows, :], row_of(k.gain2))

    def attended_exchange(h):
        rows = piece(h, t)
        n2_low = rs_sum("zn2", h, k.n2p, k.n2r).astype(BF16)
        k.n2g[rows, :] = n2_low
        low_piece = middle_backward(n2_low.astype(F32), rows).astype(BF16)
        for tt in range(nt):
            k.dasrc[h, tt] = mm_nt(low_piece, k.ow[tt]).astype(BF16)
        for j in range(1, nt):
            z_copy("zda", j, k.dasrc.at[h, z_peer(j)], k.datok.at[h, t], h).start()
        k.datok[h, t] = k.dasrc[h, t]

    def attended_arrived(h):
        z_all("zda", k.datok.at[h, pl.ds(0, nt - 1)], h).wait_recv()
        att_grad = jnp.transpose(k.datok[h].reshape(T, W).astype(F32)).astype(BF16)
        k.qd[b, W : 2 * W, half(h)] = att_grad
        ag_start("da%d" % h, da_at(h))
        weighted = att_grad.astype(F32) * k.acc[:, half(h)]
        for i in range(H):
            k.st[b, H + i : H + i + 1, half(h)] = jnp.sum(
                weighted[i * HEAD_DIM : (i + 1) * HEAD_DIM], axis=0, keepdims=True
            )

    grads2(0)
    attended_exchange(0)
    grads2(1)
    attended_exchange(1)
    attended_arrived(0)
    attended_arrived(1)
    ag_start("st", st_at)
    for h in range(2):
        gather_start("zn2g", h, k.n2g)
    grads3(0)
    grads3(1)
    k.dq[...] = jnp.zeros((W, L), F32)
    k.dk[...] = jnp.zeros((W, L), F32)
    k.dv[...] = jnp.zeros((W, L), F32)
    my_column = id_column(b)

    def score_grads(allowed, scores, dots, stats):
        probs = {
            (h, i): jnp.exp(jnp.where(allowed[i], x, MASKED) - stats[i][h : h + 1])
            for (h, i), x in scores.items()
        }
        grads = {
            (h, i): (x * (dots[h, i] - stats[i][H + h : H + h + 1])).astype(BF16)
            for (h, i), x in probs.items()
        }
        return probs, grads

    @pl.loop(0, s.half)
    def _(step):
        bands = [2 * step, 2 * step + 1]
        tiles = [(h, i) for h in range(H) for i in range(2)]
        allowed = [id_column(band) == id_row(b) for band in bands]
        scores = {(h, i): mm_tn(k.kv[bands[i], head(h), :], k.qd[b, head(h), :]) for h, i in tiles}
        dots = {
            (h, i): mm_tn(k.kv[bands[i], value_head(h), :], k.qd[b, value_head(h), :]) for h, i in tiles
        }
        outs = [k.dq[head(h), :] for h in range(H)]
        _, grads = score_grads(allowed, scores, dots, [k.st[b]] * 2)
        for h, i in tiles:
            outs[h] += mm_nn(k.kv[bands[i], head(h), :], grads[h, i])
        for h in range(H):
            k.dq[head(h), :] = outs[h]

    grads4(0)
    grads4(1)
    ag_wait_relay("q", q_at, 0)
    ag_arrived("q", q_all)

    def backward_bands(bands):
        tiles = [(h, i) for h in range(H) for i in range(len(bands))]
        allowed = [my_column == id_row(band) for band in bands]
        scores = {(h, i): mm_tn(k.kv[b, head(h), :], k.qd[bands[i], head(h), :]) for h, i in tiles}
        dots = {
            (h, i): mm_tn(k.kv[b, value_head(h), :], k.qd[bands[i], value_head(h), :]) for h, i in tiles
        }
        key_outs = [k.dk[head(h), :] for h in range(H)]
        value_outs = [k.dv[head(h), :] for h in range(H)]
        probs, grads = score_grads(allowed, scores, dots, [k.st[band] for band in bands])
        for h, i in tiles:
            key_outs[h] += mm_nt(k.qd[bands[i], head(h), :], grads[h, i])
            value_outs[h] += mm_nt(k.qd[bands[i], value_head(h), :], probs[h, i].astype(BF16))
        for h in range(H):
            k.dk[head(h), :] = key_outs[h]
            k.dv[head(h), :] = value_outs[h]

    da_kinds = (
        ("da0", da_at(0), da_all(0)),
        ("da1", da_at(1), da_all(1)),
        ("st", st_at, st_all),
    )
    for name, at, _ in da_kinds:
        ag_wait_relay(name, at, 0)
    backward_bands([b, sib])
    for name, at, all_at in da_kinds:
        ag_pass_on(name, at, all_at)
    for name, at, all_at in da_kinds:
        ag_arrived(name, all_at)

    def backward_loop(start, stop):
        @pl.loop(start, stop)
        def _(i):
            backward_bands([band_same(i), band_sib(i)])

    backward_loop(1, s.half // 2)
    grads5(0)
    backward_loop(s.half // 2, s.half - s.half // 4)
    backward_loop(s.half - s.half // 4, s.half)
    k.dp[0] = (k.dq[...] * SCALE).astype(BF16)
    k.dp[1] = k.dk[...].astype(BF16)
    k.dp[2] = k.dv[...].astype(BF16)
    for h in range(2):
        k.ngp[half(h), :] = mm_tn(
            k.dp[:, :, half(h)].reshape(3 * W, T), k.qkv[...].reshape(3 * W, D)
        ).astype(BF16)
        rs_start("zng", h, k.ngp, k.ngr)
    grads5(1)
    base = s.bases[2]
    for h in range(2):
        gather_wait("zn2g", h, k.n2g)
    n2_grad = k.n2g[...].astype(F32)
    gain2_grad = jnp.sum(n2_grad * k.u2[...], axis=0, keepdims=True)
    bias2_grad = jnp.sum(n2_grad, axis=0, keepdims=True)
    middle_grad = middle_backward(n2_grad, pl.ds(0, L))
    k.cot[...] = middle_grad
    k.gsrc[base : base + W, :] = mm_nn(k.att[t], middle_grad.astype(BF16)).astype(BF16)
    k.gsrc[base + W : base + 2 * W, :] = mm_nn(k.dp[0], k.normed[...]).astype(BF16)
    grads1(2)

    base = s.bases[3]
    k.gsrc[base : base + 2 * W, :] = mm_nn(k.dp[1:3].reshape(2 * W, L), k.normed[...]).astype(BF16)
    grads1(3)
    grads6(0)
    direct2(2)
    k.ngg[piece(0, t), :] = rs_sum("zng", 0, k.ngp, k.ngr).astype(BF16)
    gather_start("zngg", 0, k.ngg)
    direct2(3)
    grads6(1)
    k.ngg[piece(1, t), :] = rs_sum("zng", 1, k.ngp, k.ngr).astype(BF16)
    gather_start("zngg", 1, k.ngg)
    direct3(2)
    direct3(3)
    grads7(0)
    grads7(1)
    swap_wait("ent", every)
    k.ent_sum[...] = jnp.sum(k.ent[...], axis=0)
    ent_copy = pltpu.make_async_copy(k.ent_sum, o_ent, k.stores.at[6])
    ent_copy.start()
    gather_wait("zngg", 0, k.ngg)
    direct6(2)
    direct6(3)
    gather_wait("zngg", 1, k.ngg)
    n1_grad = k.ngg[...].astype(F32)
    unit1 = k.u1[...]
    gain1_grad = jnp.sum(n1_grad * unit1, axis=0, keepdims=True)
    bias1_grad = jnp.sum(n1_grad, axis=0, keepdims=True)
    hidden_grad = k.cot[...] + norm_backward(n1_grad, unit1, k.r1[...], row_of(k.gain1))
    k.patches[...] = hidden_grad
    hidden_copy = pltpu.make_async_copy(k.patches, o_hidden, k.stores.at[5])
    hidden_copy.start()
    coarse = hidden_grad.astype(BF16)
    fine = (hidden_grad - coarse.astype(F32)).astype(BF16)
    k.vb[near[1]] = (mm_nn(lead_hot, coarse) + mm_nn(lead_hot, fine)).astype(BF16)
    swap_start("vb", near)
    lanes = D // 128
    packed = [
        x[:, 128 * i : 128 * (i + 1)]
        for x in (gain1_grad, bias1_grad, gain2_grad, bias2_grad)
        for i in range(lanes)
    ]
    packed.append(jnp.zeros((s.packed - 4 * lanes, 128), F32))
    k.vc[near[1]] = jnp.concatenate(packed, axis=0).astype(BF16)
    swap_start("vc", near)
    grads7(2)
    grads7(3)
    k.vb_sum[...] = swap_sum("vb")
    k.vc_sum[...] = swap_sum("vc")
    vb_copy = pltpu.make_async_copy(k.vb_sum, o_vb, k.stores.at[7])
    vc_copy = pltpu.make_async_copy(k.vc_sum, o_vc, k.stores.at[8])
    vb_copy.start()
    vc_copy.start()

    z_all("zmask", k.mask.at[pl.ds(0, nt - 1)]).wait_send()
    z_all("zgate", k.gatec.at[pl.ds(0, nt - 1)]).wait_send()
    z_all("zow", ow_all).wait_send()
    for name in ("zowy", "zowr", "zowq"):
        ow_copy(name, ow_all, sib).wait_send()
    for h in range(2):
        z_all("zatt", k.att.at[pl.ds(0, nt - 1), :, half(h)], h).wait_send()
        z_all("zda", k.datok.at[h, pl.ds(0, nt - 1)], h).wait_send()
    rs_finish("zff", k.ffr)
    gather_finish("zblk", k.blow)
    rs_finish("zn2", k.n2r)
    gather_finish("zn2g", k.n2g)
    rs_finish("zng", k.ngr)
    gather_finish("zngg", k.ngg)
    ag_finish("kv", lambda count: k.kv.at[pl.ds(0, count)])
    ag_finish("q", q_all)
    ag_finish("da0", da_all(0))
    ag_finish("da1", da_all(1))
    ag_finish("st", st_all)
    swap_finish("cnt", every)
    swap_finish("ent", every)
    for i in range(4):
        grads_store(i).wait()
    for copy in (block_copy, hidden_copy, ent_copy, vb_copy, vc_copy):
        copy.wait()


def last_kernel(
    s, cuts, block, hidden, grads, ent, vb, vc,
    o_block, o_hidden, o_qkv, o_out, o_up, o_down, o_pen, o_lead, o_g1, o_b1, o_g2, o_b2, o_gate,
    low, wide, low_block, wide_block, keep, load_sem, store_sem,
):
    outs = {"down": o_down, "up": o_up, "out": o_out, "q": o_qkv.at[0], "k": o_qkv.at[1], "v": o_qkv.at[2]}
    loads = [
        pltpu.make_async_copy(block, low_block, load_sem.at[0]),
        pltpu.make_async_copy(hidden, keep, load_sem.at[1]),
    ]
    stores = [
        pltpu.make_async_copy(wide_block, o_block, store_sem.at[0]),
        pltpu.make_async_copy(keep, o_hidden, store_sem.at[1]),
    ]
    for i, (row, name, start, size) in enumerate(cuts):
        rows = pl.ds(row, size)
        loads.append(pltpu.make_async_copy(grads.at[rows], low.at[rows], load_sem.at[i + 2]))
        stores.append(
            pltpu.make_async_copy(wide.at[rows], outs[name].at[pl.ds(start, size)], store_sem.at[i + 2])
        )
    gate_rows = pl.ds(s.bases[1] + s.D, 32)
    gate_load = pltpu.make_async_copy(grads.at[gate_rows], low.at[gate_rows], load_sem.at[len(cuts) + 2])
    for copy in loads + [gate_load]:
        copy.start()
    loads[0].wait()
    wide_block[...] = low_block[...].astype(F32)
    stores[0].start()
    loads[1].wait()
    stores[1].start()
    for i, (row, name, start, size) in enumerate(cuts):
        loads[i + 2].wait()
        rows = pl.ds(row, size)
        wide[rows, :] = low[rows, :].astype(F32)
        stores[i + 2].start()
    gate_load.wait()
    small = low[gate_rows, :].astype(F32)
    for e in range(3):
        o_gate[e] = small[8 * e : 8 * e + 4]
    o_pen[...] = ent[0:1, 0:1]
    o_lead[...] = vb[...]
    lanes = s.D // 128
    for i, out in enumerate((o_g1, o_b1, o_g2, o_b2)):
        for j in range(lanes):
            row = i * lanes + j
            out[128 * j : 128 * (j + 1)] = vc[row : row + 1, :].reshape(128)
    for copy in stores:
        copy.wait()


def local(
    nb,
    nt,
    patches,
    window_ids,
    lead_index,
    lead_table,
    attention_gain,
    attention_bias,
    query_key_value,
    out_weight,
    feedforward_gain,
    feedforward_bias,
    up_weight,
    down_weight,
    gate_head,
    pixel_mask,
    cotangent,
):
    L, D = patches.shape
    leads = lead_table.shape[0]
    W = out_weight.shape[0]
    F = up_weight.shape[1]
    s = dims_of(nb, nt, L, D, W, F, leads, L * nb * pixel_mask.shape[0] * nt)
    scratch = scratch_of(s)
    vm = pl.BlockSpec(memory_space=pltpu.VMEM)
    block, hidden, grads, ent, vb, vc = pl.pallas_call(
        partial(main_kernel, s, tuple(scratch)),
        out_shape=(
            jax.ShapeDtypeStruct((L, D), BF16),
            jax.ShapeDtypeStruct((L, D), F32),
            jax.ShapeDtypeStruct((s.rows, D), BF16),
            jax.ShapeDtypeStruct((8, 128), F32),
            jax.ShapeDtypeStruct((leads, D), F32),
            jax.ShapeDtypeStruct((s.packed, 128), F32),
        ),
        in_specs=[pl.BlockSpec(memory_space=pltpu.HBM)] * 15,
        out_specs=(pl.BlockSpec(memory_space=pl.ANY),) * 6,
        scratch_shapes=list(scratch.values()),
        compiler_params=pltpu.CompilerParams(
            collective_id=0,
            has_side_effects=True,
            vmem_limit_bytes=VMEM_LIMIT,
        ),
        cost_estimate=pl.CostEstimate(
            flops=2 * s.rows * D * L * 3 + 14 * L * nb * L * W, bytes_accessed=16 * 2**20, transcendentals=0
        ),
        name="block_step",
    )(
        patches,
        window_ids,
        lead_index,
        lead_table,
        attention_gain,
        attention_bias,
        jnp.transpose(query_key_value, (0, 2, 1)),
        out_weight,
        feedforward_gain,
        feedforward_bias,
        up_weight,
        down_weight,
        gate_head,
        pixel_mask,
        cotangent,
    )
    vec = jax.ShapeDtypeStruct((D,), F32)
    cuts = []
    first = s.bases[2]
    places = (
        ("down", 0, F),
        ("up", F, D),
        ("out", first, W),
        ("q", first + W, W),
        ("k", s.bases[3], W),
        ("v", s.bases[3] + W, W),
    )
    for name, row, size in places:
        for start in range(0, size, 256):
            cuts.append((row + start, name, start, min(256, size - start)))
    hbm = pl.BlockSpec(memory_space=pl.ANY)
    wide, high, qkv_grad, out_grad, up_grad, down_grad, pen, lead, g1, b1, g2, b2, gates = pl.pallas_call(
        partial(last_kernel, s, cuts),
        out_shape=(
            jax.ShapeDtypeStruct((L, D), F32),
            jax.ShapeDtypeStruct((L, D), F32),
            jax.ShapeDtypeStruct((3, W, D), F32),
            jax.ShapeDtypeStruct((W, D), F32),
            jax.ShapeDtypeStruct((D, F), F32),
            jax.ShapeDtypeStruct((F, D), F32),
            jax.ShapeDtypeStruct((1, 1), F32),
            jax.ShapeDtypeStruct((leads, D), F32),
            vec,
            vec,
            vec,
            vec,
            jax.ShapeDtypeStruct(gate_head.shape, F32),
        ),
        in_specs=[hbm] * 3 + [vm] * 3,
        out_specs=(hbm,) * 6 + (vm,) * 7,
        scratch_shapes=[
            pltpu.VMEM((s.rows, D), BF16),
            pltpu.VMEM((s.rows, D), F32),
            pltpu.VMEM((L, D), BF16),
            pltpu.VMEM((L, D), F32),
            pltpu.VMEM((L, D), F32),
            pltpu.SemaphoreType.DMA((len(cuts) + 3,)),
            pltpu.SemaphoreType.DMA((len(cuts) + 2,)),
        ],
        compiler_params=pltpu.CompilerParams(vmem_limit_bytes=VMEM_LIMIT),
        name="write_out",
    )(block, hidden, grads, ent, vb, vc)
    return (
        wide,
        pen.reshape(()),
        high,
        lead,
        g1,
        b1,
        jnp.transpose(qkv_grad, (0, 2, 1)),
        out_grad,
        g2,
        b2,
        up_grad,
        down_grad,
        gates,
    )


def solution(mesh):
    in_specs = (
        P("blk", None),
        P(),
        P("blk"),
        P(),
        P(),
        P(),
        P(None, None, "tp"),
        P("tp", None),
        P(),
        P(),
        P(None, "tp"),
        P("tp", None),
        P(None, "tp", None),
        P("tp", "blk"),
        P("blk", None),
    )
    out_specs = (
        P("blk", None),
        P(),
        P("blk", None),
        P(),
        P(),
        P(),
        P(None, None, "tp"),
        P("tp", None),
        P(),
        P(),
        P(None, "tp"),
        P("tp", None),
        P(None, "tp", None),
    )
    return jax.shard_map(
        partial(local, mesh.shape["blk"], mesh.shape["tp"]),
        mesh=mesh,
        in_specs=in_specs,
        out_specs=out_specs,
        check_vma=False,
    )
```

```python
from functools import partial
from types import SimpleNamespace

import jax
import jax.numpy as jnp
from jax import lax
from jax.experimental import pallas as pl
from jax.experimental.pallas import tpu as pltpu
from jax.sharding import PartitionSpec as P

HEAD_DIM = 64
EPS = 1e-05
MASKED = -1e30
SCALE = HEAD_DIM ** (-0.5)
GROUP = 8
F32 = jnp.float32
BF16 = jnp.bfloat16
MESH = pl.DeviceIdType.MESH
VMEM_LIMIT = 61 * 2**20
INV_SQRT2 = 0.7071067811865476
INV_SQRT_2PI = 0.3989422804014327


def dot(a, b, ca, cb):
    return lax.dot_general(a, b, (((ca,), (cb,)), ((), ())), preferred_element_type=F32)


def mm_nn(a, b):
    return dot(a, b, 1, 0)


def mm_nt(a, b):
    return dot(a, b, 1, 1)


def mm_tn(a, b):
    return dot(a, b, 0, 0)


def norm_stats(values):
    mean = jnp.mean(values, axis=-1, keepdims=True)
    centered = values - mean
    inverse = lax.rsqrt(jnp.mean(centered * centered, axis=-1, keepdims=True) + EPS)
    return centered * inverse, inverse


def norm_backward(incoming, unit_rows, inverse, gain):
    scaled = incoming * gain
    return inverse * (
        scaled
        - jnp.mean(scaled, axis=-1, keepdims=True)
        - unit_rows * jnp.mean(scaled * unit_rows, axis=-1, keepdims=True)
    )


def row_of(ref):
    return ref[...].reshape(1, ref.shape[0])


def total(x):
    return jnp.sum(jnp.sum(x, axis=0, keepdims=True), axis=1, keepdims=True)


def dims_of(nb, nt, tokens, width, local_width, hidden, leads, pixels):
    s = SimpleNamespace(nb=nb, nt=nt, L=tokens, D=width, W=local_width, F=hidden, leads=leads)
    s.H = local_width // HEAD_DIM
    s.T = tokens // 2
    s.R = s.T // nt
    s.half = nb // 2
    s.groups = nb // GROUP
    s.pixels = pixels
    s.sizes = (hidden, width + 128, local_width * 2, local_width * 2)
    s.bases = tuple(sum(s.sizes[:i]) for i in range(4))
    s.rows = sum(s.sizes)
    s.packed = (4 * width // 128 + 15) // 16 * 16
    return s


def scratch_of(s):
    L, D, W, F, nb, nt, R = s.L, s.D, s.W, s.F, s.nb, s.nt, s.R
    v = pltpu.VMEM
    out = {
        "patches": v((L, D), F32),
        "windows": v((nb * L,), jnp.int32),
        "lead_index": v((L,), jnp.int32),
        "table": v((s.leads, D), BF16),
        "gain1": v((D,), F32),
        "bias1": v((D,), F32),
        "gain2": v((D,), F32),
        "bias2": v((D,), F32),
        "pix": v((4, L), jnp.int32),
        "head": v((3, 4, D), BF16),
        "ids": v((nb, L), F32),
        "qkv": v((3, W, D), BF16),
        "ow": v((nt, W, D), BF16),
        "up": v((D, F), BF16),
        "down": v((F, D), BF16),
        "cot": v((L, D), F32),
        "gatec": v((nt, 16, D), BF16),
        "gate": v((nt * 32, D), BF16),
        "mask": v((nt, 8, L), F32),
        "cnt": v((nb, 8, 128), F32),
        "u1": v((L, D), F32),
        "r1": v((L, 1), F32),
        "normed": v((L, D), BF16),
        "kv": v((nb, 2 * W, L), BF16),
        "qd": v((nb, 2 * W, L), BF16),
        "st": v((nb, 8, L), F32),
        "m": v((8, L), F32),
        "l": v((8, L), F32),
        "acc": v((W, L), F32),
        "att": v((nt, W, L), BF16),
        "mid": v((L, D), F32),
        "u2": v((L, D), F32),
        "r2": v((L, 1), F32),
        "n2low": v((L, D), BF16),
        "upw": v((L, F), F32),
        "actlow": v((L, F), BF16),
        "ffp": v((L, D), BF16),
        "ffr": v((2, nt - 1, R, D), BF16),
        "blow": v((L, D), BF16),
        "lg": v((nt * 32, L), BF16),
        "oglow": v((L, D), BF16),
        "ug": v((L, F), BF16),
        "n2p": v((L, D), BF16),
        "n2r": v((2, nt - 1, R, D), BF16),
        "n2g": v((L, D), BF16),
        "dasrc": v((2, nt, R, W), BF16),
        "datok": v((2, nt, R, W), BF16),
        "dq": v((W, L), F32),
        "dk": v((W, L), F32),
        "dv": v((W, L), F32),
        "dp": v((3, W, L), BF16),
        "ngp": v((L, D), BF16),
        "ngr": v((2, nt - 1, R, D), BF16),
        "ngg": v((L, D), BF16),
        "vb": v((GROUP, s.leads, D), BF16),
        "vc": v((GROUP, s.packed, 128), BF16),
        "ent": v((nb, 8, 128), F32),
        "ent_sum": v((8, 128), F32),
        "vb_sum": v((s.leads, D), F32),
        "vc_sum": v((s.packed, 128), F32),
        "gsrc": v((s.rows, D), BF16),
        "gout": v((s.rows, D), BF16),
    }
    dma = pltpu.SemaphoreType.DMA
    out["loads"] = dma((15,))
    out["stores"] = dma((9,))
    for name in ("zmask", "zgate", "zow", "zowy", "zowr", "zowq"):
        out[name + "_s"] = dma((1,))
        out[name + "_r"] = dma((1,))
    for name in ("zatt", "zff", "zblk", "zn2", "zn2g", "zda", "zng", "zngg"):
        out[name + "_s"] = dma((2,))
        out[name + "_r"] = dma((2,))
    for name in ("kv", "q", "da0", "da1", "st"):
        count = s.half if name == "kv" else 2
        out[name + "_s"] = dma((1,))
        out[name + "_r"] = dma((count,))
        out[name + "_rs"] = dma((1,))
        out[name + "_rr"] = dma((count,))
    for name in ("cnt", "ent", "vb", "vc"):
        out[name + "_s"] = dma((1,))
        out[name + "_r"] = dma((1,))
    if s.groups > 1:
        out["vb2"] = v((s.groups, s.leads, D), BF16)
        out["vc2"] = v((s.groups, s.packed, 128), BF16)
        for name in ("vb2", "vc2"):
            out[name + "_s"] = dma((1,))
            out[name + "_r"] = dma((1,))
    for i, rows in enumerate(s.sizes):
        hr = rows // 2
        qr = hr // 4
        out["core%d" % i] = v((hr, D), BF16)
        out["quart%d" % i] = v((3, qr, D), BF16)
        if s.groups > 1:
            out["sup%d" % i] = v((s.groups, qr, D), BF16)
            out["sup%d_s" % i] = dma((1,))
            out["sup%d_r" % i] = dma((1,))
        out["gs%d" % i] = dma((6 if i < 2 else 4,))
        out["gr%d" % i] = dma((6 if i < 2 else 4,))
    return out


def main_kernel(s, names, *refs):
    (
        patches,
        windows_in,
        leads_in,
        table,
        gain1,
        bias1,
        qkv,
        out_weight,
        gain2,
        bias2,
        up,
        down,
        gate,
        pixel_mask,
        cotangent,
        o_block,
        o_hidden,
        o_grads,
        o_ent,
        o_vb,
        o_vc,
    ) = refs[:21]
    k = SimpleNamespace(**dict(zip(names, refs[21:])))
    sem = vars(k)
    L, D, W, F, H, T, R, nb, nt = s.L, s.D, s.W, s.F, s.H, s.T, s.R, s.nb, s.nt
    b = lax.axis_index("blk")
    t = lax.axis_index("tp")
    core = lax.rem(b, 2)
    pair = b // 2
    sib = b + 1 - 2 * core

    def z_peer(j):
        return lax.rem(t + j, nt)

    def z_from(j):
        return lax.rem(t + nt - j, nt)

    def remote(src, dst, send, recv, device):
        return pltpu.make_async_remote_copy(
            src, dst, send, recv, device_id=device, device_id_type=MESH
        )

    def z_copy(name, j, src, dst, h=0):
        return remote(src, dst, sem[name + "_s"].at[h], sem[name + "_r"].at[h], (b, z_peer(j)))

    def z_all(name, ref, h=0):
        return z_copy(name, 1, ref, ref, h)

    def half(h):
        return pl.ds(h * T, T)

    def piece(h, tt):
        return pl.ds(pl.multiple_of(h * T + tt * R, R), R)

    def ag_copy(name, at, i, dst_band):
        slot = i if name == "kv" else 0
        return remote(at(b), at(b), sem[name + "_s"].at[0], sem[name + "_r"].at[slot], (dst_band, t))

    def relay_copy(name, at, i, band):
        slot = i if name == "kv" or isinstance(i, int) else 1
        return remote(at(band), at(band), sem[name + "_rs"].at[0], sem[name + "_rr"].at[slot], (sib, t))

    def band_same(i):
        return lax.rem(b + nb - 2 * i, nb)

    def band_sib(i):
        return lax.rem(sib + nb - 2 * i, nb)

    def ag_start(name, at):
        @pl.loop(1, s.half)
        def _(i):
            ag_copy(name, at, i, lax.rem(b + 2 * i, nb)).start()

        relay_copy(name, at, 0, b).start()

    def ag_wait(name, at, i):
        band = band_same(i)
        remote(at(band), at(band), sem[name + "_s"].at[0], sem[name + "_r"].at[i], (sib, t)).wait_recv()

    def ag_relay(name, at, i):
        relay_copy(name, at, i, band_same(i)).start()

    def ag_wait_relay(name, at, i):
        relay_copy(name, at, i, band_sib(i)).wait_recv()

    def ag_pass_on(name, at, all_at):
        ref = all_at(s.half - 1)
        remote(ref, ref, sem[name + "_s"].at[0], sem[name + "_r"].at[0], (sib, t)).wait_recv()

        @pl.loop(1, s.half)
        def _(i):
            ag_relay(name, at, i)

    def ag_arrived(name, all_at):
        ref = all_at(s.half - 1)
        remote(ref, ref, sem[name + "_rs"].at[0], sem[name + "_rr"].at[1], (sib, t)).wait_recv()

    def ag_finish(name, all_at):
        ref = all_at(s.half - 1)
        remote(ref, ref, sem[name + "_s"].at[0], sem[name + "_r"].at[0], (sib, t)).wait_send()
        ref = all_at(s.half)
        remote(ref, ref, sem[name + "_rs"].at[0], sem[name + "_rr"].at[0], (sib, t)).wait_send()

    every = (nb, b, lambda i: i)
    near = (GROUP, lax.rem(b, GROUP), lambda i: b // GROUP * GROUP + i)
    far = (s.groups, b // GROUP, lambda i: i * GROUP + lax.rem(b, GROUP))

    def swap_copy(name, members, ref, to):
        return remote(ref, ref, sem[name + "_s"].at[0], sem[name + "_r"].at[0], (members[2](to), t))

    def swap_start(name, members):
        count, me, _ = members

        @pl.loop(1, count)
        def _(i):
            swap_copy(name, members, sem[name].at[me], lax.rem(me + i, count)).start()

    def swap_all(name, members):
        return swap_copy(name, members, sem[name].at[pl.ds(0, members[0] - 1)], 0)

    def swap_wait(name, members):
        swap_all(name, members).wait_recv()

    def swap_finish(name, members):
        swap_all(name, members).wait_send()

    def slots_sum(ref, count):
        return lax.fori_loop(
            1, count, lambda i, acc: acc + ref[i].astype(F32), ref[0].astype(F32)
        )

    def swap_sum(name):
        swap_wait(name, near)
        out = slots_sum(sem[name], GROUP)
        if s.groups > 1:
            sem[name + "2"][far[1]] = out.astype(BF16)
            swap_start(name + "2", far)
            swap_wait(name + "2", far)
            out = slots_sum(sem[name + "2"], s.groups)
            swap_finish(name + "2", far)
        swap_finish(name, near)
        return out

    def rs_start(name, h, part, recv):
        for j in range(1, nt):
            z_copy(name, j, part.at[piece(h, z_peer(j))], recv.at[h, j - 1], h).start()

    def rs_sum(name, h, part, recv):
        z_all(name, recv.at[h], h).wait_recv()
        acc = part[piece(h, t), :].astype(F32)
        for j in range(1, nt):
            acc = acc + recv[h, j - 1].astype(F32)
        return acc

    def rs_finish(name, recv):
        for h in range(2):
            z_all(name, recv.at[h], h).wait_send()

    def gather_start(name, h, ref):
        for j in range(1, nt):
            z_copy(name, j, ref.at[piece(h, t)], ref.at[piece(h, t)], h).start()

    def gather_all(name, h, ref):
        return z_all(name, ref.at[pl.ds(h * T, (nt - 1) * R)], h)

    def gather_wait(name, h, ref):
        gather_all(name, h, ref).wait_recv()

    def gather_finish(name, ref):
        for h in range(2):
            gather_all(name, h, ref).wait_send()

    quarter = lax.rem(pair, 4)
    first_pair = pair - quarter
    group = pair // 4
    low_peer = quarter + 1 - 2 * lax.rem(quarter, 2)
    high_peer = lax.rem(quarter + 2, 4)
    first = low_peer * (1 - core) + high_peer * core
    second = low_peer * core + high_peer * (1 - core)
    across = lax.rem(low_peer + 2, 4)

    def g_rows(i, q):
        hr = s.sizes[i] // 2
        qr = hr // 4
        return pl.ds(pl.multiple_of(s.bases[i] + core * hr + q * qr, 16), qr)

    def g_half(i, c):
        hr = s.sizes[i] // 2
        return pl.ds(pl.multiple_of(s.bases[i] + c * hr, 16), hr)

    def q_rows(i, q):
        qr = s.sizes[i] // 8
        return pl.ds(pl.multiple_of(q * qr, 16), qr)

    def g_copy(i, slot, src, dst, q):
        dev = ((first_pair + q) * 2 + core, t)
        return remote(src, dst, sem["gs%d" % i].at[slot], sem["gr%d" % i].at[slot], dev)

    def sib_copy(i, slot, src, dst):
        return remote(src, dst, sem["gs%d" % i].at[slot], sem["gr%d" % i].at[slot], (sib, t))

    def c1_copy(i):
        return sib_copy(i, 0, k.gsrc.at[g_half(i, 1 - core)], sem["core%d" % i])

    def rs_copies(i):
        hs = sem["core%d" % i]
        land = sem["quart%d" % i]
        return (
            g_copy(i, 1, hs.at[q_rows(i, first)], land.at[0], first),
            g_copy(i, 1, hs.at[q_rows(i, across)], land.at[1], first),
        )

    def land_all(i, slot, count):
        ref = sem["quart%d" % i].at[pl.ds(0, count)]
        return g_copy(i, slot, ref, ref, first)

    def out_all(i, slot, count):
        ref = k.gout.at[pl.ds(s.bases[i], count * (s.sizes[i] // 8))]
        return g_copy(i, slot, ref, ref, first)

    def rs_copy_b(i):
        return g_copy(i, 2, sem["core%d" % i].at[q_rows(i, second)], sem["quart%d" % i].at[2], second)

    def out_copy(i, slot, q, to):
        rows = g_rows(i, q)
        return g_copy(i, slot, k.gout.at[rows], k.gout.at[rows], to)

    def c2_copy(i, c):
        rows = g_half(i, c)
        return sib_copy(i, 3, k.gout.at[rows], k.gout.at[rows])

    def across_groups(i, acc):
        if s.groups > 1:
            ref = sem["sup%d" % i]
            ref[group] = acc.astype(BF16)

            def copy(j, at):
                dev = ((lax.rem(group + j, s.groups) * 4 + quarter) * 2 + core, t)
                return remote(at, at, sem["sup%d_s" % i].at[0], sem["sup%d_r" % i].at[0], dev)

            for j in range(1, s.groups):
                copy(j, ref.at[group]).start()
            copy(1, ref.at[pl.ds(0, s.groups - 1)]).wait()
            acc = ref[0].astype(F32)
            for g in range(1, s.groups):
                acc = acc + ref[g].astype(F32)
        return acc.astype(BF16)

    def grads1(i):
        c1_copy(i).start()

    def pair_sum(i):
        c1_copy(i).wait()
        hs = sem["core%d" % i]
        hs[...] = (k.gsrc[g_half(i, core), :].astype(F32) + hs[...].astype(F32)).astype(BF16)

    def grads2(i):
        pair_sum(i)
        for copy in rs_copies(i):
            copy.start()

    def grads3(i):
        land_all(i, 1, 2).wait()
        hs = sem["core%d" % i]
        rows = q_rows(i, second)
        hs[rows, :] = (hs[rows, :].astype(F32) + sem["quart%d" % i][1].astype(F32)).astype(BF16)
        rs_copy_b(i).start()

    def grads4(i):
        rs_copy_b(i).wait()
        land = sem["quart%d" % i]
        acc = sem["core%d" % i][q_rows(i, quarter), :].astype(F32)
        acc = acc + land[0].astype(F32) + land[2].astype(F32)
        k.gout[g_rows(i, quarter), :] = across_groups(i, acc)
        out_copy(i, 4, quarter, second).start()

    def grads5(i):
        out_copy(i, 4, quarter, second).wait_send()
        out_copy(i, 4, second, second).wait_recv()
        out_copy(i, 5, quarter, first).start()
        out_copy(i, 5, second, first).start()

    def grads6(i):
        out_all(i, 5, 2).wait()
        c2_copy(i, core).start()

    def q_peer(j):
        return lax.rem(quarter + j, 4)

    def direct2(i):
        pair_sum(i)
        for j in range(1, 4):
            src = sem["core%d" % i].at[q_rows(i, q_peer(j))]
            g_copy(i, 1, src, sem["quart%d" % i].at[j - 1], q_peer(j)).start()

    def direct3(i):
        land_all(i, 1, 3).wait()
        acc = sem["core%d" % i][q_rows(i, quarter), :].astype(F32)
        for j in range(3):
            acc = acc + sem["quart%d" % i][j].astype(F32)
        k.gout[g_rows(i, quarter), :] = across_groups(i, acc)
        for j in range(1, 4):
            out_copy(i, 2, quarter, q_peer(j)).start()

    def direct6(i):
        out_all(i, 2, 3).wait()
        c2_copy(i, core).start()

    def grads_store(i):
        rows = pl.ds(s.bases[i], s.sizes[i])
        return pltpu.make_async_copy(k.gout.at[rows], o_grads.at[rows], k.stores.at[i])

    def grads7(i):
        c2_copy(i, core).wait_send()
        c2_copy(i, 1 - core).wait_recv()
        grads_store(i).start()

    def load(i, src, dst):
        return pltpu.make_async_copy(src, dst, k.loads.at[i])

    first_loads = [
        load(0, patches, k.patches),
        load(1, leads_in, k.lead_index),
        load(2, table, k.table),
        load(3, gain1, k.gain1),
        load(4, bias1, k.bias1),
    ]
    ow_load = load(5, out_weight, k.ow.at[t])
    small_loads = [
        load(6, pixel_mask, k.pix),
        load(7, gate, k.head),
        load(8, windows_in, k.windows),
    ]
    qkv_load = load(9, qkv, k.qkv)
    late_loads = [
        load(10, gain2, k.gain2),
        load(11, bias2, k.bias2),
        load(12, up, k.up),
        load(13, down, k.down),
        load(14, cotangent, k.cot),
    ]
    for copy in first_loads + small_loads + [qkv_load, ow_load]:
        copy.start()
    barrier = pltpu.get_barrier_semaphore()

    @pl.loop(1, nb)
    def _(i):
        pl.semaphore_signal(barrier, inc=1, device_id=(lax.rem(b + i, nb), t), device_id_type=MESH)

    for j in range(1, nt):
        pl.semaphore_signal(barrier, inc=1, device_id=(b, z_peer(j)), device_id_type=MESH)

    for copy in first_loads:
        copy.wait()
    lead_hot = lax.broadcasted_iota(jnp.int32, (s.leads, L), 0) == row_of(k.lead_index)
    lead_hot = lead_hot.astype(F32).astype(BF16)
    hidden = k.patches[...] + mm_tn(lead_hot, k.table[...])
    unit1, inverse1 = norm_stats(hidden)
    k.u1[...] = unit1
    k.r1[...] = inverse1
    k.mid[...] = hidden
    k.normed[...] = (unit1 * row_of(k.gain1) + row_of(k.bias1)).astype(BF16)
    for copy in small_loads:
        copy.wait()
    compact = [k.head[e].astype(F32) for e in range(3)] + [jnp.zeros((4, D), F32)]
    k.gatec[t] = jnp.concatenate(compact, axis=0).astype(BF16)
    k.mask[t] = jnp.concatenate([k.pix[...].astype(F32), jnp.zeros((4, L), F32)], axis=0)
    part = W // 4
    upper = quarter // 2

    def ow_part(tt, c, u):
        return k.ow.at[tt, pl.ds(pl.multiple_of((c + 2 * u) * part, part), part)]

    def ow_copy(name, at, dev):
        return remote(at, at, sem[name + "_s"].at[0], sem[name + "_r"].at[0], (dev, t))

    ow_all = k.ow.at[pl.ds(0, nt - 1), pl.ds(0, part)]
    high_dev = (first_pair + high_peer) * 2 + core

    qkv_load.wait()

    def project(c):
        return mm_nt(k.qkv[c], k.normed[...])

    k.kv[b, 0:W, :] = project(1).astype(BF16)
    k.kv[b, W : 2 * W, :] = project(2).astype(BF16)
    ow_load.wait()
    pl.semaphore_wait(barrier, nb - 1 + nt - 1)

    def kv_at(band):
        return k.kv.at[band]

    ag_start("kv", kv_at)
    for j in range(1, nt):
        z_copy("zmask", j, k.mask.at[t], k.mask.at[t]).start()
        z_copy("zow", j, ow_part(t, core, upper), ow_part(t, core, upper)).start()
        z_copy("zgate", j, k.gatec.at[t], k.gatec.at[t]).start()
    for copy in late_loads:
        copy.start()
    k.qd[b, 0:W, :] = (project(0).astype(BF16).astype(F32) * SCALE).astype(BF16)

    k.ids[...] = k.windows[...].reshape(nb, L).astype(F32)

    def id_row(band):
        return k.ids[pl.ds(band, 1), :]

    def id_column(band):
        return jnp.transpose(jnp.broadcast_to(id_row(band), (128, L)))[:, 0:1]

    def head(h):
        return pl.ds(h * HEAD_DIM, HEAD_DIM)

    def value_head(h):
        return pl.ds(W + h * HEAD_DIM, HEAD_DIM)

    k.m[...] = jnp.full((8, L), MASKED, F32)
    k.l[...] = jnp.zeros((8, L), F32)
    k.acc[...] = jnp.zeros((W, L), F32)

    def forward_bands(bands):
        tiles = [(h, i) for h in range(H) for i in range(len(bands))]
        allowed = [id_column(band) == id_row(b) for band in bands]
        scores = {
            (h, i): jnp.where(
                allowed[i], mm_tn(k.kv[bands[i], head(h), :], k.qd[b, head(h), :]), MASKED
            )
            for h, i in tiles
        }
        old_high = [k.m[h : h + 1, :] for h in range(H)]
        sums = [k.l[h : h + 1, :] for h in range(H)]
        outs = [k.acc[head(h), :] for h in range(H)]
        high = list(old_high)
        for h, i in tiles:
            high[h] = jnp.maximum(high[h], jnp.max(scores[h, i], axis=0, keepdims=True))
        weights = {(h, i): jnp.exp(scores[h, i] - high[h]) for h, i in tiles}
        factor = [jnp.exp(x - y) for x, y in zip(old_high, high)]
        outs = [x * f for x, f in zip(outs, factor)]
        sums = [x * f for x, f in zip(sums, factor)]
        for h, i in tiles:
            outs[h] += mm_nn(k.kv[bands[i], value_head(h), :], weights[h, i].astype(BF16))
            sums[h] += jnp.sum(weights[h, i], axis=0, keepdims=True)
        for h in range(H):
            k.m[h : h + 1, :] = high[h]
            k.l[h : h + 1, :] = sums[h]
            k.acc[head(h), :] = outs[h]

    def ow_pass_on():
        z_all("zow", ow_all).wait_recv()
        for j in range(1, nt):
            at = ow_part(z_from(j), core, upper)
            ow_copy("zowy", at, high_dev).start()
            ow_copy("zowr", at, sib).start()

    def ow_pass_second():
        ow_copy("zowy", ow_all, high_dev).wait_recv()
        for j in range(1, nt):
            ow_copy("zowq", ow_part(z_from(j), core, 1 - upper), sib).start()

    ag_wait_relay("kv", kv_at, 0)
    forward_bands([b, sib])
    z_all("zmask", k.mask.at[pl.ds(0, nt - 1)]).wait_recv()
    k.cnt[b] = jnp.broadcast_to(total(jnp.sum(k.mask[...], axis=0)), (8, 128))
    swap_start("cnt", every)

    @pl.loop(1, s.half)
    def _(i):
        ag_wait("kv", kv_at, i)
        ag_relay("kv", kv_at, i)

    ow_pass_on()

    @pl.loop(0, s.half // 2 - 1)
    def _(i):
        forward_bands([band_same(2 * i + 1), band_same(2 * i + 2)])

    ag_wait_relay("kv", kv_at, 1)
    forward_bands([band_same(s.half - 1), band_sib(1)])

    @pl.loop(1, s.half // 2)
    def _(i):
        ag_wait_relay("kv", kv_at, 2 * i)
        ag_wait_relay("kv", kv_at, 2 * i + 1)
        forward_bands([band_sib(2 * i), band_sib(2 * i + 1)])

    for h in range(H):
        att = k.acc[head(h), :] / k.l[h : h + 1, :]
        k.acc[head(h), :] = att
        k.att[t, head(h), :] = att.astype(BF16)
        k.st[b, h : h + 1, :] = k.m[h : h + 1, :] + jnp.log(k.l[h : h + 1, :])

    def att_half(tt, h):
        return k.att.at[tt, :, half(h)]

    for h in range(2):
        for j in range(1, nt):
            z_copy("zatt", j, att_half(t, h), att_half(t, h), h).start()

    def q_at(band):
        return k.qd.at[band, pl.ds(0, W)]

    def da_at(h):
        return lambda band: k.qd.at[band, pl.ds(W, W), half(h)]

    def st_at(band):
        return k.st.at[band]

    def q_all(count):
        return k.qd.at[pl.ds(0, count), pl.ds(0, W)]

    def da_all(h):
        return lambda count: k.qd.at[pl.ds(0, count), pl.ds(W, W), half(h)]

    def st_all(count):
        return k.st.at[pl.ds(0, count)]

    ag_start("q", q_at)
    ow_pass_second()
    for copy in late_loads:
        copy.wait()
    ow_copy("zowr", ow_all, sib).wait_recv()
    ow_copy("zowq", ow_all, sib).wait_recv()

    for h in range(2):
        z_all("zatt", k.att.at[pl.ds(0, nt - 1), :, half(h)], h).wait_recv()
        rows = half(h)
        middle = k.mid[rows, :] + mm_tn(
            k.att[:, :, half(h)].reshape(nt * W, T), k.ow[...].reshape(nt * W, D)
        )
        k.mid[rows, :] = middle
        unit2, inverse2 = norm_stats(middle)
        k.u2[rows, :] = unit2
        k.r2[rows, :] = inverse2
        k.n2low[rows, :] = (unit2 * row_of(k.gain2) + row_of(k.bias2)).astype(BF16)
        upward = mm_nn(k.n2low[rows, :], k.up[...])
        k.upw[rows, :] = upward
        k.actlow[rows, :] = (0.5 * upward * (1.0 + lax.erf(upward * INV_SQRT2))).astype(BF16)
        k.ffp[rows, :] = mm_nn(k.actlow[rows, :], k.down[...]).astype(BF16)
        rs_start("zff", h, k.ffp, k.ffr)
    upward = k.upw[...]
    k.upw[...] = 0.5 * (1.0 + lax.erf(upward * INV_SQRT2)) + upward * (
        jnp.exp(-0.5 * upward * upward) * INV_SQRT_2PI
    )
    z_all("zgate", k.gatec.at[pl.ds(0, nt - 1)]).wait_recv()
    for tt in range(nt):
        x = k.gatec[tt].astype(F32)
        pad = jnp.zeros((4, D), F32)
        parts = []
        for e in range(3):
            parts += [x[4 * e : 4 * e + 4], pad]
        k.gate[tt * 32 : (tt + 1) * 32, :] = jnp.concatenate(parts + [pad, pad], axis=0).astype(BF16)
    swap_wait("cnt", every)
    pixel_count = jnp.sum(k.cnt[...], axis=0)[0:1, 0:1]
    for h in range(2):
        block_piece = k.mid[piece(h, t), :] + rs_sum("zff", h, k.ffp, k.ffr)
        k.blow[piece(h, t), :] = block_piece.astype(BF16)
        gather_start("zblk", h, k.blow)

    ag_pass_on("q", q_at, q_all)

    entropy_sum = jnp.zeros((1, 1), F32)
    for h in range(2):
        rows = half(h)
        gather_wait("zblk", h, k.blow)
        logits = mm_nt(k.gate[...], k.blow[rows, :]).reshape(nt, 4, 8, T)
        parts = [logits[:, e] for e in range(3)]
        high = jnp.maximum(jnp.maximum(parts[0], parts[1]), parts[2])
        logs = jnp.log(sum(jnp.exp(x - high) for x in parts))
        log_probs = [x - high - logs for x in parts]
        probs = [jnp.exp(x) for x in log_probs]
        entropy = -sum(p * x for p, x in zip(probs, log_probs))
        mask = k.mask[:, :, half(h)]
        entropy_sum += total(jnp.sum(mask * entropy, axis=0))
        weight = mask * (float(s.pixels) / pixel_count)[None]
        grads = [-p * (x + entropy) * weight for p, x in zip(probs, log_probs)]
        grads.append(jnp.zeros((nt, 8, T), F32))
        k.lg[:, half(h)] = jnp.stack(grads, axis=1).reshape(nt * 32, T).astype(BF16)
        out_grad = k.cot[rows, :] + mm_tn(k.lg[:, half(h)], k.gate[...])
        k.cot[rows, :] = out_grad
        k.oglow[rows, :] = out_grad.astype(BF16)
        if h == 1:
            k.gsrc[0:F, :] = mm_tn(k.actlow[...], k.oglow[...]).astype(BF16)
            grads1(0)
        k.ug[rows, :] = (mm_nt(k.oglow[rows, :], k.down[...]) * k.upw[rows, :]).astype(BF16)
        k.n2p[rows, :] = mm_nt(k.ug[rows, :], k.up[...]).astype(BF16)
        rs_start("zn2", h, k.n2p, k.n2r)
    block_copy = pltpu.make_async_copy(k.blow, o_block, k.stores.at[4])
    block_copy.start()
    k.gsrc[F : F + D, :] = mm_tn(k.n2low[...], k.ug[...]).astype(BF16)
    own_lg = k.lg[pl.ds(pl.multiple_of(t * 32, 32), 32), :]
    base = s.bases[1] + D
    k.gsrc[base : base + 32, :] = mm_nn(own_lg, k.blow[...]).astype(BF16)
    k.gsrc[base + 32 : base + 128, :] = jnp.zeros((96, D), BF16)
    grads1(1)
    k.ent[b] = jnp.broadcast_to(entropy_sum / pixel_count, (8, 128))
    swap_start("ent", every)

    def middle_backward(n2_grad, rows):
        return k.cot[rows, :] + norm_backward(n2_grad, k.u2[rows, :], k.r2[rows, :], row_of(k.gain2))

    def attended_exchange(h):
        rows = piece(h, t)
        n2_low = rs_sum("zn2", h, k.n2p, k.n2r).astype(BF16)
        k.n2g[rows, :] = n2_low
        low_piece = middle_backward(n2_low.astype(F32), rows).astype(BF16)
        for tt in range(nt):
            k.dasrc[h, tt] = mm_nt(low_piece, k.ow[tt]).astype(BF16)
        for j in range(1, nt):
            z_copy("zda", j, k.dasrc.at[h, z_peer(j)], k.datok.at[h, t], h).start()
        k.datok[h, t] = k.dasrc[h, t]

    def attended_arrived(h):
        z_all("zda", k.datok.at[h, pl.ds(0, nt - 1)], h).wait_recv()
        att_grad = jnp.transpose(k.datok[h].reshape(T, W).astype(F32)).astype(BF16)
        k.qd[b, W : 2 * W, half(h)] = att_grad
        ag_start("da%d" % h, da_at(h))
        weighted = att_grad.astype(F32) * k.acc[:, half(h)]
        for i in range(H):
            k.st[b, H + i : H + i + 1, half(h)] = jnp.sum(
                weighted[i * HEAD_DIM : (i + 1) * HEAD_DIM], axis=0, keepdims=True
            )

    grads2(0)
    attended_exchange(0)
    grads2(1)
    attended_exchange(1)
    attended_arrived(0)
    attended_arrived(1)
    ag_start("st", st_at)
    for h in range(2):
        gather_start("zn2g", h, k.n2g)
    grads3(0)
    grads3(1)
    k.dq[...] = jnp.zeros((W, L), F32)
    k.dk[...] = jnp.zeros((W, L), F32)
    k.dv[...] = jnp.zeros((W, L), F32)
    my_column = id_column(b)

    def score_grads(allowed, scores, dots, stats):
        probs = {
            (h, i): jnp.exp(jnp.where(allowed[i], x, MASKED) - stats[i][h : h + 1])
            for (h, i), x in scores.items()
        }
        grads = {
            (h, i): (x * (dots[h, i] - stats[i][H + h : H + h + 1])).astype(BF16)
            for (h, i), x in probs.items()
        }
        return probs, grads

    @pl.loop(0, s.half)
    def _(step):
        bands = [2 * step, 2 * step + 1]
        tiles = [(h, i) for h in range(H) for i in range(2)]
        allowed = [id_column(band) == id_row(b) for band in bands]
        scores = {(h, i): mm_tn(k.kv[bands[i], head(h), :], k.qd[b, head(h), :]) for h, i in tiles}
        dots = {
            (h, i): mm_tn(k.kv[bands[i], value_head(h), :], k.qd[b, value_head(h), :]) for h, i in tiles
        }
        outs = [k.dq[head(h), :] for h in range(H)]
        _, grads = score_grads(allowed, scores, dots, [k.st[b]] * 2)
        for h, i in tiles:
            outs[h] += mm_nn(k.kv[bands[i], head(h), :], grads[h, i])
        for h in range(H):
            k.dq[head(h), :] = outs[h]

    grads4(0)
    grads4(1)
    ag_wait_relay("q", q_at, 0)
    ag_arrived("q", q_all)

    def backward_bands(bands):
        tiles = [(h, i) for h in range(H) for i in range(len(bands))]
        allowed = [my_column == id_row(band) for band in bands]
        scores = {(h, i): mm_tn(k.kv[b, head(h), :], k.qd[bands[i], head(h), :]) for h, i in tiles}
        dots = {
            (h, i): mm_tn(k.kv[b, value_head(h), :], k.qd[bands[i], value_head(h), :]) for h, i in tiles
        }
        key_outs = [k.dk[head(h), :] for h in range(H)]
        value_outs = [k.dv[head(h), :] for h in range(H)]
        probs, grads = score_grads(allowed, scores, dots, [k.st[band] for band in bands])
        for h, i in tiles:
            key_outs[h] += mm_nt(k.qd[bands[i], head(h), :], grads[h, i])
            value_outs[h] += mm_nt(k.qd[bands[i], value_head(h), :], probs[h, i].astype(BF16))
        for h in range(H):
            k.dk[head(h), :] = key_outs[h]
            k.dv[head(h), :] = value_outs[h]

    da_kinds = (
        ("da0", da_at(0), da_all(0)),
        ("da1", da_at(1), da_all(1)),
        ("st", st_at, st_all),
    )
    for name, at, all_at in da_kinds:
        ag_pass_on(name, at, all_at)
    for name, at, all_at in da_kinds:
        ag_arrived(name, all_at)

    for name, at, _ in da_kinds:
        ag_wait_relay(name, at, 0)
    backward_bands([b, sib])
    def backward_loop(start, stop):
        @pl.loop(start, stop)
        def _(i):
            backward_bands([band_same(i), band_sib(i)])

    backward_loop(1, s.half // 2)
    grads5(0)
    backward_loop(s.half // 2, s.half - s.half // 4)
    backward_loop(s.half - s.half // 4, s.half)
    k.dp[0] = (k.dq[...] * SCALE).astype(BF16)
    k.dp[1] = k.dk[...].astype(BF16)
    k.dp[2] = k.dv[...].astype(BF16)
    for h in range(2):
        k.ngp[half(h), :] = mm_tn(
            k.dp[:, :, half(h)].reshape(3 * W, T), k.qkv[...].reshape(3 * W, D)
        ).astype(BF16)
        rs_start("zng", h, k.ngp, k.ngr)
    grads5(1)
    base = s.bases[2]
    for h in range(2):
        gather_wait("zn2g", h, k.n2g)
    n2_grad = k.n2g[...].astype(F32)
    gain2_grad = jnp.sum(n2_grad * k.u2[...], axis=0, keepdims=True)
    bias2_grad = jnp.sum(n2_grad, axis=0, keepdims=True)
    middle_grad = middle_backward(n2_grad, pl.ds(0, L))
    k.cot[...] = middle_grad
    k.gsrc[base : base + W, :] = mm_nn(k.att[t], middle_grad.astype(BF16)).astype(BF16)
    k.gsrc[base + W : base + 2 * W, :] = mm_nn(k.dp[0], k.normed[...]).astype(BF16)
    grads1(2)

    base = s.bases[3]
    k.gsrc[base : base + 2 * W, :] = mm_nn(k.dp[1:3].reshape(2 * W, L), k.normed[...]).astype(BF16)
    grads1(3)
    grads6(0)
    direct2(2)
    k.ngg[piece(0, t), :] = rs_sum("zng", 0, k.ngp, k.ngr).astype(BF16)
    gather_start("zngg", 0, k.ngg)
    direct2(3)
    grads6(1)
    k.ngg[piece(1, t), :] = rs_sum("zng", 1, k.ngp, k.ngr).astype(BF16)
    gather_start("zngg", 1, k.ngg)
    direct3(2)
    direct3(3)
    grads7(0)
    grads7(1)
    swap_wait("ent", every)
    k.ent_sum[...] = jnp.sum(k.ent[...], axis=0)
    ent_copy = pltpu.make_async_copy(k.ent_sum, o_ent, k.stores.at[6])
    ent_copy.start()
    gain1_grad = jnp.zeros((1, D), F32)
    bias1_grad = jnp.zeros((1, D), F32)
    lead_grad = jnp.zeros((s.leads, D), F32)
    for h in range(2):
        rows = half(h)
        gather_wait("zngg", h, k.ngg)
        n1_grad = k.ngg[rows, :].astype(F32)
        unit1 = k.u1[rows, :]
        gain1_grad += jnp.sum(n1_grad * unit1, axis=0, keepdims=True)
        bias1_grad += jnp.sum(n1_grad, axis=0, keepdims=True)
        hidden_grad = k.cot[rows, :] + norm_backward(n1_grad, unit1, k.r1[rows, :], row_of(k.gain1))
        k.patches[rows, :] = hidden_grad
        coarse = hidden_grad.astype(BF16)
        fine = (hidden_grad - coarse.astype(F32)).astype(BF16)
        hot = lead_hot[:, h * T : (h + 1) * T]
        lead_grad += mm_nn(hot, coarse) + mm_nn(hot, fine)
        if h == 0:
            direct6(2)
            direct6(3)
    k.vb[near[1]] = lead_grad.astype(BF16)
    swap_start("vb", near)
    hidden_copy = pltpu.make_async_copy(k.patches, o_hidden, k.stores.at[5])
    hidden_copy.start()
    lanes = D // 128
    packed = [
        x[:, 128 * i : 128 * (i + 1)]
        for x in (gain1_grad, bias1_grad, gain2_grad, bias2_grad)
        for i in range(lanes)
    ]
    packed.append(jnp.zeros((s.packed - 4 * lanes, 128), F32))
    k.vc[near[1]] = jnp.concatenate(packed, axis=0).astype(BF16)
    swap_start("vc", near)
    grads7(2)
    grads7(3)
    k.vb_sum[...] = swap_sum("vb")
    k.vc_sum[...] = swap_sum("vc")
    vb_copy = pltpu.make_async_copy(k.vb_sum, o_vb, k.stores.at[7])
    vc_copy = pltpu.make_async_copy(k.vc_sum, o_vc, k.stores.at[8])
    vb_copy.start()
    vc_copy.start()

    z_all("zmask", k.mask.at[pl.ds(0, nt - 1)]).wait_send()
    z_all("zgate", k.gatec.at[pl.ds(0, nt - 1)]).wait_send()
    z_all("zow", ow_all).wait_send()
    for name in ("zowy", "zowr", "zowq"):
        ow_copy(name, ow_all, sib).wait_send()
    for h in range(2):
        z_all("zatt", k.att.at[pl.ds(0, nt - 1), :, half(h)], h).wait_send()
        z_all("zda", k.datok.at[h, pl.ds(0, nt - 1)], h).wait_send()
    rs_finish("zff", k.ffr)
    gather_finish("zblk", k.blow)
    rs_finish("zn2", k.n2r)
    gather_finish("zn2g", k.n2g)
    rs_finish("zng", k.ngr)
    gather_finish("zngg", k.ngg)
    ag_finish("kv", lambda count: k.kv.at[pl.ds(0, count)])
    ag_finish("q", q_all)
    ag_finish("da0", da_all(0))
    ag_finish("da1", da_all(1))
    ag_finish("st", st_all)
    swap_finish("cnt", every)
    swap_finish("ent", every)
    for i in range(4):
        grads_store(i).wait()
    for copy in (block_copy, hidden_copy, ent_copy, vb_copy, vc_copy):
        copy.wait()


def last_kernel(
    s, cuts, block, hidden, grads, ent, vb, vc,
    o_block, o_hidden, o_qkv, o_out, o_up, o_down, o_pen, o_lead, o_g1, o_b1, o_g2, o_b2, o_gate,
    low, wide, low_block, wide_block, keep, load_sem, store_sem,
):
    outs = {"down": o_down, "up": o_up, "out": o_out, "q": o_qkv.at[0], "k": o_qkv.at[1], "v": o_qkv.at[2]}
    loads = [
        pltpu.make_async_copy(block, low_block, load_sem.at[0]),
        pltpu.make_async_copy(hidden, keep, load_sem.at[1]),
    ]
    stores = [
        pltpu.make_async_copy(wide_block, o_block, store_sem.at[0]),
        pltpu.make_async_copy(keep, o_hidden, store_sem.at[1]),
    ]
    for i, (row, name, start, size) in enumerate(cuts):
        rows = pl.ds(row, size)
        loads.append(pltpu.make_async_copy(grads.at[rows], low.at[rows], load_sem.at[i + 2]))
        stores.append(
            pltpu.make_async_copy(wide.at[rows], outs[name].at[pl.ds(start, size)], store_sem.at[i + 2])
        )
    gate_rows = pl.ds(s.bases[1] + s.D, 32)
    gate_load = pltpu.make_async_copy(grads.at[gate_rows], low.at[gate_rows], load_sem.at[len(cuts) + 2])
    for copy in loads + [gate_load]:
        copy.start()
    loads[0].wait()
    wide_block[...] = low_block[...].astype(F32)
    stores[0].start()
    loads[1].wait()
    stores[1].start()
    for i, (row, name, start, size) in enumerate(cuts):
        loads[i + 2].wait()
        rows = pl.ds(row, size)
        wide[rows, :] = low[rows, :].astype(F32)
        stores[i + 2].start()
    gate_load.wait()
    small = low[gate_rows, :].astype(F32)
    for e in range(3):
        o_gate[e] = small[8 * e : 8 * e + 4]
    o_pen[...] = ent[0:1, 0:1]
    o_lead[...] = vb[...]
    lanes = s.D // 128
    for i, out in enumerate((o_g1, o_b1, o_g2, o_b2)):
        for j in range(lanes):
            row = i * lanes + j
            out[128 * j : 128 * (j + 1)] = vc[row : row + 1, :].reshape(128)
    for copy in stores:
        copy.wait()


def local(
    nb,
    nt,
    patches,
    window_ids,
    lead_index,
    lead_table,
    attention_gain,
    attention_bias,
    query_key_value,
    out_weight,
    feedforward_gain,
    feedforward_bias,
    up_weight,
    down_weight,
    gate_head,
    pixel_mask,
    cotangent,
):
    L, D = patches.shape
    leads = lead_table.shape[0]
    W = out_weight.shape[0]
    F = up_weight.shape[1]
    s = dims_of(nb, nt, L, D, W, F, leads, L * nb * pixel_mask.shape[0] * nt)
    scratch = scratch_of(s)
    vm = pl.BlockSpec(memory_space=pltpu.VMEM)
    block, hidden, grads, ent, vb, vc = pl.pallas_call(
        partial(main_kernel, s, tuple(scratch)),
        out_shape=(
            jax.ShapeDtypeStruct((L, D), BF16),
            jax.ShapeDtypeStruct((L, D), F32),
            jax.ShapeDtypeStruct((s.rows, D), BF16),
            jax.ShapeDtypeStruct((8, 128), F32),
            jax.ShapeDtypeStruct((leads, D), F32),
            jax.ShapeDtypeStruct((s.packed, 128), F32),
        ),
        in_specs=[pl.BlockSpec(memory_space=pltpu.HBM)] * 15,
        out_specs=(pl.BlockSpec(memory_space=pl.ANY),) * 6,
        scratch_shapes=list(scratch.values()),
        compiler_params=pltpu.CompilerParams(
            collective_id=0,
            has_side_effects=True,
            vmem_limit_bytes=VMEM_LIMIT,
        ),
        cost_estimate=pl.CostEstimate(
            flops=2 * s.rows * D * L * 3 + 14 * L * nb * L * W, bytes_accessed=16 * 2**20, transcendentals=0
        ),
        name="block_step",
    )(
        patches,
        window_ids,
        lead_index,
        lead_table,
        attention_gain,
        attention_bias,
        jnp.transpose(query_key_value, (0, 2, 1)),
        out_weight,
        feedforward_gain,
        feedforward_bias,
        up_weight,
        down_weight,
        gate_head,
        pixel_mask,
        cotangent,
    )
    vec = jax.ShapeDtypeStruct((D,), F32)
    cuts = []
    first = s.bases[2]
    places = (
        ("down", 0, F),
        ("up", F, D),
        ("out", first, W),
        ("q", first + W, W),
        ("k", s.bases[3], W),
        ("v", s.bases[3] + W, W),
    )
    for name, row, size in places:
        for start in range(0, size, 256):
            cuts.append((row + start, name, start, min(256, size - start)))
    hbm = pl.BlockSpec(memory_space=pl.ANY)
    wide, high, qkv_grad, out_grad, up_grad, down_grad, pen, lead, g1, b1, g2, b2, gates = pl.pallas_call(
        partial(last_kernel, s, cuts),
        out_shape=(
            jax.ShapeDtypeStruct((L, D), F32),
            jax.ShapeDtypeStruct((L, D), F32),
            jax.ShapeDtypeStruct((3, W, D), F32),
            jax.ShapeDtypeStruct((W, D), F32),
            jax.ShapeDtypeStruct((D, F), F32),
            jax.ShapeDtypeStruct((F, D), F32),
            jax.ShapeDtypeStruct((1, 1), F32),
            jax.ShapeDtypeStruct((leads, D), F32),
            vec,
            vec,
            vec,
            vec,
            jax.ShapeDtypeStruct(gate_head.shape, F32),
        ),
        in_specs=[hbm] * 3 + [vm] * 3,
        out_specs=(hbm,) * 6 + (vm,) * 7,
        scratch_shapes=[
            pltpu.VMEM((s.rows, D), BF16),
            pltpu.VMEM((s.rows, D), F32),
            pltpu.VMEM((L, D), BF16),
            pltpu.VMEM((L, D), F32),
            pltpu.VMEM((L, D), F32),
            pltpu.SemaphoreType.DMA((len(cuts) + 3,)),
            pltpu.SemaphoreType.DMA((len(cuts) + 2,)),
        ],
        compiler_params=pltpu.CompilerParams(vmem_limit_bytes=VMEM_LIMIT),
        name="write_out",
    )(block, hidden, grads, ent, vb, vc)
    return (
        wide,
        pen.reshape(()),
        high,
        lead,
        g1,
        b1,
        jnp.transpose(qkv_grad, (0, 2, 1)),
        out_grad,
        g2,
        b2,
        up_grad,
        down_grad,
        gates,
    )


def solution(mesh):
    in_specs = (
        P("blk", None),
        P(),
        P("blk"),
        P(),
        P(),
        P(),
        P(None, None, "tp"),
        P("tp", None),
        P(),
        P(),
        P(None, "tp"),
        P("tp", None),
        P(None, "tp", None),
        P("tp", "blk"),
        P("blk", None),
    )
    out_specs = (
        P("blk", None),
        P(),
        P("blk", None),
        P(),
        P(),
        P(),
        P(None, None, "tp"),
        P("tp", None),
        P(),
        P(),
        P(None, "tp"),
        P("tp", None),
        P(None, "tp", None),
    )
    return jax.shard_map(
        partial(local, mesh.shape["blk"], mesh.shape["tp"]),
        mesh=mesh,
        in_specs=in_specs,
        out_specs=out_specs,
        check_vma=False,
    )
```

```python
from functools import partial
from types import SimpleNamespace

import jax
import jax.numpy as jnp
from jax import lax
from jax.experimental import pallas as pl
from jax.experimental.pallas import tpu as pltpu
from jax.sharding import PartitionSpec as P

HEAD_DIM = 64
EPS = 1e-05
MASKED = -1e30
SCALE = HEAD_DIM ** (-0.5)
GROUP = 8
F32 = jnp.float32
BF16 = jnp.bfloat16
MESH = pl.DeviceIdType.MESH
VMEM_LIMIT = 61 * 2**20
INV_SQRT2 = 0.7071067811865476
INV_SQRT_2PI = 0.3989422804014327


def dot(a, b, ca, cb):
    return lax.dot_general(a, b, (((ca,), (cb,)), ((), ())), preferred_element_type=F32)


def mm_nn(a, b):
    return dot(a, b, 1, 0)


def mm_nt(a, b):
    return dot(a, b, 1, 1)


def mm_tn(a, b):
    return dot(a, b, 0, 0)


def norm_stats(values):
    mean = jnp.mean(values, axis=-1, keepdims=True)
    centered = values - mean
    inverse = lax.rsqrt(jnp.mean(centered * centered, axis=-1, keepdims=True) + EPS)
    return centered * inverse, inverse


def norm_backward(incoming, unit_rows, inverse, gain):
    scaled = incoming * gain
    return inverse * (
        scaled
        - jnp.mean(scaled, axis=-1, keepdims=True)
        - unit_rows * jnp.mean(scaled * unit_rows, axis=-1, keepdims=True)
    )


def row_of(ref):
    return ref[...].reshape(1, ref.shape[0])


def total(x):
    return jnp.sum(jnp.sum(x, axis=0, keepdims=True), axis=1, keepdims=True)


def dims_of(nb, nt, tokens, width, local_width, hidden, leads, pixels):
    s = SimpleNamespace(nb=nb, nt=nt, L=tokens, D=width, W=local_width, F=hidden, leads=leads)
    s.H = local_width // HEAD_DIM
    s.T = tokens // 2
    s.R = s.T // nt
    s.half = nb // 2
    s.groups = nb // GROUP
    s.pixels = pixels
    s.sizes = (hidden, width + 128, local_width * 2, local_width * 2)
    s.bases = tuple(sum(s.sizes[:i]) for i in range(4))
    s.rows = sum(s.sizes)
    s.packed = (4 * width // 128 + 15) // 16 * 16
    return s


def scratch_of(s):
    L, D, W, F, nb, nt, R = s.L, s.D, s.W, s.F, s.nb, s.nt, s.R
    v = pltpu.VMEM
    out = {
        "patches": v((L, D), F32),
        "windows": v((nb * L,), jnp.int32),
        "lead_index": v((L,), jnp.int32),
        "table": v((s.leads, D), BF16),
        "gain1": v((D,), F32),
        "bias1": v((D,), F32),
        "gain2": v((D,), F32),
        "bias2": v((D,), F32),
        "pix": v((4, L), jnp.int32),
        "head": v((3, 4, D), BF16),
        "ids": v((nb, L), F32),
        "qkv": v((3, W, D), BF16),
        "ow": v((nt, W, D), BF16),
        "up": v((D, F), BF16),
        "down": v((F, D), BF16),
        "cot": v((L, D), F32),
        "gatec": v((nt, 16, D), BF16),
        "gate": v((nt * 32, D), BF16),
        "mask": v((nt, 8, L), F32),
        "cnt": v((nb, 8, 128), F32),
        "u1": v((L, D), F32),
        "r1": v((L, 1), F32),
        "normed": v((L, D), BF16),
        "kv": v((nb, 2 * W, L), BF16),
        "qd": v((nb, 2 * W, L), BF16),
        "st": v((nb, 8, L), F32),
        "m": v((8, L), F32),
        "l": v((8, L), F32),
        "acc": v((W, L), F32),
        "att": v((nt, W, L), BF16),
        "mid": v((L, D), F32),
        "u2": v((L, D), F32),
        "r2": v((L, 1), F32),
        "n2low": v((L, D), BF16),
        "upw": v((L, F), F32),
        "actlow": v((L, F), BF16),
        "ffp": v((L, D), BF16),
        "ffr": v((2, nt - 1, R, D), BF16),
        "blow": v((L, D), BF16),
        "lg": v((nt * 32, L), BF16),
        "oglow": v((L, D), BF16),
        "ug": v((L, F), BF16),
        "n2p": v((L, D), BF16),
        "n2r": v((2, nt - 1, R, D), BF16),
        "n2g": v((L, D), BF16),
        "dasrc": v((2, nt, R, W), BF16),
        "datok": v((2, nt, R, W), BF16),
        "dq": v((W, L), F32),
        "dk": v((W, L), F32),
        "dv": v((W, L), F32),
        "dp": v((3, W, L), BF16),
        "ngp": v((L, D), BF16),
        "ngr": v((2, nt - 1, R, D), BF16),
        "ngg": v((L, D), BF16),
        "vb": v((GROUP, s.leads, D), BF16),
        "vc": v((GROUP, s.packed, 128), BF16),
        "ent": v((nb, 8, 128), F32),
        "ent_sum": v((8, 128), F32),
        "vb_sum": v((s.leads, D), F32),
        "vc_sum": v((s.packed, 128), F32),
        "gsrc": v((s.rows, D), BF16),
        "gout": v((s.rows, D), BF16),
    }
    dma = pltpu.SemaphoreType.DMA
    out["loads"] = dma((15,))
    out["stores"] = dma((9,))
    for name in ("zmask", "zgate", "zow", "zowy", "zowr", "zowq"):
        out[name + "_s"] = dma((1,))
        out[name + "_r"] = dma((1,))
    for name in ("zatt", "zff", "zblk", "zn2", "zn2g", "zda", "zng", "zngg"):
        out[name + "_s"] = dma((2,))
        out[name + "_r"] = dma((2,))
    for name in ("kv", "q", "da0", "da1", "st"):
        count = s.half if name == "kv" else 2
        out[name + "_s"] = dma((1,))
        out[name + "_r"] = dma((count,))
        out[name + "_rs"] = dma((1,))
        out[name + "_rr"] = dma((count,))
    for name in ("cnt", "ent", "vb", "vc"):
        out[name + "_s"] = dma((1,))
        out[name + "_r"] = dma((1,))
    if s.groups > 1:
        out["vb2"] = v((s.groups, s.leads, D), BF16)
        out["vc2"] = v((s.groups, s.packed, 128), BF16)
        for name in ("vb2", "vc2"):
            out[name + "_s"] = dma((1,))
            out[name + "_r"] = dma((1,))
    for i, rows in enumerate(s.sizes):
        hr = rows // 2
        qr = hr // 4
        out["core%d" % i] = v((hr, D), BF16)
        out["quart%d" % i] = v((3, qr, D), BF16)
        if s.groups > 1:
            out["sup%d" % i] = v((s.groups, qr, D), BF16)
            out["sup%d_s" % i] = dma((1,))
            out["sup%d_r" % i] = dma((1,))
        out["gs%d" % i] = dma((6 if i < 2 else 4,))
        out["gr%d" % i] = dma((6 if i < 2 else 4,))
    return out


def main_kernel(s, names, *refs):
    (
        patches,
        windows_in,
        leads_in,
        table,
        gain1,
        bias1,
        qkv,
        out_weight,
        gain2,
        bias2,
        up,
        down,
        gate,
        pixel_mask,
        cotangent,
        o_block,
        o_hidden,
        o_grads,
        o_ent,
        o_vb,
        o_vc,
    ) = refs[:21]
    k = SimpleNamespace(**dict(zip(names, refs[21:])))
    sem = vars(k)
    L, D, W, F, H, T, R, nb, nt = s.L, s.D, s.W, s.F, s.H, s.T, s.R, s.nb, s.nt
    b = lax.axis_index("blk")
    t = lax.axis_index("tp")
    core = lax.rem(b, 2)
    pair = b // 2
    sib = b + 1 - 2 * core

    def z_peer(j):
        return lax.rem(t + j, nt)

    def z_from(j):
        return lax.rem(t + nt - j, nt)

    def remote(src, dst, send, recv, device):
        return pltpu.make_async_remote_copy(
            src, dst, send, recv, device_id=device, device_id_type=MESH
        )

    def z_copy(name, j, src, dst, h=0):
        return remote(src, dst, sem[name + "_s"].at[h], sem[name + "_r"].at[h], (b, z_peer(j)))

    def z_all(name, ref, h=0):
        return z_copy(name, 1, ref, ref, h)

    def half(h):
        return pl.ds(h * T, T)

    def piece(h, tt):
        return pl.ds(pl.multiple_of(h * T + tt * R, R), R)

    def ag_copy(name, at, i, dst_band):
        slot = i if name == "kv" else 0
        return remote(at(b), at(b), sem[name + "_s"].at[0], sem[name + "_r"].at[slot], (dst_band, t))

    def relay_copy(name, at, i, band):
        slot = i if name == "kv" or isinstance(i, int) else 1
        return remote(at(band), at(band), sem[name + "_rs"].at[0], sem[name + "_rr"].at[slot], (sib, t))

    def band_same(i):
        return lax.rem(b + nb - 2 * i, nb)

    def band_sib(i):
        return lax.rem(sib + nb - 2 * i, nb)

    def ag_start(name, at):
        @pl.loop(1, s.half)
        def _(i):
            ag_copy(name, at, i, lax.rem(b + 2 * i, nb)).start()

        relay_copy(name, at, 0, b).start()

    def ag_wait(name, at, i):
        band = band_same(i)
        remote(at(band), at(band), sem[name + "_s"].at[0], sem[name + "_r"].at[i], (sib, t)).wait_recv()

    def ag_relay(name, at, i):
        relay_copy(name, at, i, band_same(i)).start()

    def ag_wait_relay(name, at, i):
        relay_copy(name, at, i, band_sib(i)).wait_recv()

    def ag_pass_on(name, at, all_at):
        ref = all_at(s.half - 1)
        remote(ref, ref, sem[name + "_s"].at[0], sem[name + "_r"].at[0], (sib, t)).wait_recv()

        @pl.loop(1, s.half)
        def _(i):
            ag_relay(name, at, i)

    def ag_arrived(name, all_at):
        ref = all_at(s.half - 1)
        remote(ref, ref, sem[name + "_rs"].at[0], sem[name + "_rr"].at[1], (sib, t)).wait_recv()

    def ag_finish(name, all_at):
        ref = all_at(s.half - 1)
        remote(ref, ref, sem[name + "_s"].at[0], sem[name + "_r"].at[0], (sib, t)).wait_send()
        ref = all_at(s.half)
        remote(ref, ref, sem[name + "_rs"].at[0], sem[name + "_rr"].at[0], (sib, t)).wait_send()

    every = (nb, b, lambda i: i)
    near = (GROUP, lax.rem(b, GROUP), lambda i: b // GROUP * GROUP + i)
    far = (s.groups, b // GROUP, lambda i: i * GROUP + lax.rem(b, GROUP))

    def swap_copy(name, members, ref, to):
        return remote(ref, ref, sem[name + "_s"].at[0], sem[name + "_r"].at[0], (members[2](to), t))

    def swap_start(name, members):
        count, me, _ = members

        @pl.loop(1, count)
        def _(i):
            swap_copy(name, members, sem[name].at[me], lax.rem(me + i, count)).start()

    def swap_all(name, members):
        return swap_copy(name, members, sem[name].at[pl.ds(0, members[0] - 1)], 0)

    def swap_wait(name, members):
        swap_all(name, members).wait_recv()

    def swap_finish(name, members):
        swap_all(name, members).wait_send()

    def slots_sum(ref, count):
        return lax.fori_loop(
            1, count, lambda i, acc: acc + ref[i].astype(F32), ref[0].astype(F32)
        )

    def swap_sum(name):
        swap_wait(name, near)
        out = slots_sum(sem[name], GROUP)
        if s.groups > 1:
            sem[name + "2"][far[1]] = out.astype(BF16)
            swap_start(name + "2", far)
            swap_wait(name + "2", far)
            out = slots_sum(sem[name + "2"], s.groups)
            swap_finish(name + "2", far)
        swap_finish(name, near)
        return out

    def rs_start(name, h, part, recv):
        for j in range(1, nt):
            z_copy(name, j, part.at[piece(h, z_peer(j))], recv.at[h, j - 1], h).start()

    def rs_sum(name, h, part, recv):
        z_all(name, recv.at[h], h).wait_recv()
        acc = part[piece(h, t), :].astype(F32)
        for j in range(1, nt):
            acc = acc + recv[h, j - 1].astype(F32)
        return acc

    def rs_finish(name, recv):
        for h in range(2):
            z_all(name, recv.at[h], h).wait_send()

    def gather_start(name, h, ref):
        for j in range(1, nt):
            z_copy(name, j, ref.at[piece(h, t)], ref.at[piece(h, t)], h).start()

    def gather_all(name, h, ref):
        return z_all(name, ref.at[pl.ds(h * T, (nt - 1) * R)], h)

    def gather_wait(name, h, ref):
        gather_all(name, h, ref).wait_recv()

    def gather_finish(name, ref):
        for h in range(2):
            gather_all(name, h, ref).wait_send()

    quarter = lax.rem(pair, 4)
    first_pair = pair - quarter
    group = pair // 4
    low_peer = quarter + 1 - 2 * lax.rem(quarter, 2)
    high_peer = lax.rem(quarter + 2, 4)
    first = low_peer * (1 - core) + high_peer * core
    second = low_peer * core + high_peer * (1 - core)
    across = lax.rem(low_peer + 2, 4)

    def g_rows(i, q):
        hr = s.sizes[i] // 2
        qr = hr // 4
        return pl.ds(pl.multiple_of(s.bases[i] + core * hr + q * qr, 16), qr)

    def g_half(i, c):
        hr = s.sizes[i] // 2
        return pl.ds(pl.multiple_of(s.bases[i] + c * hr, 16), hr)

    def q_rows(i, q):
        qr = s.sizes[i] // 8
        return pl.ds(pl.multiple_of(q * qr, 16), qr)

    def g_copy(i, slot, src, dst, q):
        dev = ((first_pair + q) * 2 + core, t)
        return remote(src, dst, sem["gs%d" % i].at[slot], sem["gr%d" % i].at[slot], dev)

    def sib_copy(i, slot, src, dst):
        return remote(src, dst, sem["gs%d" % i].at[slot], sem["gr%d" % i].at[slot], (sib, t))

    def c1_copy(i):
        return sib_copy(i, 0, k.gsrc.at[g_half(i, 1 - core)], sem["core%d" % i])

    def rs_copies(i):
        hs = sem["core%d" % i]
        land = sem["quart%d" % i]
        return (
            g_copy(i, 1, hs.at[q_rows(i, first)], land.at[0], first),
            g_copy(i, 1, hs.at[q_rows(i, across)], land.at[1], first),
        )

    def land_all(i, slot, count):
        ref = sem["quart%d" % i].at[pl.ds(0, count)]
        return g_copy(i, slot, ref, ref, first)

    def out_all(i, slot, count):
        ref = k.gout.at[pl.ds(s.bases[i], count * (s.sizes[i] // 8))]
        return g_copy(i, slot, ref, ref, first)

    def rs_copy_b(i):
        return g_copy(i, 2, sem["core%d" % i].at[q_rows(i, second)], sem["quart%d" % i].at[2], second)

    def out_copy(i, slot, q, to):
        rows = g_rows(i, q)
        return g_copy(i, slot, k.gout.at[rows], k.gout.at[rows], to)

    def c2_copy(i, c):
        rows = g_half(i, c)
        return sib_copy(i, 3, k.gout.at[rows], k.gout.at[rows])

    def across_groups(i, acc):
        if s.groups > 1:
            ref = sem["sup%d" % i]
            ref[group] = acc.astype(BF16)

            def copy(j, at):
                dev = ((lax.rem(group + j, s.groups) * 4 + quarter) * 2 + core, t)
                return remote(at, at, sem["sup%d_s" % i].at[0], sem["sup%d_r" % i].at[0], dev)

            for j in range(1, s.groups):
                copy(j, ref.at[group]).start()
            copy(1, ref.at[pl.ds(0, s.groups - 1)]).wait()
            acc = ref[0].astype(F32)
            for g in range(1, s.groups):
                acc = acc + ref[g].astype(F32)
        return acc.astype(BF16)

    def grads1(i):
        c1_copy(i).start()

    def pair_sum(i):
        c1_copy(i).wait()
        hs = sem["core%d" % i]
        hs[...] = (k.gsrc[g_half(i, core), :].astype(F32) + hs[...].astype(F32)).astype(BF16)

    def grads2(i):
        pair_sum(i)
        for copy in rs_copies(i):
            copy.start()

    def grads3(i):
        land_all(i, 1, 2).wait()
        hs = sem["core%d" % i]
        rows = q_rows(i, second)
        hs[rows, :] = (hs[rows, :].astype(F32) + sem["quart%d" % i][1].astype(F32)).astype(BF16)
        rs_copy_b(i).start()

    def grads4(i):
        rs_copy_b(i).wait()
        land = sem["quart%d" % i]
        acc = sem["core%d" % i][q_rows(i, quarter), :].astype(F32)
        acc = acc + land[0].astype(F32) + land[2].astype(F32)
        k.gout[g_rows(i, quarter), :] = across_groups(i, acc)
        out_copy(i, 4, quarter, second).start()

    def grads5(i):
        out_copy(i, 4, quarter, second).wait_send()
        out_copy(i, 4, second, second).wait_recv()
        out_copy(i, 5, quarter, first).start()
        out_copy(i, 5, second, first).start()

    def grads6(i):
        out_all(i, 5, 2).wait()
        c2_copy(i, core).start()

    def q_peer(j):
        return lax.rem(quarter + j, 4)

    def direct2(i):
        pair_sum(i)
        for j in range(1, 4):
            src = sem["core%d" % i].at[q_rows(i, q_peer(j))]
            g_copy(i, 1, src, sem["quart%d" % i].at[j - 1], q_peer(j)).start()

    def direct3(i):
        land_all(i, 1, 3).wait()
        acc = sem["core%d" % i][q_rows(i, quarter), :].astype(F32)
        for j in range(3):
            acc = acc + sem["quart%d" % i][j].astype(F32)
        k.gout[g_rows(i, quarter), :] = across_groups(i, acc)
        for j in range(1, 4):
            out_copy(i, 2, quarter, q_peer(j)).start()

    def direct6(i):
        out_all(i, 2, 3).wait()
        c2_copy(i, core).start()

    def grads_store(i):
        rows = pl.ds(s.bases[i], s.sizes[i])
        return pltpu.make_async_copy(k.gout.at[rows], o_grads.at[rows], k.stores.at[i])

    def grads7(i):
        c2_copy(i, core).wait_send()
        c2_copy(i, 1 - core).wait_recv()
        grads_store(i).start()

    def load(i, src, dst):
        return pltpu.make_async_copy(src, dst, k.loads.at[i])

    first_loads = [
        load(0, patches, k.patches),
        load(1, leads_in, k.lead_index),
        load(2, table, k.table),
        load(3, gain1, k.gain1),
        load(4, bias1, k.bias1),
    ]
    ow_load = load(5, out_weight, k.ow.at[t])
    small_loads = [
        load(6, pixel_mask, k.pix),
        load(7, gate, k.head),
        load(8, windows_in, k.windows),
    ]
    qkv_load = load(9, qkv, k.qkv)
    late_loads = [
        load(10, gain2, k.gain2),
        load(11, bias2, k.bias2),
        load(12, up, k.up),
        load(13, down, k.down),
        load(14, cotangent, k.cot),
    ]
    for copy in first_loads + small_loads + [qkv_load, ow_load]:
        copy.start()
    barrier = pltpu.get_barrier_semaphore()

    @pl.loop(1, nb)
    def _(i):
        pl.semaphore_signal(barrier, inc=1, device_id=(lax.rem(b + i, nb), t), device_id_type=MESH)

    for j in range(1, nt):
        pl.semaphore_signal(barrier, inc=1, device_id=(b, z_peer(j)), device_id_type=MESH)

    for copy in first_loads:
        copy.wait()
    lead_hot = lax.broadcasted_iota(jnp.int32, (s.leads, L), 0) == row_of(k.lead_index)
    lead_hot = lead_hot.astype(F32).astype(BF16)
    hidden = k.patches[...] + mm_tn(lead_hot, k.table[...])
    unit1, inverse1 = norm_stats(hidden)
    k.u1[...] = unit1
    k.r1[...] = inverse1
    k.mid[...] = hidden
    k.normed[...] = (unit1 * row_of(k.gain1) + row_of(k.bias1)).astype(BF16)
    for copy in small_loads:
        copy.wait()
    compact = [k.head[e].astype(F32) for e in range(3)] + [jnp.zeros((4, D), F32)]
    k.gatec[t] = jnp.concatenate(compact, axis=0).astype(BF16)
    k.mask[t] = jnp.concatenate([k.pix[...].astype(F32), jnp.zeros((4, L), F32)], axis=0)
    part = W // 4
    upper = quarter // 2

    def ow_part(tt, c, u):
        return k.ow.at[tt, pl.ds(pl.multiple_of((c + 2 * u) * part, part), part)]

    def ow_copy(name, at, dev):
        return remote(at, at, sem[name + "_s"].at[0], sem[name + "_r"].at[0], (dev, t))

    ow_all = k.ow.at[pl.ds(0, nt - 1), pl.ds(0, part)]
    high_dev = (first_pair + high_peer) * 2 + core

    qkv_load.wait()

    def project(c):
        return mm_nt(k.qkv[c], k.normed[...])

    k.kv[b, 0:W, :] = project(1).astype(BF16)
    k.kv[b, W : 2 * W, :] = project(2).astype(BF16)
    ow_load.wait()
    pl.semaphore_wait(barrier, nb - 1 + nt - 1)

    def kv_at(band):
        return k.kv.at[band]

    ag_start("kv", kv_at)
    for j in range(1, nt):
        z_copy("zmask", j, k.mask.at[t], k.mask.at[t]).start()
        z_copy("zow", j, ow_part(t, core, upper), ow_part(t, core, upper)).start()
        z_copy("zgate", j, k.gatec.at[t], k.gatec.at[t]).start()
    for copy in late_loads:
        copy.start()
    k.qd[b, 0:W, :] = (project(0).astype(BF16).astype(F32) * SCALE).astype(BF16)

    k.ids[...] = k.windows[...].reshape(nb, L).astype(F32)

    def id_row(band):
        return k.ids[pl.ds(band, 1), :]

    def id_column(band):
        return jnp.transpose(jnp.broadcast_to(id_row(band), (128, L)))[:, 0:1]

    def head(h):
        return pl.ds(h * HEAD_DIM, HEAD_DIM)

    def value_head(h):
        return pl.ds(W + h * HEAD_DIM, HEAD_DIM)

    k.m[...] = jnp.full((8, L), MASKED, F32)
    k.l[...] = jnp.zeros((8, L), F32)
    k.acc[...] = jnp.zeros((W, L), F32)

    def forward_bands(bands):
        tiles = [(h, i) for h in range(H) for i in range(len(bands))]
        allowed = [id_column(band) == id_row(b) for band in bands]
        scores = {
            (h, i): jnp.where(
                allowed[i], mm_tn(k.kv[bands[i], head(h), :], k.qd[b, head(h), :]), MASKED
            )
            for h, i in tiles
        }
        old_high = [k.m[h : h + 1, :] for h in range(H)]
        sums = [k.l[h : h + 1, :] for h in range(H)]
        outs = [k.acc[head(h), :] for h in range(H)]
        high = list(old_high)
        for h, i in tiles:
            high[h] = jnp.maximum(high[h], jnp.max(scores[h, i], axis=0, keepdims=True))
        weights = {(h, i): jnp.exp(scores[h, i] - high[h]) for h, i in tiles}
        factor = [jnp.exp(x - y) for x, y in zip(old_high, high)]
        outs = [x * f for x, f in zip(outs, factor)]
        sums = [x * f for x, f in zip(sums, factor)]
        for h, i in tiles:
            outs[h] += mm_nn(k.kv[bands[i], value_head(h), :], weights[h, i].astype(BF16))
            sums[h] += jnp.sum(weights[h, i], axis=0, keepdims=True)
        for h in range(H):
            k.m[h : h + 1, :] = high[h]
            k.l[h : h + 1, :] = sums[h]
            k.acc[head(h), :] = outs[h]

    def ow_pass_on():
        z_all("zow", ow_all).wait_recv()
        for j in range(1, nt):
            at = ow_part(z_from(j), core, upper)
            ow_copy("zowy", at, high_dev).start()
            ow_copy("zowr", at, sib).start()

    def ow_pass_second():
        ow_copy("zowy", ow_all, high_dev).wait_recv()
        for j in range(1, nt):
            ow_copy("zowq", ow_part(z_from(j), core, 1 - upper), sib).start()

    ag_wait_relay("kv", kv_at, 0)
    forward_bands([b, sib])
    z_all("zmask", k.mask.at[pl.ds(0, nt - 1)]).wait_recv()
    k.cnt[b] = jnp.broadcast_to(total(jnp.sum(k.mask[...], axis=0)), (8, 128))
    swap_start("cnt", every)

    @pl.loop(1, s.half)
    def _(i):
        ag_wait("kv", kv_at, i)
        ag_relay("kv", kv_at, i)

    ow_pass_on()

    @pl.loop(0, s.half // 2 - 1)
    def _(i):
        forward_bands([band_same(2 * i + 1), band_same(2 * i + 2)])

    ag_wait_relay("kv", kv_at, 1)
    forward_bands([band_same(s.half - 1), band_sib(1)])

    @pl.loop(1, s.half // 2)
    def _(i):
        ag_wait_relay("kv", kv_at, 2 * i)
        ag_wait_relay("kv", kv_at, 2 * i + 1)
        forward_bands([band_sib(2 * i), band_sib(2 * i + 1)])

    for h in range(H):
        att = k.acc[head(h), :] / k.l[h : h + 1, :]
        k.acc[head(h), :] = att
        k.att[t, head(h), :] = att.astype(BF16)
        k.st[b, h : h + 1, :] = k.m[h : h + 1, :] + jnp.log(k.l[h : h + 1, :])

    def att_half(tt, h):
        return k.att.at[tt, :, half(h)]

    for h in range(2):
        for j in range(1, nt):
            z_copy("zatt", j, att_half(t, h), att_half(t, h), h).start()

    def q_at(band):
        return k.qd.at[band, pl.ds(0, W)]

    def da_at(h):
        return lambda band: k.qd.at[band, pl.ds(W, W), half(h)]

    def st_at(band):
        return k.st.at[band]

    def q_all(count):
        return k.qd.at[pl.ds(0, count), pl.ds(0, W)]

    def da_all(h):
        return lambda count: k.qd.at[pl.ds(0, count), pl.ds(W, W), half(h)]

    def st_all(count):
        return k.st.at[pl.ds(0, count)]

    ag_start("q", q_at)
    ow_pass_second()
    for copy in late_loads:
        copy.wait()
    ow_copy("zowr", ow_all, sib).wait_recv()
    ow_copy("zowq", ow_all, sib).wait_recv()

    for h in range(2):
        z_all("zatt", k.att.at[pl.ds(0, nt - 1), :, half(h)], h).wait_recv()
        rows = half(h)
        middle = k.mid[rows, :] + mm_tn(
            k.att[:, :, half(h)].reshape(nt * W, T), k.ow[...].reshape(nt * W, D)
        )
        k.mid[rows, :] = middle
        unit2, inverse2 = norm_stats(middle)
        k.u2[rows, :] = unit2
        k.r2[rows, :] = inverse2
        k.n2low[rows, :] = (unit2 * row_of(k.gain2) + row_of(k.bias2)).astype(BF16)
        upward = mm_nn(k.n2low[rows, :], k.up[...])
        k.upw[rows, :] = upward
        k.actlow[rows, :] = (0.5 * upward * (1.0 + lax.erf(upward * INV_SQRT2))).astype(BF16)
        k.ffp[rows, :] = mm_nn(k.actlow[rows, :], k.down[...]).astype(BF16)
        rs_start("zff", h, k.ffp, k.ffr)
    upward = k.upw[...]
    k.upw[...] = 0.5 * (1.0 + lax.erf(upward * INV_SQRT2)) + upward * (
        jnp.exp(-0.5 * upward * upward) * INV_SQRT_2PI
    )
    z_all("zgate", k.gatec.at[pl.ds(0, nt - 1)]).wait_recv()
    for tt in range(nt):
        x = k.gatec[tt].astype(F32)
        pad = jnp.zeros((4, D), F32)
        parts = []
        for e in range(3):
            parts += [x[4 * e : 4 * e + 4], pad]
        k.gate[tt * 32 : (tt + 1) * 32, :] = jnp.concatenate(parts + [pad, pad], axis=0).astype(BF16)
    swap_wait("cnt", every)
    pixel_count = jnp.sum(k.cnt[...], axis=0)[0:1, 0:1]
    for h in range(2):
        block_piece = k.mid[piece(h, t), :] + rs_sum("zff", h, k.ffp, k.ffr)
        k.blow[piece(h, t), :] = block_piece.astype(BF16)
        gather_start("zblk", h, k.blow)

    ag_pass_on("q", q_at, q_all)

    entropy_sum = jnp.zeros((1, 1), F32)
    for h in range(2):
        rows = half(h)
        gather_wait("zblk", h, k.blow)
        logits = mm_nt(k.gate[...], k.blow[rows, :]).reshape(nt, 4, 8, T)
        parts = [logits[:, e] for e in range(3)]
        high = jnp.maximum(jnp.maximum(parts[0], parts[1]), parts[2])
        logs = jnp.log(sum(jnp.exp(x - high) for x in parts))
        log_probs = [x - high - logs for x in parts]
        probs = [jnp.exp(x) for x in log_probs]
        entropy = -sum(p * x for p, x in zip(probs, log_probs))
        mask = k.mask[:, :, half(h)]
        entropy_sum += total(jnp.sum(mask * entropy, axis=0))
        weight = mask * (float(s.pixels) / pixel_count)[None]
        grads = [-p * (x + entropy) * weight for p, x in zip(probs, log_probs)]
        grads.append(jnp.zeros((nt, 8, T), F32))
        k.lg[:, half(h)] = jnp.stack(grads, axis=1).reshape(nt * 32, T).astype(BF16)
        out_grad = k.cot[rows, :] + mm_tn(k.lg[:, half(h)], k.gate[...])
        k.cot[rows, :] = out_grad
        k.oglow[rows, :] = out_grad.astype(BF16)
        if h == 1:
            k.gsrc[0:F, :] = mm_tn(k.actlow[...], k.oglow[...]).astype(BF16)
            grads1(0)
        k.ug[rows, :] = (mm_nt(k.oglow[rows, :], k.down[...]) * k.upw[rows, :]).astype(BF16)
        k.n2p[rows, :] = mm_nt(k.ug[rows, :], k.up[...]).astype(BF16)
        rs_start("zn2", h, k.n2p, k.n2r)
    block_copy = pltpu.make_async_copy(k.blow, o_block, k.stores.at[4])
    block_copy.start()
    k.gsrc[F : F + D, :] = mm_tn(k.n2low[...], k.ug[...]).astype(BF16)
    own_lg = k.lg[pl.ds(pl.multiple_of(t * 32, 32), 32), :]
    base = s.bases[1] + D
    k.gsrc[base : base + 32, :] = mm_nn(own_lg, k.blow[...]).astype(BF16)
    k.gsrc[base + 32 : base + 128, :] = jnp.zeros((96, D), BF16)
    grads1(1)
    k.ent[b] = jnp.broadcast_to(entropy_sum / pixel_count, (8, 128))
    swap_start("ent", every)

    def middle_backward(n2_grad, rows):
        return k.cot[rows, :] + norm_backward(n2_grad, k.u2[rows, :], k.r2[rows, :], row_of(k.gain2))

    def attended_exchange(h):
        rows = piece(h, t)
        n2_low = rs_sum("zn2", h, k.n2p, k.n2r).astype(BF16)
        k.n2g[rows, :] = n2_low
        low_piece = middle_backward(n2_low.astype(F32), rows).astype(BF16)
        for tt in range(nt):
            k.dasrc[h, tt] = mm_nt(low_piece, k.ow[tt]).astype(BF16)
        for j in range(1, nt):
            z_copy("zda", j, k.dasrc.at[h, z_peer(j)], k.datok.at[h, t], h).start()
        k.datok[h, t] = k.dasrc[h, t]

    def attended_arrived(h):
        z_all("zda", k.datok.at[h, pl.ds(0, nt - 1)], h).wait_recv()
        att_grad = jnp.transpose(k.datok[h].reshape(T, W).astype(F32)).astype(BF16)
        k.qd[b, W : 2 * W, half(h)] = att_grad
        ag_start("da%d" % h, da_at(h))
        weighted = att_grad.astype(F32) * k.acc[:, half(h)]
        for i in range(H):
            k.st[b, H + i : H + i + 1, half(h)] = jnp.sum(
                weighted[i * HEAD_DIM : (i + 1) * HEAD_DIM], axis=0, keepdims=True
            )

    grads2(0)
    attended_exchange(0)
    grads2(1)
    attended_exchange(1)
    attended_arrived(0)
    attended_arrived(1)
    ag_start("st", st_at)
    for h in range(2):
        gather_start("zn2g", h, k.n2g)
    grads3(0)
    grads3(1)
    k.dq[...] = jnp.zeros((W, L), F32)
    k.dk[...] = jnp.zeros((W, L), F32)
    k.dv[...] = jnp.zeros((W, L), F32)
    my_column = id_column(b)

    def score_grads(allowed, scores, dots, stats):
        probs = {
            (h, i): jnp.exp(jnp.where(allowed[i], x, MASKED) - stats[i][h : h + 1])
            for (h, i), x in scores.items()
        }
        grads = {
            (h, i): (x * (dots[h, i] - stats[i][H + h : H + h + 1])).astype(BF16)
            for (h, i), x in probs.items()
        }
        return probs, grads

    @pl.loop(0, s.half)
    def _(step):
        bands = [2 * step, 2 * step + 1]
        tiles = [(h, i) for h in range(H) for i in range(2)]
        allowed = [id_column(band) == id_row(b) for band in bands]
        scores = {(h, i): mm_tn(k.kv[bands[i], head(h), :], k.qd[b, head(h), :]) for h, i in tiles}
        dots = {
            (h, i): mm_tn(k.kv[bands[i], value_head(h), :], k.qd[b, value_head(h), :]) for h, i in tiles
        }
        outs = [k.dq[head(h), :] for h in range(H)]
        _, grads = score_grads(allowed, scores, dots, [k.st[b]] * 2)
        for h, i in tiles:
            outs[h] += mm_nn(k.kv[bands[i], head(h), :], grads[h, i])
        for h in range(H):
            k.dq[head(h), :] = outs[h]

    grads4(0)
    grads4(1)
    ag_wait_relay("q", q_at, 0)
    ag_arrived("q", q_all)

    def backward_bands(bands):
        tiles = [(h, i) for h in range(H) for i in range(len(bands))]
        allowed = [my_column == id_row(band) for band in bands]
        scores = {(h, i): mm_tn(k.kv[b, head(h), :], k.qd[bands[i], head(h), :]) for h, i in tiles}
        dots = {
            (h, i): mm_tn(k.kv[b, value_head(h), :], k.qd[bands[i], value_head(h), :]) for h, i in tiles
        }
        key_outs = [k.dk[head(h), :] for h in range(H)]
        value_outs = [k.dv[head(h), :] for h in range(H)]
        probs, grads = score_grads(allowed, scores, dots, [k.st[band] for band in bands])
        for h, i in tiles:
            key_outs[h] += mm_nt(k.qd[bands[i], head(h), :], grads[h, i])
            value_outs[h] += mm_nt(k.qd[bands[i], value_head(h), :], probs[h, i].astype(BF16))
        for h in range(H):
            k.dk[head(h), :] = key_outs[h]
            k.dv[head(h), :] = value_outs[h]

    da_kinds = (
        ("da0", da_at(0), da_all(0)),
        ("da1", da_at(1), da_all(1)),
        ("st", st_at, st_all),
    )
    for name, at, all_at in da_kinds:
        ag_pass_on(name, at, all_at)
    for name, at, all_at in da_kinds:
        ag_arrived(name, all_at)

    for name, at, _ in da_kinds:
        ag_wait_relay(name, at, 0)
    backward_bands([b, sib])
    def backward_loop(start, stop):
        @pl.loop(start, stop)
        def _(i):
            backward_bands([band_same(i), band_sib(i)])

    backward_loop(1, s.half // 2)
    grads5(0)
    backward_loop(s.half // 2, s.half - s.half // 4)
    backward_loop(s.half - s.half // 4, s.half)
    k.dp[0] = (k.dq[...] * SCALE).astype(BF16)
    k.dp[1] = k.dk[...].astype(BF16)
    k.dp[2] = k.dv[...].astype(BF16)
    for h in range(2):
        k.ngp[half(h), :] = mm_tn(
            k.dp[:, :, half(h)].reshape(3 * W, T), k.qkv[...].reshape(3 * W, D)
        ).astype(BF16)
        rs_start("zng", h, k.ngp, k.ngr)
    grads5(1)
    base = s.bases[2]
    for h in range(2):
        gather_wait("zn2g", h, k.n2g)
    n2_grad = k.n2g[...].astype(F32)
    gain2_grad = jnp.sum(n2_grad * k.u2[...], axis=0, keepdims=True)
    bias2_grad = jnp.sum(n2_grad, axis=0, keepdims=True)
    middle_grad = middle_backward(n2_grad, pl.ds(0, L))
    k.cot[...] = middle_grad
    k.gsrc[base : base + W, :] = mm_nn(k.att[t], middle_grad.astype(BF16)).astype(BF16)
    k.gsrc[base + W : base + 2 * W, :] = mm_nn(k.dp[0], k.normed[...]).astype(BF16)
    grads1(2)

    base = s.bases[3]
    k.gsrc[base : base + 2 * W, :] = mm_nn(k.dp[1:3].reshape(2 * W, L), k.normed[...]).astype(BF16)
    grads1(3)
    grads6(0)
    direct2(2)
    k.ngg[piece(0, t), :] = rs_sum("zng", 0, k.ngp, k.ngr).astype(BF16)
    gather_start("zngg", 0, k.ngg)
    direct2(3)
    grads6(1)
    k.ngg[piece(1, t), :] = rs_sum("zng", 1, k.ngp, k.ngr).astype(BF16)
    gather_start("zngg", 1, k.ngg)
    direct3(2)
    direct3(3)
    grads7(0)
    grads7(1)
    swap_wait("ent", every)
    k.ent_sum[...] = jnp.sum(k.ent[...], axis=0)
    ent_copy = pltpu.make_async_copy(k.ent_sum, o_ent, k.stores.at[6])
    ent_copy.start()
    gain1_grad = jnp.zeros((1, D), F32)
    bias1_grad = jnp.zeros((1, D), F32)
    lead_grad = jnp.zeros((s.leads, D), F32)
    for h in range(2):
        rows = half(h)
        gather_wait("zngg", h, k.ngg)
        n1_grad = k.ngg[rows, :].astype(F32)
        unit1 = k.u1[rows, :]
        gain1_grad += jnp.sum(n1_grad * unit1, axis=0, keepdims=True)
        bias1_grad += jnp.sum(n1_grad, axis=0, keepdims=True)
        hidden_grad = k.cot[rows, :] + norm_backward(n1_grad, unit1, k.r1[rows, :], row_of(k.gain1))
        k.patches[rows, :] = hidden_grad
        coarse = hidden_grad.astype(BF16)
        fine = (hidden_grad - coarse.astype(F32)).astype(BF16)
        hot = lead_hot[:, h * T : (h + 1) * T]
        lead_grad += mm_nn(hot, coarse) + mm_nn(hot, fine)
        if h == 0:
            direct6(2)
            direct6(3)
    k.vb[near[1]] = lead_grad.astype(BF16)
    swap_start("vb", near)
    hidden_copy = pltpu.make_async_copy(k.patches, o_hidden, k.stores.at[5])
    hidden_copy.start()
    lanes = D // 128
    packed = [
        x[:, 128 * i : 128 * (i + 1)]
        for x in (gain1_grad, bias1_grad, gain2_grad, bias2_grad)
        for i in range(lanes)
    ]
    packed.append(jnp.zeros((s.packed - 4 * lanes, 128), F32))
    k.vc[near[1]] = jnp.concatenate(packed, axis=0).astype(BF16)
    swap_start("vc", near)
    grads7(2)
    grads7(3)
    k.vb_sum[...] = swap_sum("vb")
    k.vc_sum[...] = swap_sum("vc")
    vb_copy = pltpu.make_async_copy(k.vb_sum, o_vb, k.stores.at[7])
    vc_copy = pltpu.make_async_copy(k.vc_sum, o_vc, k.stores.at[8])
    vb_copy.start()
    vc_copy.start()

    z_all("zmask", k.mask.at[pl.ds(0, nt - 1)]).wait_send()
    z_all("zgate", k.gatec.at[pl.ds(0, nt - 1)]).wait_send()
    z_all("zow", ow_all).wait_send()
    for name in ("zowy", "zowr", "zowq"):
        ow_copy(name, ow_all, sib).wait_send()
    for h in range(2):
        z_all("zatt", k.att.at[pl.ds(0, nt - 1), :, half(h)], h).wait_send()
        z_all("zda", k.datok.at[h, pl.ds(0, nt - 1)], h).wait_send()
    rs_finish("zff", k.ffr)
    gather_finish("zblk", k.blow)
    rs_finish("zn2", k.n2r)
    gather_finish("zn2g", k.n2g)
    rs_finish("zng", k.ngr)
    gather_finish("zngg", k.ngg)
    ag_finish("kv", lambda count: k.kv.at[pl.ds(0, count)])
    ag_finish("q", q_all)
    ag_finish("da0", da_all(0))
    ag_finish("da1", da_all(1))
    ag_finish("st", st_all)
    swap_finish("cnt", every)
    swap_finish("ent", every)
    for i in range(4):
        grads_store(i).wait()
    for copy in (block_copy, hidden_copy, ent_copy, vb_copy, vc_copy):
        copy.wait()


def last_kernel(
    s, cuts, block, hidden, grads, ent, vb, vc,
    o_block, o_hidden, o_qkv, o_out, o_up, o_down, o_pen, o_lead, o_g1, o_b1, o_g2, o_b2, o_gate,
    low, wide, low_block, wide_block, keep, load_sem, store_sem,
):
    outs = {"down": o_down, "up": o_up, "out": o_out, "q": o_qkv.at[0], "k": o_qkv.at[1], "v": o_qkv.at[2]}
    loads = [
        pltpu.make_async_copy(block, low_block, load_sem.at[0]),
        pltpu.make_async_copy(hidden, keep, load_sem.at[1]),
    ]
    stores = [
        pltpu.make_async_copy(wide_block, o_block, store_sem.at[0]),
        pltpu.make_async_copy(keep, o_hidden, store_sem.at[1]),
    ]
    for i, (row, name, start, size) in enumerate(cuts):
        rows = pl.ds(row, size)
        loads.append(pltpu.make_async_copy(grads.at[rows], low.at[rows], load_sem.at[i + 2]))
        stores.append(
            pltpu.make_async_copy(wide.at[rows], outs[name].at[pl.ds(start, size)], store_sem.at[i + 2])
        )
    gate_rows = pl.ds(s.bases[1] + s.D, 32)
    gate_load = pltpu.make_async_copy(grads.at[gate_rows], low.at[gate_rows], load_sem.at[len(cuts) + 2])
    for copy in loads + [gate_load]:
        copy.start()
    loads[0].wait()
    wide_block[...] = low_block[...].astype(F32)
    stores[0].start()
    loads[1].wait()
    stores[1].start()
    for i, (row, name, start, size) in enumerate(cuts):
        loads[i + 2].wait()
        rows = pl.ds(row, size)
        wide[rows, :] = low[rows, :].astype(F32)
        stores[i + 2].start()
    gate_load.wait()
    small = low[gate_rows, :].astype(F32)
    for e in range(3):
        o_gate[e] = small[8 * e : 8 * e + 4]
    o_pen[...] = ent[0:1, 0:1]
    o_lead[...] = vb[...]
    lanes = s.D // 128
    for i, out in enumerate((o_g1, o_b1, o_g2, o_b2)):
        for j in range(lanes):
            row = i * lanes + j
            out[128 * j : 128 * (j + 1)] = vc[row : row + 1, :].reshape(128)
    for copy in stores:
        copy.wait()


def local(
    nb,
    nt,
    patches,
    window_ids,
    lead_index,
    lead_table,
    attention_gain,
    attention_bias,
    query_key_value,
    out_weight,
    feedforward_gain,
    feedforward_bias,
    up_weight,
    down_weight,
    gate_head,
    pixel_mask,
    cotangent,
):
    L, D = patches.shape
    leads = lead_table.shape[0]
    W = out_weight.shape[0]
    F = up_weight.shape[1]
    s = dims_of(nb, nt, L, D, W, F, leads, L * nb * pixel_mask.shape[0] * nt)
    scratch = scratch_of(s)
    vm = pl.BlockSpec(memory_space=pltpu.VMEM)
    block, hidden, grads, ent, vb, vc = pl.pallas_call(
        partial(main_kernel, s, tuple(scratch)),
        out_shape=(
            jax.ShapeDtypeStruct((L, D), BF16),
            jax.ShapeDtypeStruct((L, D), F32),
            jax.ShapeDtypeStruct((s.rows, D), BF16),
            jax.ShapeDtypeStruct((8, 128), F32),
            jax.ShapeDtypeStruct((leads, D), F32),
            jax.ShapeDtypeStruct((s.packed, 128), F32),
        ),
        in_specs=[pl.BlockSpec(memory_space=pltpu.HBM)] * 15,
        out_specs=(pl.BlockSpec(memory_space=pl.ANY),) * 6,
        scratch_shapes=list(scratch.values()),
        compiler_params=pltpu.CompilerParams(
            collective_id=0,
            has_side_effects=True,
            vmem_limit_bytes=VMEM_LIMIT,
        ),
        cost_estimate=pl.CostEstimate(
            flops=2 * s.rows * D * L * 3 + 14 * L * nb * L * W, bytes_accessed=16 * 2**20, transcendentals=0
        ),
        name="block_step",
    )(
        patches,
        window_ids,
        lead_index,
        lead_table,
        attention_gain,
        attention_bias,
        jnp.transpose(query_key_value, (0, 2, 1)),
        out_weight,
        feedforward_gain,
        feedforward_bias,
        up_weight,
        down_weight,
        gate_head,
        pixel_mask,
        cotangent,
    )
    vec = jax.ShapeDtypeStruct((D,), F32)
    cuts = []
    first = s.bases[2]
    places = (
        ("down", 0, F),
        ("up", F, D),
        ("out", first, W),
        ("q", first + W, W),
        ("k", s.bases[3], W),
        ("v", s.bases[3] + W, W),
    )
    for name, row, size in places:
        for start in range(0, size, 384):
            cuts.append((row + start, name, start, min(384, size - start)))
    hbm = pl.BlockSpec(memory_space=pl.ANY)
    wide, high, qkv_grad, out_grad, up_grad, down_grad, pen, lead, g1, b1, g2, b2, gates = pl.pallas_call(
        partial(last_kernel, s, cuts),
        out_shape=(
            jax.ShapeDtypeStruct((L, D), F32),
            jax.ShapeDtypeStruct((L, D), F32),
            jax.ShapeDtypeStruct((3, W, D), F32),
            jax.ShapeDtypeStruct((W, D), F32),
            jax.ShapeDtypeStruct((D, F), F32),
            jax.ShapeDtypeStruct((F, D), F32),
            jax.ShapeDtypeStruct((1, 1), F32),
            jax.ShapeDtypeStruct((leads, D), F32),
            vec,
            vec,
            vec,
            vec,
            jax.ShapeDtypeStruct(gate_head.shape, F32),
        ),
        in_specs=[hbm] * 3 + [vm] * 3,
        out_specs=(hbm,) * 6 + (vm,) * 7,
        scratch_shapes=[
            pltpu.VMEM((s.rows, D), BF16),
            pltpu.VMEM((s.rows, D), F32),
            pltpu.VMEM((L, D), BF16),
            pltpu.VMEM((L, D), F32),
            pltpu.VMEM((L, D), F32),
            pltpu.SemaphoreType.DMA((len(cuts) + 3,)),
            pltpu.SemaphoreType.DMA((len(cuts) + 2,)),
        ],
        compiler_params=pltpu.CompilerParams(vmem_limit_bytes=VMEM_LIMIT),
        name="write_out",
    )(block, hidden, grads, ent, vb, vc)
    return (
        wide,
        pen.reshape(()),
        high,
        lead,
        g1,
        b1,
        jnp.transpose(qkv_grad, (0, 2, 1)),
        out_grad,
        g2,
        b2,
        up_grad,
        down_grad,
        gates,
    )


def solution(mesh):
    in_specs = (
        P("blk", None),
        P(),
        P("blk"),
        P(),
        P(),
        P(),
        P(None, None, "tp"),
        P("tp", None),
        P(),
        P(),
        P(None, "tp"),
        P("tp", None),
        P(None, "tp", None),
        P("tp", "blk"),
        P("blk", None),
    )
    out_specs = (
        P("blk", None),
        P(),
        P("blk", None),
        P(),
        P(),
        P(),
        P(None, None, "tp"),
        P("tp", None),
        P(),
        P(),
        P(None, "tp"),
        P("tp", None),
        P(None, "tp", None),
    )
    return jax.shard_map(
        partial(local, mesh.shape["blk"], mesh.shape["tp"]),
        mesh=mesh,
        in_specs=in_specs,
        out_specs=out_specs,
        check_vma=False,
    )
```
